32 devices in a mesh: sub: 8 (over z, core), root: 4 (over y, x).
Axes of the slice: x: 2, y: 2, z: 4, core: 2. Of those that a mesh axis runs over, the one named last changes fastest.
Arguments:
- right_side: bfloat16 [4, 16384, 256], P('root', 'sub'), may hold values from -6 to 6
- leaf_inverse: bfloat16 [4, 16384, 512], P('root', 'sub'), may hold values from -0.25 to 0.25
- leaf_basis: bfloat16 [4, 16384, 256], P('root', 'sub'), may hold values from -0.25 to 0.25
- local_merge: bfloat16 [4, 12288, 512], P('root', 'sub'), may hold values from -0.25 to 0.25
- local_transfer: bfloat16 [4, 12288, 256], P('root', 'sub'), may hold values from -0.25 to 0.25
- upper_merge: bfloat16 [4, 3584, 512], P('root', 'sub'), may hold values from -0.25 to 0.25
- upper_transfer: bfloat16 [4, 3584, 256], P('root', 'sub'), may hold values from -0.25 to 0.25
- top_inverse: bfloat16 [1024, 1024], P('root', 'sub'), may hold values from -0.1875 to 0.1875
Outputs:
- solution: float32 [4, 16384, 256], P('root', 'sub')
The draws below stay inside these ranges and needn't reach their ends.
All inputs are finite; a program needn't handle non-finite values.
Results may differ from the reference program's by a relative error of at most 0.02.
Values may be sent and summed in bfloat16 or wider, within the bound.
No kernel may reach another device: no remote copies, remote signals or barrier semaphores. Data moves between devices by JAX's collectives and lax.ppermute only.
A program may use at most 128 MiB of HBM per device.

```python
import jax
import jax.numpy as jnp
from jax import lax

LEAF = 512
RANK = 256
NRHS = 256
LEAVES_DEV = 4
LOG_LEAF = 2
LOG_SUB = 3
UPPER_ROWS = 448
TOP_ORDER = 1024
N_SUB = 8
N_ROOT = 4


def block_scale(key, dims, split, low, high):
    gain = 1.0
    for axis_at, shards_of in split:
        steps = jax.random.uniform(jax.random.fold_in(jax.random.fold_in(key, 6), axis_at), (shards_of,), jnp.float32, low / len(split), high / len(split))
        gain = gain * jnp.repeat(jnp.exp(steps), dims[axis_at] // shards_of).reshape((-1,) + (1,) * (len(dims) - 1 - axis_at))
    return gain


def centred(stream_key, shape, width, limit, shards=(), kind=jnp.bfloat16):
    gain = block_scale(stream_key, shape, shards, -0.22, 0.18) if shards else 1.0
    array = jax.random.normal(stream_key, shape, jnp.float32) * width * gain
    return jnp.minimum(jnp.maximum(array, -limit), limit).astype(kind)


def setup_inputs(seed: int = 0) -> dict:
    keys = jax.random.split(jax.random.key(seed), 9)
    return {
        "right_side": centred(keys[0], (N_ROOT, N_SUB * LEAVES_DEV * LEAF, NRHS), 1.0, 6.0, ((0, 4), (1, 8))),
        "leaf_inverse": centred(keys[1], (N_ROOT, N_SUB * LEAVES_DEV * LEAF, LEAF), LEAF ** -0.5, 0.25, ((0, 4), (1, 8))),
        "leaf_basis": centred(keys[2], (N_ROOT, N_SUB * LEAVES_DEV * LEAF, RANK), LEAF ** -0.5, 0.25, ((0, 4), (1, 8))),
        "local_merge": centred(keys[3], (N_ROOT, N_SUB * (LEAVES_DEV - 1) * 2 * RANK, 2 * RANK), (2 * RANK) ** -0.5, 0.25, ((0, 4), (1, 8))),
        "local_transfer": centred(keys[4], (N_ROOT, N_SUB * (LEAVES_DEV - 1) * 2 * RANK, RANK), (2 * RANK) ** -0.5, 0.25, ((0, 4), (1, 8))),
        "upper_merge": centred(keys[5], (N_ROOT, N_SUB * UPPER_ROWS, 2 * RANK), (2 * RANK) ** -0.5, 0.25, ((0, 4), (1, 8))),
        "upper_transfer": centred(keys[6], (N_ROOT, N_SUB * UPPER_ROWS, RANK), (2 * RANK) ** -0.5, 0.25, ((0, 4), (1, 8))),
        "top_inverse": centred(keys[7], (TOP_ORDER, TOP_ORDER), TOP_ORDER ** -0.5, 0.1875, ((0, 4), (1, 8))),
    }


def batch_product(left, right):
    return jnp.einsum("nij,njk->nik", left.astype(jnp.float32), right.astype(jnp.float32))


def batch_transposed(left, right):
    return jnp.einsum("nji,njk->nik", left.astype(jnp.float32), right.astype(jnp.float32))


def merge_up(coeffs, merge_mat, transfer):
    paired = coeffs.astype(jnp.bfloat16).reshape(merge_mat.shape[0], 2 * RANK, NRHS)
    inner_part = batch_product(merge_mat, paired)
    parent = batch_transposed(transfer, inner_part.astype(jnp.bfloat16))
    return inner_part, parent


def merge_down(parent, inner_part, merge_mat, transfer):
    lifted = batch_product(transfer, parent.astype(jnp.bfloat16)).astype(jnp.bfloat16)
    children = inner_part - batch_product(merge_mat, lifted)
    return children.reshape(-1, RANK, NRHS)


def local_level(block, tier_no):
    node_count = LEAVES_DEV >> tier_no
    start = LEAVES_DEV - 2 * node_count
    shaped = block.reshape(N_SUB, LEAVES_DEV - 1, 2 * RANK, block.shape[-1])
    return shaped[:, start:start + node_count].reshape(N_SUB * node_count, 2 * RANK, block.shape[-1])


def upper_level(block, tier_no):
    height = (2 * RANK) >> tier_no
    offset = 2 * RANK - 2 * height
    shaped = block.reshape(N_SUB, block.shape[0] // N_SUB, block.shape[-1])
    return shaped[:, offset:offset + height].reshape(N_SUB >> tier_no, 2 * RANK, block.shape[-1])


def climb(operands):
    right_side, leaf_inv, basis_block, local_m, local_w, upper_m, upper_w = operands
    leaves = N_SUB * LEAVES_DEV
    solved = batch_product(leaf_inv.reshape(leaves, LEAF, LEAF), right_side.reshape(leaves, LEAF, NRHS))
    coeffs = batch_transposed(basis_block.reshape(leaves, LEAF, RANK), solved.astype(jnp.bfloat16))
    inner_saved = []
    for tier_no in range(1, LOG_LEAF + 1):
        inner_part, coeffs = merge_up(coeffs, local_level(local_m, tier_no), local_level(local_w, tier_no))
        inner_saved.append(inner_part)
    for tier_no in range(1, LOG_SUB + 1):
        inner_part, coeffs = merge_up(coeffs, upper_level(upper_m, tier_no), upper_level(upper_w, tier_no))
        inner_saved.append(inner_part)
    return solved, tuple(inner_saved), coeffs[0].astype(jnp.bfloat16)


def descend(operands):
    coupling, solved, inner_saved, leaf_inv, basis_block, local_m, local_w, upper_m, upper_w = operands
    leaves = N_SUB * LEAVES_DEV
    parent = coupling[None]
    for tier_no in range(LOG_SUB, 0, -1):
        parent = merge_down(parent, inner_saved[LOG_LEAF + tier_no - 1], upper_level(upper_m, tier_no), upper_level(upper_w, tier_no))
    for tier_no in range(LOG_LEAF, 0, -1):
        parent = merge_down(parent, inner_saved[tier_no - 1], local_level(local_m, tier_no), local_level(local_w, tier_no))
    spread = batch_product(basis_block.reshape(leaves, LEAF, RANK), parent.astype(jnp.bfloat16)).astype(jnp.bfloat16)
    result = solved - batch_product(leaf_inv.reshape(leaves, LEAF, LEAF), spread)
    return result.reshape(leaves * LEAF, NRHS)


def reference(right_side, leaf_inverse, leaf_basis, local_merge, local_transfer, upper_merge, upper_transfer, top_inverse):
    solved, inner_saved, roots = lax.map(climb, (right_side, leaf_inverse, leaf_basis, local_merge, local_transfer, upper_merge, upper_transfer))
    stacked = roots.reshape(N_ROOT * RANK, NRHS)
    coupling = jnp.dot(top_inverse, stacked, preferred_element_type=jnp.float32).reshape(N_ROOT, RANK, NRHS)
    return lax.map(descend, (coupling, solved, inner_saved, leaf_inverse, leaf_basis, local_merge, local_transfer, upper_merge, upper_transfer))
```

```python
import jax
import jax.numpy as jnp
from jax import lax
from jax.sharding import PartitionSpec as P

BF16 = jnp.bfloat16
F32 = jnp.float32


def product(left, right):
    return jnp.einsum("nij,njk->nik", left, right, preferred_element_type=F32)


def product_left_transposed(left, right):
    return jnp.einsum("nji,njk->nik", left, right, preferred_element_type=F32)


def product_right_transposed(left, right):
    return jnp.einsum("nij,nkj->nik", left, right, preferred_element_type=F32)


def flip(block, axis, mask):
    count = lax.axis_size(axis)
    return lax.ppermute(block, axis, [(i, i ^ mask) for i in range(count)])


def ordered(first, mine, other, axis):
    return jnp.where(
        first, jnp.concatenate([mine, other], axis), jnp.concatenate([other, mine], axis)
    )


def hop(block, source, target, chips):
    pairs = []
    for core in range(2):
        pairs.append((2 * source + core, 2 * target + core))
        pairs.append((2 * (chips - 1 - source) + core, 2 * (chips - 1 - target) + core))
    return lax.ppermute(block, "sub", pairs)


def climb_node(paired, merge_mat, transfer):
    inner = product_right_transposed(paired, merge_mat).astype(BF16)
    return product(inner, transfer).astype(BF16)


def descend_node(parent, paired, merge_mat, transfer):
    lifted = product_right_transposed(parent, transfer)
    rest = (paired.astype(F32) - lifted).astype(BF16)
    return product_right_transposed(rest, merge_mat).astype(BF16)


def body(
    right_side,
    leaf_inverse,
    leaf_basis,
    local_merge,
    local_transfer,
    upper_merge,
    upper_transfer,
    top_inverse,
):
    leaf_size = leaf_inverse.shape[2]
    rank = leaf_basis.shape[2]
    columns = right_side.shape[2]
    double = 2 * rank
    leaf_count = right_side.shape[1] // leaf_size
    leaf_depth = leaf_count.bit_length() - 1
    sub_count = lax.axis_size("sub")
    sub_depth = sub_count.bit_length() - 1
    root_count = lax.axis_size("root")
    chips = sub_count // 2
    middle = chips // 2 - 1
    position = lax.axis_index("sub")
    root_at = lax.axis_index("root")
    chip = position // 2
    core_0 = position % 2 == 0
    lower = chip < chips // 2
    near_chip = jnp.where(lower, chip, chips - 1 - chip)

    split = double >> 1
    pack = jnp.concatenate([upper_merge[0, split:], upper_transfer[0, split:]], 1)
    pair_pack = jnp.concatenate([upper_merge[0, :split], upper_transfer[0, :split]], 1)
    pair_other = flip(pair_pack, "sub", 1)
    packs, tops = [], []
    for source in range(chips):
        packs.append(pack if source == middle else hop(pack, source, middle, chips))
    for source in range(chips):
        tops.append(top_inverse if source == middle else hop(top_inverse, source, middle, chips))

    leaf_inv = leaf_inverse.reshape(leaf_count, leaf_size, leaf_size)
    basis = leaf_basis.reshape(leaf_count, leaf_size, rank)
    sides = right_side.reshape(leaf_count, leaf_size, columns)
    local_m = local_merge.reshape(leaf_count - 1, double, double)
    local_w = local_transfer.reshape(leaf_count - 1, double, rank)
    solved = product(leaf_inv, sides).astype(BF16)
    coeffs = product_left_transposed(basis, solved).astype(BF16)
    local_paired = []
    for tier in range(1, leaf_depth + 1):
        nodes = leaf_count >> tier
        start = leaf_count - 2 * nodes
        paired = coeffs.reshape(nodes, double, columns)
        local_paired.append(paired)
        inner = product(local_m[start : start + nodes], paired).astype(BF16)
        if tier < leaf_depth:
            coeffs = product_left_transposed(local_w[start : start + nodes], inner).astype(BF16)
        else:
            coeffs = product_left_transposed(inner, local_w[start : start + nodes]).astype(BF16)
    own = coeffs[0]

    other_packs = [flip(item, "sub", 1) for item in packs]
    other_tops = [flip(item, "sub", 1) for item in tops]

    half = columns // 2
    pair_both = ordered(core_0, pair_pack, pair_other, 0)[None]
    pair_m, pair_w = pair_both[:, :, :double], pair_both[:, :, double:]
    keep = jnp.where(core_0, own[:half], own[half:])
    send = jnp.where(core_0, own[half:], own[:half])
    pair_paired = ordered(core_0, keep, flip(send, "sub", 1), 1)[None]
    pair_coeffs = climb_node(pair_paired, pair_m, pair_w)[0]

    quarter = half // 2
    near = jnp.where(lower, pair_coeffs[:quarter], pair_coeffs[quarter:])
    far = jnp.where(lower, pair_coeffs[quarter:], pair_coeffs[:quarter])
    parts = []
    for source in range(chips):
        if source == middle:
            parts.append(near)
        else:
            parts.append(hop(near if source < middle else far, source, middle, chips))

    def natural(items):
        return [jnp.where(lower, items[i], items[chips - 1 - i]) for i in range(chips)]

    ordered_packs = natural(
        [ordered(core_0, mine, other, 0) for mine, other in zip(packs, other_packs)]
    )
    ordered_tops = natural(
        [ordered(core_0, mine, other, 1) for mine, other in zip(tops, other_tops)]
    )
    upper = []
    rows = pack.shape[0]
    for tier in range(2, sub_depth + 1):
        height = double >> tier
        offset = double - 2 * height - split
        pieces = []
        for item in ordered_packs:
            pieces += [item[offset : offset + height], item[rows + offset : rows + offset + height]]
        whole = jnp.concatenate(pieces, 0).reshape(sub_count >> tier, double, double + rank)
        upper.append((whole[:, :, :double], whole[:, :, double:]))
    top_rows = jnp.concatenate(ordered_tops, 1)

    level = jnp.stack(natural(parts))
    upper_paired = []
    for merge_mat, transfer in upper:
        level = level.reshape(-1, 2, quarter, rank)
        paired = jnp.concatenate([level[:, 0], level[:, 1]], 2)
        upper_paired.append(paired)
        level = climb_node(paired, merge_mat, transfer)

    roots = [level[0]]
    for mask in range(1, root_count):
        roots.append(flip(level[0], "root", mask))
    bit = 1
    while bit < root_count:
        swap = root_at & bit != 0
        roots = [jnp.where(swap, roots[i ^ bit], roots[i]) for i in range(root_count)]
        bit *= 2
    stacked = jnp.concatenate(roots, 1)
    level = product_right_transposed(stacked[None], top_rows[None]).astype(BF16)

    for (merge_mat, transfer), paired in zip(upper[::-1], upper_paired[::-1]):
        children = descend_node(level, paired, merge_mat, transfer)
        level = jnp.stack([children[:, :, :rank], children[:, :, rank:]], 1).reshape(
            -1, quarter, rank
        )

    parts = natural([level[i] for i in range(chips)])
    near, far = parts[middle], None
    for target in range(chips):
        if target == middle:
            continue
        part = hop(parts[target], middle, target, chips)
        if target < middle:
            near = jnp.where(near_chip == target, part, near)
        else:
            far = part if far is None else jnp.where(near_chip == chips - 1 - target, part, far)
    parent = ordered(lower, near, far, 0)[None]

    children = descend_node(parent, pair_paired, pair_m, pair_w)[0]
    keep = jnp.where(core_0, children[:, :rank], children[:, rank:])
    send = jnp.where(core_0, children[:, rank:], children[:, :rank])
    parent = ordered(core_0, keep, flip(send, "sub", 1), 0)[None]

    for tier in range(leaf_depth, 0, -1):
        nodes = leaf_count >> tier
        start = leaf_count - 2 * nodes
        transfer = local_w[start : start + nodes]
        if tier == leaf_depth:
            lifted = product_right_transposed(transfer, parent)
        else:
            lifted = product(transfer, parent)
        rest = (local_paired[tier - 1].astype(F32) - lifted).astype(BF16)
        children = product(local_m[start : start + nodes], rest).astype(BF16)
        parent = children.reshape(2 * nodes, rank, columns)
    rest = (sides.astype(F32) - product(basis, parent)).astype(BF16)
    return product(leaf_inv, rest).reshape(1, leaf_count * leaf_size, columns)


def solution(mesh):
    return jax.shard_map(
        body,
        mesh=mesh,
        in_specs=(
            P("root", "sub", None),
            P("root", "sub", None),
            P("root", "sub", None),
            P("root", "sub", None),
            P("root", "sub", None),
            P("root", "sub", None),
            P("root", "sub", None),
            P("root", "sub"),
        ),
        out_specs=P("root", "sub", None),
        check_vma=False,
    )
```

```python
import functools

import jax
import jax.numpy as jnp
from jax import lax
from jax.experimental import pallas as pl
from jax.experimental.pallas import tpu as pltpu
from jax.sharding import PartitionSpec as P

BF16 = jnp.bfloat16
F32 = jnp.float32
MIB = 1 << 20


def dot(left, right):
    return lax.dot_general(left, right, (((1,), (0,)), ((), ())), preferred_element_type=F32)


def dot_left_t(left, right):
    return lax.dot_general(left, right, (((0,), (0,)), ((), ())), preferred_element_type=F32)


def dot_right_t(left, right):
    return lax.dot_general(left, right, (((1,), (1,)), ((), ())), preferred_element_type=F32)


def vmem_call(kernel, outs, args, scratch=(), limit=4 * MIB):
    return pl.pallas_call(
        kernel,
        out_shape=[pltpu.VMEM(shape, BF16) for shape in outs],
        in_specs=[pl.BlockSpec(memory_space=pltpu.VMEM)] * len(args),
        out_specs=[pl.BlockSpec(memory_space=pltpu.VMEM)] * len(outs),
        scratch_shapes=list(scratch),
        compiler_params=pltpu.CompilerParams(vmem_limit_bytes=limit),
        cost_estimate=pl.CostEstimate(flops=1, bytes_accessed=1, transcendentals=0),
    )(*[pltpu.with_memory_space_constraint(a, pltpu.VMEM) for a in args])


def flip(block, axis, mask):
    count = lax.axis_size(axis)
    return lax.ppermute(block, axis, [(i, i ^ mask) for i in range(count)])


def held(blocks, *until):
    return lax.optimization_barrier((blocks, until))[0]


def hop(block, source, target, chips):
    pairs = []
    for core in range(2):
        pairs.append((2 * source + core, 2 * target + core))
        pairs.append((2 * (chips - 1 - source) + core, 2 * (chips - 1 - target) + core))
    return lax.ppermute(block, "sub", pairs)


def core_of():
    return lax.axis_index("sub") % 2


def chip_of():
    return lax.axis_index("sub") // 2


def in_lower(chips):
    return chip_of() < chips // 2


def mirrored(chip, chips):
    return jnp.where(in_lower(chips), chip, chips - 1 - chip)


def split_rows(value, first, keep, send, work):
    half = value.shape[0] // 2
    work[...] = value
    keep[...] = work[pl.ds(pl.multiple_of(first * half, half), half), :]
    send[...] = work[pl.ds(pl.multiple_of((1 - first) * half, half), half), :]


def split_lanes(value, first, keep, send, work):
    half = value.shape[1] // 2
    work[...] = value
    keep[...] = work[:, pl.ds(pl.multiple_of(first * half, half), half)]
    send[...] = work[:, pl.ds(pl.multiple_of((1 - first) * half, half), half)]


def join_rows(mine, other, first, work):
    half = mine.shape[0]
    work[pl.ds(pl.multiple_of(first * half, half), half), :] = mine
    work[pl.ds(pl.multiple_of((1 - first) * half, half), half), :] = other


def join_lanes(mine, other, first, work):
    half = mine.shape[1]
    work[:, pl.ds(pl.multiple_of(first * half, half), half)] = mine
    work[:, pl.ds(pl.multiple_of((1 - first) * half, half), half)] = other


def climb(paired, merge_mat, transfer):
    inner = dot_right_t(paired, merge_mat).astype(BF16)
    return dot(inner, transfer).astype(BF16)


def descend(parent, paired, merge_mat, transfer):
    rest = (paired.astype(F32) - dot_right_t(parent, transfer)).astype(BF16)
    return dot_right_t(rest, merge_mat).astype(BF16)


def pack_kernel(merge_ref, transfer_ref, pack_ref, quad_ref, high_ref, sems):
    rows, double = merge_ref.shape
    width = pack_ref.shape[1]
    quad_at, high_at = double // 2, double // 2 + double // 4
    places = [(pack_ref, 0, rows), (quad_ref, quad_at, high_at), (high_ref, high_at, rows)]
    copies = []
    for i, (target, low, high) in enumerate(places):
        copies.append(
            pltpu.make_async_copy(
                merge_ref.at[pl.ds(low, high - low), :],
                target.at[:, pl.ds(0, double)],
                sems.at[2 * i],
            )
        )
        copies.append(
            pltpu.make_async_copy(
                transfer_ref.at[pl.ds(low, high - low), :],
                target.at[:, pl.ds(double, width - double)],
                sems.at[2 * i + 1],
            )
        )
    for copy in copies:
        copy.start()
    for copy in copies:
        copy.wait()


def climb_local_kernel(
    sides_in, inverse_in, basis_in, merge_in, transfer_in, keep, send, low_paired, high_paired, sides,
    inverse, basis, merge, transfer, work, sems, *, leaf_count
):
    leaf = inverse.shape[1]
    rank = basis.shape[1]
    double = 2 * rank
    kept = {1: low_paired, 2: high_paired}
    depth = leaf_count.bit_length() - 1
    nodes = leaf_count - 1
    copies = []

    def fetch(source, target, low, size):
        rows = pl.ds(low, size)
        copies.append(
            pltpu.make_async_copy(source.at[rows, :], target.at[rows, :], sems.at[len(copies)])
        )
        copies[-1].start()

    for i in range(leaf_count):
        fetch(inverse_in, inverse, i * leaf, leaf)
        fetch(sides_in, sides, i * leaf, leaf)
        fetch(basis_in, basis, i * leaf, leaf)
    for e in range(nodes):
        fetch(merge_in, merge, e * double, double)
        fetch(transfer_in, transfer, e * double, double)
    for i in range(leaf_count):
        rows = pl.ds(i * leaf, leaf)
        copies[3 * i].wait()
        copies[3 * i + 1].wait()
        solved = dot(inverse[rows, :], sides[rows, :]).astype(BF16)
        copies[3 * i + 2].wait()
        coeffs = dot_left_t(solved, basis[rows, :]).astype(BF16)
        kept[1][i // 2, :, pl.ds((i % 2) * rank, rank)] = coeffs
    for tier in range(1, depth + 1):
        count = leaf_count >> tier
        start = leaf_count - 2 * count
        for e in range(count):
            rows = pl.ds((start + e) * double, double)
            copies[3 * leaf_count + 2 * (start + e)].wait()
            copies[3 * leaf_count + 2 * (start + e) + 1].wait()
            coeffs = climb(kept[tier][e], merge[rows, :], transfer[rows, :])
            if tier < depth:
                kept[tier + 1][e // 2, :, pl.ds((e % 2) * rank, rank)] = coeffs
            else:
                split_rows(coeffs, core_of(), keep, send, work)


def descend_local_kernel(
    mine, other, low_paired, high_paired, sides, inverse, basis, merge, transfer, out, parent, result,
    sems, *, leaf_count
):
    leaf = inverse.shape[1]
    rank = basis.shape[1]
    double = 2 * rank
    kept = {1: low_paired, 2: high_paired}
    depth = leaf_count.bit_length() - 1
    join_rows(mine[...], other[...], core_of(), parent)
    level = [parent[...]]
    for tier in range(depth, 0, -1):
        nodes = leaf_count >> tier
        start = leaf_count - 2 * nodes
        below = []
        for e in range(nodes):
            rows = pl.ds((start + e) * double, double)
            children = descend(level[e], kept[tier][e], merge[rows, :], transfer[rows, :])
            below += [children[:, :rank], children[:, rank:]]
        level = below
    copies = []
    for i in range(leaf_count):
        rows = pl.ds(i * leaf, leaf)
        spread = dot_right_t(basis[rows, :], level[i])
        rest = (sides[rows, :].astype(F32) - spread).astype(BF16)
        result[i] = dot(inverse[rows, :], rest)
        copies.append(pltpu.make_async_copy(result.at[i], out.at[rows, :], sems.at[i]))
        copies[-1].start()
    for copy in copies:
        copy.wait()


def pair_matrix_kernel(mine, other, out):
    half = out.shape[0] // 2
    core = core_of()
    out[pl.ds(pl.multiple_of(core * half, half), half), :] = mine[pl.ds(0, half), :]
    out[pl.ds(pl.multiple_of((1 - core) * half, half), half), :] = other[pl.ds(0, half), :]


def quad_matrix_kernel(mine, other, far, far_other, out):
    height = far.shape[0]
    core, side = core_of(), chip_of() % 2
    rows = pl.ds(2 * height, height)
    blocks = [(side, core, mine[rows, :]), (side, 1 - core, other[rows, :])]
    blocks += [(1 - side, core, far[...]), (1 - side, 1 - core, far_other[...])]
    for chip, which, value in blocks:
        at = pl.multiple_of((2 * chip + which) * height, height)
        out[pl.ds(at, height), :] = value


def stack_kernel(*refs):
    for i, ref in enumerate(refs[:-1]):
        refs[-1][i] = ref[...]


def high_matrix_kernel(mine, other, far, far_other, *outs, chips, first_row, heights):
    core, middle = core_of(), chips // 2 - 1
    offset = 0
    for out, height in zip(outs, heights):
        for source in range(chips):
            chip = mirrored(source, chips)
            for which, near, away in ((core, mine, far), (1 - core, other, far_other)):
                if source == middle:
                    value = near[pl.ds(first_row + offset, height), :]
                else:
                    value = away[source - (source > middle), pl.ds(offset, height), :]
                at = pl.multiple_of((2 * chip + which) * height, height)
                out[pl.ds(at, height), :] = value
        offset += height


def top_matrix_kernel(mine, other, out, *, chips):
    core = core_of()
    width = mine.shape[2]
    for source in range(chips):
        chip = mirrored(source, chips)
        for which, ref in ((core, mine), (1 - core, other)):
            at = pl.multiple_of((2 * chip + which) * width, width)
            out[:, pl.ds(at, width)] = ref[source]


def pair_up_kernel(mine, other, matrix, paired, keep, send, work):
    double = paired.shape[1]
    join_lanes(mine[...], other[...], core_of(), paired)
    coeffs = climb(paired[...], matrix[:, pl.ds(0, double)], matrix[:, pl.ds(double, double // 2)])
    split_rows(coeffs, chip_of() % 2, keep, send, work)


def quad_up_kernel(mine, other, matrix, paired, coeffs):
    double = paired.shape[1]
    join_lanes(mine[...], other[...], chip_of() % 2, paired)
    coeffs[...] = climb(
        paired[...], matrix[:, pl.ds(0, double)], matrix[:, pl.ds(double, double // 2)]
    )


def high_up_kernel(*refs, chips, levels):
    quads = chips // 2
    parts, matrices = refs[:quads], refs[quads : quads + levels]
    kept, coeffs = refs[quads + levels : quads + 2 * levels], refs[-1]
    rank = coeffs.shape[1]
    double = 2 * rank
    for i, part in enumerate(parts):
        at = jnp.where(in_lower(chips), i, quads - 1 - i)
        lanes = pl.ds(pl.multiple_of((at % 2) * rank, rank), rank)
        kept[0][at // 2, :, lanes] = part[...]
    for tier in range(levels):
        nodes = quads >> tier + 1
        for e in range(nodes):
            rows = pl.ds(e * double, double)
            matrix = matrices[tier]
            value = climb(
                kept[tier][e], matrix[rows, pl.ds(0, double)], matrix[rows, pl.ds(double, rank)]
            )
            if tier + 1 < levels:
                kept[tier + 1][e // 2, :, pl.ds((e % 2) * rank, rank)] = value
            else:
                coeffs[...] = value


def high_down_kernel(*refs, chips, levels, roots):
    quads = chips // 2
    own, top = refs[:roots], refs[roots]
    matrices = refs[roots + 1 : roots + 1 + levels]
    kept = refs[roots + 1 + levels : roots + 1 + 2 * levels]
    outs = refs[roots + 1 + 2 * levels : -2]
    stacked, below = refs[-2:]
    rank = outs[0].shape[1]
    double = 2 * rank
    me = lax.axis_index("root")
    for mask in range(roots):
        at = pl.multiple_of((me ^ mask) * rank, rank)
        stacked[:, pl.ds(at, rank)] = own[mask][...]
    level = [dot_right_t(stacked[...], top[...]).astype(BF16)]
    for tier in range(levels - 1, -1, -1):
        values = []
        for e in range(quads >> tier + 1):
            rows = pl.ds(e * double, double)
            matrix = matrices[tier]
            children = descend(
                level[e],
                kept[tier][e],
                matrix[rows, pl.ds(0, double)],
                matrix[rows, pl.ds(double, rank)],
            )
            values += [children[:, :rank], children[:, rank:]]
        level = values
    for i in range(quads):
        below[i] = level[i]
    for i in range(quads):
        outs[i][...] = below[jnp.where(in_lower(chips), i, quads - 1 - i)]


def quad_down_kernel(*refs, chips):
    own, parts, (paired, matrix, keep, send, work, parent) = refs[0], refs[1:-6], refs[-6:]
    double = paired.shape[1]
    at = chip_of()
    is_middle = (at == chips // 2 - 1) | (at == chips // 2)

    @pl.when(is_middle)
    def _():
        parent[...] = own[...]

    @pl.when(jnp.logical_not(is_middle))
    def _():
        total = parts[0][...].astype(F32)
        for part in parts[1:]:
            total += part[...].astype(F32)
        parent[...] = total.astype(BF16)

    children = descend(
        parent[...], paired[...], matrix[:, pl.ds(0, double)], matrix[:, pl.ds(double, double // 2)]
    )
    split_lanes(children, at % 2, keep, send, work)


def pair_down_kernel(mine, other, paired, matrix, keep, send, parent, work):
    double = paired.shape[1]
    join_rows(mine[...], other[...], chip_of() % 2, parent)
    children = descend(
        parent[...], paired[...], matrix[:, pl.ds(0, double)], matrix[:, pl.ds(double, double // 2)]
    )
    split_lanes(children, core_of(), keep, send, work)


def body(
    right_side,
    leaf_inverse,
    leaf_basis,
    local_merge,
    local_transfer,
    upper_merge,
    upper_transfer,
    top_inverse,
):
    leaf = leaf_inverse.shape[2]
    rank = leaf_basis.shape[2]
    columns = right_side.shape[2]
    double = 2 * rank
    wide = double + rank
    leaf_count = right_side.shape[1] // leaf
    sub_count = lax.axis_size("sub")
    sub_depth = sub_count.bit_length() - 1
    root_count = lax.axis_size("root")
    chips = sub_count // 2
    middle = chips // 2 - 1
    half, quarter = columns // 2, columns // 4
    others = [chip for chip in range(chips) if chip != middle]
    heights = [double >> tier for tier in range(3, sub_depth + 1)]
    levels = len(heights)
    quads = chips // 2
    odd = [chip for chip in range(1, chips, 2)]

    upper_m, upper_w = upper_merge[0], upper_transfer[0]
    upper_rows = upper_m.shape[0]
    high_row = double // 2 + double // 4

    any_spec, vmem_spec = pl.BlockSpec(memory_space=pl.ANY), pl.BlockSpec(memory_space=pltpu.VMEM)
    pack, quad, high = pl.pallas_call(
        pack_kernel,
        out_shape=[
            pltpu.VMEM((upper_rows, wide), BF16),
            pltpu.VMEM((double // 4, wide), BF16),
            pltpu.VMEM((upper_rows - high_row, wide), BF16),
        ],
        in_specs=[any_spec] * 2,
        out_specs=[vmem_spec] * 3,
        scratch_shapes=[pltpu.SemaphoreType.DMA((6,))],
        compiler_params=pltpu.CompilerParams(vmem_limit_bytes=2 * MIB),
        cost_estimate=pl.CostEstimate(flops=1, bytes_accessed=1, transcendentals=0),
    )(*[pltpu.with_memory_space_constraint(a, pltpu.HBM) for a in (upper_m, upper_w)])
    quad_far = flip(quad, "sub", 2)
    high_far = [hop(high, source, middle, chips) for source in others]
    pack_other = flip(pack, "sub", 1)

    given = [right_side[0], leaf_inverse[0], leaf_basis[0], local_merge[0], local_transfer[0]]
    shapes = [
        (half, rank),
        (half, rank),
        (leaf_count // 2, columns, double),
        (leaf_count // 4, columns, double),
    ] + [a.shape for a in given]
    keep, send, low_paired, high_paired, *local = pl.pallas_call(
        functools.partial(climb_local_kernel, leaf_count=leaf_count),
        out_shape=[pltpu.VMEM(shape, BF16) for shape in shapes],
        in_specs=[any_spec] * len(given),
        out_specs=[vmem_spec] * len(shapes),
        scratch_shapes=[
            pltpu.VMEM((columns, rank), BF16),
            pltpu.SemaphoreType.DMA((5 * leaf_count - 2,)),
        ],
        compiler_params=pltpu.CompilerParams(vmem_limit_bytes=16 * MIB),
        cost_estimate=pl.CostEstimate(flops=1, bytes_accessed=1, transcendentals=0),
    )(*[pltpu.with_memory_space_constraint(a, pltpu.HBM) for a in given])

    recv = flip(send, "sub", 1)
    pack_other, quad_far = held((pack_other, quad_far), send)
    quad_far_other = flip(quad_far, "sub", 1)
    (pair_matrix,) = vmem_call(pair_matrix_kernel, [(double, wide)], [pack, pack_other])
    pair_paired, keep, send = vmem_call(
        pair_up_kernel,
        [(half, double), (quarter, rank), (quarter, rank)],
        [keep, recv, pair_matrix],
        [pltpu.VMEM((half, rank), BF16)],
    )

    recv = flip(send, "sub", 2)
    quad_far_other, high_far, top = held((quad_far_other, high_far, top_inverse), send)
    (quad_matrix,) = vmem_call(
        quad_matrix_kernel, [(double, wide)], [pack, pack_other, quad_far, quad_far_other]
    )
    (high_stack,) = vmem_call(
        stack_kernel, [(len(others), upper_rows - high_row, wide)], high_far
    )
    high_stack_other = flip(high_stack, "sub", 1)
    tops = [
        top if source == middle else hop(top, source, middle, chips) for source in range(chips)
    ]
    quad_paired, coeffs = vmem_call(
        quad_up_kernel,
        [(quarter, double), (quarter, rank)],
        [keep, recv, quad_matrix],
    )

    parts = [coeffs if s == middle else hop(coeffs, s, middle, chips) for s in odd]
    high_stack_other = held(high_stack_other, coeffs)
    high_matrices = vmem_call(
        functools.partial(
            high_matrix_kernel, chips=chips, first_row=high_row, heights=heights
        ),
        [(sub_count * height, wide) for height in heights],
        [pack, pack_other, high_stack, high_stack_other],
        limit=8 * MIB,
    )
    *high_paired_up, coeffs = vmem_call(
        functools.partial(high_up_kernel, chips=chips, levels=levels),
        [(quads >> t + 1, quarter, double) for t in range(levels)] + [(quarter, rank)],
        parts + list(high_matrices),
        limit=8 * MIB,
    )

    roots = [coeffs] + [flip(coeffs, "root", mask) for mask in range(1, root_count)]
    tops = held(tops, coeffs)
    top_rows, top_width = top_inverse.shape
    (top_stack,) = vmem_call(stack_kernel, [(chips, top_rows, top_width)], tops)
    top_stack_other = flip(top_stack, "sub", 1)
    (top_matrix,) = vmem_call(
        functools.partial(top_matrix_kernel, chips=chips),
        [(top_rows, sub_count * top_width)],
        [top_stack, top_stack_other],
        limit=8 * MIB,
    )
    values = vmem_call(
        functools.partial(high_down_kernel, chips=chips, levels=levels, roots=root_count),
        [(quarter, rank)] * quads,
        roots + [top_matrix] + list(high_matrices) + list(high_paired_up),
        [
            pltpu.VMEM((quarter, root_count * rank), BF16),
            pltpu.VMEM((quads, quarter, rank), BF16),
        ],
        limit=8 * MIB,
    )

    own = values[odd.index(middle)]
    parts = [hop(value, middle, s, chips) for s, value in zip(odd, values) if s != middle]
    keep, send = vmem_call(
        functools.partial(quad_down_kernel, chips=chips),
        [(quarter, rank), (quarter, rank)],
        [own] + parts + [quad_paired, quad_matrix],
        [pltpu.VMEM((quarter, double), BF16), pltpu.VMEM((quarter, rank), BF16)],
    )
    recv = flip(send, "sub", 2)
    keep, send = vmem_call(
        pair_down_kernel,
        [(half, rank), (half, rank)],
        [keep, recv, pair_paired, pair_matrix],
        [pltpu.VMEM((half, rank), BF16), pltpu.VMEM((half, double), BF16)],
    )
    recv = flip(send, "sub", 1)

    args = [keep, recv, low_paired, high_paired] + local
    out = pl.pallas_call(
        functools.partial(descend_local_kernel, leaf_count=leaf_count),
        out_shape=jax.ShapeDtypeStruct((leaf_count * leaf, columns), F32),
        in_specs=[vmem_spec] * len(args),
        out_specs=any_spec,
        scratch_shapes=[
            pltpu.VMEM((columns, rank), BF16),
            pltpu.VMEM((leaf_count, leaf, columns), F32),
            pltpu.SemaphoreType.DMA((leaf_count,)),
        ],
        compiler_params=pltpu.CompilerParams(vmem_limit_bytes=16 * MIB),
        cost_estimate=pl.CostEstimate(flops=1, bytes_accessed=1, transcendentals=0),
    )(*[pltpu.with_memory_space_constraint(a, pltpu.VMEM) for a in args])
    return out[None]


def solution(mesh):
    return jax.shard_map(
        body,
        mesh=mesh,
        in_specs=(
            P("root", "sub", None),
            P("root", "sub", None),
            P("root", "sub", None),
            P("root", "sub", None),
            P("root", "sub", None),
            P("root", "sub", None),
            P("root", "sub", None),
            P("root", "sub"),
        ),
        out_specs=P("root", "sub", None),
        check_vma=False,
    )
```

```python
import functools

import jax
import jax.numpy as jnp
from jax import lax
from jax.experimental import pallas as pl
from jax.experimental.pallas import tpu as pltpu
from jax.sharding import PartitionSpec as P

BF16 = jnp.bfloat16
F32 = jnp.float32
MIB = 1 << 20


def dot(left, right):
    return lax.dot_general(left, right, (((1,), (0,)), ((), ())), preferred_element_type=F32)


def dot_left_t(left, right):
    return lax.dot_general(left, right, (((0,), (0,)), ((), ())), preferred_element_type=F32)


def dot_right_t(left, right):
    return lax.dot_general(left, right, (((1,), (1,)), ((), ())), preferred_element_type=F32)


def cost(micros):
    return pl.CostEstimate(flops=int(micros * 1e9), bytes_accessed=1, transcendentals=0)


def vmem_call(kernel, outs, args, scratch=(), limit=4 * MIB, micros=0.1, after=()):
    count = len(args)
    args = list(args) + list(after)
    return pl.pallas_call(
        lambda *refs: kernel(*refs[:count], *refs[len(args) :]),
        out_shape=[pltpu.VMEM(shape, BF16) for shape in outs],
        in_specs=[pl.BlockSpec(memory_space=pltpu.VMEM)] * len(args),
        out_specs=[pl.BlockSpec(memory_space=pltpu.VMEM)] * len(outs),
        scratch_shapes=list(scratch),
        compiler_params=pltpu.CompilerParams(vmem_limit_bytes=limit),
        cost_estimate=cost(micros),
    )(*[pltpu.with_memory_space_constraint(a, pltpu.VMEM) for a in args])


def mark_kernel(value, out):
    out[...] = value[pl.ds(0, out.shape[0]), pl.ds(0, out.shape[1])]


def mark(value):
    return vmem_call(mark_kernel, [(16, 128)], [value], micros=0.02)[0]


def flip(block, axis, mask):
    count = lax.axis_size(axis)
    return lax.ppermute(block, axis, [(i, i ^ mask) for i in range(count)])


def hop(block, source, target, chips):
    pairs = []
    for core in range(2):
        pairs.append((2 * source + core, 2 * target + core))
        pairs.append((2 * (chips - 1 - source) + core, 2 * (chips - 1 - target) + core))
    return lax.ppermute(block, "sub", pairs)


def core_of():
    return lax.axis_index("sub") % 2


def chip_of():
    return lax.axis_index("sub") // 2


def in_lower(chips):
    return chip_of() < chips // 2


def mirrored(chip, chips):
    return jnp.where(in_lower(chips), chip, chips - 1 - chip)


def split_rows(value, first, keep, send, work):
    half = value.shape[0] // 2
    work[...] = value
    keep[...] = work[pl.ds(pl.multiple_of(first * half, half), half), :]
    send[...] = work[pl.ds(pl.multiple_of((1 - first) * half, half), half), :]


def split_lanes(value, first, keep, send, work):
    half = value.shape[1] // 2
    work[...] = value
    keep[...] = work[:, pl.ds(pl.multiple_of(first * half, half), half)]
    send[...] = work[:, pl.ds(pl.multiple_of((1 - first) * half, half), half)]


def join_rows(mine, other, first, work):
    half = mine.shape[0]
    work[pl.ds(pl.multiple_of(first * half, half), half), :] = mine
    work[pl.ds(pl.multiple_of((1 - first) * half, half), half), :] = other


def join_lanes(mine, other, first, work):
    half = mine.shape[1]
    work[:, pl.ds(pl.multiple_of(first * half, half), half)] = mine
    work[:, pl.ds(pl.multiple_of((1 - first) * half, half), half)] = other


def climb(paired, merge_mat, transfer):
    inner = dot_right_t(paired, merge_mat).astype(BF16)
    return dot(inner, transfer).astype(BF16)


def descend(parent, paired, merge_mat, transfer):
    rest = (paired.astype(F32) - dot_right_t(parent, transfer)).astype(BF16)
    return dot_right_t(rest, merge_mat).astype(BF16)


def pack_kernel(merge, transfer, top, sides_in, inverse_in, basis_in, *refs):
    pair, quad_high, quad, high, sides, inverse, basis, sems = refs
    rows, double = merge.shape
    rank = transfer.shape[1]
    steps = []

    def fetch(source, target):
        steps.append(pltpu.make_async_copy(source, target, sems.at[len(steps)]))

    def level_rows(low, size, target, at):
        for lanes in range(double // rank):
            fetch(
                merge.at[pl.ds(low, size), pl.ds(lanes * rank, rank)], target.at[pl.ds(at, size), :]
            )
            at += size
        fetch(transfer.at[pl.ds(low, size), :], target.at[pl.ds(at, size), :])
        return at + size

    quad_low, high_low = double // 2, double // 2 + double // 4
    high_at = level_rows(quad_low, high_low - quad_low, quad_high, 0)
    at = level_rows(high_low, rows - high_low, quad_high, high_at)
    width = top.shape[1]
    size = top.shape[0] * width // rank
    for piece in range(rank // width):
        fetch(
            top.at[pl.ds(piece * size, size), :],
            quad_high.at[pl.ds(at, size), pl.ds(piece * width, width)],
        )
    level_rows(0, quad_low, pair, 0)
    for source, target in ((inverse_in, inverse), (sides_in, sides), (basis_in, basis)):
        fetch(source.at[pl.ds(0, target.shape[0]), :], target)
    for step in steps:
        step.start()
    for step in steps:
        step.wait()
    quad[...] = quad_high[pl.ds(0, high_at), :]
    high[...] = quad_high[pl.ds(high_at, high.shape[0]), :]


def climb_local_kernel(
    sides_in, inverse_in, basis_in, merge_in, transfer_in, sides_0, inverse_0, basis_0, keep, send,
    low_paired, high_paired, sides, inverse, basis, merge, transfer, work, sems
):
    leaf = inverse.shape[1]
    rank = basis.shape[1]
    double = 2 * rank
    kept = {1: low_paired, 2: high_paired}
    leaf_count = sides_in.shape[0] // leaf
    depth = leaf_count.bit_length() - 1
    nodes = leaf_count - 1
    copies = []

    def fetch(source, target, low, at, size):
        copies.append(
            pltpu.make_async_copy(
                source.at[pl.ds(low, size), :], target.at[pl.ds(at, size), :], sems.at[len(copies)]
            )
        )

    for i in range(1, leaf_count):
        fetch(inverse_in, inverse, i * leaf, (i - 1) * leaf, leaf)
        fetch(sides_in, sides, i * leaf, (i - 1) * leaf, leaf)
        fetch(basis_in, basis, i * leaf, (i - 1) * leaf, leaf)
    first = len(copies)
    for e in range(nodes):
        fetch(merge_in, merge, e * double, e * double, double)
        fetch(transfer_in, transfer, e * double, e * double, double)
    for copy in copies:
        copy.start()
    for i in range(leaf_count):
        rows = pl.ds(max(i - 1, 0) * leaf, leaf)
        if i:
            for copy in copies[3 * i - 3 : 3 * i]:
                copy.wait()
        arrays = (inverse, sides, basis) if i else (inverse_0, sides_0, basis_0)
        solved = dot(arrays[0][rows, :], arrays[1][rows, :]).astype(BF16)
        coeffs = dot_left_t(solved, arrays[2][rows, :]).astype(BF16)
        kept[1][i // 2, :, pl.ds((i % 2) * rank, rank)] = coeffs
    for tier in range(1, depth + 1):
        count = leaf_count >> tier
        start = leaf_count - 2 * count
        for e in range(count):
            rows = pl.ds((start + e) * double, double)
            for copy in copies[first + 2 * (start + e) : first + 2 * (start + e) + 2]:
                copy.wait()
            coeffs = climb(kept[tier][e], merge[rows, :], transfer[rows, :])
            if tier < depth:
                kept[tier + 1][e // 2, :, pl.ds((e % 2) * rank, rank)] = coeffs
            else:
                split_rows(coeffs, core_of(), keep, send, work)


def descend_local_kernel(
    mine, other, low_paired, high_paired, sides_0, inverse_0, basis_0, sides, inverse, basis, merge,
    transfer, out, parent, result, sems
):
    leaf = inverse.shape[1]
    rank = basis.shape[1]
    double = 2 * rank
    kept = {1: low_paired, 2: high_paired}
    leaf_count = out.shape[0] // leaf
    depth = leaf_count.bit_length() - 1
    join_rows(mine[...], other[...], core_of(), parent)
    level = [parent[...]]
    for tier in range(depth, 0, -1):
        nodes = leaf_count >> tier
        start = leaf_count - 2 * nodes
        below = []
        for e in range(nodes):
            rows = pl.ds((start + e) * double, double)
            children = descend(level[e], kept[tier][e], merge[rows, :], transfer[rows, :])
            below += [children[:, :rank], children[:, rank:]]
        level = below
    copies = []
    for i in range(leaf_count):
        rows = pl.ds(max(i - 1, 0) * leaf, leaf)
        arrays = (inverse, sides, basis) if i else (inverse_0, sides_0, basis_0)
        spread = dot_right_t(arrays[2][rows, :], level[i])
        rest = (arrays[1][rows, :].astype(F32) - spread).astype(BF16)
        result[i] = dot(arrays[0][rows, :], rest)
        copies.append(
            pltpu.make_async_copy(result.at[i], out.at[pl.ds(i * leaf, leaf), :], sems.at[i])
        )
        copies[-1].start()
    for copy in copies:
        copy.wait()


def place_rows(block, low, size, out, at):
    width = block.shape[-1]
    for lanes in range(out.shape[1] // width):
        out[pl.ds(at, size), pl.ds(lanes * width, width)] = block[pl.ds(low + lanes * size, size), :]


def pair_matrix_kernel(mine, other, out):
    size = out.shape[0] // 2
    core = core_of()
    place_rows(mine, 0, size, out, pl.multiple_of(core * size, size))
    place_rows(other, 0, size, out, pl.multiple_of((1 - core) * size, size))


def quad_matrix_kernel(mine, other, far, far_other, out):
    size = out.shape[0] // 4
    core, side = core_of(), chip_of() % 2
    blocks = [(side, core, mine), (side, 1 - core, other)]
    blocks += [(1 - side, core, far), (1 - side, 1 - core, far_other)]
    for chip, which, ref in blocks:
        place_rows(ref, 0, size, out, pl.multiple_of((2 * chip + which) * size, size))


def stack_kernel(*refs):
    for i, ref in enumerate(refs[:-1]):
        refs[-1][i] = ref[...]


def high_matrix_kernel(mine, other, rest, rest_other, *outs, chips, start, heights):
    top = outs[-1]
    core, middle = core_of(), chips // 2 - 1
    for source in range(chips):
        chip = mirrored(source, chips)
        if source == middle:
            pair, low = (mine, other), start
        else:
            at = source - (source > middle)
            pair, low = (rest.at[at], rest_other.at[at]), 0
        for which, ref in zip((core, 1 - core), pair):
            device = 2 * chip + which
            rows = sum(heights)
            offset = 0
            for out, height in zip(outs, heights):
                width = ref.shape[-1]
                for lanes in range(out.shape[1] // width):
                    out[
                        pl.ds(pl.multiple_of(device * height, height), height),
                        pl.ds(lanes * width, width),
                    ] = ref[pl.ds(low + lanes * rows + offset, height), :]
                offset += height
            at = low + rows * (outs[0].shape[1] // ref.shape[-1])
            width = top.shape[1] // (2 * chips)
            size = top.shape[0] * width // ref.shape[-1]
            for piece in range(ref.shape[-1] // width):
                top[
                    pl.ds(piece * size, size), pl.ds(pl.multiple_of(device * width, width), width)
                ] = ref[pl.ds(at, size), pl.ds(piece * width, width)]


def pair_up_kernel(mine, other, matrix, paired, keep, send, work):
    double = paired.shape[1]
    join_lanes(mine[...], other[...], core_of(), paired)
    coeffs = climb(paired[...], matrix[:, pl.ds(0, double)], matrix[:, pl.ds(double, double // 2)])
    split_rows(coeffs, chip_of() % 2, keep, send, work)


def quad_up_kernel(mine, other, matrix, paired, coeffs):
    double = paired.shape[1]
    join_lanes(mine[...], other[...], chip_of() % 2, paired)
    coeffs[...] = climb(
        paired[...], matrix[:, pl.ds(0, double)], matrix[:, pl.ds(double, double // 2)]
    )


def high_up_kernel(*refs, chips, levels):
    quads = chips // 2
    parts, matrices = refs[:quads], refs[quads : quads + levels]
    kept, coeffs = refs[quads + levels : quads + 2 * levels], refs[-1]
    rank = coeffs.shape[1]
    double = 2 * rank
    for i, part in enumerate(parts):
        at = jnp.where(in_lower(chips), i, quads - 1 - i)
        lanes = pl.ds(pl.multiple_of((at % 2) * rank, rank), rank)
        kept[0][at // 2, :, lanes] = part[...]
    for tier in range(levels):
        nodes = quads >> tier + 1
        for e in range(nodes):
            rows = pl.ds(e * double, double)
            matrix = matrices[tier]
            value = climb(
                kept[tier][e], matrix[rows, pl.ds(0, double)], matrix[rows, pl.ds(double, rank)]
            )
            if tier + 1 < levels:
                kept[tier + 1][e // 2, :, pl.ds((e % 2) * rank, rank)] = value
            else:
                coeffs[...] = value


def high_down_kernel(*refs, chips, levels, roots):
    quads = chips // 2
    own, top = refs[:roots], refs[roots]
    matrices = refs[roots + 1 : roots + 1 + levels]
    kept = refs[roots + 1 + levels : roots + 1 + 2 * levels]
    outs = refs[roots + 1 + 2 * levels : -2]
    stacked, below = refs[-2:]
    rank = outs[0].shape[1]
    double = 2 * rank
    me = lax.axis_index("root")
    for mask in range(roots):
        at = pl.multiple_of((me ^ mask) * rank, rank)
        stacked[:, pl.ds(at, rank)] = own[mask][...]
    level = [dot_right_t(stacked[...], top[...]).astype(BF16)]
    for tier in range(levels - 1, -1, -1):
        values = []
        for e in range(quads >> tier + 1):
            rows = pl.ds(e * double, double)
            matrix = matrices[tier]
            children = descend(
                level[e],
                kept[tier][e],
                matrix[rows, pl.ds(0, double)],
                matrix[rows, pl.ds(double, rank)],
            )
            values += [children[:, :rank], children[:, rank:]]
        level = values
    for i in range(quads):
        below[i] = level[i]
    for i in range(quads):
        outs[i][...] = below[jnp.where(in_lower(chips), i, quads - 1 - i)]


def quad_down_kernel(*refs, chips):
    own, parts, (paired, matrix, keep, send, work, parent) = refs[0], refs[1:-6], refs[-6:]
    double = paired.shape[1]
    at = chip_of()
    is_middle = (at == chips // 2 - 1) | (at == chips // 2)

    @pl.when(is_middle)
    def _():
        parent[...] = own[...]

    @pl.when(jnp.logical_not(is_middle))
    def _():
        total = parts[0][...].astype(F32)
        for part in parts[1:]:
            total += part[...].astype(F32)
        parent[...] = total.astype(BF16)

    children = descend(
        parent[...], paired[...], matrix[:, pl.ds(0, double)], matrix[:, pl.ds(double, double // 2)]
    )
    split_lanes(children, at % 2, keep, send, work)


def pair_down_kernel(mine, other, paired, matrix, keep, send, parent, work):
    double = paired.shape[1]
    join_rows(mine[...], other[...], chip_of() % 2, parent)
    children = descend(
        parent[...], paired[...], matrix[:, pl.ds(0, double)], matrix[:, pl.ds(double, double // 2)]
    )
    split_lanes(children, core_of(), keep, send, work)


def body(
    right_side,
    leaf_inverse,
    leaf_basis,
    local_merge,
    local_transfer,
    upper_merge,
    upper_transfer,
    top_inverse,
):
    leaf = leaf_inverse.shape[2]
    rank = leaf_basis.shape[2]
    columns = right_side.shape[2]
    double = 2 * rank
    wide = double + rank
    leaf_count = right_side.shape[1] // leaf
    sub_count = lax.axis_size("sub")
    sub_depth = sub_count.bit_length() - 1
    root_count = lax.axis_size("root")
    chips = sub_count // 2
    middle = chips // 2 - 1
    half, quarter = columns // 2, columns // 4
    heights = [double >> tier for tier in range(3, sub_depth + 1)]
    levels = len(heights)
    quads = chips // 2
    odd = [chip for chip in range(1, chips, 2)]

    local = [right_side[0], leaf_inverse[0], leaf_basis[0]]
    tree = [local_merge[0], local_transfer[0]]
    first_shapes = [(leaf, a.shape[1]) for a in local]
    blocks = wide // rank
    top_rows, top_width = top_inverse.shape
    quad_rows = blocks * (double // 4)
    high_rows = blocks * sum(heights) + top_rows * top_width // rank
    any_spec, vmem_spec = pl.BlockSpec(memory_space=pl.ANY), pl.BlockSpec(memory_space=pltpu.VMEM)
    shapes = [(blocks * (double // 2), rank)]
    shapes += [(rows, rank) for rows in (quad_rows + high_rows, quad_rows, high_rows)]
    shapes += first_shapes
    args = [upper_merge[0], upper_transfer[0], top_inverse] + local
    pair, quad_high, quad, high, *first = pl.pallas_call(
        pack_kernel,
        out_shape=[pltpu.VMEM(shape, BF16) for shape in shapes],
        in_specs=[any_spec] * len(args),
        out_specs=[vmem_spec] * len(shapes),
        scratch_shapes=[pltpu.SemaphoreType.DMA((3 * blocks + rank // top_width + 3,))],
        compiler_params=pltpu.CompilerParams(vmem_limit_bytes=2 * MIB),
        cost_estimate=cost(1.5),
    )(*[pltpu.with_memory_space_constraint(a, pltpu.HBM) for a in args])
    far = flip(quad, "sub", 2)
    rest = {s: hop(high, s, middle, chips) for s in range(chips) if abs(s - middle) > 1}
    early = list(rest.values())
    pair_other = flip(pair, "sub", 1)
    other = flip(quad_high, "sub", 1)

    shapes = [
        (half, rank),
        (half, rank),
        (leaf_count // 2, columns, double),
        (leaf_count // 4, columns, double),
    ]
    shapes += [(a.shape[0] - leaf, a.shape[1]) for a in local] + [a.shape for a in tree]
    args = [pltpu.with_memory_space_constraint(a, pltpu.HBM) for a in local + tree]
    args += [pltpu.with_memory_space_constraint(a, pltpu.VMEM) for a in first]
    keep, send, low_paired, high_paired, *local = pl.pallas_call(
        climb_local_kernel,
        out_shape=[pltpu.VMEM(shape, BF16) for shape in shapes],
        in_specs=[any_spec] * 5 + [vmem_spec] * 3,
        out_specs=[vmem_spec] * len(shapes),
        scratch_shapes=[
            pltpu.VMEM((columns, rank), BF16),
            pltpu.SemaphoreType.DMA((5 * leaf_count - 5,)),
        ],
        compiler_params=pltpu.CompilerParams(vmem_limit_bytes=16 * MIB),
        cost_estimate=cost(0.01),
    )(*args)

    recv = flip(send, "sub", 1)
    pair_other, high, token = lax.optimization_barrier((pair_other, high, mark(send)))
    rest[middle + 1] = hop(high, middle + 1, middle, chips)
    (pair_matrix,) = vmem_call(pair_matrix_kernel, [(double, wide)], [pair, pair_other])
    pair_paired, keep, send = vmem_call(
        pair_up_kernel,
        [(half, double), (quarter, rank), (quarter, rank)],
        [keep, recv, pair_matrix],
        [pltpu.VMEM((half, rank), BF16)],
        micros=0.05,
        after=[token] + early,
    )

    recv = flip(send, "sub", 2)
    far, high, token = lax.optimization_barrier((far, high, mark(send)))
    far_other = flip(far, "sub", 1)
    rest[middle - 1] = flip(high, "sub", 2)
    (quad_matrix,) = vmem_call(quad_matrix_kernel, [(double, wide)], [quad_high, other, far, far_other])
    quad_paired, coeffs = vmem_call(
        quad_up_kernel,
        [(quarter, double), (quarter, rank)],
        [keep, recv, quad_matrix],
        micros=2,
        after=[token],
    )

    parts = [hop(coeffs, s, middle, chips) for s in odd if s != middle]
    rest = [rest[s] for s in range(chips) if s != middle]
    rest, coeffs = lax.optimization_barrier((rest, coeffs))
    (rest,) = vmem_call(stack_kernel, [(len(rest), high_rows, rank)], list(rest))
    rest_other = flip(rest, "sub", 1)
    *high_matrices, top_matrix = vmem_call(
        functools.partial(high_matrix_kernel, chips=chips, start=quad_rows, heights=heights),
        [(sub_count * height, wide) for height in heights] + [(top_rows, sub_count * top_width)],
        [quad_high, other, rest, rest_other],
        limit=8 * MIB,
        micros=0.2,
    )
    *high_paired_up, coeffs = vmem_call(
        functools.partial(high_up_kernel, chips=chips, levels=levels),
        [(quads >> t + 1, quarter, double) for t in range(levels)] + [(quarter, rank)],
        parts[: odd.index(middle)] + [coeffs] + parts[odd.index(middle) :] + high_matrices,
        limit=8 * MIB,
        micros=0.4,
    )

    roots = [coeffs] + [flip(coeffs, "root", mask) for mask in range(1, root_count)]
    values = vmem_call(
        functools.partial(high_down_kernel, chips=chips, levels=levels, roots=root_count),
        [(quarter, rank)] * quads,
        roots + [top_matrix] + high_matrices + high_paired_up,
        [
            pltpu.VMEM((quarter, root_count * rank), BF16),
            pltpu.VMEM((quads, quarter, rank), BF16),
        ],
        limit=8 * MIB,
        micros=0.7,
    )

    own = values[odd.index(middle)]
    parts = [hop(value, middle, s, chips) for s, value in zip(odd, values) if s != middle]
    keep, send = vmem_call(
        functools.partial(quad_down_kernel, chips=chips),
        [(quarter, rank), (quarter, rank)],
        [own] + parts + [quad_paired, quad_matrix],
        [pltpu.VMEM((quarter, double), BF16), pltpu.VMEM((quarter, rank), BF16)],
        micros=0.4,
    )
    recv = flip(send, "sub", 2)
    keep, send = vmem_call(
        pair_down_kernel,
        [(half, rank), (half, rank)],
        [keep, recv, pair_paired, pair_matrix],
        [pltpu.VMEM((half, rank), BF16), pltpu.VMEM((half, double), BF16)],
        micros=0.4,
    )
    recv = flip(send, "sub", 1)

    args = [keep, recv, low_paired, high_paired] + first + local
    out = pl.pallas_call(
        descend_local_kernel,
        out_shape=jax.ShapeDtypeStruct((leaf_count * leaf, columns), F32),
        in_specs=[vmem_spec] * len(args),
        out_specs=any_spec,
        scratch_shapes=[
            pltpu.VMEM((columns, rank), BF16),
            pltpu.VMEM((leaf_count, leaf, columns), F32),
            pltpu.SemaphoreType.DMA((leaf_count,)),
        ],
        compiler_params=pltpu.CompilerParams(vmem_limit_bytes=16 * MIB),
        cost_estimate=cost(3),
    )(*[pltpu.with_memory_space_constraint(a, pltpu.VMEM) for a in args])
    return out[None]


def solution(mesh):
    return jax.shard_map(
        body,
        mesh=mesh,
        in_specs=(
            P("root", "sub", None),
            P("root", "sub", None),
            P("root", "sub", None),
            P("root", "sub", None),
            P("root", "sub", None),
            P("root", "sub", None),
            P("root", "sub", None),
            P("root", "sub"),
        ),
        out_specs=P("root", "sub", None),
        check_vma=False,
    )
```

```python
import functools

import jax
import jax.numpy as jnp
from jax import lax
from jax.experimental import pallas as pl
from jax.experimental.pallas import tpu as pltpu
from jax.sharding import PartitionSpec as P

BF16 = jnp.bfloat16
F32 = jnp.float32
MIB = 1 << 20


def dot(left, right):
    return lax.dot_general(left, right, (((1,), (0,)), ((), ())), preferred_element_type=F32)


def dot_left_t(left, right):
    return lax.dot_general(left, right, (((0,), (0,)), ((), ())), preferred_element_type=F32)


def dot_right_t(left, right):
    return lax.dot_general(left, right, (((1,), (1,)), ((), ())), preferred_element_type=F32)


def cost(micros):
    return pl.CostEstimate(flops=int(micros * 1e9), bytes_accessed=1, transcendentals=0)


def vmem_call(kernel, outs, args, scratch=(), limit=4 * MIB, micros=0.1, after=()):
    count = len(args)
    args = list(args) + list(after)
    return pl.pallas_call(
        lambda *refs: kernel(*refs[:count], *refs[len(args) :]),
        out_shape=[pltpu.VMEM(shape, BF16) for shape in outs],
        in_specs=[pl.BlockSpec(memory_space=pltpu.VMEM)] * len(args),
        out_specs=[pl.BlockSpec(memory_space=pltpu.VMEM)] * len(outs),
        scratch_shapes=list(scratch),
        compiler_params=pltpu.CompilerParams(vmem_limit_bytes=limit),
        cost_estimate=cost(micros),
    )(*[pltpu.with_memory_space_constraint(a, pltpu.VMEM) for a in args])


def flip(block, axis, mask):
    count = lax.axis_size(axis)
    return lax.ppermute(block, axis, [(i, i ^ mask) for i in range(count)])


def side_of(bit):
    return (lax.axis_index("sub") >> bit) % 2


def split_rows(value, first, keep, send, work):
    half = value.shape[0] // 2
    work[...] = value
    keep[...] = work[pl.ds(pl.multiple_of(first * half, half), half), :]
    send[...] = work[pl.ds(pl.multiple_of((1 - first) * half, half), half), :]


def split_lanes(value, first, keep, send, work):
    half = value.shape[1] // 2
    work[...] = value
    keep[...] = work[:, pl.ds(pl.multiple_of(first * half, half), half)]
    send[...] = work[:, pl.ds(pl.multiple_of((1 - first) * half, half), half)]


def join_rows(mine, other, first, work):
    half = mine.shape[0]
    work[pl.ds(pl.multiple_of(first * half, half), half), :] = mine
    work[pl.ds(pl.multiple_of((1 - first) * half, half), half), :] = other


def join_lanes(mine, other, first, work):
    half = mine.shape[1]
    work[:, pl.ds(pl.multiple_of(first * half, half), half)] = mine
    work[:, pl.ds(pl.multiple_of((1 - first) * half, half), half)] = other


def climb(paired, merge_mat, transfer):
    inner = dot_right_t(paired, merge_mat).astype(BF16)
    return dot(inner, transfer).astype(BF16)


def descend(parent, paired, merge_mat, transfer):
    rest = (paired.astype(F32) - dot_right_t(parent, transfer)).astype(BF16)
    return dot_right_t(rest, merge_mat).astype(BF16)


def pack_kernel(merge, transfer, sides_in, inverse_in, basis_in, *refs):
    pair, quad, high, sides, inverse, basis, sems = refs
    double = merge.shape[1]
    steps = []

    def fetch(source, target):
        steps.append(pltpu.make_async_copy(source, target, sems.at[len(steps)]))

    low = 0
    for target in (pair, quad, high):
        size = target.shape[0]
        rows = pl.ds(low, size)
        fetch(merge.at[rows, :], target.at[:, pl.ds(0, double)])
        fetch(transfer.at[rows, :], target.at[:, pl.ds(double, transfer.shape[1])])
        low += size
    for source, target in ((inverse_in, inverse), (sides_in, sides), (basis_in, basis)):
        fetch(source.at[pl.ds(0, target.shape[0]), :], target)
    for step in steps:
        step.start()
    for step in steps:
        step.wait()


def climb_local_kernel(
    sides_in, inverse_in, basis_in, merge_in, transfer_in, sides_0, inverse_0, basis_0, keep, send,
    low_paired, high_paired, sides, inverse, basis, merge, transfer, work, sems
):
    leaf = inverse.shape[1]
    rank = basis.shape[1]
    double = 2 * rank
    kept = {1: low_paired, 2: high_paired}
    leaf_count = sides_in.shape[0] // leaf
    depth = leaf_count.bit_length() - 1
    nodes = leaf_count - 1
    copies = []

    def fetch(source, target, low, at, size):
        copies.append(
            pltpu.make_async_copy(
                source.at[pl.ds(low, size), :], target.at[pl.ds(at, size), :], sems.at[len(copies)]
            )
        )

    for i in range(1, leaf_count):
        fetch(inverse_in, inverse, i * leaf, (i - 1) * leaf, leaf)
        fetch(sides_in, sides, i * leaf, (i - 1) * leaf, leaf)
        fetch(basis_in, basis, i * leaf, (i - 1) * leaf, leaf)
    first = len(copies)
    for e in range(nodes):
        fetch(merge_in, merge, e * double, e * double, double)
        fetch(transfer_in, transfer, e * double, e * double, double)
    for copy in copies:
        copy.start()
    for i in range(leaf_count):
        rows = pl.ds(max(i - 1, 0) * leaf, leaf)
        if i:
            for copy in copies[3 * i - 3 : 3 * i]:
                copy.wait()
        arrays = (inverse, sides, basis) if i else (inverse_0, sides_0, basis_0)
        solved = dot(arrays[0][rows, :], arrays[1][rows, :]).astype(BF16)
        coeffs = dot_left_t(solved, arrays[2][rows, :]).astype(BF16)
        kept[1][i // 2, :, pl.ds((i % 2) * rank, rank)] = coeffs
    for tier in range(1, depth + 1):
        count = leaf_count >> tier
        start = leaf_count - 2 * count
        for e in range(count):
            rows = pl.ds((start + e) * double, double)
            for copy in copies[first + 2 * (start + e) : first + 2 * (start + e) + 2]:
                copy.wait()
            coeffs = climb(kept[tier][e], merge[rows, :], transfer[rows, :])
            if tier < depth:
                kept[tier + 1][e // 2, :, pl.ds((e % 2) * rank, rank)] = coeffs
            else:
                split_rows(coeffs, side_of(0), keep, send, work)


def descend_local_kernel(
    mine, other, low_paired, high_paired, sides_0, inverse_0, basis_0, sides, inverse, basis, merge,
    transfer, out, parent, result, sems
):
    leaf = inverse.shape[1]
    rank = basis.shape[1]
    double = 2 * rank
    kept = {1: low_paired, 2: high_paired}
    leaf_count = out.shape[0] // leaf
    depth = leaf_count.bit_length() - 1
    join_rows(mine[...], other[...], side_of(0), parent)
    level = [parent[...]]
    for tier in range(depth, 0, -1):
        nodes = leaf_count >> tier
        start = leaf_count - 2 * nodes
        below = []
        for e in range(nodes):
            rows = pl.ds((start + e) * double, double)
            children = descend(level[e], kept[tier][e], merge[rows, :], transfer[rows, :])
            below += [children[:, :rank], children[:, rank:]]
        level = below
    copies = []
    for i in range(leaf_count):
        rows = pl.ds(max(i - 1, 0) * leaf, leaf)
        arrays = (inverse, sides, basis) if i else (inverse_0, sides_0, basis_0)
        spread = dot_right_t(arrays[2][rows, :], level[i])
        rest = (arrays[1][rows, :].astype(F32) - spread).astype(BF16)
        result[i] = dot(arrays[0][rows, :], rest)
        copies.append(
            pltpu.make_async_copy(result.at[i], out.at[pl.ds(i * leaf, leaf), :], sems.at[i])
        )
        copies[-1].start()
    for copy in copies:
        copy.wait()


def pair_matrix_kernel(mine, other, out):
    join_rows(mine[...], other[...], side_of(0), out)


def fetch_quad_kernel(source, out, sem):
    copy = pltpu.make_async_copy(source, out, sem.at[0])
    copy.start()
    copy.wait()


def fetch_high_kernel(high, top_in, *refs):
    *outs, top, sems = refs
    steps = [pltpu.make_async_copy(top_in, top, sems.at[0])]
    offset = 0
    for i, out in enumerate(outs):
        tier = 3 + i
        height = out.shape[0] >> tier
        first = (lax.axis_index("sub") >> tier) << tier
        for k in range(1 << tier):
            steps.append(
                pltpu.make_async_copy(
                    high.at[first + k, pl.ds(offset, height), :],
                    out.at[pl.ds(k * height, height), :],
                    sems.at[len(steps)],
                )
            )
        offset += height
    for step in steps:
        step.start()
    for step in steps:
        step.wait()


def level_up_kernel(mine, other, matrix, paired, *refs, bit, last):
    double = paired.shape[1]
    join_lanes(mine[...], other[...], side_of(bit), paired)
    coeffs = climb(paired[...], matrix[:, pl.ds(0, double)], matrix[:, pl.ds(double, double // 2)])
    if last:
        refs[0][...] = coeffs
    else:
        keep, send, work = refs
        split_rows(coeffs, side_of(bit + 1), keep, send, work)


def top_down_kernel(*refs, bit, roots):
    own, (top, paired, matrix, keep, send, stacked, work) = refs[:roots], refs[roots:]
    rank, double = matrix.shape[1] - paired.shape[1], paired.shape[1]
    me = lax.axis_index("root")
    for mask in range(roots):
        stacked[:, pl.ds(pl.multiple_of((me ^ mask) * rank, rank), rank)] = own[mask][...]
    count, _, width = top.shape
    total = dot_right_t(stacked[:, pl.ds(0, width)], top[0])
    for i in range(1, count):
        total += dot_right_t(stacked[:, pl.ds(i * width, width)], top[i])
    children = descend(
        total.astype(BF16), paired[...], matrix[:, pl.ds(0, double)], matrix[:, pl.ds(double, rank)]
    )
    split_lanes(children, side_of(bit), keep, send, work)


def level_down_kernel(mine, other, paired, matrix, keep, send, parent, work, *, bit):
    double = paired.shape[1]
    join_rows(mine[...], other[...], side_of(bit + 1), parent)
    children = descend(
        parent[...], paired[...], matrix[:, pl.ds(0, double)], matrix[:, pl.ds(double, double // 2)]
    )
    split_lanes(children, side_of(bit), keep, send, work)


def body(
    right_side,
    leaf_inverse,
    leaf_basis,
    local_merge,
    local_transfer,
    upper_merge,
    upper_transfer,
    top_inverse,
):
    leaf = leaf_inverse.shape[2]
    rank = leaf_basis.shape[2]
    columns = right_side.shape[2]
    double = 2 * rank
    wide = double + rank
    leaf_count = right_side.shape[1] // leaf
    sub_count = lax.axis_size("sub")
    sub_depth = sub_count.bit_length() - 1
    root_count = lax.axis_size("root")
    half = columns // 2

    local = [right_side[0], leaf_inverse[0], leaf_basis[0]]
    tree = [local_merge[0], local_transfer[0]]
    any_spec, vmem_spec = pl.BlockSpec(memory_space=pl.ANY), pl.BlockSpec(memory_space=pltpu.VMEM)
    upper_rows = upper_merge.shape[1]
    high_rows = upper_rows - double // 2 - double // 4
    shapes = [pltpu.VMEM((double // 2, wide), BF16)]
    shapes += [pltpu.HBM((rows, wide), BF16) for rows in (double // 4, high_rows)]
    shapes += [pltpu.VMEM((leaf, a.shape[1]), BF16) for a in local]
    args = [upper_merge[0], upper_transfer[0]] + local
    pair, quad, high, *first = pl.pallas_call(
        pack_kernel,
        out_shape=shapes,
        in_specs=[any_spec] * len(args),
        out_specs=[vmem_spec] + [any_spec] * 2 + [vmem_spec] * 3,
        scratch_shapes=[pltpu.SemaphoreType.DMA((9,))],
        compiler_params=pltpu.CompilerParams(vmem_limit_bytes=2 * MIB),
        cost_estimate=cost(1.5),
    )(*[pltpu.with_memory_space_constraint(a, pltpu.HBM) for a in args])
    groups = [[4 * g + i for i in range(4)] for g in range(sub_count // 4)]
    quad = lax.all_gather(quad, "sub", axis_index_groups=groups, tiled=True)
    high = lax.all_gather(high, "sub")
    top = lax.all_gather(top_inverse, "sub")
    pair_other = flip(pair, "sub", 1)

    shapes = [
        (half, rank),
        (half, rank),
        (leaf_count // 2, columns, double),
        (leaf_count // 4, columns, double),
    ]
    shapes += [(a.shape[0] - leaf, a.shape[1]) for a in local] + [a.shape for a in tree]
    args = [pltpu.with_memory_space_constraint(a, pltpu.HBM) for a in local + tree]
    args += [pltpu.with_memory_space_constraint(a, pltpu.VMEM) for a in first]
    keep, send, low_paired, high_paired, *local = pl.pallas_call(
        climb_local_kernel,
        out_shape=[pltpu.VMEM(shape, BF16) for shape in shapes],
        in_specs=[any_spec] * 5 + [vmem_spec] * 3,
        out_specs=[vmem_spec] * len(shapes),
        scratch_shapes=[
            pltpu.VMEM((columns, rank), BF16),
            pltpu.SemaphoreType.DMA((5 * leaf_count - 5,)),
        ],
        compiler_params=pltpu.CompilerParams(vmem_limit_bytes=16 * MIB),
        cost_estimate=cost(5),
    )(*args)

    def fetched(kernel, shapes, args, copies):
        return pl.pallas_call(
            kernel,
            out_shape=[pltpu.VMEM(shape, BF16) for shape in shapes],
            in_specs=[any_spec] * len(args),
            out_specs=[vmem_spec] * len(shapes),
            scratch_shapes=[pltpu.SemaphoreType.DMA((copies,))],
            compiler_params=pltpu.CompilerParams(vmem_limit_bytes=2 * MIB),
            cost_estimate=cost(1),
        )(*[pltpu.with_memory_space_constraint(a, pltpu.HBM) for a in args])

    matrices, kept = [], []
    for tier in range(1, sub_depth + 1):
        bit = tier - 1
        share = columns >> tier
        recv = flip(send, "sub", 1 << bit)
        if tier == 1:
            matrices += vmem_call(pair_matrix_kernel, [(double, wide)], [pair, pair_other])
        elif tier == 2:
            quad, token = lax.optimization_barrier((quad, send))
            matrices += fetched(fetch_quad_kernel, [(double, wide)], [quad], 1)
        elif tier == 3:
            count = 1 + sum(1 << t for t in range(3, sub_depth + 1))
            shapes = [(double, wide)] * (sub_depth - 2) + [top.shape]
            high, top, token = lax.optimization_barrier((high, top, send))
            *more, top = fetched(fetch_high_kernel, shapes, [high, top], count)
            matrices += more
        last = tier == sub_depth
        paired, *coeffs = vmem_call(
            functools.partial(level_up_kernel, bit=bit, last=last),
            [(share, double)] + ([(share, rank)] if last else [(share // 2, rank)] * 2),
            [keep, recv, matrices[-1] if tier < 3 else matrices[bit]],
            [] if last else [pltpu.VMEM((share, rank), BF16)],
            micros=0.4,
            after=[token] if tier in (2, 3) else [],
        )
        kept.append(paired)
        if not last:
            keep, send = coeffs

    share = columns >> sub_depth
    roots = coeffs + [flip(coeffs[0], "root", mask) for mask in range(1, root_count)]
    keep, send = vmem_call(
        functools.partial(top_down_kernel, bit=sub_depth - 1, roots=root_count),
        [(share, rank)] * 2,
        roots + [top, kept[-1], matrices[-1]],
        [pltpu.VMEM((share, root_count * rank), BF16), pltpu.VMEM((share, double), BF16)],
        limit=8 * MIB,
        micros=0.7,
    )

    for tier in range(sub_depth - 1, 0, -1):
        recv = flip(send, "sub", 1 << tier)
        share = columns >> tier
        keep, send = vmem_call(
            functools.partial(level_down_kernel, bit=tier - 1),
            [(share, rank)] * 2,
            [keep, recv, kept[tier - 1], matrices[tier - 1]],
            [pltpu.VMEM((share, rank), BF16), pltpu.VMEM((share, double), BF16)],
            micros=0.4,
        )
    recv = flip(send, "sub", 1)

    args = [keep, recv, low_paired, high_paired] + first + local
    out = pl.pallas_call(
        descend_local_kernel,
        out_shape=jax.ShapeDtypeStruct((leaf_count * leaf, columns), F32),
        in_specs=[vmem_spec] * len(args),
        out_specs=any_spec,
        scratch_shapes=[
            pltpu.VMEM((columns, rank), BF16),
            pltpu.VMEM((leaf_count, leaf, columns), F32),
            pltpu.SemaphoreType.DMA((leaf_count,)),
        ],
        compiler_params=pltpu.CompilerParams(vmem_limit_bytes=16 * MIB),
        cost_estimate=cost(3),
    )(*[pltpu.with_memory_space_constraint(a, pltpu.VMEM) for a in args])
    return out[None]


def solution(mesh):
    return jax.shard_map(
        body,
        mesh=mesh,
        in_specs=(
            P("root", "sub", None),
            P("root", "sub", None),
            P("root", "sub", None),
            P("root", "sub", None),
            P("root", "sub", None),
            P("root", "sub", None),
            P("root", "sub", None),
            P("root", "sub"),
        ),
        out_specs=P("root", "sub", None),
        check_vma=False,
    )
```

```python
import functools

import jax
import jax.numpy as jnp
from jax import lax
from jax.experimental import pallas as pl
from jax.experimental.pallas import tpu as pltpu
from jax.sharding import PartitionSpec as P

BF16 = jnp.bfloat16
F32 = jnp.float32
MIB = 1 << 20


def dot(left, right):
    return lax.dot_general(left, right, (((1,), (0,)), ((), ())), preferred_element_type=F32)


def dot_left_t(left, right):
    return lax.dot_general(left, right, (((0,), (0,)), ((), ())), preferred_element_type=F32)


def dot_right_t(left, right):
    return lax.dot_general(left, right, (((1,), (1,)), ((), ())), preferred_element_type=F32)


def cost(micros):
    return pl.CostEstimate(flops=int(micros * 1e9), bytes_accessed=1, transcendentals=0)


def vmem_call(kernel, outs, args, scratch=(), limit=4 * MIB, micros=0.1, after=()):
    count = len(args)
    args = list(args) + list(after)
    return pl.pallas_call(
        lambda *refs: kernel(*refs[:count], *refs[len(args) :]),
        out_shape=[pltpu.VMEM(shape, BF16) for shape in outs],
        in_specs=[pl.BlockSpec(memory_space=pltpu.VMEM)] * len(args),
        out_specs=[pl.BlockSpec(memory_space=pltpu.VMEM)] * len(outs),
        scratch_shapes=list(scratch),
        compiler_params=pltpu.CompilerParams(vmem_limit_bytes=limit),
        cost_estimate=cost(micros),
    )(*[pltpu.with_memory_space_constraint(a, pltpu.VMEM) for a in args])


def mark_kernel(value, out):
    out[...] = value[pl.ds(0, out.shape[0]), pl.ds(0, out.shape[1])]


def mark(value):
    return vmem_call(mark_kernel, [(16, 128)], [value], micros=0.02)[0]


def flip(block, axis, mask):
    count = lax.axis_size(axis)
    return lax.ppermute(block, axis, [(i, i ^ mask) for i in range(count)])


def gather_pair(block, sources, target, chips):
    pairs = []
    for core, source in enumerate(sources):
        pairs.append((2 * source + core, 2 * target + core))
        pairs.append((2 * (chips - 1 - source) + core, 2 * (chips - 1 - target) + core))
    return lax.ppermute(block, "sub", pairs)


def hop(block, source, target, chips):
    pairs = []
    for core in range(2):
        pairs.append((2 * source + core, 2 * target + core))
        pairs.append((2 * (chips - 1 - source) + core, 2 * (chips - 1 - target) + core))
    return lax.ppermute(block, "sub", pairs)


def core_of():
    return lax.axis_index("sub") % 2


def chip_of():
    return lax.axis_index("sub") // 2


def in_lower(chips):
    return chip_of() < chips // 2


def mirrored(chip, chips):
    return jnp.where(in_lower(chips), chip, chips - 1 - chip)


def split_rows(value, first, keep, send, work):
    half = value.shape[0] // 2
    work[...] = value
    keep[...] = work[pl.ds(pl.multiple_of(first * half, half), half), :]
    send[...] = work[pl.ds(pl.multiple_of((1 - first) * half, half), half), :]


def split_lanes(value, first, keep, send, work):
    half = value.shape[1] // 2
    work[...] = value
    keep[...] = work[:, pl.ds(pl.multiple_of(first * half, half), half)]
    send[...] = work[:, pl.ds(pl.multiple_of((1 - first) * half, half), half)]


def join_rows(mine, other, first, work):
    half = mine.shape[0]
    work[pl.ds(pl.multiple_of(first * half, half), half), :] = mine
    work[pl.ds(pl.multiple_of((1 - first) * half, half), half), :] = other


def join_lanes(mine, other, first, work):
    half = mine.shape[1]
    work[:, pl.ds(pl.multiple_of(first * half, half), half)] = mine
    work[:, pl.ds(pl.multiple_of((1 - first) * half, half), half)] = other


def climb(paired, merge_mat, transfer):
    inner = dot_right_t(paired, merge_mat).astype(BF16)
    return dot(inner, transfer).astype(BF16)


def descend(parent, paired, merge_mat, transfer):
    rest = (paired.astype(F32) - dot_right_t(parent, transfer)).astype(BF16)
    return dot_right_t(rest, merge_mat).astype(BF16)


def pack_kernel(merge, transfer, top, sides_in, inverse_in, basis_in, *refs):
    pair, quad, high, sides, inverse, basis, sems = refs
    rows, double = merge.shape
    rank = transfer.shape[1]
    steps = []

    def fetch(source, target):
        steps.append(pltpu.make_async_copy(source, target, sems.at[len(steps)]))

    def level_rows(low, size, target, at):
        for lanes in range(double // rank):
            fetch(
                merge.at[pl.ds(low, size), pl.ds(lanes * rank, rank)], target.at[pl.ds(at, size), :]
            )
            at += size
        fetch(transfer.at[pl.ds(low, size), :], target.at[pl.ds(at, size), :])
        return at + size

    quad_low, high_low = double // 2, double // 2 + double // 4
    level_rows(quad_low, high_low - quad_low, quad, 0)
    at = level_rows(high_low, rows - high_low, high, 0)
    width = top.shape[1]
    size = top.shape[0] * width // rank
    for piece in range(rank // width):
        fetch(
            top.at[pl.ds(piece * size, size), :],
            high.at[pl.ds(at, size), pl.ds(piece * width, width)],
        )
    level_rows(0, quad_low, pair, 0)
    for source, target in ((inverse_in, inverse), (sides_in, sides), (basis_in, basis)):
        fetch(source.at[pl.ds(0, target.shape[0]), :], target)
    for step in steps:
        step.start()
    for step in steps:
        step.wait()


def climb_local_kernel(
    sides_in, inverse_in, basis_in, merge_in, transfer_in, sides_0, inverse_0, basis_0, keep, send,
    low_paired, high_paired, sides, inverse, basis, merge, transfer, work, sems
):
    leaf = inverse.shape[1]
    rank = basis.shape[1]
    double = 2 * rank
    kept = {1: low_paired, 2: high_paired}
    leaf_count = sides_in.shape[0] // leaf
    depth = leaf_count.bit_length() - 1
    nodes = leaf_count - 1
    copies = []

    def fetch(source, target, low, at, size):
        copies.append(
            pltpu.make_async_copy(
                source.at[pl.ds(low, size), :], target.at[pl.ds(at, size), :], sems.at[len(copies)]
            )
        )

    for i in range(1, leaf_count):
        fetch(inverse_in, inverse, i * leaf, (i - 1) * leaf, leaf)
        fetch(sides_in, sides, i * leaf, (i - 1) * leaf, leaf)
        fetch(basis_in, basis, i * leaf, (i - 1) * leaf, leaf)
    first = len(copies)
    for e in range(nodes):
        fetch(merge_in, merge, e * double, e * double, double)
        fetch(transfer_in, transfer, e * double, e * double, double)
    for copy in copies:
        copy.start()
    for i in range(leaf_count):
        rows = pl.ds(max(i - 1, 0) * leaf, leaf)
        if i:
            for copy in copies[3 * i - 3 : 3 * i]:
                copy.wait()
        arrays = (inverse, sides, basis) if i else (inverse_0, sides_0, basis_0)
        solved = dot(arrays[0][rows, :], arrays[1][rows, :]).astype(BF16)
        coeffs = dot_left_t(solved, arrays[2][rows, :]).astype(BF16)
        kept[1][i // 2, :, pl.ds((i % 2) * rank, rank)] = coeffs
    for tier in range(1, depth + 1):
        count = leaf_count >> tier
        start = leaf_count - 2 * count
        for e in range(count):
            rows = pl.ds((start + e) * double, double)
            for copy in copies[first + 2 * (start + e) : first + 2 * (start + e) + 2]:
                copy.wait()
            coeffs = climb(kept[tier][e], merge[rows, :], transfer[rows, :])
            if tier < depth:
                kept[tier + 1][e // 2, :, pl.ds((e % 2) * rank, rank)] = coeffs
            else:
                split_rows(coeffs, core_of(), keep, send, work)


def descend_local_kernel(
    mine, other, low_paired, high_paired, sides_0, inverse_0, basis_0, sides, inverse, basis, merge,
    transfer, out, parent, result, sems
):
    leaf = inverse.shape[1]
    rank = basis.shape[1]
    double = 2 * rank
    kept = {1: low_paired, 2: high_paired}
    leaf_count = out.shape[0] // leaf
    depth = leaf_count.bit_length() - 1
    join_rows(mine[...], other[...], core_of(), parent)
    level = [parent[...]]
    for tier in range(depth, 0, -1):
        nodes = leaf_count >> tier
        start = leaf_count - 2 * nodes
        below = []
        for e in range(nodes):
            rows = pl.ds((start + e) * double, double)
            children = descend(level[e], kept[tier][e], merge[rows, :], transfer[rows, :])
            below += [children[:, :rank], children[:, rank:]]
        level = below
    copies = []
    for i in range(leaf_count):
        rows = pl.ds(max(i - 1, 0) * leaf, leaf)
        arrays = (inverse, sides, basis) if i else (inverse_0, sides_0, basis_0)
        spread = dot_right_t(arrays[2][rows, :], level[i])
        rest = (arrays[1][rows, :].astype(F32) - spread).astype(BF16)
        result[i] = dot(arrays[0][rows, :], rest)
        copies.append(
            pltpu.make_async_copy(result.at[i], out.at[pl.ds(i * leaf, leaf), :], sems.at[i])
        )
        copies[-1].start()
    for copy in copies:
        copy.wait()


def place_rows(block, low, size, out, at):
    width = block.shape[-1]
    for lanes in range(out.shape[1] // width):
        out[pl.ds(at, size), pl.ds(lanes * width, width)] = block[pl.ds(low + lanes * size, size), :]


def pair_matrix_kernel(mine, other, out):
    size = out.shape[0] // 2
    core = core_of()
    place_rows(mine, 0, size, out, pl.multiple_of(core * size, size))
    place_rows(other, 0, size, out, pl.multiple_of((1 - core) * size, size))


def quad_matrix_kernel(mine, other, far, far_other, out):
    size = out.shape[0] // 4
    core, side = core_of(), chip_of() % 2
    blocks = [(side, core, mine), (side, 1 - core, other)]
    blocks += [(1 - side, core, far), (1 - side, 1 - core, far_other)]
    for chip, which, ref in blocks:
        place_rows(ref, 0, size, out, pl.multiple_of((2 * chip + which) * size, size))


def both_kernel(mine, other, out):
    core = core_of()
    out[core] = mine[...]
    out[1 - core] = other[...]


def stack_kernel(*refs):
    *ins, out = refs
    at = 0
    for ref in ins:
        if len(ref.shape) == 2:
            out[at] = ref[...]
            at += 1
        else:
            out[pl.ds(at, ref.shape[0])] = ref[...]
            at += ref.shape[0]


def high_matrix_kernel(own, rest, rest_other, *outs, chips, heights):
    top = outs[-1]
    core, middle = core_of(), chips // 2 - 1
    away = [source for source in range(chips) if source not in (middle - 1, middle)]
    blocks = [(middle, 0, own.at[0]), (middle, 1, own.at[1])]
    blocks += [(middle - 1, core, rest.at[0]), (middle - 1, 1 - core, rest_other.at[0])]
    for i in range(0, len(away), 2):
        for k in range(2):
            mine = jnp.where(core == 0, away[i], away[i + 1])
            theirs = jnp.where(core == 0, away[i + 1], away[i])
            blocks += [(mine, k, rest.at[1 + i + k]), (theirs, k, rest_other.at[1 + i + k])]
    for source, which, ref in blocks:
        chip = mirrored(source, chips)
        device = 2 * chip + which
        rows = sum(heights)
        offset = 0
        for out, height in zip(outs, heights):
            width = ref.shape[-1]
            for lanes in range(out.shape[1] // width):
                out[
                    pl.ds(pl.multiple_of(device * height, height), height),
                    pl.ds(lanes * width, width),
                ] = ref[pl.ds(lanes * rows + offset, height), :]
            offset += height
        at = rows * (outs[0].shape[1] // ref.shape[-1])
        width = top.shape[1] // (2 * chips)
        size = top.shape[0] * width // ref.shape[-1]
        for piece in range(ref.shape[-1] // width):
            top[
                pl.ds(piece * size, size), pl.ds(pl.multiple_of(device * width, width), width)
            ] = ref[pl.ds(at, size), pl.ds(piece * width, width)]


def pair_up_kernel(mine, other, matrix, paired, keep, send, work):
    double = paired.shape[1]
    join_lanes(mine[...], other[...], core_of(), paired)
    coeffs = climb(paired[...], matrix[:, pl.ds(0, double)], matrix[:, pl.ds(double, double // 2)])
    split_rows(coeffs, chip_of() % 2, keep, send, work)


def quad_up_kernel(mine, other, matrix, paired, coeffs):
    double = paired.shape[1]
    join_lanes(mine[...], other[...], chip_of() % 2, paired)
    coeffs[...] = climb(
        paired[...], matrix[:, pl.ds(0, double)], matrix[:, pl.ds(double, double // 2)]
    )


def high_up_kernel(*refs, chips, levels):
    quads = chips // 2
    parts, matrices = refs[:quads], refs[quads : quads + levels]
    kept, coeffs = refs[quads + levels : quads + 2 * levels], refs[-1]
    rank = coeffs.shape[1]
    double = 2 * rank
    for i, part in enumerate(parts):
        at = jnp.where(in_lower(chips), i, quads - 1 - i)
        lanes = pl.ds(pl.multiple_of((at % 2) * rank, rank), rank)
        kept[0][at // 2, :, lanes] = part[...]
    for tier in range(levels):
        nodes = quads >> tier + 1
        for e in range(nodes):
            rows = pl.ds(e * double, double)
            matrix = matrices[tier]
            value = climb(
                kept[tier][e], matrix[rows, pl.ds(0, double)], matrix[rows, pl.ds(double, rank)]
            )
            if tier + 1 < levels:
                kept[tier + 1][e // 2, :, pl.ds((e % 2) * rank, rank)] = value
            else:
                coeffs[...] = value


def high_down_kernel(*refs, chips, levels, roots):
    quads = chips // 2
    own, top = refs[:roots], refs[roots]
    matrices = refs[roots + 1 : roots + 1 + levels]
    kept = refs[roots + 1 + levels : roots + 1 + 2 * levels]
    outs = refs[roots + 1 + 2 * levels : -2]
    stacked, below = refs[-2:]
    rank = outs[0].shape[1]
    double = 2 * rank
    me = lax.axis_index("root")
    for mask in range(roots):
        at = pl.multiple_of((me ^ mask) * rank, rank)
        stacked[:, pl.ds(at, rank)] = own[mask][...]
    level = [dot_right_t(stacked[...], top[...]).astype(BF16)]
    for tier in range(levels - 1, -1, -1):
        values = []
        for e in range(quads >> tier + 1):
            rows = pl.ds(e * double, double)
            matrix = matrices[tier]
            children = descend(
                level[e],
                kept[tier][e],
                matrix[rows, pl.ds(0, double)],
                matrix[rows, pl.ds(double, rank)],
            )
            values += [children[:, :rank], children[:, rank:]]
        level = values
    for i in range(quads):
        below[i] = level[i]
    for i in range(quads):
        outs[i][...] = below[jnp.where(in_lower(chips), i, quads - 1 - i)]


def quad_down_kernel(*refs, chips):
    own, parts, (paired, matrix, keep, send, work, parent) = refs[0], refs[1:-6], refs[-6:]
    double = paired.shape[1]
    at = chip_of()
    is_middle = (at == chips // 2 - 1) | (at == chips // 2)

    @pl.when(is_middle)
    def _():
        parent[...] = own[...]

    @pl.when(jnp.logical_not(is_middle))
    def _():
        total = parts[0][...].astype(F32)
        for part in parts[1:]:
            total += part[...].astype(F32)
        parent[...] = total.astype(BF16)

    children = descend(
        parent[...], paired[...], matrix[:, pl.ds(0, double)], matrix[:, pl.ds(double, double // 2)]
    )
    split_lanes(children, at % 2, keep, send, work)


def pair_down_kernel(mine, other, paired, matrix, keep, send, parent, work):
    double = paired.shape[1]
    join_rows(mine[...], other[...], chip_of() % 2, parent)
    children = descend(
        parent[...], paired[...], matrix[:, pl.ds(0, double)], matrix[:, pl.ds(double, double // 2)]
    )
    split_lanes(children, core_of(), keep, send, work)


def body(
    right_side,
    leaf_inverse,
    leaf_basis,
    local_merge,
    local_transfer,
    upper_merge,
    upper_transfer,
    top_inverse,
):
    leaf = leaf_inverse.shape[2]
    rank = leaf_basis.shape[2]
    columns = right_side.shape[2]
    double = 2 * rank
    wide = double + rank
    leaf_count = right_side.shape[1] // leaf
    sub_count = lax.axis_size("sub")
    sub_depth = sub_count.bit_length() - 1
    root_count = lax.axis_size("root")
    chips = sub_count // 2
    middle = chips // 2 - 1
    half, quarter = columns // 2, columns // 4
    heights = [double >> tier for tier in range(3, sub_depth + 1)]
    levels = len(heights)
    quads = chips // 2
    odd = [chip for chip in range(1, chips, 2)]

    local = [right_side[0], leaf_inverse[0], leaf_basis[0]]
    tree = [local_merge[0], local_transfer[0]]
    first_shapes = [(leaf, a.shape[1]) for a in local]
    blocks = wide // rank
    top_rows, top_width = top_inverse.shape
    quad_rows = blocks * (double // 4)
    high_rows = blocks * sum(heights) + top_rows * top_width // rank
    any_spec, vmem_spec = pl.BlockSpec(memory_space=pl.ANY), pl.BlockSpec(memory_space=pltpu.VMEM)
    shapes = [(blocks * (double // 2), rank)]
    shapes += [(rows, rank) for rows in (quad_rows, high_rows)]
    shapes += first_shapes
    args = [upper_merge[0], upper_transfer[0], top_inverse] + local
    pair, quad, high, *first = pl.pallas_call(
        pack_kernel,
        out_shape=[pltpu.VMEM(shape, BF16) for shape in shapes],
        in_specs=[any_spec] * len(args),
        out_specs=[vmem_spec] * len(shapes),
        scratch_shapes=[pltpu.SemaphoreType.DMA((3 * blocks + rank // top_width + 3,))],
        compiler_params=pltpu.CompilerParams(vmem_limit_bytes=2 * MIB),
        cost_estimate=cost(1.5),
    )(*[pltpu.with_memory_space_constraint(a, pltpu.HBM) for a in args])
    high_other = flip(high, "sub", 1)
    far = flip(quad, "sub", 2)
    (high_both,) = vmem_call(both_kernel, [(2, high_rows, rank)], [high, high_other])
    away = [s for s in range(chips) if s not in (middle - 1, middle)]
    rest = [
        gather_pair(high_both, away[i : i + 2], middle, chips) for i in range(0, len(away), 2)
    ]
    rest.insert(0, flip(high, "sub", 2))
    pair_other = flip(pair, "sub", 1)
    other = flip(quad, "sub", 1)

    shapes = [
        (half, rank),
        (half, rank),
        (leaf_count // 2, columns, double),
        (leaf_count // 4, columns, double),
    ]
    shapes += [(a.shape[0] - leaf, a.shape[1]) for a in local] + [a.shape for a in tree]
    args = [pltpu.with_memory_space_constraint(a, pltpu.HBM) for a in local + tree]
    args += [pltpu.with_memory_space_constraint(a, pltpu.VMEM) for a in first]
    keep, send, low_paired, high_paired, *local = pl.pallas_call(
        climb_local_kernel,
        out_shape=[pltpu.VMEM(shape, BF16) for shape in shapes],
        in_specs=[any_spec] * 5 + [vmem_spec] * 3,
        out_specs=[vmem_spec] * len(shapes),
        scratch_shapes=[
            pltpu.VMEM((columns, rank), BF16),
            pltpu.SemaphoreType.DMA((5 * leaf_count - 5,)),
        ],
        compiler_params=pltpu.CompilerParams(vmem_limit_bytes=16 * MIB),
        cost_estimate=cost(0.01),
    )(*args)

    recv = flip(send, "sub", 1)
    pair_other, token = lax.optimization_barrier((pair_other, mark(send)))
    (pair_matrix,) = vmem_call(pair_matrix_kernel, [(double, wide)], [pair, pair_other])
    pair_paired, keep, send = vmem_call(
        pair_up_kernel,
        [(half, double), (quarter, rank), (quarter, rank)],
        [keep, recv, pair_matrix],
        [pltpu.VMEM((half, rank), BF16)],
        micros=0.05,
        after=[token],
    )

    recv = flip(send, "sub", 2)
    far, token = lax.optimization_barrier((far, mark(send)))
    far_other = flip(far, "sub", 1)
    (quad_matrix,) = vmem_call(quad_matrix_kernel, [(double, wide)], [quad, other, far, far_other])
    quad_paired, coeffs = vmem_call(
        quad_up_kernel,
        [(quarter, double), (quarter, rank)],
        [keep, recv, quad_matrix],
        micros=0.05,
        after=[token],
    )

    parts = [hop(coeffs, s, middle, chips) for s in odd if s != middle]
    rest, coeffs = lax.optimization_barrier((rest, coeffs))
    (rest,) = vmem_call(stack_kernel, [(chips - 1, high_rows, rank)], list(rest))
    rest_other = flip(rest, "sub", 1)
    *high_matrices, top_matrix = vmem_call(
        functools.partial(high_matrix_kernel, chips=chips, heights=heights),
        [(sub_count * height, wide) for height in heights] + [(top_rows, sub_count * top_width)],
        [high_both, rest, rest_other],
        limit=8 * MIB,
        micros=0.2,
    )
    *high_paired_up, coeffs = vmem_call(
        functools.partial(high_up_kernel, chips=chips, levels=levels),
        [(quads >> t + 1, quarter, double) for t in range(levels)] + [(quarter, rank)],
        parts[: odd.index(middle)] + [coeffs] + parts[odd.index(middle) :] + high_matrices,
        limit=8 * MIB,
        micros=0.4,
    )

    roots = [coeffs] + [flip(coeffs, "root", mask) for mask in range(1, root_count)]
    values = vmem_call(
        functools.partial(high_down_kernel, chips=chips, levels=levels, roots=root_count),
        [(quarter, rank)] * quads,
        roots + [top_matrix] + high_matrices + high_paired_up,
        [
            pltpu.VMEM((quarter, root_count * rank), BF16),
            pltpu.VMEM((quads, quarter, rank), BF16),
        ],
        limit=8 * MIB,
        micros=0.7,
    )

    own = values[odd.index(middle)]
    parts = [hop(value, middle, s, chips) for s, value in zip(odd, values) if s != middle]
    keep, send = vmem_call(
        functools.partial(quad_down_kernel, chips=chips),
        [(quarter, rank), (quarter, rank)],
        [own] + parts + [quad_paired, quad_matrix],
        [pltpu.VMEM((quarter, double), BF16), pltpu.VMEM((quarter, rank), BF16)],
        micros=0.4,
    )
    recv = flip(send, "sub", 2)
    keep, send = vmem_call(
        pair_down_kernel,
        [(half, rank), (half, rank)],
        [keep, recv, pair_paired, pair_matrix],
        [pltpu.VMEM((half, rank), BF16), pltpu.VMEM((half, double), BF16)],
        micros=0.4,
    )
    recv = flip(send, "sub", 1)

    args = [keep, recv, low_paired, high_paired] + first + local
    out = pl.pallas_call(
        descend_local_kernel,
        out_shape=jax.ShapeDtypeStruct((leaf_count * leaf, columns), F32),
        in_specs=[vmem_spec] * len(args),
        out_specs=any_spec,
        scratch_shapes=[
            pltpu.VMEM((columns, rank), BF16),
            pltpu.VMEM((leaf_count, leaf, columns), F32),
            pltpu.SemaphoreType.DMA((leaf_count,)),
        ],
        compiler_params=pltpu.CompilerParams(vmem_limit_bytes=16 * MIB),
        cost_estimate=cost(3),
    )(*[pltpu.with_memory_space_constraint(a, pltpu.VMEM) for a in args])
    return out[None]


def solution(mesh):
    return jax.shard_map(
        body,
        mesh=mesh,
        in_specs=(
            P("root", "sub", None),
            P("root", "sub", None),
            P("root", "sub", None),
            P("root", "sub", None),
            P("root", "sub", None),
            P("root", "sub", None),
            P("root", "sub", None),
            P("root", "sub"),
        ),
        out_specs=P("root", "sub", None),
        check_vma=False,
    )
```

```python
import functools

import jax
import jax.numpy as jnp
from jax import lax
from jax.experimental import pallas as pl
from jax.experimental.pallas import tpu as pltpu
from jax.sharding import PartitionSpec as P

BF16 = jnp.bfloat16
F32 = jnp.float32
MIB = 1 << 20


def dot(left, right):
    return lax.dot_general(left, right, (((1,), (0,)), ((), ())), preferred_element_type=F32)


def dot_left_t(left, right):
    return lax.dot_general(left, right, (((0,), (0,)), ((), ())), preferred_element_type=F32)


def dot_right_t(left, right):
    return lax.dot_general(left, right, (((1,), (1,)), ((), ())), preferred_element_type=F32)


def cost(micros):
    return pl.CostEstimate(flops=int(micros * 1e9), bytes_accessed=1, transcendentals=0)


def vmem_call(kernel, outs, args, scratch=(), limit=4 * MIB, micros=0.1, after=()):
    count = len(args)
    args = list(args) + list(after)
    return pl.pallas_call(
        lambda *refs: kernel(*refs[:count], *refs[len(args) :]),
        out_shape=[pltpu.VMEM(shape, BF16) for shape in outs],
        in_specs=[pl.BlockSpec(memory_space=pltpu.VMEM)] * len(args),
        out_specs=[pl.BlockSpec(memory_space=pltpu.VMEM)] * len(outs),
        scratch_shapes=list(scratch),
        compiler_params=pltpu.CompilerParams(vmem_limit_bytes=limit),
        cost_estimate=cost(micros),
    )(*[pltpu.with_memory_space_constraint(a, pltpu.VMEM) for a in args])


def copy_kernel(value, out):
    out[...] = value[...]


def passed(value):
    return vmem_call(copy_kernel, [value.shape], [value], micros=10)[0]


def mark_kernel(value, out):
    out[...] = value[pl.ds(0, out.shape[0]), pl.ds(0, out.shape[1])]


def mark(value):
    return vmem_call(mark_kernel, [(16, 128)], [value], micros=0.02)[0]


def flip(block, axis, mask):
    count = lax.axis_size(axis)
    return lax.ppermute(block, axis, [(i, i ^ mask) for i in range(count)])


def gather_pair(block, sources, target, chips):
    pairs = []
    for core, source in enumerate(sources):
        pairs.append((2 * source + core, 2 * target + core))
        pairs.append((2 * (chips - 1 - source) + core, 2 * (chips - 1 - target) + core))
    return lax.ppermute(block, "sub", pairs)


def inner_chips(chips):
    return [chip for chip in range(chips) if (chip % 2 == 1) == (chip < chips // 2)]


def inward(block, chips, back=False):
    pairs = []
    for inner in inner_chips(chips):
        for core in range(2):
            pairs.append((2 * (inner ^ 1) + core, 2 * inner + core))
    return lax.ppermute(block, "sub", [pair[::-1] if back else pair for pair in pairs])


def hop(block, source, target, chips):
    pairs = []
    for core in range(2):
        pairs.append((2 * source + core, 2 * target + core))
        pairs.append((2 * (chips - 1 - source) + core, 2 * (chips - 1 - target) + core))
    return lax.ppermute(block, "sub", pairs)


def core_of():
    return lax.axis_index("sub") % 2


def chip_of():
    return lax.axis_index("sub") // 2


def in_lower(chips):
    return chip_of() < chips // 2


def mirrored(chip, chips):
    return jnp.where(in_lower(chips), chip, chips - 1 - chip)


def split_rows(value, first, keep, send, work):
    half = value.shape[0] // 2
    work[...] = value
    keep[...] = work[pl.ds(pl.multiple_of(first * half, half), half), :]
    send[...] = work[pl.ds(pl.multiple_of((1 - first) * half, half), half), :]


def split_lanes(value, first, keep, send, work):
    half = value.shape[1] // 2
    work[...] = value
    keep[...] = work[:, pl.ds(pl.multiple_of(first * half, half), half)]
    send[...] = work[:, pl.ds(pl.multiple_of((1 - first) * half, half), half)]


def join_rows(mine, other, first, work):
    half = mine.shape[0]
    work[pl.ds(pl.multiple_of(first * half, half), half), :] = mine
    work[pl.ds(pl.multiple_of((1 - first) * half, half), half), :] = other


def join_lanes(mine, other, first, work):
    half = mine.shape[1]
    work[:, pl.ds(pl.multiple_of(first * half, half), half)] = mine
    work[:, pl.ds(pl.multiple_of((1 - first) * half, half), half)] = other


def climb(paired, merge_mat, transfer):
    inner = dot_right_t(paired, merge_mat).astype(BF16)
    return dot(inner, transfer).astype(BF16)


def descend(parent, paired, merge_mat, transfer):
    rest = (paired.astype(F32) - dot_right_t(parent, transfer)).astype(BF16)
    return dot_right_t(rest, merge_mat).astype(BF16)


def pack_kernel(merge, transfer, top, sides_in, inverse_in, basis_in, *refs):
    pair, quad_high, high, sides, inverse, basis, sems = refs
    rows, double = merge.shape
    rank = transfer.shape[1]
    steps = []

    def fetch(source, target):
        steps.append(pltpu.make_async_copy(source, target, sems.at[len(steps)]))

    def level_rows(low, size, target, at):
        for lanes in range(double // rank):
            fetch(
                merge.at[pl.ds(low, size), pl.ds(lanes * rank, rank)], target.at[pl.ds(at, size), :]
            )
            at += size
        fetch(transfer.at[pl.ds(low, size), :], target.at[pl.ds(at, size), :])
        return at + size

    quad_low, high_low = double // 2, double // 2 + double // 4
    high_at = level_rows(quad_low, high_low - quad_low, quad_high, 0)
    at = level_rows(high_low, rows - high_low, quad_high, high_at)
    width = top.shape[1]
    size = top.shape[0] * width // rank
    for piece in range(rank // width):
        fetch(
            top.at[pl.ds(piece * size, size), :],
            quad_high.at[pl.ds(at, size), pl.ds(piece * width, width)],
        )
    level_rows(0, quad_low, pair, 0)
    for source, target in ((inverse_in, inverse), (sides_in, sides), (basis_in, basis)):
        fetch(source.at[pl.ds(0, target.shape[0]), :], target)
    for step in steps:
        step.start()
    for step in steps:
        step.wait()
    high[...] = quad_high[pl.ds(high_at, high.shape[0]), :]


def climb_local_kernel(
    sides_in, inverse_in, basis_in, merge_in, transfer_in, sides_0, inverse_0, basis_0, keep, send,
    low_paired, high_paired, sides, inverse, basis, merge, transfer, work, sems
):
    leaf = inverse.shape[1]
    rank = basis.shape[1]
    double = 2 * rank
    kept = {1: low_paired, 2: high_paired}
    leaf_count = sides_in.shape[0] // leaf
    depth = leaf_count.bit_length() - 1
    nodes = leaf_count - 1
    copies = []

    def fetch(source, target, low, at, size):
        copies.append(
            pltpu.make_async_copy(
                source.at[pl.ds(low, size), :], target.at[pl.ds(at, size), :], sems.at[len(copies)]
            )
        )

    for i in range(1, leaf_count):
        fetch(inverse_in, inverse, i * leaf, (i - 1) * leaf, leaf)
        fetch(sides_in, sides, i * leaf, (i - 1) * leaf, leaf)
        fetch(basis_in, basis, i * leaf, (i - 1) * leaf, leaf)
    first = len(copies)
    for e in range(nodes):
        fetch(merge_in, merge, e * double, e * double, double)
        fetch(transfer_in, transfer, e * double, e * double, double)
    for copy in copies:
        copy.start()
    for i in range(leaf_count):
        rows = pl.ds(max(i - 1, 0) * leaf, leaf)
        if i:
            for copy in copies[3 * i - 3 : 3 * i]:
                copy.wait()
        arrays = (inverse, sides, basis) if i else (inverse_0, sides_0, basis_0)
        solved = dot(arrays[0][rows, :], arrays[1][rows, :]).astype(BF16)
        coeffs = dot_left_t(solved, arrays[2][rows, :]).astype(BF16)
        kept[1][i // 2, :, pl.ds((i % 2) * rank, rank)] = coeffs
    for tier in range(1, depth + 1):
        count = leaf_count >> tier
        start = leaf_count - 2 * count
        for e in range(count):
            rows = pl.ds((start + e) * double, double)
            for copy in copies[first + 2 * (start + e) : first + 2 * (start + e) + 2]:
                copy.wait()
            coeffs = climb(kept[tier][e], merge[rows, :], transfer[rows, :])
            if tier < depth:
                kept[tier + 1][e // 2, :, pl.ds((e % 2) * rank, rank)] = coeffs
            else:
                split_rows(coeffs, core_of(), keep, send, work)


def descend_local_kernel(
    mine, other, low_paired, high_paired, sides_0, inverse_0, basis_0, sides, inverse, basis, merge,
    transfer, out, parent, result, sems
):
    leaf = inverse.shape[1]
    rank = basis.shape[1]
    double = 2 * rank
    kept = {1: low_paired, 2: high_paired}
    leaf_count = out.shape[0] // leaf
    depth = leaf_count.bit_length() - 1
    join_rows(mine[...], other[...], core_of(), parent)
    level = [parent[...]]
    for tier in range(depth, 0, -1):
        nodes = leaf_count >> tier
        start = leaf_count - 2 * nodes
        below = []
        for e in range(nodes):
            rows = pl.ds((start + e) * double, double)
            children = descend(level[e], kept[tier][e], merge[rows, :], transfer[rows, :])
            below += [children[:, :rank], children[:, rank:]]
        level = below
    copies = []
    for i in range(leaf_count):
        rows = pl.ds(max(i - 1, 0) * leaf, leaf)
        arrays = (inverse, sides, basis) if i else (inverse_0, sides_0, basis_0)
        spread = dot_right_t(arrays[2][rows, :], level[i])
        rest = (arrays[1][rows, :].astype(F32) - spread).astype(BF16)
        result[i] = dot(arrays[0][rows, :], rest)
        copies.append(
            pltpu.make_async_copy(result.at[i], out.at[pl.ds(i * leaf, leaf), :], sems.at[i])
        )
        copies[-1].start()
    for copy in copies:
        copy.wait()


def place_rows(block, low, size, out, at):
    width = block.shape[-1]
    for lanes in range(out.shape[1] // width):
        out[pl.ds(at, size), pl.ds(lanes * width, width)] = block[pl.ds(low + lanes * size, size), :]


def pair_matrix_kernel(mine, other, out):
    size = out.shape[0] // 2
    core = core_of()
    place_rows(mine, 0, size, out, pl.multiple_of(core * size, size))
    place_rows(other, 0, size, out, pl.multiple_of((1 - core) * size, size))


def quad_matrix_kernel(mine, other, far, far_other, out):
    size = out.shape[0] // 4
    core, side = core_of(), chip_of() % 2
    blocks = [(side, core, mine), (side, 1 - core, other)]
    blocks += [(1 - side, core, far), (1 - side, 1 - core, far_other)]
    for chip, which, ref in blocks:
        place_rows(ref, 0, size, out, pl.multiple_of((2 * chip + which) * size, size))


def both_kernel(mine, other, out):
    core = core_of()
    out[core] = mine[...]
    out[1 - core] = other[...]


def extend_kernel(mine, other, out):
    out[pl.ds(0, mine.shape[0]), :] = mine[...]
    out[pl.ds(mine.shape[0], other.shape[0]), :] = other[...]


def stack_kernel(*refs):
    *ins, out = refs
    at = 0
    for ref in ins:
        if len(ref.shape) == 2:
            out[at] = ref[...]
            at += 1
        else:
            out[pl.ds(at, ref.shape[0])] = ref[...]
            at += ref.shape[0]


def high_matrix_kernel(own, far, far_other, rest, rest_other, *outs, chips, heights):
    top = outs[-1]
    core, middle = core_of(), chips // 2 - 1
    away = [source for source in range(chips) if source not in (middle - 1, middle)]
    blocks = [(middle, 0, own.at[0]), (middle, 1, own.at[1])]
    last = pl.ds(far.shape[0] - own.shape[1], own.shape[1])
    blocks += [(middle - 1, core, far.at[last]), (middle - 1, 1 - core, far_other.at[last])]
    for i in range(0, len(away), 2):
        for k in range(2):
            mine = jnp.where(core == 0, away[i], away[i + 1])
            theirs = jnp.where(core == 0, away[i + 1], away[i])
            blocks += [(mine, k, rest.at[i + k]), (theirs, k, rest_other.at[i + k])]
    for source, which, ref in blocks:
        chip = mirrored(source, chips)
        device = 2 * chip + which
        rows = sum(heights)
        offset = 0
        for out, height in zip(outs, heights):
            width = ref.shape[-1]
            for lanes in range(out.shape[1] // width):
                out[
                    pl.ds(pl.multiple_of(device * height, height), height),
                    pl.ds(lanes * width, width),
                ] = ref[pl.ds(lanes * rows + offset, height), :]
            offset += height
        at = rows * (outs[0].shape[1] // ref.shape[-1])
        width = top.shape[1] // (2 * chips)
        size = top.shape[0] * width // ref.shape[-1]
        for piece in range(ref.shape[-1] // width):
            top[
                pl.ds(piece * size, size), pl.ds(pl.multiple_of(device * width, width), width)
            ] = ref[pl.ds(at, size), pl.ds(piece * width, width)]


def pair_up_kernel(mine, other, matrix, paired, coeffs):
    double = paired.shape[1]
    join_lanes(mine[...], other[...], core_of(), paired)
    coeffs[...] = climb(
        paired[...], matrix[:, pl.ds(0, double)], matrix[:, pl.ds(double, double // 2)]
    )


def quad_up_kernel(mine, other, matrix, paired, near, far, work, *, chips):
    double = paired.shape[1]
    join_lanes(mine[...], other[...], chip_of() % 2, paired)
    coeffs = climb(paired[...], matrix[:, pl.ds(0, double)], matrix[:, pl.ds(double, double // 2)])
    split_rows(coeffs, jnp.where(in_lower(chips), 0, 1), near, far, work)


def high_up_kernel(*refs, chips, levels):
    quads = chips // 2
    parts, matrices = refs[:quads], refs[quads : quads + levels]
    kept, coeffs = refs[quads + levels : quads + 2 * levels], refs[-1]
    rank = coeffs.shape[1]
    double = 2 * rank
    for i, part in enumerate(parts):
        at = jnp.where(in_lower(chips), i, quads - 1 - i)
        lanes = pl.ds(pl.multiple_of((at % 2) * rank, rank), rank)
        kept[0][at // 2, :, lanes] = part[...]
    for tier in range(levels):
        nodes = quads >> tier + 1
        for e in range(nodes):
            rows = pl.ds(e * double, double)
            matrix = matrices[tier]
            value = climb(
                kept[tier][e], matrix[rows, pl.ds(0, double)], matrix[rows, pl.ds(double, rank)]
            )
            if tier + 1 < levels:
                kept[tier + 1][e // 2, :, pl.ds((e % 2) * rank, rank)] = value
            else:
                coeffs[...] = value


def high_down_kernel(*refs, chips, levels, roots):
    quads = chips // 2
    own, top = refs[:2]
    matrices, kept, outs = refs[2 : 2 + levels], refs[2 + levels : 2 + 2 * levels], refs[2 + 2 * levels : -2]
    stacked, below = refs[-2:]
    rank = outs[0].shape[1]
    double = 2 * rank
    me = lax.axis_index("root")
    share = stacked.shape[0]
    for mask in range(roots):
        at = pl.multiple_of((me ^ mask) * rank, rank)
        stacked[:, pl.ds(at, rank)] = own[pl.ds(mask * share, share), :]
    level = [dot_right_t(stacked[...], top[...]).astype(BF16)]
    for tier in range(levels - 1, -1, -1):
        values = []
        for e in range(quads >> tier + 1):
            rows = pl.ds(e * double, double)
            matrix = matrices[tier]
            children = descend(
                level[e],
                kept[tier][e],
                matrix[rows, pl.ds(0, double)],
                matrix[rows, pl.ds(double, rank)],
            )
            values += [children[:, :rank], children[:, rank:]]
        level = values
    for i in range(quads):
        below[i] = level[i]
    for i in range(quads):
        outs[i][...] = below[jnp.where(in_lower(chips), i, quads - 1 - i)]


def quad_down_kernel(*refs, chips):
    own, parts, (paired, matrix, keep, send, parent, work) = refs[0], refs[1:-6], refs[-6:]
    double = paired.shape[1]
    at = chip_of()
    is_middle = (at == chips // 2 - 1) | (at == chips // 2)
    sides = []
    for group in (parts[: len(parts) // 2], parts[len(parts) // 2 :]):
        total = jnp.zeros(own.shape, F32)
        for part in group:
            total += part[...].astype(F32)
        sides.append(total.astype(BF16))
    near = jnp.where(is_middle, own[...], sides[0])
    join_rows(near, sides[1], jnp.where(in_lower(chips), 0, 1), parent)
    children = descend(
        parent[...], paired[...], matrix[:, pl.ds(0, double)], matrix[:, pl.ds(double, double // 2)]
    )
    split_lanes(children, at % 2, keep, send, work)


def pair_down_kernel(mine, other, paired, matrix, keep, send, work, *, chips):
    double = paired.shape[1]
    inner = (chip_of() % 2 == 1) == in_lower(chips)
    parent = jnp.where(inner, mine[...], other[...])
    children = descend(
        parent, paired[...], matrix[:, pl.ds(0, double)], matrix[:, pl.ds(double, double // 2)]
    )
    split_lanes(children, core_of(), keep, send, work)


def body(
    right_side,
    leaf_inverse,
    leaf_basis,
    local_merge,
    local_transfer,
    upper_merge,
    upper_transfer,
    top_inverse,
):
    leaf = leaf_inverse.shape[2]
    rank = leaf_basis.shape[2]
    columns = right_side.shape[2]
    double = 2 * rank
    wide = double + rank
    leaf_count = right_side.shape[1] // leaf
    sub_count = lax.axis_size("sub")
    sub_depth = sub_count.bit_length() - 1
    root_count = lax.axis_size("root")
    chips = sub_count // 2
    middle = chips // 2 - 1
    half, quarter = columns // 2, columns // 4
    heights = [double >> tier for tier in range(3, sub_depth + 1)]
    levels = len(heights)
    quads = chips // 2

    local = [right_side[0], leaf_inverse[0], leaf_basis[0]]
    tree = [local_merge[0], local_transfer[0]]
    first_shapes = [(leaf, a.shape[1]) for a in local]
    blocks = wide // rank
    top_rows, top_width = top_inverse.shape
    quad_rows = blocks * (double // 4)
    high_rows = blocks * sum(heights) + top_rows * top_width // rank
    any_spec, vmem_spec = pl.BlockSpec(memory_space=pl.ANY), pl.BlockSpec(memory_space=pltpu.VMEM)
    shapes = [(blocks * (double // 2), rank)]
    shapes += [(rows, rank) for rows in (quad_rows + high_rows, high_rows)]
    shapes += first_shapes
    args = [upper_merge[0], upper_transfer[0], top_inverse] + local
    pair, quad_high, high, *first = pl.pallas_call(
        pack_kernel,
        out_shape=[pltpu.VMEM(shape, BF16) for shape in shapes],
        in_specs=[any_spec] * len(args),
        out_specs=[vmem_spec] * len(shapes),
        scratch_shapes=[pltpu.SemaphoreType.DMA((3 * blocks + rank // top_width + 3,))],
        compiler_params=pltpu.CompilerParams(vmem_limit_bytes=2 * MIB),
        cost_estimate=cost(1.5),
    )(*[pltpu.with_memory_space_constraint(a, pltpu.HBM) for a in args])
    high_other = flip(high, "sub", 1)
    far = inward(quad_high, chips)
    (high_both,) = vmem_call(both_kernel, [(2, high_rows, rank)], [high, high_other])
    away = [s for s in range(chips) if s not in (middle - 1, middle)]
    rest = [
        gather_pair(high_both, away[i : i + 2], middle, chips) for i in range(0, len(away), 2)
    ]
    pair_other = flip(pair, "sub", 1)
    other = flip(quad_high, "sub", 1)

    shapes = [
        (half, rank),
        (half, rank),
        (leaf_count // 2, columns, double),
        (leaf_count // 4, columns, double),
    ]
    shapes += [(a.shape[0] - leaf, a.shape[1]) for a in local] + [a.shape for a in tree]
    args = [pltpu.with_memory_space_constraint(a, pltpu.HBM) for a in local + tree]
    args += [pltpu.with_memory_space_constraint(a, pltpu.VMEM) for a in first]
    keep, send, low_paired, high_paired, *local = pl.pallas_call(
        climb_local_kernel,
        out_shape=[pltpu.VMEM(shape, BF16) for shape in shapes],
        in_specs=[any_spec] * 5 + [vmem_spec] * 3,
        out_specs=[vmem_spec] * len(shapes),
        scratch_shapes=[
            pltpu.VMEM((columns, rank), BF16),
            pltpu.SemaphoreType.DMA((5 * leaf_count - 5,)),
        ],
        compiler_params=pltpu.CompilerParams(vmem_limit_bytes=16 * MIB),
        cost_estimate=cost(0.01),
    )(*args)

    recv = flip(send, "sub", 1)
    pair_other, token = lax.optimization_barrier((pair_other, mark(send)))
    (pair_matrix,) = vmem_call(pair_matrix_kernel, [(double, wide)], [pair, pair_other])
    pair_paired, coeffs = vmem_call(
        pair_up_kernel,
        [(half, double), (half, rank)],
        [keep, recv, pair_matrix],
        micros=0.05,
        after=[token],
    )

    recv = inward(coeffs, chips)
    recv = passed(recv)
    far, rest, token = lax.optimization_barrier((far, rest, mark(coeffs)))
    far_other = flip(far, "sub", 1)
    (quad_matrix,) = vmem_call(
        quad_matrix_kernel, [(double, wide)], [quad_high, other, far, far_other], after=[recv]
    )
    quad_paired, near, send = vmem_call(
        functools.partial(quad_up_kernel, chips=chips),
        [(half, double), (quarter, rank), (quarter, rank)],
        [coeffs, recv, quad_matrix],
        [pltpu.VMEM((half, rank), BF16)],
        micros=0.05,
        after=[token],
    )

    inner = inner_chips(chips)
    own = inner.index(middle)
    parts = [
        passed(hop(near if s < middle else send, s, middle, chips)) for s in inner if s != middle
    ]
    rest, near = lax.optimization_barrier((rest, near))
    if len(rest) > 1:
        rest = vmem_call(stack_kernel, [(chips - 2, high_rows, rank)], list(rest))
    (rest,) = rest
    rest_other = flip(rest, "sub", 1)
    *high_matrices, top_matrix = vmem_call(
        functools.partial(high_matrix_kernel, chips=chips, heights=heights),
        [(sub_count * height, wide) for height in heights] + [(top_rows, sub_count * top_width)],
        [high_both, far, far_other, rest, rest_other],
        limit=8 * MIB,
        micros=0.2,
        after=parts,
    )
    *high_paired_up, coeffs = vmem_call(
        functools.partial(high_up_kernel, chips=chips, levels=levels),
        [(quads >> t + 1, quarter, double) for t in range(levels)] + [(quarter, rank)],
        parts[:own] + [near] + parts[own:] + high_matrices,
        limit=8 * MIB,
        micros=0.4,
    )

    mask = 1
    while mask < root_count:
        recv = flip(coeffs, "root", mask)
        (coeffs,) = vmem_call(extend_kernel, [(2 * coeffs.shape[0], rank)], [coeffs, recv])
        mask *= 2
    values = vmem_call(
        functools.partial(high_down_kernel, chips=chips, levels=levels, roots=root_count),
        [(quarter, rank)] * quads,
        [coeffs, top_matrix] + high_matrices + high_paired_up,
        [
            pltpu.VMEM((quarter, root_count * rank), BF16),
            pltpu.VMEM((quads, quarter, rank), BF16),
        ],
        limit=8 * MIB,
        micros=0.7,
    )

    parts = [hop(value, middle, s, chips) for s, value in zip(inner, values) if s != middle]
    if len(parts) == 1:
        parts.insert(0, values[own])
    keep, send = vmem_call(
        functools.partial(quad_down_kernel, chips=chips),
        [(half, rank), (half, rank)],
        [values[own]] + parts + [quad_paired, quad_matrix],
        [pltpu.VMEM((half, rank), BF16), pltpu.VMEM((half, double), BF16)],
        micros=0.4,
    )
    recv = inward(send, chips, back=True)
    keep, send = vmem_call(
        functools.partial(pair_down_kernel, chips=chips),
        [(half, rank), (half, rank)],
        [keep, recv, pair_paired, pair_matrix],
        [pltpu.VMEM((half, double), BF16)],
        micros=0.4,
    )
    recv = flip(send, "sub", 1)

    args = [keep, recv, low_paired, high_paired] + first + local
    out = pl.pallas_call(
        descend_local_kernel,
        out_shape=jax.ShapeDtypeStruct((leaf_count * leaf, columns), F32),
        in_specs=[vmem_spec] * len(args),
        out_specs=any_spec,
        scratch_shapes=[
            pltpu.VMEM((columns, rank), BF16),
            pltpu.VMEM((leaf_count, leaf, columns), F32),
            pltpu.SemaphoreType.DMA((leaf_count,)),
        ],
        compiler_params=pltpu.CompilerParams(vmem_limit_bytes=16 * MIB),
        cost_estimate=cost(3),
    )(*[pltpu.with_memory_space_constraint(a, pltpu.VMEM) for a in args])
    return out[None]


def solution(mesh):
    return jax.shard_map(
        body,
        mesh=mesh,
        in_specs=(
            P("root", "sub", None),
            P("root", "sub", None),
            P("root", "sub", None),
            P("root", "sub", None),
            P("root", "sub", None),
            P("root", "sub", None),
            P("root", "sub", None),
            P("root", "sub"),
        ),
        out_specs=P("root", "sub", None),
        check_vma=False,
    )
```

```python
import functools

import jax
import jax.numpy as jnp
from jax import lax
from jax.experimental import pallas as pl
from jax.experimental.pallas import tpu as pltpu
from jax.sharding import PartitionSpec as P

BF16 = jnp.bfloat16
F32 = jnp.float32
MIB = 1 << 20


def dot(left, right):
    return lax.dot_general(left, right, (((1,), (0,)), ((), ())), preferred_element_type=F32)


def dot_left_t(left, right):
    return lax.dot_general(left, right, (((0,), (0,)), ((), ())), preferred_element_type=F32)


def dot_right_t(left, right):
    return lax.dot_general(left, right, (((1,), (1,)), ((), ())), preferred_element_type=F32)


def cost(micros):
    return pl.CostEstimate(flops=int(micros * 1e9), bytes_accessed=1, transcendentals=0)


def vmem_call(kernel, outs, args, scratch=(), limit=4 * MIB, micros=0.1, after=()):
    count = len(args)
    args = list(args) + list(after)
    return pl.pallas_call(
        lambda *refs: kernel(*refs[:count], *refs[len(args) :]),
        out_shape=[pltpu.VMEM(shape, BF16) for shape in outs],
        in_specs=[pl.BlockSpec(memory_space=pltpu.VMEM)] * len(args),
        out_specs=[pl.BlockSpec(memory_space=pltpu.VMEM)] * len(outs),
        scratch_shapes=list(scratch),
        compiler_params=pltpu.CompilerParams(vmem_limit_bytes=limit),
        cost_estimate=cost(micros),
    )(*[pltpu.with_memory_space_constraint(a, pltpu.VMEM) for a in args])


def copy_kernel(value, out):
    out[...] = value[...]


def passed(value):
    return vmem_call(copy_kernel, [value.shape], [value], micros=10)[0]


def mark_kernel(value, out):
    out[...] = value[pl.ds(0, out.shape[0]), pl.ds(0, out.shape[1])]


def mark(value):
    return vmem_call(mark_kernel, [(16, 128)], [value], micros=0.02)[0]


def flip(block, axis, mask):
    count = lax.axis_size(axis)
    return lax.ppermute(block, axis, [(i, i ^ mask) for i in range(count)])


def gather_pair(block, sources, target, chips):
    pairs = []
    for core, source in enumerate(sources):
        pairs.append((2 * source + core, 2 * target + core))
        pairs.append((2 * (chips - 1 - source) + core, 2 * (chips - 1 - target) + core))
    return lax.ppermute(block, "sub", pairs)


def inner_chips(chips):
    return [chip for chip in range(chips) if (chip % 2 == 0) == (chip < chips // 2)]


def inward(block, chips, back=False):
    pairs = []
    for inner in inner_chips(chips):
        for core in range(2):
            pairs.append((2 * (inner ^ 1) + core, 2 * inner + core))
    return lax.ppermute(block, "sub", [pair[::-1] if back else pair for pair in pairs])


def hop(block, source, target, chips):
    pairs = []
    for core in range(2):
        pairs.append((2 * source + core, 2 * target + core))
        pairs.append((2 * (chips - 1 - source) + core, 2 * (chips - 1 - target) + core))
    return lax.ppermute(block, "sub", pairs)


def core_of():
    return lax.axis_index("sub") % 2


def chip_of():
    return lax.axis_index("sub") // 2


def in_lower(chips):
    return chip_of() < chips // 2


def mirrored(chip, chips):
    return jnp.where(in_lower(chips), chip, chips - 1 - chip)


def split_rows(value, first, keep, send, work):
    half = value.shape[0] // 2
    work[...] = value
    keep[...] = work[pl.ds(pl.multiple_of(first * half, half), half), :]
    send[...] = work[pl.ds(pl.multiple_of((1 - first) * half, half), half), :]


def split_lanes(value, first, keep, send, work):
    half = value.shape[1] // 2
    work[...] = value
    keep[...] = work[:, pl.ds(pl.multiple_of(first * half, half), half)]
    send[...] = work[:, pl.ds(pl.multiple_of((1 - first) * half, half), half)]


def join_rows(mine, other, first, work):
    half = mine.shape[0]
    work[pl.ds(pl.multiple_of(first * half, half), half), :] = mine
    work[pl.ds(pl.multiple_of((1 - first) * half, half), half), :] = other


def join_lanes(mine, other, first, work):
    half = mine.shape[1]
    work[:, pl.ds(pl.multiple_of(first * half, half), half)] = mine
    work[:, pl.ds(pl.multiple_of((1 - first) * half, half), half)] = other


def climb(paired, merge_mat, transfer):
    inner = dot_right_t(paired, merge_mat).astype(BF16)
    return dot(inner, transfer).astype(BF16)


def descend(parent, paired, merge_mat, transfer):
    rest = (paired.astype(F32) - dot_right_t(parent, transfer)).astype(BF16)
    return dot_right_t(rest, merge_mat).astype(BF16)


def pack_kernel(merge, transfer, top, sides_in, inverse_in, basis_in, *refs):
    pair, quad_high, high, sides, inverse, basis, sems = refs
    rows, double = merge.shape
    rank = transfer.shape[1]
    steps = []

    def fetch(source, target):
        steps.append(pltpu.make_async_copy(source, target, sems.at[len(steps)]))

    def level_rows(low, size, target, at):
        for lanes in range(double // rank):
            fetch(
                merge.at[pl.ds(low, size), pl.ds(lanes * rank, rank)], target.at[pl.ds(at, size), :]
            )
            at += size
        fetch(transfer.at[pl.ds(low, size), :], target.at[pl.ds(at, size), :])
        return at + size

    quad_low, high_low = double // 2, double // 2 + double // 4
    high_at = level_rows(quad_low, high_low - quad_low, quad_high, 0)
    at = level_rows(high_low, rows - high_low, quad_high, high_at)
    width = top.shape[1]
    size = top.shape[0] * width // rank
    for piece in range(rank // width):
        fetch(
            top.at[pl.ds(piece * size, size), :],
            quad_high.at[pl.ds(at, size), pl.ds(piece * width, width)],
        )
    level_rows(0, quad_low, pair, 0)
    for source, target in ((inverse_in, inverse), (sides_in, sides), (basis_in, basis)):
        fetch(source.at[pl.ds(0, target.shape[0]), :], target)
    for step in steps:
        step.start()
    for step in steps:
        step.wait()
    high[...] = quad_high[pl.ds(high_at, high.shape[0]), :]


def climb_local_kernel(
    sides_in, inverse_in, basis_in, merge_in, transfer_in, sides_0, inverse_0, basis_0, keep, send,
    low_paired, high_paired, sides, inverse, basis, merge, transfer, work, sems
):
    leaf = inverse.shape[1]
    rank = basis.shape[1]
    double = 2 * rank
    kept = {1: low_paired, 2: high_paired}
    leaf_count = sides_in.shape[0] // leaf
    depth = leaf_count.bit_length() - 1
    nodes = leaf_count - 1
    copies = []

    def fetch(source, target, low, at, size):
        copies.append(
            pltpu.make_async_copy(
                source.at[pl.ds(low, size), :], target.at[pl.ds(at, size), :], sems.at[len(copies)]
            )
        )

    for i in range(1, leaf_count):
        fetch(inverse_in, inverse, i * leaf, (i - 1) * leaf, leaf)
        fetch(sides_in, sides, i * leaf, (i - 1) * leaf, leaf)
        fetch(basis_in, basis, i * leaf, (i - 1) * leaf, leaf)
    first = len(copies)
    for e in range(nodes):
        fetch(merge_in, merge, e * double, e * double, double)
        fetch(transfer_in, transfer, e * double, e * double, double)
    for copy in copies:
        copy.start()
    for i in range(leaf_count):
        rows = pl.ds(max(i - 1, 0) * leaf, leaf)
        if i:
            for copy in copies[3 * i - 3 : 3 * i]:
                copy.wait()
        arrays = (inverse, sides, basis) if i else (inverse_0, sides_0, basis_0)
        solved = dot(arrays[0][rows, :], arrays[1][rows, :]).astype(BF16)
        coeffs = dot_left_t(solved, arrays[2][rows, :]).astype(BF16)
        kept[1][i // 2, :, pl.ds((i % 2) * rank, rank)] = coeffs
    for tier in range(1, depth + 1):
        count = leaf_count >> tier
        start = leaf_count - 2 * count
        for e in range(count):
            rows = pl.ds((start + e) * double, double)
            for copy in copies[first + 2 * (start + e) : first + 2 * (start + e) + 2]:
                copy.wait()
            coeffs = climb(kept[tier][e], merge[rows, :], transfer[rows, :])
            if tier < depth:
                kept[tier + 1][e // 2, :, pl.ds((e % 2) * rank, rank)] = coeffs
            else:
                split_rows(coeffs, core_of(), keep, send, work)


def descend_local_kernel(
    mine, other, low_paired, high_paired, sides_0, inverse_0, basis_0, sides, inverse, basis, merge,
    transfer, out, parent, result, sems
):
    leaf = inverse.shape[1]
    rank = basis.shape[1]
    double = 2 * rank
    kept = {1: low_paired, 2: high_paired}
    leaf_count = out.shape[0] // leaf
    depth = leaf_count.bit_length() - 1
    join_rows(mine[...], other[...], core_of(), parent)
    level = [parent[...]]
    for tier in range(depth, 0, -1):
        nodes = leaf_count >> tier
        start = leaf_count - 2 * nodes
        below = []
        for e in range(nodes):
            rows = pl.ds((start + e) * double, double)
            children = descend(level[e], kept[tier][e], merge[rows, :], transfer[rows, :])
            below += [children[:, :rank], children[:, rank:]]
        level = below
    copies = []
    for i in range(leaf_count):
        rows = pl.ds(max(i - 1, 0) * leaf, leaf)
        arrays = (inverse, sides, basis) if i else (inverse_0, sides_0, basis_0)
        spread = dot_right_t(arrays[2][rows, :], level[i])
        rest = (arrays[1][rows, :].astype(F32) - spread).astype(BF16)
        result[i] = dot(arrays[0][rows, :], rest)
        copies.append(
            pltpu.make_async_copy(result.at[i], out.at[pl.ds(i * leaf, leaf), :], sems.at[i])
        )
        copies[-1].start()
    for copy in copies:
        copy.wait()


def place_rows(block, low, size, out, at):
    width = block.shape[-1]
    for lanes in range(out.shape[1] // width):
        out[pl.ds(at, size), pl.ds(lanes * width, width)] = block[pl.ds(low + lanes * size, size), :]


def pair_matrix_kernel(mine, other, out):
    size = out.shape[0] // 2
    core = core_of()
    place_rows(mine, 0, size, out, pl.multiple_of(core * size, size))
    place_rows(other, 0, size, out, pl.multiple_of((1 - core) * size, size))


def quad_matrix_kernel(mine, other, far, far_other, out):
    size = out.shape[0] // 4
    core, side = core_of(), chip_of() % 2
    blocks = [(side, core, mine), (side, 1 - core, other)]
    blocks += [(1 - side, core, far), (1 - side, 1 - core, far_other)]
    for chip, which, ref in blocks:
        place_rows(ref, 0, size, out, pl.multiple_of((2 * chip + which) * size, size))


def both_kernel(mine, other, out):
    core = core_of()
    out[core] = mine[...]
    out[1 - core] = other[...]


def extend_kernel(mine, other, out):
    out[pl.ds(0, mine.shape[0]), :] = mine[...]
    out[pl.ds(mine.shape[0], other.shape[0]), :] = other[...]


def stack_kernel(*refs):
    *ins, out = refs
    at = 0
    for ref in ins:
        if len(ref.shape) == 2:
            out[at] = ref[...]
            at += 1
        else:
            out[pl.ds(at, ref.shape[0])] = ref[...]
            at += ref.shape[0]


def high_matrix_kernel(own, far, far_other, rest, rest_other, *outs, chips, heights):
    top = outs[-1]
    core, middle = core_of(), 0
    away = [source for source in range(chips) if source not in (middle ^ 1, middle)]
    blocks = [(middle, 0, own.at[0]), (middle, 1, own.at[1])]
    last = pl.ds(far.shape[0] - own.shape[1], own.shape[1])
    blocks += [(middle ^ 1, core, far.at[last]), (middle ^ 1, 1 - core, far_other.at[last])]
    for i in range(0, len(away), 2):
        for k in range(2):
            mine = jnp.where(core == 0, away[i], away[i + 1])
            theirs = jnp.where(core == 0, away[i + 1], away[i])
            blocks += [(mine, k, rest.at[i + k]), (theirs, k, rest_other.at[i + k])]
    for source, which, ref in blocks:
        chip = mirrored(source, chips)
        device = 2 * chip + which
        rows = sum(heights)
        offset = 0
        for out, height in zip(outs, heights):
            width = ref.shape[-1]
            for lanes in range(out.shape[1] // width):
                out[
                    pl.ds(pl.multiple_of(device * height, height), height),
                    pl.ds(lanes * width, width),
                ] = ref[pl.ds(lanes * rows + offset, height), :]
            offset += height
        at = rows * (outs[0].shape[1] // ref.shape[-1])
        width = top.shape[1] // (2 * chips)
        size = top.shape[0] * width // ref.shape[-1]
        for piece in range(ref.shape[-1] // width):
            top[
                pl.ds(piece * size, size), pl.ds(pl.multiple_of(device * width, width), width)
            ] = ref[pl.ds(at, size), pl.ds(piece * width, width)]


def pair_up_kernel(mine, other, matrix, paired, coeffs):
    double = paired.shape[1]
    join_lanes(mine[...], other[...], core_of(), paired)
    coeffs[...] = climb(
        paired[...], matrix[:, pl.ds(0, double)], matrix[:, pl.ds(double, double // 2)]
    )


def quad_up_kernel(mine, other, matrix, paired, near, far, work, *, chips):
    double = paired.shape[1]
    join_lanes(mine[...], other[...], chip_of() % 2, paired)
    coeffs = climb(paired[...], matrix[:, pl.ds(0, double)], matrix[:, pl.ds(double, double // 2)])
    split_rows(coeffs, jnp.where(in_lower(chips), 0, 1), near, far, work)


def high_up_kernel(*refs, chips, levels):
    quads = chips // 2
    parts, matrices = refs[:quads], refs[quads : quads + levels]
    kept, coeffs = refs[quads + levels : quads + 2 * levels], refs[-1]
    rank = coeffs.shape[1]
    double = 2 * rank
    for i, part in enumerate(parts):
        at = jnp.where(in_lower(chips), i, quads - 1 - i)
        lanes = pl.ds(pl.multiple_of((at % 2) * rank, rank), rank)
        kept[0][at // 2, :, lanes] = part[...]
    for tier in range(levels):
        nodes = quads >> tier + 1
        for e in range(nodes):
            rows = pl.ds(e * double, double)
            matrix = matrices[tier]
            value = climb(
                kept[tier][e], matrix[rows, pl.ds(0, double)], matrix[rows, pl.ds(double, rank)]
            )
            if tier + 1 < levels:
                kept[tier + 1][e // 2, :, pl.ds((e % 2) * rank, rank)] = value
            else:
                coeffs[...] = value


def high_down_kernel(*refs, chips, levels, roots):
    quads = chips // 2
    own, top = refs[:2]
    matrices, kept, outs = refs[2 : 2 + levels], refs[2 + levels : 2 + 2 * levels], refs[2 + 2 * levels : -2]
    stacked, below = refs[-2:]
    rank = outs[0].shape[1]
    double = 2 * rank
    me = lax.axis_index("root")
    share = stacked.shape[0]
    for mask in range(roots):
        at = pl.multiple_of((me ^ mask) * rank, rank)
        stacked[:, pl.ds(at, rank)] = own[pl.ds(mask * share, share), :]
    level = [dot_right_t(stacked[...], top[...]).astype(BF16)]
    for tier in range(levels - 1, -1, -1):
        values = []
        for e in range(quads >> tier + 1):
            rows = pl.ds(e * double, double)
            matrix = matrices[tier]
            children = descend(
                level[e],
                kept[tier][e],
                matrix[rows, pl.ds(0, double)],
                matrix[rows, pl.ds(double, rank)],
            )
            values += [children[:, :rank], children[:, rank:]]
        level = values
    for i in range(quads):
        below[i] = level[i]
    for i in range(quads):
        outs[i][...] = below[jnp.where(in_lower(chips), i, quads - 1 - i)]


def quad_down_kernel(*refs, chips):
    own, parts, (paired, matrix, keep, send, parent, work) = refs[0], refs[1:-6], refs[-6:]
    double = paired.shape[1]
    at = chip_of()
    is_middle = (at == 0) | (at == chips - 1)
    sides = []
    for group in (parts[: len(parts) // 2], parts[len(parts) // 2 :]):
        total = jnp.zeros(own.shape, F32)
        for part in group:
            total += part[...].astype(F32)
        sides.append(total.astype(BF16))
    near = jnp.where(is_middle, own[...], sides[0])
    join_rows(near, sides[1], jnp.where(in_lower(chips), 0, 1), parent)
    children = descend(
        parent[...], paired[...], matrix[:, pl.ds(0, double)], matrix[:, pl.ds(double, double // 2)]
    )
    split_lanes(children, at % 2, keep, send, work)


def pair_down_kernel(mine, other, paired, matrix, keep, send, work, *, chips):
    double = paired.shape[1]
    inner = (chip_of() % 2 == 0) == in_lower(chips)
    parent = jnp.where(inner, mine[...], other[...])
    children = descend(
        parent, paired[...], matrix[:, pl.ds(0, double)], matrix[:, pl.ds(double, double // 2)]
    )
    split_lanes(children, core_of(), keep, send, work)


def body(
    right_side,
    leaf_inverse,
    leaf_basis,
    local_merge,
    local_transfer,
    upper_merge,
    upper_transfer,
    top_inverse,
):
    leaf = leaf_inverse.shape[2]
    rank = leaf_basis.shape[2]
    columns = right_side.shape[2]
    double = 2 * rank
    wide = double + rank
    leaf_count = right_side.shape[1] // leaf
    sub_count = lax.axis_size("sub")
    sub_depth = sub_count.bit_length() - 1
    root_count = lax.axis_size("root")
    chips = sub_count // 2
    middle = 0
    half, quarter = columns // 2, columns // 4
    heights = [double >> tier for tier in range(3, sub_depth + 1)]
    levels = len(heights)
    quads = chips // 2

    local = [right_side[0], leaf_inverse[0], leaf_basis[0]]
    tree = [local_merge[0], local_transfer[0]]
    first_shapes = [(leaf, a.shape[1]) for a in local]
    blocks = wide // rank
    top_rows, top_width = top_inverse.shape
    quad_rows = blocks * (double // 4)
    high_rows = blocks * sum(heights) + top_rows * top_width // rank
    any_spec, vmem_spec = pl.BlockSpec(memory_space=pl.ANY), pl.BlockSpec(memory_space=pltpu.VMEM)
    shapes = [(blocks * (double // 2), rank)]
    shapes += [(rows, rank) for rows in (quad_rows + high_rows, high_rows)]
    shapes += first_shapes
    args = [upper_merge[0], upper_transfer[0], top_inverse] + local
    pair, quad_high, high, *first = pl.pallas_call(
        pack_kernel,
        out_shape=[pltpu.VMEM(shape, BF16) for shape in shapes],
        in_specs=[any_spec] * len(args),
        out_specs=[vmem_spec] * len(shapes),
        scratch_shapes=[pltpu.SemaphoreType.DMA((3 * blocks + rank // top_width + 3,))],
        compiler_params=pltpu.CompilerParams(vmem_limit_bytes=2 * MIB),
        cost_estimate=cost(1.5),
    )(*[pltpu.with_memory_space_constraint(a, pltpu.HBM) for a in args])
    high_other = flip(high, "sub", 1)
    far = inward(quad_high, chips)
    (high_both,) = vmem_call(both_kernel, [(2, high_rows, rank)], [high, high_other])
    away = [s for s in range(chips) if s not in (middle ^ 1, middle)]
    rest = [
        gather_pair(high_both, away[i : i + 2], middle, chips) for i in range(0, len(away), 2)
    ]
    pair_other = flip(pair, "sub", 1)
    other = flip(quad_high, "sub", 1)

    shapes = [
        (half, rank),
        (half, rank),
        (leaf_count // 2, columns, double),
        (leaf_count // 4, columns, double),
    ]
    shapes += [(a.shape[0] - leaf, a.shape[1]) for a in local] + [a.shape for a in tree]
    args = [pltpu.with_memory_space_constraint(a, pltpu.HBM) for a in local + tree]
    args += [pltpu.with_memory_space_constraint(a, pltpu.VMEM) for a in first]
    keep, send, low_paired, high_paired, *local = pl.pallas_call(
        climb_local_kernel,
        out_shape=[pltpu.VMEM(shape, BF16) for shape in shapes],
        in_specs=[any_spec] * 5 + [vmem_spec] * 3,
        out_specs=[vmem_spec] * len(shapes),
        scratch_shapes=[
            pltpu.VMEM((columns, rank), BF16),
            pltpu.SemaphoreType.DMA((5 * leaf_count - 5,)),
        ],
        compiler_params=pltpu.CompilerParams(vmem_limit_bytes=16 * MIB),
        cost_estimate=cost(0.01),
    )(*args)

    recv = flip(send, "sub", 1)
    pair_other, token = lax.optimization_barrier((pair_other, mark(send)))
    (pair_matrix,) = vmem_call(pair_matrix_kernel, [(double, wide)], [pair, pair_other])
    pair_paired, coeffs = vmem_call(
        pair_up_kernel,
        [(half, double), (half, rank)],
        [keep, recv, pair_matrix],
        micros=0.05,
        after=[token],
    )

    recv = inward(coeffs, chips)
    recv = passed(recv)
    far, rest, token = lax.optimization_barrier((far, rest, mark(coeffs)))
    far_other = flip(far, "sub", 1)
    (quad_matrix,) = vmem_call(
        quad_matrix_kernel, [(double, wide)], [quad_high, other, far, far_other], after=[recv]
    )
    quad_paired, near, send = vmem_call(
        functools.partial(quad_up_kernel, chips=chips),
        [(half, double), (quarter, rank), (quarter, rank)],
        [coeffs, recv, quad_matrix],
        [pltpu.VMEM((half, rank), BF16)],
        micros=0.05,
        after=[token],
    )

    inner = inner_chips(chips)
    own = inner.index(middle)
    parts = [
        passed(hop(near if s < chips // 2 else send, s, middle, chips)) for s in inner if s != middle
    ]
    rest, near = lax.optimization_barrier((rest, near))
    if len(rest) > 1:
        rest = vmem_call(stack_kernel, [(chips - 2, high_rows, rank)], list(rest))
    (rest,) = rest
    rest_other = flip(rest, "sub", 1)
    *high_matrices, top_matrix = vmem_call(
        functools.partial(high_matrix_kernel, chips=chips, heights=heights),
        [(sub_count * height, wide) for height in heights] + [(top_rows, sub_count * top_width)],
        [high_both, far, far_other, rest, rest_other],
        limit=8 * MIB,
        micros=0.2,
        after=parts,
    )
    *high_paired_up, coeffs = vmem_call(
        functools.partial(high_up_kernel, chips=chips, levels=levels),
        [(quads >> t + 1, quarter, double) for t in range(levels)] + [(quarter, rank)],
        parts[:own] + [near] + parts[own:] + high_matrices,
        limit=8 * MIB,
        micros=0.4,
    )

    mask = 1
    while mask < root_count:
        recv = flip(coeffs, "root", mask)
        (coeffs,) = vmem_call(extend_kernel, [(2 * coeffs.shape[0], rank)], [coeffs, recv])
        mask *= 2
    values = vmem_call(
        functools.partial(high_down_kernel, chips=chips, levels=levels, roots=root_count),
        [(quarter, rank)] * quads,
        [coeffs, top_matrix] + high_matrices + high_paired_up,
        [
            pltpu.VMEM((quarter, root_count * rank), BF16),
            pltpu.VMEM((quads, quarter, rank), BF16),
        ],
        limit=8 * MIB,
        micros=0.7,
    )

    parts = [hop(value, middle, s, chips) for s, value in zip(inner, values) if s != middle]
    if len(parts) == 1:
        parts.insert(0, values[own])
    keep, send = vmem_call(
        functools.partial(quad_down_kernel, chips=chips),
        [(half, rank), (half, rank)],
        [values[own]] + parts + [quad_paired, quad_matrix],
        [pltpu.VMEM((half, rank), BF16), pltpu.VMEM((half, double), BF16)],
        micros=0.4,
    )
    recv = inward(send, chips, back=True)
    keep, send = vmem_call(
        functools.partial(pair_down_kernel, chips=chips),
        [(half, rank), (half, rank)],
        [keep, recv, pair_paired, pair_matrix],
        [pltpu.VMEM((half, double), BF16)],
        micros=0.4,
    )
    recv = flip(send, "sub", 1)

    args = [keep, recv, low_paired, high_paired] + first + local
    out = pl.pallas_call(
        descend_local_kernel,
        out_shape=jax.ShapeDtypeStruct((leaf_count * leaf, columns), F32),
        in_specs=[vmem_spec] * len(args),
        out_specs=any_spec,
        scratch_shapes=[
            pltpu.VMEM((columns, rank), BF16),
            pltpu.VMEM((leaf_count, leaf, columns), F32),
            pltpu.SemaphoreType.DMA((leaf_count,)),
        ],
        compiler_params=pltpu.CompilerParams(vmem_limit_bytes=16 * MIB),
        cost_estimate=cost(3),
    )(*[pltpu.with_memory_space_constraint(a, pltpu.VMEM) for a in args])
    return out[None]


def solution(mesh):
    return jax.shard_map(
        body,
        mesh=mesh,
        in_specs=(
            P("root", "sub", None),
            P("root", "sub", None),
            P("root", "sub", None),
            P("root", "sub", None),
            P("root", "sub", None),
            P("root", "sub", None),
            P("root", "sub", None),
            P("root", "sub"),
        ),
        out_specs=P("root", "sub", None),
        check_vma=False,
    )
```

```python
import functools

import jax
import jax.numpy as jnp
from jax import lax
from jax.experimental import pallas as pl
from jax.experimental.pallas import tpu as pltpu
from jax.sharding import PartitionSpec as P

BF16 = jnp.bfloat16
F32 = jnp.float32
MIB = 1 << 20


def dot(left, right):
    return lax.dot_general(left, right, (((1,), (0,)), ((), ())), preferred_element_type=F32)


def dot_left_t(left, right):
    return lax.dot_general(left, right, (((0,), (0,)), ((), ())), preferred_element_type=F32)


def dot_right_t(left, right):
    return lax.dot_general(left, right, (((1,), (1,)), ((), ())), preferred_element_type=F32)


def cost(micros):
    return pl.CostEstimate(flops=int(micros * 1e9), bytes_accessed=1, transcendentals=0)


def vmem_call(kernel, outs, args, scratch=(), limit=4 * MIB, micros=0.1, after=()):
    count = len(args)
    args = list(args) + list(after)
    return pl.pallas_call(
        lambda *refs: kernel(*refs[:count], *refs[len(args) :]),
        out_shape=[pltpu.VMEM(shape, BF16) for shape in outs],
        in_specs=[pl.BlockSpec(memory_space=pltpu.VMEM)] * len(args),
        out_specs=[pl.BlockSpec(memory_space=pltpu.VMEM)] * len(outs),
        scratch_shapes=list(scratch),
        compiler_params=pltpu.CompilerParams(vmem_limit_bytes=limit),
        cost_estimate=cost(micros),
    )(*[pltpu.with_memory_space_constraint(a, pltpu.VMEM) for a in args])


def copy_kernel(value, out):
    out[...] = value[...]


def passed(value):
    return vmem_call(copy_kernel, [value.shape], [value], micros=10)[0]


def mark_kernel(value, out):
    out[...] = value[pl.ds(0, out.shape[0]), pl.ds(0, out.shape[1])]


def mark(value):
    return vmem_call(mark_kernel, [(16, 128)], [value], micros=0.02)[0]


def flip(block, axis, mask):
    count = lax.axis_size(axis)
    return lax.ppermute(block, axis, [(i, i ^ mask) for i in range(count)])


def swap_with(sources, target, chips):
    count = 2 * chips
    partner = list(range(count))
    for core, source in enumerate(sources):
        for low, high in ((source, target), (chips - 1 - source, chips - 1 - target)):
            partner[2 * low + core], partner[2 * high + core] = 2 * high + core, 2 * low + core
    return list(enumerate(partner))


def inner_chips(chips):
    return [chip for chip in range(chips) if (chip % 2 == 1) == (chip < chips // 2)]


def swapped(block, sources, target, chips):
    return lax.ppermute(block, "sub", swap_with(sources, target, chips))


def core_of():
    return lax.axis_index("sub") % 2


def chip_of():
    return lax.axis_index("sub") // 2


def in_lower(chips):
    return chip_of() < chips // 2


def mirrored(chip, chips):
    return jnp.where(in_lower(chips), chip, chips - 1 - chip)


def split_rows(value, first, keep, send, work):
    half = value.shape[0] // 2
    work[...] = value
    keep[...] = work[pl.ds(pl.multiple_of(first * half, half), half), :]
    send[...] = work[pl.ds(pl.multiple_of((1 - first) * half, half), half), :]


def split_lanes(value, first, keep, send, work):
    half = value.shape[1] // 2
    work[...] = value
    keep[...] = work[:, pl.ds(pl.multiple_of(first * half, half), half)]
    send[...] = work[:, pl.ds(pl.multiple_of((1 - first) * half, half), half)]


def join_rows(mine, other, first, work):
    half = mine.shape[0]
    work[pl.ds(pl.multiple_of(first * half, half), half), :] = mine
    work[pl.ds(pl.multiple_of((1 - first) * half, half), half), :] = other


def join_lanes(mine, other, first, work):
    half = mine.shape[1]
    work[:, pl.ds(pl.multiple_of(first * half, half), half)] = mine
    work[:, pl.ds(pl.multiple_of((1 - first) * half, half), half)] = other


def climb(paired, merge_mat, transfer):
    inner = dot_right_t(paired, merge_mat).astype(BF16)
    return dot(inner, transfer).astype(BF16)


def descend(parent, paired, merge_mat, transfer):
    rest = (paired.astype(F32) - dot_right_t(parent, transfer)).astype(BF16)
    return dot_right_t(rest, merge_mat).astype(BF16)


def pack_kernel(merge, transfer, top, sides_in, inverse_in, basis_in, *refs):
    pair, quad_high, high, sides, inverse, basis, sems = refs
    rows, double = merge.shape
    rank = transfer.shape[1]
    steps = []

    def fetch(source, target):
        steps.append(pltpu.make_async_copy(source, target, sems.at[len(steps)]))

    def level_rows(low, size, target, at):
        for lanes in range(double // rank):
            fetch(
                merge.at[pl.ds(low, size), pl.ds(lanes * rank, rank)], target.at[pl.ds(at, size), :]
            )
            at += size
        fetch(transfer.at[pl.ds(low, size), :], target.at[pl.ds(at, size), :])
        return at + size

    quad_low, high_low = double // 2, double // 2 + double // 4
    high_at = level_rows(quad_low, high_low - quad_low, quad_high, 0)
    at = level_rows(high_low, rows - high_low, quad_high, high_at)
    width = top.shape[1]
    size = top.shape[0] * width // rank
    for piece in range(rank // width):
        fetch(
            top.at[pl.ds(piece * size, size), :],
            quad_high.at[pl.ds(at, size), pl.ds(piece * width, width)],
        )
    level_rows(0, quad_low, pair, 0)
    for source, target in ((inverse_in, inverse), (sides_in, sides), (basis_in, basis)):
        fetch(source.at[pl.ds(0, target.shape[0]), :], target)
    for step in steps:
        step.start()
    for step in steps:
        step.wait()
    high[...] = quad_high[pl.ds(high_at, high.shape[0]), :]


def climb_local_kernel(
    sides_in, inverse_in, basis_in, merge_in, transfer_in, sides_0, inverse_0, basis_0, keep, send,
    low_paired, high_paired, sides, inverse, basis, merge, transfer, work, sems
):
    leaf = inverse.shape[1]
    rank = basis.shape[1]
    double = 2 * rank
    kept = {1: low_paired, 2: high_paired}
    leaf_count = sides_in.shape[0] // leaf
    depth = leaf_count.bit_length() - 1
    nodes = leaf_count - 1
    copies = []

    def fetch(source, target, low, at, size):
        copies.append(
            pltpu.make_async_copy(
                source.at[pl.ds(low, size), :], target.at[pl.ds(at, size), :], sems.at[len(copies)]
            )
        )

    for i in range(1, leaf_count):
        fetch(inverse_in, inverse, i * leaf, (i - 1) * leaf, leaf)
        fetch(sides_in, sides, i * leaf, (i - 1) * leaf, leaf)
        fetch(basis_in, basis, i * leaf, (i - 1) * leaf, leaf)
    first = len(copies)
    for e in range(nodes):
        fetch(merge_in, merge, e * double, e * double, double)
        fetch(transfer_in, transfer, e * double, e * double, double)
    for copy in copies:
        copy.start()
    for i in range(leaf_count):
        rows = pl.ds(max(i - 1, 0) * leaf, leaf)
        if i:
            for copy in copies[3 * i - 3 : 3 * i]:
                copy.wait()
        arrays = (inverse, sides, basis) if i else (inverse_0, sides_0, basis_0)
        solved = dot(arrays[0][rows, :], arrays[1][rows, :]).astype(BF16)
        coeffs = dot_left_t(solved, arrays[2][rows, :]).astype(BF16)
        kept[1][i // 2, :, pl.ds((i % 2) * rank, rank)] = coeffs
    for tier in range(1, depth + 1):
        count = leaf_count >> tier
        start = leaf_count - 2 * count
        for e in range(count):
            rows = pl.ds((start + e) * double, double)
            for copy in copies[first + 2 * (start + e) : first + 2 * (start + e) + 2]:
                copy.wait()
            coeffs = climb(kept[tier][e], merge[rows, :], transfer[rows, :])
            if tier < depth:
                kept[tier + 1][e // 2, :, pl.ds((e % 2) * rank, rank)] = coeffs
            else:
                split_rows(coeffs, core_of(), keep, send, work)


def descend_local_kernel(
    mine, other, low_paired, high_paired, sides_0, inverse_0, basis_0, sides, inverse, basis, merge,
    transfer, out, parent, result, sems
):
    leaf = inverse.shape[1]
    rank = basis.shape[1]
    double = 2 * rank
    kept = {1: low_paired, 2: high_paired}
    leaf_count = out.shape[0] // leaf
    depth = leaf_count.bit_length() - 1
    join_rows(mine[...], other[...], core_of(), parent)
    level = [parent[...]]
    for tier in range(depth, 0, -1):
        nodes = leaf_count >> tier
        start = leaf_count - 2 * nodes
        below = []
        for e in range(nodes):
            rows = pl.ds((start + e) * double, double)
            children = descend(level[e], kept[tier][e], merge[rows, :], transfer[rows, :])
            below += [children[:, :rank], children[:, rank:]]
        level = below
    copies = []
    for i in range(leaf_count):
        rows = pl.ds(max(i - 1, 0) * leaf, leaf)
        arrays = (inverse, sides, basis) if i else (inverse_0, sides_0, basis_0)
        spread = dot_right_t(arrays[2][rows, :], level[i])
        rest = (arrays[1][rows, :].astype(F32) - spread).astype(BF16)
        result[i] = dot(arrays[0][rows, :], rest)
        copies.append(
            pltpu.make_async_copy(result.at[i], out.at[pl.ds(i * leaf, leaf), :], sems.at[i])
        )
        copies[-1].start()
    for copy in copies:
        copy.wait()


def place_rows(block, low, size, out, at):
    width = block.shape[-1]
    for lanes in range(out.shape[1] // width):
        out[pl.ds(at, size), pl.ds(lanes * width, width)] = block[pl.ds(low + lanes * size, size), :]


def pair_matrix_kernel(mine, other, out):
    size = out.shape[0] // 2
    core = core_of()
    place_rows(mine, 0, size, out, pl.multiple_of(core * size, size))
    place_rows(other, 0, size, out, pl.multiple_of((1 - core) * size, size))


def quad_matrix_kernel(mine, other, far, far_other, out):
    size = out.shape[0] // 4
    core, side = core_of(), chip_of() % 2
    blocks = [(side, core, mine), (side, 1 - core, other)]
    blocks += [(1 - side, core, far), (1 - side, 1 - core, far_other)]
    for chip, which, ref in blocks:
        place_rows(ref, 0, size, out, pl.multiple_of((2 * chip + which) * size, size))


def both_kernel(mine, other, out):
    core = core_of()
    out[core] = mine[...]
    out[1 - core] = other[...]


def extend_kernel(mine, other, out):
    out[pl.ds(0, mine.shape[0]), :] = mine[...]
    out[pl.ds(mine.shape[0], other.shape[0]), :] = other[...]


def stack_kernel(*refs):
    *ins, out = refs
    at = 0
    for ref in ins:
        if len(ref.shape) == 2:
            out[at] = ref[...]
            at += 1
        else:
            out[pl.ds(at, ref.shape[0])] = ref[...]
            at += ref.shape[0]


def high_matrix_kernel(own, far, far_other, rest, rest_other, *outs, chips, heights):
    top = outs[-1]
    core, middle = core_of(), chips // 2 - 1
    away = [source for source in range(chips) if source not in (middle - 1, middle)]
    blocks = [(middle, 0, own.at[0]), (middle, 1, own.at[1])]
    last = pl.ds(far.shape[0] - own.shape[1], own.shape[1])
    blocks += [(middle - 1, core, far.at[last]), (middle - 1, 1 - core, far_other.at[last])]
    for i in range(0, len(away), 2):
        for k in range(2):
            mine = jnp.where(core == 0, away[i], away[i + 1])
            theirs = jnp.where(core == 0, away[i + 1], away[i])
            blocks += [(mine, k, rest.at[i + k]), (theirs, k, rest_other.at[i + k])]
    for source, which, ref in blocks:
        chip = mirrored(source, chips)
        device = 2 * chip + which
        rows = sum(heights)
        offset = 0
        for out, height in zip(outs, heights):
            width = ref.shape[-1]
            for lanes in range(out.shape[1] // width):
                out[
                    pl.ds(pl.multiple_of(device * height, height), height),
                    pl.ds(lanes * width, width),
                ] = ref[pl.ds(lanes * rows + offset, height), :]
            offset += height
        at = rows * (outs[0].shape[1] // ref.shape[-1])
        width = top.shape[1] // (2 * chips)
        size = top.shape[0] * width // ref.shape[-1]
        for piece in range(ref.shape[-1] // width):
            top[
                pl.ds(piece * size, size), pl.ds(pl.multiple_of(device * width, width), width)
            ] = ref[pl.ds(at, size), pl.ds(piece * width, width)]


def pair_up_kernel(mine, other, matrix, paired, coeffs):
    double = paired.shape[1]
    join_lanes(mine[...], other[...], core_of(), paired)
    coeffs[...] = climb(
        paired[...], matrix[:, pl.ds(0, double)], matrix[:, pl.ds(double, double // 2)]
    )


def quad_up_kernel(mine, other, matrix, paired, near, far, work, *, chips):
    double = paired.shape[1]
    join_lanes(mine[...], other[...], chip_of() % 2, paired)
    coeffs = climb(paired[...], matrix[:, pl.ds(0, double)], matrix[:, pl.ds(double, double // 2)])
    split_rows(coeffs, jnp.where(in_lower(chips), 0, 1), near, far, work)


def high_up_kernel(*refs, chips, levels):
    quads = chips // 2
    parts, matrices = refs[:quads], refs[quads : quads + levels]
    kept, coeffs = refs[quads + levels : quads + 2 * levels], refs[-1]
    rank = coeffs.shape[1]
    double = 2 * rank
    for i, part in enumerate(parts):
        at = jnp.where(in_lower(chips), i, quads - 1 - i)
        lanes = pl.ds(pl.multiple_of((at % 2) * rank, rank), rank)
        kept[0][at // 2, :, lanes] = part[...]
    for tier in range(levels):
        nodes = quads >> tier + 1
        for e in range(nodes):
            rows = pl.ds(e * double, double)
            matrix = matrices[tier]
            value = climb(
                kept[tier][e], matrix[rows, pl.ds(0, double)], matrix[rows, pl.ds(double, rank)]
            )
            if tier + 1 < levels:
                kept[tier + 1][e // 2, :, pl.ds((e % 2) * rank, rank)] = value
            else:
                coeffs[...] = value


def high_down_kernel(*refs, chips, levels, roots):
    quads = chips // 2
    own, top = refs[:2]
    matrices, kept, outs = refs[2 : 2 + levels], refs[2 + levels : 2 + 2 * levels], refs[2 + 2 * levels : -2]
    stacked, below = refs[-2:]
    rank = outs[0].shape[1]
    double = 2 * rank
    me = lax.axis_index("root")
    share = stacked.shape[0]
    for mask in range(roots):
        at = pl.multiple_of((me ^ mask) * rank, rank)
        stacked[:, pl.ds(at, rank)] = own[pl.ds(mask * share, share), :]
    level = [dot_right_t(stacked[...], top[...]).astype(BF16)]
    for tier in range(levels - 1, -1, -1):
        values = []
        for e in range(quads >> tier + 1):
            rows = pl.ds(e * double, double)
            matrix = matrices[tier]
            children = descend(
                level[e],
                kept[tier][e],
                matrix[rows, pl.ds(0, double)],
                matrix[rows, pl.ds(double, rank)],
            )
            values += [children[:, :rank], children[:, rank:]]
        level = values
    for i in range(quads):
        below[i] = level[i]
    for i in range(quads):
        outs[i][...] = below[jnp.where(in_lower(chips), i, quads - 1 - i)]


def quad_down_kernel(*refs, chips):
    parts, (paired, matrix, keep, send, parent, work) = refs[:-6], refs[-6:]
    double = paired.shape[1]
    at = chip_of()
    line = mirrored(at, chips)
    near, far = parts[0][...], parts[-1][...]
    for source, part in zip(inner_chips(chips), parts):
        near = jnp.where(line == source, part[...], near)
        far = jnp.where(line == chips - 1 - source, part[...], far)
    join_rows(near, far, jnp.where(in_lower(chips), 0, 1), parent)
    children = descend(
        parent[...], paired[...], matrix[:, pl.ds(0, double)], matrix[:, pl.ds(double, double // 2)]
    )
    split_lanes(children, at % 2, keep, send, work)


def pair_down_kernel(mine, other, paired, matrix, keep, send, work, *, chips):
    double = paired.shape[1]
    inner = (chip_of() % 2 == 1) == in_lower(chips)
    parent = jnp.where(inner, mine[...], other[...])
    children = descend(
        parent, paired[...], matrix[:, pl.ds(0, double)], matrix[:, pl.ds(double, double // 2)]
    )
    split_lanes(children, core_of(), keep, send, work)


def body(
    right_side,
    leaf_inverse,
    leaf_basis,
    local_merge,
    local_transfer,
    upper_merge,
    upper_transfer,
    top_inverse,
):
    leaf = leaf_inverse.shape[2]
    rank = leaf_basis.shape[2]
    columns = right_side.shape[2]
    double = 2 * rank
    wide = double + rank
    leaf_count = right_side.shape[1] // leaf
    sub_count = lax.axis_size("sub")
    sub_depth = sub_count.bit_length() - 1
    root_count = lax.axis_size("root")
    chips = sub_count // 2
    middle = chips // 2 - 1
    half, quarter = columns // 2, columns // 4
    heights = [double >> tier for tier in range(3, sub_depth + 1)]
    levels = len(heights)
    quads = chips // 2

    local = [right_side[0], leaf_inverse[0], leaf_basis[0]]
    tree = [local_merge[0], local_transfer[0]]
    first_shapes = [(leaf, a.shape[1]) for a in local]
    blocks = wide // rank
    top_rows, top_width = top_inverse.shape
    quad_rows = blocks * (double // 4)
    high_rows = blocks * sum(heights) + top_rows * top_width // rank
    any_spec, vmem_spec = pl.BlockSpec(memory_space=pl.ANY), pl.BlockSpec(memory_space=pltpu.VMEM)
    shapes = [(blocks * (double // 2), rank)]
    shapes += [(rows, rank) for rows in (quad_rows + high_rows, high_rows)]
    shapes += first_shapes
    args = [upper_merge[0], upper_transfer[0], top_inverse] + local
    pair, quad_high, high, *first = pl.pallas_call(
        pack_kernel,
        out_shape=[pltpu.VMEM(shape, BF16) for shape in shapes],
        in_specs=[any_spec] * len(args),
        out_specs=[vmem_spec] * len(shapes),
        scratch_shapes=[pltpu.SemaphoreType.DMA((3 * blocks + rank // top_width + 3,))],
        compiler_params=pltpu.CompilerParams(vmem_limit_bytes=2 * MIB),
        cost_estimate=cost(1.5),
    )(*[pltpu.with_memory_space_constraint(a, pltpu.HBM) for a in args])
    high_other = flip(high, "sub", 1)
    far = flip(quad_high, "sub", 2)
    (high_both,) = vmem_call(both_kernel, [(2, high_rows, rank)], [high, high_other])
    away = [s for s in range(chips) if s not in (middle - 1, middle)]
    rest = [
        swapped(high_both, away[i : i + 2], middle, chips) for i in range(0, len(away), 2)
    ]
    pair_other = flip(pair, "sub", 1)
    other = flip(quad_high, "sub", 1)

    shapes = [
        (half, rank),
        (half, rank),
        (leaf_count // 2, columns, double),
        (leaf_count // 4, columns, double),
    ]
    shapes += [(a.shape[0] - leaf, a.shape[1]) for a in local] + [a.shape for a in tree]
    args = [pltpu.with_memory_space_constraint(a, pltpu.HBM) for a in local + tree]
    args += [pltpu.with_memory_space_constraint(a, pltpu.VMEM) for a in first]
    keep, send, low_paired, high_paired, *local = pl.pallas_call(
        climb_local_kernel,
        out_shape=[pltpu.VMEM(shape, BF16) for shape in shapes],
        in_specs=[any_spec] * 5 + [vmem_spec] * 3,
        out_specs=[vmem_spec] * len(shapes),
        scratch_shapes=[
            pltpu.VMEM((columns, rank), BF16),
            pltpu.SemaphoreType.DMA((5 * leaf_count - 5,)),
        ],
        compiler_params=pltpu.CompilerParams(vmem_limit_bytes=16 * MIB),
        cost_estimate=cost(0.01),
    )(*args)

    recv = flip(send, "sub", 1)
    pair_other, token = lax.optimization_barrier((pair_other, mark(send)))
    (pair_matrix,) = vmem_call(pair_matrix_kernel, [(double, wide)], [pair, pair_other])
    pair_paired, coeffs = vmem_call(
        pair_up_kernel,
        [(half, double), (half, rank)],
        [keep, recv, pair_matrix],
        micros=0.05,
        after=[token],
    )

    recv = flip(coeffs, "sub", 2)
    recv = passed(recv)
    far, rest, token = lax.optimization_barrier((far, rest, mark(coeffs)))
    far_other = flip(far, "sub", 1)
    (quad_matrix,) = vmem_call(
        quad_matrix_kernel, [(double, wide)], [quad_high, other, far, far_other], after=[recv]
    )
    quad_paired, near, send = vmem_call(
        functools.partial(quad_up_kernel, chips=chips),
        [(half, double), (quarter, rank), (quarter, rank)],
        [coeffs, recv, quad_matrix],
        [pltpu.VMEM((half, rank), BF16)],
        micros=0.05,
        after=[token],
    )

    inner = inner_chips(chips)
    own = inner.index(middle)
    parts = [
        passed(swapped(near if s < middle else send, [s, s], middle, chips))
        for s in inner
        if s != middle
    ]
    rest, near = lax.optimization_barrier((rest, near))
    if len(rest) > 1:
        rest = vmem_call(stack_kernel, [(chips - 2, high_rows, rank)], list(rest))
    (rest,) = rest
    rest_other = flip(rest, "sub", 1)
    *high_matrices, top_matrix = vmem_call(
        functools.partial(high_matrix_kernel, chips=chips, heights=heights),
        [(sub_count * height, wide) for height in heights] + [(top_rows, sub_count * top_width)],
        [high_both, far, far_other, rest, rest_other],
        limit=8 * MIB,
        micros=0.2,
        after=parts,
    )
    *high_paired_up, coeffs = vmem_call(
        functools.partial(high_up_kernel, chips=chips, levels=levels),
        [(quads >> t + 1, quarter, double) for t in range(levels)] + [(quarter, rank)],
        parts[:own] + [near] + parts[own:] + high_matrices,
        limit=8 * MIB,
        micros=0.4,
    )

    mask = 1
    while mask < root_count:
        recv = flip(coeffs, "root", mask)
        (coeffs,) = vmem_call(extend_kernel, [(2 * coeffs.shape[0], rank)], [coeffs, recv])
        mask *= 2
    values = vmem_call(
        functools.partial(high_down_kernel, chips=chips, levels=levels, roots=root_count),
        [(quarter, rank)] * quads,
        [coeffs, top_matrix] + high_matrices + high_paired_up,
        [
            pltpu.VMEM((quarter, root_count * rank), BF16),
            pltpu.VMEM((quads, quarter, rank), BF16),
        ],
        limit=8 * MIB,
        micros=0.7,
    )

    parts = [
        value if s == middle else swapped(value, [s, s], middle, chips)
        for s, value in zip(inner, values)
    ]
    keep, send = vmem_call(
        functools.partial(quad_down_kernel, chips=chips),
        [(half, rank), (half, rank)],
        parts + [quad_paired, quad_matrix],
        [pltpu.VMEM((half, rank), BF16), pltpu.VMEM((half, double), BF16)],
        micros=0.4,
    )
    recv = flip(send, "sub", 2)
    keep, send = vmem_call(
        functools.partial(pair_down_kernel, chips=chips),
        [(half, rank), (half, rank)],
        [keep, recv, pair_paired, pair_matrix],
        [pltpu.VMEM((half, double), BF16)],
        micros=0.4,
    )
    recv = flip(send, "sub", 1)

    args = [keep, recv, low_paired, high_paired] + first + local
    out = pl.pallas_call(
        descend_local_kernel,
        out_shape=jax.ShapeDtypeStruct((leaf_count * leaf, columns), F32),
        in_specs=[vmem_spec] * len(args),
        out_specs=any_spec,
        scratch_shapes=[
            pltpu.VMEM((columns, rank), BF16),
            pltpu.VMEM((leaf_count, leaf, columns), F32),
            pltpu.SemaphoreType.DMA((leaf_count,)),
        ],
        compiler_params=pltpu.CompilerParams(vmem_limit_bytes=16 * MIB),
        cost_estimate=cost(3),
    )(*[pltpu.with_memory_space_constraint(a, pltpu.VMEM) for a in args])
    return out[None]


def solution(mesh):
    return jax.shard_map(
        body,
        mesh=mesh,
        in_specs=(
            P("root", "sub", None),
            P("root", "sub", None),
            P("root", "sub", None),
            P("root", "sub", None),
            P("root", "sub", None),
            P("root", "sub", None),
            P("root", "sub", None),
            P("root", "sub"),
        ),
        out_specs=P("root", "sub", None),
        check_vma=False,
    )
```

```python
import functools

import jax
import jax.numpy as jnp
from jax import lax
from jax.experimental import pallas as pl
from jax.experimental.pallas import tpu as pltpu
from jax.sharding import PartitionSpec as P

BF16 = jnp.bfloat16
F32 = jnp.float32
MIB = 1 << 20


def dot(left, right):
    return lax.dot_general(left, right, (((1,), (0,)), ((), ())), preferred_element_type=F32)


def dot_left_t(left, right):
    return lax.dot_general(left, right, (((0,), (0,)), ((), ())), preferred_element_type=F32)


def dot_right_t(left, right):
    return lax.dot_general(left, right, (((1,), (1,)), ((), ())), preferred_element_type=F32)


def cost(micros):
    return pl.CostEstimate(flops=int(micros * 1e9), bytes_accessed=1, transcendentals=0)


def vmem_call(kernel, outs, args, scratch=(), limit=4 * MIB, micros=0.1, after=()):
    count = len(args)
    args = list(args) + list(after)
    return pl.pallas_call(
        lambda *refs: kernel(*refs[:count], *refs[len(args) :]),
        out_shape=[pltpu.VMEM(shape, BF16) for shape in outs],
        in_specs=[pl.BlockSpec(memory_space=pltpu.VMEM)] * len(args),
        out_specs=[pl.BlockSpec(memory_space=pltpu.VMEM)] * len(outs),
        scratch_shapes=list(scratch),
        compiler_params=pltpu.CompilerParams(vmem_limit_bytes=limit),
        cost_estimate=cost(micros),
    )(*[pltpu.with_memory_space_constraint(a, pltpu.VMEM) for a in args])


def copy_kernel(value, out):
    out[...] = value[...]


def passed(value):
    return vmem_call(copy_kernel, [value.shape], [value], micros=10)[0]


def mark_kernel(value, out):
    out[...] = value[pl.ds(0, out.shape[0]), pl.ds(0, out.shape[1])]


def mark(value):
    return vmem_call(mark_kernel, [(16, 128)], [value], micros=0.02)[0]


def flip(block, axis, mask):
    count = lax.axis_size(axis)
    return lax.ppermute(block, axis, [(i, i ^ mask) for i in range(count)])


def swap_with(source, target, chips):
    partner = [device ^ 1 for device in range(2 * chips)]
    for low, high in ((source, target), (chips - 1 - source, chips - 1 - target)):
        for core in range(2):
            partner[2 * low + core], partner[2 * high + core] = 2 * high + core, 2 * low + core
    return list(enumerate(partner))


def inner_chips(chips):
    return [chip for chip in range(chips) if (chip % 2 == 1) == (chip < chips // 2)]


def swapped(block, source, target, chips):
    return lax.ppermute(block, "sub", swap_with(source, target, chips))


def core_of():
    return lax.axis_index("sub") % 2


def chip_of():
    return lax.axis_index("sub") // 2


def in_lower(chips):
    return chip_of() < chips // 2


def mirrored(chip, chips):
    return jnp.where(in_lower(chips), chip, chips - 1 - chip)


def split_rows(value, first, keep, send, work):
    half = value.shape[0] // 2
    work[...] = value
    keep[...] = work[pl.ds(pl.multiple_of(first * half, half), half), :]
    send[...] = work[pl.ds(pl.multiple_of((1 - first) * half, half), half), :]


def split_lanes(value, first, keep, send, work):
    half = value.shape[1] // 2
    work[...] = value
    keep[...] = work[:, pl.ds(pl.multiple_of(first * half, half), half)]
    send[...] = work[:, pl.ds(pl.multiple_of((1 - first) * half, half), half)]


def join_rows(mine, other, first, work):
    half = mine.shape[0]
    work[pl.ds(pl.multiple_of(first * half, half), half), :] = mine
    work[pl.ds(pl.multiple_of((1 - first) * half, half), half), :] = other


def join_lanes(mine, other, first, work):
    half = mine.shape[1]
    work[:, pl.ds(pl.multiple_of(first * half, half), half)] = mine
    work[:, pl.ds(pl.multiple_of((1 - first) * half, half), half)] = other


def climb(paired, merge_mat, transfer):
    inner = dot_right_t(paired, merge_mat).astype(BF16)
    return dot(inner, transfer).astype(BF16)


def descend(parent, paired, merge_mat, transfer):
    rest = (paired.astype(F32) - dot_right_t(parent, transfer)).astype(BF16)
    return dot_right_t(rest, merge_mat).astype(BF16)


def pack_kernel(merge, transfer, top, sides_in, inverse_in, basis_in, *refs):
    pair, quad_high, sides, inverse, basis, sems = refs
    rows, double = merge.shape
    rank = transfer.shape[1]
    steps = []

    def fetch(source, target):
        steps.append(pltpu.make_async_copy(source, target, sems.at[len(steps)]))

    def level_rows(low, size, target, at):
        for lanes in range(double // rank):
            fetch(
                merge.at[pl.ds(low, size), pl.ds(lanes * rank, rank)], target.at[pl.ds(at, size), :]
            )
            at += size
        fetch(transfer.at[pl.ds(low, size), :], target.at[pl.ds(at, size), :])
        return at + size

    quad_low, high_low = double // 2, double // 2 + double // 4
    high_at = level_rows(quad_low, high_low - quad_low, quad_high, 0)
    at = level_rows(high_low, rows - high_low, quad_high, high_at)
    width = top.shape[1]
    size = top.shape[0] * width // rank
    for piece in range(rank // width):
        fetch(
            top.at[pl.ds(piece * size, size), :],
            quad_high.at[pl.ds(at, size), pl.ds(piece * width, width)],
        )
    level_rows(0, quad_low, pair, 0)
    for source, target in ((inverse_in, inverse), (sides_in, sides), (basis_in, basis)):
        fetch(source.at[pl.ds(0, target.shape[0]), :], target)
    for step in steps:
        step.start()
    for step in steps:
        step.wait()


def climb_local_kernel(
    sides_in, inverse_in, basis_in, merge_in, transfer_in, sides_0, inverse_0, basis_0, keep, send,
    low_paired, high_paired, sides, inverse, basis, merge, transfer, work, sems
):
    leaf = inverse.shape[1]
    rank = basis.shape[1]
    double = 2 * rank
    kept = {1: low_paired, 2: high_paired}
    leaf_count = sides_in.shape[0] // leaf
    depth = leaf_count.bit_length() - 1
    nodes = leaf_count - 1
    copies = []

    def fetch(source, target, low, at, size):
        copies.append(
            pltpu.make_async_copy(
                source.at[pl.ds(low, size), :], target.at[pl.ds(at, size), :], sems.at[len(copies)]
            )
        )

    for i in range(1, leaf_count):
        fetch(inverse_in, inverse, i * leaf, (i - 1) * leaf, leaf)
        fetch(sides_in, sides, i * leaf, (i - 1) * leaf, leaf)
        fetch(basis_in, basis, i * leaf, (i - 1) * leaf, leaf)
    first = len(copies)
    for e in range(nodes):
        fetch(merge_in, merge, e * double, e * double, double)
        fetch(transfer_in, transfer, e * double, e * double, double)
    for copy in copies:
        copy.start()
    for i in range(leaf_count):
        rows = pl.ds(max(i - 1, 0) * leaf, leaf)
        if i:
            for copy in copies[3 * i - 3 : 3 * i]:
                copy.wait()
        arrays = (inverse, sides, basis) if i else (inverse_0, sides_0, basis_0)
        solved = dot(arrays[0][rows, :], arrays[1][rows, :]).astype(BF16)
        coeffs = dot_left_t(solved, arrays[2][rows, :]).astype(BF16)
        kept[1][i // 2, :, pl.ds((i % 2) * rank, rank)] = coeffs
    for tier in range(1, depth + 1):
        count = leaf_count >> tier
        start = leaf_count - 2 * count
        for e in range(count):
            rows = pl.ds((start + e) * double, double)
            for copy in copies[first + 2 * (start + e) : first + 2 * (start + e) + 2]:
                copy.wait()
            coeffs = climb(kept[tier][e], merge[rows, :], transfer[rows, :])
            if tier < depth:
                kept[tier + 1][e // 2, :, pl.ds((e % 2) * rank, rank)] = coeffs
            else:
                split_rows(coeffs, core_of(), keep, send, work)


def descend_local_kernel(
    mine, other, low_paired, high_paired, sides_0, inverse_0, basis_0, sides, inverse, basis, merge,
    transfer, out, parent, result, sems
):
    leaf = inverse.shape[1]
    rank = basis.shape[1]
    double = 2 * rank
    kept = {1: low_paired, 2: high_paired}
    leaf_count = out.shape[0] // leaf
    depth = leaf_count.bit_length() - 1
    join_rows(mine[...], other[...], core_of(), parent)
    level = [parent[...]]
    for tier in range(depth, 0, -1):
        nodes = leaf_count >> tier
        start = leaf_count - 2 * nodes
        below = []
        for e in range(nodes):
            rows = pl.ds((start + e) * double, double)
            children = descend(level[e], kept[tier][e], merge[rows, :], transfer[rows, :])
            below += [children[:, :rank], children[:, rank:]]
        level = below
    copies = []
    for i in range(leaf_count):
        rows = pl.ds(max(i - 1, 0) * leaf, leaf)
        arrays = (inverse, sides, basis) if i else (inverse_0, sides_0, basis_0)
        spread = dot_right_t(arrays[2][rows, :], level[i])
        rest = (arrays[1][rows, :].astype(F32) - spread).astype(BF16)
        result[i] = dot(arrays[0][rows, :], rest)
        copies.append(
            pltpu.make_async_copy(result.at[i], out.at[pl.ds(i * leaf, leaf), :], sems.at[i])
        )
        copies[-1].start()
    for copy in copies:
        copy.wait()


def place_rows(block, low, size, out, at):
    width = block.shape[-1]
    for lanes in range(out.shape[1] // width):
        out[pl.ds(at, size), pl.ds(lanes * width, width)] = block[pl.ds(low + lanes * size, size), :]


def pair_matrix_kernel(mine, other, out):
    size = out.shape[0] // 2
    core = core_of()
    place_rows(mine, 0, size, out, pl.multiple_of(core * size, size))
    place_rows(other, 0, size, out, pl.multiple_of((1 - core) * size, size))


def quad_matrix_kernel(mine, other, far, far_other, out):
    size = out.shape[0] // 4
    core, side = core_of(), chip_of() % 2
    blocks = [(side, core, mine), (side, 1 - core, other)]
    blocks += [(1 - side, core, far), (1 - side, 1 - core, far_other)]
    for chip, which, ref in blocks:
        place_rows(ref, 0, size, out, pl.multiple_of((2 * chip + which) * size, size))


def split_high_kernel(mine, far, levels, top):
    for i, ref in enumerate((mine, far)):
        at = ref.shape[0] - top.shape[1]
        top[i] = ref[pl.ds(at, top.shape[1]), :]
        levels[i] = ref[pl.ds(at - levels.shape[1], levels.shape[1]), :]


def extend_kernel(mine, other, out):
    out[pl.ds(0, mine.shape[0]), :] = mine[...]
    out[pl.ds(mine.shape[0], other.shape[0]), :] = other[...]


def stack_kernel(*refs):
    *ins, out = refs
    at = 0
    for ref in ins:
        if len(ref.shape) == 2:
            out[at] = ref[...]
            at += 1
        else:
            out[pl.ds(at, ref.shape[0])] = ref[...]
            at += ref.shape[0]


def device_blocks(refs, chips):
    inner, core = inner_chips(chips), core_of()
    own = inner.index(chips // 2 - 1)
    order = [inner[own]] + inner[:own] + inner[own + 1 :]
    for source, mine, other in zip(order, refs[::2], refs[1::2]):
        for i, chip in enumerate((source, source ^ 1)):
            for which, ref in ((core, mine), (1 - core, other)):
                yield 2 * mirrored(chip, chips) + which, ref.at[i]


def high_matrix_kernel(*refs, chips, heights):
    refs, outs = refs[: -len(heights)], refs[-len(heights) :]
    rows = sum(heights)
    for device, ref in device_blocks(refs, chips):
        offset = 0
        for out, height in zip(outs, heights):
            width = ref.shape[-1]
            for lanes in range(out.shape[1] // width):
                out[
                    pl.ds(pl.multiple_of(device * height, height), height),
                    pl.ds(lanes * width, width),
                ] = ref[pl.ds(lanes * rows + offset, height), :]
            offset += height


def top_matrix_kernel(*refs, chips):
    refs, top = refs[:-1], refs[-1]
    width = top.shape[1] // (2 * chips)
    for device, ref in device_blocks(refs, chips):
        size = top.shape[0] * width // ref.shape[-1]
        for piece in range(ref.shape[-1] // width):
            top[pl.ds(piece * size, size), pl.ds(pl.multiple_of(device * width, width), width)] = ref[
                :, pl.ds(piece * width, width)
            ]


def pair_up_kernel(mine, other, matrix, paired, coeffs):
    double = paired.shape[1]
    join_lanes(mine[...], other[...], core_of(), paired)
    coeffs[...] = climb(
        paired[...], matrix[:, pl.ds(0, double)], matrix[:, pl.ds(double, double // 2)]
    )


def quad_up_kernel(mine, other, matrix, paired, near, far, work, *, chips):
    double = paired.shape[1]
    join_lanes(mine[...], other[...], chip_of() % 2, paired)
    coeffs = climb(paired[...], matrix[:, pl.ds(0, double)], matrix[:, pl.ds(double, double // 2)])
    split_rows(coeffs, jnp.where(in_lower(chips), 0, 1), near, far, work)


def high_up_kernel(*refs, chips, levels):
    quads = chips // 2
    parts, matrices = refs[:quads], refs[quads : quads + levels]
    kept, coeffs = refs[quads + levels : quads + 2 * levels], refs[-1]
    rank = coeffs.shape[1]
    double = 2 * rank
    for i, part in enumerate(parts):
        at = jnp.where(in_lower(chips), i, quads - 1 - i)
        lanes = pl.ds(pl.multiple_of((at % 2) * rank, rank), rank)
        kept[0][at // 2, :, lanes] = part[...]
    for tier in range(levels):
        nodes = quads >> tier + 1
        for e in range(nodes):
            rows = pl.ds(e * double, double)
            matrix = matrices[tier]
            value = climb(
                kept[tier][e], matrix[rows, pl.ds(0, double)], matrix[rows, pl.ds(double, rank)]
            )
            if tier + 1 < levels:
                kept[tier + 1][e // 2, :, pl.ds((e % 2) * rank, rank)] = value
            else:
                coeffs[...] = value


def high_down_kernel(*refs, chips, levels, roots):
    quads = chips // 2
    own, top = refs[:2]
    matrices, kept, outs = refs[2 : 2 + levels], refs[2 + levels : 2 + 2 * levels], refs[2 + 2 * levels : -2]
    stacked, below = refs[-2:]
    rank = outs[0].shape[1]
    double = 2 * rank
    me = lax.axis_index("root")
    share = stacked.shape[0]
    for mask in range(roots):
        at = pl.multiple_of((me ^ mask) * rank, rank)
        stacked[:, pl.ds(at, rank)] = own[pl.ds(mask * share, share), :]
    level = [dot_right_t(stacked[...], top[...]).astype(BF16)]
    for tier in range(levels - 1, -1, -1):
        values = []
        for e in range(quads >> tier + 1):
            rows = pl.ds(e * double, double)
            matrix = matrices[tier]
            children = descend(
                level[e],
                kept[tier][e],
                matrix[rows, pl.ds(0, double)],
                matrix[rows, pl.ds(double, rank)],
            )
            values += [children[:, :rank], children[:, rank:]]
        level = values
    for i in range(quads):
        below[i] = level[i]
    for i in range(quads):
        outs[i][...] = below[jnp.where(in_lower(chips), i, quads - 1 - i)]


def quad_down_kernel(*refs, chips):
    parts, (paired, matrix, keep, send, parent, work) = refs[:-6], refs[-6:]
    double = paired.shape[1]
    at = chip_of()
    line = mirrored(at, chips)
    near, far = parts[0][...], parts[-1][...]
    for source, part in zip(inner_chips(chips), parts):
        near = jnp.where(line == source, part[...], near)
        far = jnp.where(line == chips - 1 - source, part[...], far)
    join_rows(near, far, jnp.where(in_lower(chips), 0, 1), parent)
    children = descend(
        parent[...], paired[...], matrix[:, pl.ds(0, double)], matrix[:, pl.ds(double, double // 2)]
    )
    split_lanes(children, at % 2, keep, send, work)


def pair_down_kernel(mine, other, paired, matrix, keep, send, work, *, chips):
    double = paired.shape[1]
    inner = (chip_of() % 2 == 1) == in_lower(chips)
    parent = jnp.where(inner, mine[...], other[...])
    children = descend(
        parent, paired[...], matrix[:, pl.ds(0, double)], matrix[:, pl.ds(double, double // 2)]
    )
    split_lanes(children, core_of(), keep, send, work)


def body(
    right_side,
    leaf_inverse,
    leaf_basis,
    local_merge,
    local_transfer,
    upper_merge,
    upper_transfer,
    top_inverse,
):
    leaf = leaf_inverse.shape[2]
    rank = leaf_basis.shape[2]
    columns = right_side.shape[2]
    double = 2 * rank
    wide = double + rank
    leaf_count = right_side.shape[1] // leaf
    sub_count = lax.axis_size("sub")
    sub_depth = sub_count.bit_length() - 1
    root_count = lax.axis_size("root")
    chips = sub_count // 2
    middle = chips // 2 - 1
    half, quarter = columns // 2, columns // 4
    heights = [double >> tier for tier in range(3, sub_depth + 1)]
    levels = len(heights)
    quads = chips // 2

    local = [right_side[0], leaf_inverse[0], leaf_basis[0]]
    tree = [local_merge[0], local_transfer[0]]
    first_shapes = [(leaf, a.shape[1]) for a in local]
    blocks = wide // rank
    top_rows, top_width = top_inverse.shape
    quad_rows = blocks * (double // 4)
    top_block = top_rows * top_width // rank
    high_rows = blocks * sum(heights) + top_block
    any_spec, vmem_spec = pl.BlockSpec(memory_space=pl.ANY), pl.BlockSpec(memory_space=pltpu.VMEM)
    shapes = [(blocks * (double // 2), rank)]
    shapes += [(quad_rows + high_rows, rank)]
    shapes += first_shapes
    args = [upper_merge[0], upper_transfer[0], top_inverse] + local
    pair, quad_high, *first = pl.pallas_call(
        pack_kernel,
        out_shape=[pltpu.VMEM(shape, BF16) for shape in shapes],
        in_specs=[any_spec] * len(args),
        out_specs=[vmem_spec] * len(shapes),
        scratch_shapes=[pltpu.SemaphoreType.DMA((3 * blocks + rank // top_width + 3,))],
        compiler_params=pltpu.CompilerParams(vmem_limit_bytes=2 * MIB),
        cost_estimate=cost(1.5),
    )(*[pltpu.with_memory_space_constraint(a, pltpu.HBM) for a in args])
    far = flip(quad_high, "sub", 2)
    pair_other = flip(pair, "sub", 1)
    other = flip(quad_high, "sub", 1)

    shapes = [
        (half, rank),
        (half, rank),
        (leaf_count // 2, columns, double),
        (leaf_count // 4, columns, double),
    ]
    shapes += [(a.shape[0] - leaf, a.shape[1]) for a in local] + [a.shape for a in tree]
    args = [pltpu.with_memory_space_constraint(a, pltpu.HBM) for a in local + tree]
    args += [pltpu.with_memory_space_constraint(a, pltpu.VMEM) for a in first]
    keep, send, low_paired, high_paired, *local = pl.pallas_call(
        climb_local_kernel,
        out_shape=[pltpu.VMEM(shape, BF16) for shape in shapes],
        in_specs=[any_spec] * 5 + [vmem_spec] * 3,
        out_specs=[vmem_spec] * len(shapes),
        scratch_shapes=[
            pltpu.VMEM((columns, rank), BF16),
            pltpu.SemaphoreType.DMA((5 * leaf_count - 5,)),
        ],
        compiler_params=pltpu.CompilerParams(vmem_limit_bytes=16 * MIB),
        cost_estimate=cost(0.01),
    )(*args)

    recv = flip(send, "sub", 1)
    pair_other, token = lax.optimization_barrier((pair_other, mark(send)))
    (pair_matrix,) = vmem_call(pair_matrix_kernel, [(double, wide)], [pair, pair_other])
    pair_paired, coeffs = vmem_call(
        pair_up_kernel,
        [(half, double), (half, rank)],
        [keep, recv, pair_matrix],
        micros=0.05,
        after=[token],
    )

    recv = flip(coeffs, "sub", 2)
    recv = passed(recv)
    far, token = lax.optimization_barrier((far, mark(coeffs)))
    far_other = flip(far, "sub", 1)
    block_shapes = [(2, high_rows - top_block, rank), (2, top_block, rank)]
    blocks_mine = vmem_call(split_high_kernel, block_shapes, [quad_high, far])
    inner = inner_chips(chips)
    others = [s for s in inner if s != middle]
    rows_rest = [swapped(blocks_mine[0], s, middle, chips) for s in others]
    (quad_matrix,) = vmem_call(
        quad_matrix_kernel, [(double, wide)], [quad_high, other, far, far_other], after=[recv]
    )
    quad_paired, near, send = vmem_call(
        functools.partial(quad_up_kernel, chips=chips),
        [(half, double), (quarter, rank), (quarter, rank)],
        [coeffs, recv, quad_matrix],
        [pltpu.VMEM((half, rank), BF16)],
        micros=0.05,
        after=[token],
    )

    own = inner.index(middle)
    parts = [
        passed(swapped(near if s < middle else send, s, middle, chips)) for s in others
    ]
    blocks_other = vmem_call(split_high_kernel, block_shapes, [other, far_other])
    top_mine, near = lax.optimization_barrier((blocks_mine[1], near))
    top_rest = [swapped(top_mine, s, middle, chips) for s in others]
    stacks = [blocks_mine[0], blocks_other[0]]
    for item in rows_rest:
        stacks += [item, flip(item, "sub", 1)]
    *high_matrices, = vmem_call(
        functools.partial(high_matrix_kernel, chips=chips, heights=heights),
        [(sub_count * height, wide) for height in heights],
        stacks,
        limit=8 * MIB,
        micros=0.2,
        after=parts,
    )
    *high_paired_up, coeffs = vmem_call(
        functools.partial(high_up_kernel, chips=chips, levels=levels),
        [(quads >> t + 1, quarter, double) for t in range(levels)] + [(quarter, rank)],
        parts[:own] + [near] + parts[own:] + high_matrices,
        limit=8 * MIB,
        micros=0.4,
    )

    mask = 1
    while mask < root_count:
        recv = flip(coeffs, "root", mask)
        (coeffs,) = vmem_call(extend_kernel, [(2 * coeffs.shape[0], rank)], [coeffs, recv])
        if mask == 1:
            top_rest, coeffs = lax.optimization_barrier((top_rest, coeffs))
        mask *= 2
    stacks = [top_mine, blocks_other[1]]
    for item in top_rest:
        stacks += [item, flip(item, "sub", 1)]
    (top_matrix,) = vmem_call(
        functools.partial(top_matrix_kernel, chips=chips),
        [(top_rows, sub_count * top_width)],
        stacks,
        limit=8 * MIB,
    )
    values = vmem_call(
        functools.partial(high_down_kernel, chips=chips, levels=levels, roots=root_count),
        [(quarter, rank)] * quads,
        [coeffs, top_matrix] + high_matrices + high_paired_up,
        [
            pltpu.VMEM((quarter, root_count * rank), BF16),
            pltpu.VMEM((quads, quarter, rank), BF16),
        ],
        limit=8 * MIB,
        micros=0.7,
    )

    parts = [
        value if s == middle else swapped(value, s, middle, chips)
        for s, value in zip(inner, values)
    ]
    keep, send = vmem_call(
        functools.partial(quad_down_kernel, chips=chips),
        [(half, rank), (half, rank)],
        parts + [quad_paired, quad_matrix],
        [pltpu.VMEM((half, rank), BF16), pltpu.VMEM((half, double), BF16)],
        micros=0.4,
    )
    recv = flip(send, "sub", 2)
    keep, send = vmem_call(
        functools.partial(pair_down_kernel, chips=chips),
        [(half, rank), (half, rank)],
        [keep, recv, pair_paired, pair_matrix],
        [pltpu.VMEM((half, double), BF16)],
        micros=0.4,
    )
    recv = flip(send, "sub", 1)

    args = [keep, recv, low_paired, high_paired] + first + local
    out = pl.pallas_call(
        descend_local_kernel,
        out_shape=jax.ShapeDtypeStruct((leaf_count * leaf, columns), F32),
        in_specs=[vmem_spec] * len(args),
        out_specs=any_spec,
        scratch_shapes=[
            pltpu.VMEM((columns, rank), BF16),
            pltpu.VMEM((leaf_count, leaf, columns), F32),
            pltpu.SemaphoreType.DMA((leaf_count,)),
        ],
        compiler_params=pltpu.CompilerParams(vmem_limit_bytes=16 * MIB),
        cost_estimate=cost(3),
    )(*[pltpu.with_memory_space_constraint(a, pltpu.VMEM) for a in args])
    return out[None]


def solution(mesh):
    return jax.shard_map(
        body,
        mesh=mesh,
        in_specs=(
            P("root", "sub", None),
            P("root", "sub", None),
            P("root", "sub", None),
            P("root", "sub", None),
            P("root", "sub", None),
            P("root", "sub", None),
            P("root", "sub", None),
            P("root", "sub"),
        ),
        out_specs=P("root", "sub", None),
        check_vma=False,
    )
```

```python
import functools

import jax
import jax.numpy as jnp
from jax import lax
from jax.experimental import pallas as pl
from jax.experimental.pallas import tpu as pltpu
from jax.sharding import PartitionSpec as P

BF16 = jnp.bfloat16
F32 = jnp.float32
MIB = 1 << 20


def dot(left, right):
    return lax.dot_general(left, right, (((1,), (0,)), ((), ())), preferred_element_type=F32)


def dot_left_t(left, right):
    return lax.dot_general(left, right, (((0,), (0,)), ((), ())), preferred_element_type=F32)


def dot_right_t(left, right):
    return lax.dot_general(left, right, (((1,), (1,)), ((), ())), preferred_element_type=F32)


def cost(micros):
    return pl.CostEstimate(flops=int(micros * 1e9), bytes_accessed=1, transcendentals=0)


def vmem_call(kernel, outs, args, scratch=(), limit=4 * MIB, micros=0.1, after=()):
    count = len(args)
    args = list(args) + list(after)
    return pl.pallas_call(
        lambda *refs: kernel(*refs[:count], *refs[len(args) :]),
        out_shape=[pltpu.VMEM(shape, BF16) for shape in outs],
        in_specs=[pl.BlockSpec(memory_space=pltpu.VMEM)] * len(args),
        out_specs=[pl.BlockSpec(memory_space=pltpu.VMEM)] * len(outs),
        scratch_shapes=list(scratch),
        compiler_params=pltpu.CompilerParams(vmem_limit_bytes=limit),
        cost_estimate=cost(micros),
    )(*[pltpu.with_memory_space_constraint(a, pltpu.VMEM) for a in args])


def copy_kernel(value, out):
    out[...] = value[...]


def passed(value):
    return vmem_call(copy_kernel, [value.shape], [value], micros=10)[0]


def mark_kernel(value, out):
    out[...] = value[pl.ds(0, out.shape[0]), pl.ds(0, out.shape[1])]


def mark(value):
    return vmem_call(mark_kernel, [(16, 128)], [value], micros=0.02)[0]


def flip(block, axis, mask):
    count = lax.axis_size(axis)
    return lax.ppermute(block, axis, [(i, i ^ mask) for i in range(count)])


def swap_with(source, target, chips):
    partner = [device ^ 1 for device in range(2 * chips)]
    for low, high in ((source, target), (chips - 1 - source, chips - 1 - target)):
        for core in range(2):
            partner[2 * low + core], partner[2 * high + core] = 2 * high + core, 2 * low + core
    return list(enumerate(partner))


def inner_chips(chips):
    return [chip for chip in range(chips) if (chip % 2 == 1) == (chip < chips // 2)]


def swapped(block, source, target, chips):
    return lax.ppermute(block, "sub", swap_with(source, target, chips))


def core_of():
    return lax.axis_index("sub") % 2


def chip_of():
    return lax.axis_index("sub") // 2


def in_lower(chips):
    return chip_of() < chips // 2


def mirrored(chip, chips):
    return jnp.where(in_lower(chips), chip, chips - 1 - chip)


def split_rows(value, first, keep, send, work):
    half = value.shape[0] // 2
    work[...] = value
    keep[...] = work[pl.ds(pl.multiple_of(first * half, half), half), :]
    send[...] = work[pl.ds(pl.multiple_of((1 - first) * half, half), half), :]


def split_lanes(value, first, keep, send, work):
    half = value.shape[1] // 2
    work[...] = value
    keep[...] = work[:, pl.ds(pl.multiple_of(first * half, half), half)]
    send[...] = work[:, pl.ds(pl.multiple_of((1 - first) * half, half), half)]


def join_rows(mine, other, first, work):
    half = mine.shape[0]
    work[pl.ds(pl.multiple_of(first * half, half), half), :] = mine
    work[pl.ds(pl.multiple_of((1 - first) * half, half), half), :] = other


def join_lanes(mine, other, first, work):
    half = mine.shape[1]
    work[:, pl.ds(pl.multiple_of(first * half, half), half)] = mine
    work[:, pl.ds(pl.multiple_of((1 - first) * half, half), half)] = other


def climb(paired, merge_mat, transfer):
    inner = dot_right_t(paired, merge_mat).astype(BF16)
    return dot(inner, transfer).astype(BF16)


def descend(parent, paired, merge_mat, transfer):
    rest = (paired.astype(F32) - dot_right_t(parent, transfer)).astype(BF16)
    return dot_right_t(rest, merge_mat).astype(BF16)


def pack_kernel(merge, transfer, top, sides_in, inverse_in, basis_in, *refs):
    low, quad, high, sides, inverse, basis, sems = refs
    rows, double = merge.shape
    rank = transfer.shape[1]
    steps = []

    def fetch(source, target):
        steps.append(pltpu.make_async_copy(source, target, sems.at[len(steps)]))

    def level_rows(low, size, target, at):
        for lanes in range(double // rank):
            fetch(
                merge.at[pl.ds(low, size), pl.ds(lanes * rank, rank)], target.at[pl.ds(at, size), :]
            )
            at += size
        fetch(transfer.at[pl.ds(low, size), :], target.at[pl.ds(at, size), :])
        return at + size

    quad_low, high_low = double // 2, double // 2 + double // 4
    at = level_rows(high_low, rows - high_low, high, 0)
    width = top.shape[1]
    size = top.shape[0] * width // rank
    for piece in range(rank // width):
        fetch(
            top.at[pl.ds(piece * size, size), :],
            high.at[pl.ds(at, size), pl.ds(piece * width, width)],
        )
    level_rows(quad_low, high_low - quad_low, quad, 0)
    pair_rows = level_rows(0, quad_low, low, 0)
    for source, target in ((inverse_in, inverse), (sides_in, sides), (basis_in, basis)):
        fetch(source.at[pl.ds(0, target.shape[0]), :], target)
    for step in steps:
        step.start()
    for step in steps:
        step.wait()
    low[pl.ds(pair_rows, quad.shape[0]), :] = quad[...]


def climb_local_kernel(
    sides_in, inverse_in, basis_in, merge_in, transfer_in, sides_0, inverse_0, basis_0, keep, send,
    low_paired, high_paired, sides, inverse, basis, merge, transfer, work, sems
):
    leaf = inverse.shape[1]
    rank = basis.shape[1]
    double = 2 * rank
    kept = {1: low_paired, 2: high_paired}
    leaf_count = sides_in.shape[0] // leaf
    depth = leaf_count.bit_length() - 1
    nodes = leaf_count - 1
    copies = []

    def fetch(source, target, low, at, size):
        copies.append(
            pltpu.make_async_copy(
                source.at[pl.ds(low, size), :], target.at[pl.ds(at, size), :], sems.at[len(copies)]
            )
        )

    head = sides_0.shape[0] // leaf
    for i in range(head, leaf_count):
        fetch(inverse_in, inverse, i * leaf, (i - head) * leaf, leaf)
        fetch(sides_in, sides, i * leaf, (i - head) * leaf, leaf)
        fetch(basis_in, basis, i * leaf, (i - head) * leaf, leaf)
    first = len(copies)
    for e in range(nodes):
        fetch(merge_in, merge, e * double, e * double, double)
        fetch(transfer_in, transfer, e * double, e * double, double)
    for copy in copies:
        copy.start()
    for i in range(leaf_count):
        rows = pl.ds((i if i < head else i - head) * leaf, leaf)
        if i >= head:
            for copy in copies[3 * (i - head) : 3 * (i - head) + 3]:
                copy.wait()
        arrays = (inverse, sides, basis) if i >= head else (inverse_0, sides_0, basis_0)
        solved = dot(arrays[0][rows, :], arrays[1][rows, :]).astype(BF16)
        coeffs = dot_left_t(solved, arrays[2][rows, :]).astype(BF16)
        kept[1][i // 2, :, pl.ds((i % 2) * rank, rank)] = coeffs
    for tier in range(1, depth + 1):
        count = leaf_count >> tier
        start = leaf_count - 2 * count
        for e in range(count):
            rows = pl.ds((start + e) * double, double)
            for copy in copies[first + 2 * (start + e) : first + 2 * (start + e) + 2]:
                copy.wait()
            coeffs = climb(kept[tier][e], merge[rows, :], transfer[rows, :])
            if tier < depth:
                kept[tier + 1][e // 2, :, pl.ds((e % 2) * rank, rank)] = coeffs
            else:
                split_rows(coeffs, core_of(), keep, send, work)


def descend_local_kernel(
    mine, other, low_paired, high_paired, sides_0, inverse_0, basis_0, sides, inverse, basis, merge,
    transfer, out, parent, result, sems
):
    leaf = inverse.shape[1]
    rank = basis.shape[1]
    double = 2 * rank
    kept = {1: low_paired, 2: high_paired}
    leaf_count = out.shape[0] // leaf
    depth = leaf_count.bit_length() - 1
    join_rows(mine[...], other[...], core_of(), parent)
    level = [parent[...]]
    for tier in range(depth, 0, -1):
        nodes = leaf_count >> tier
        start = leaf_count - 2 * nodes
        below = []
        for e in range(nodes):
            rows = pl.ds((start + e) * double, double)
            children = descend(level[e], kept[tier][e], merge[rows, :], transfer[rows, :])
            below += [children[:, :rank], children[:, rank:]]
        level = below
    copies = []
    for i in range(leaf_count):
        head = sides_0.shape[0] // leaf
        rows = pl.ds((i if i < head else i - head) * leaf, leaf)
        arrays = (inverse, sides, basis) if i >= head else (inverse_0, sides_0, basis_0)
        spread = dot_right_t(arrays[2][rows, :], level[i])
        rest = (arrays[1][rows, :].astype(F32) - spread).astype(BF16)
        result[i] = dot(arrays[0][rows, :], rest)
        copies.append(
            pltpu.make_async_copy(result.at[i], out.at[pl.ds(i * leaf, leaf), :], sems.at[i])
        )
        copies[-1].start()
    for copy in copies:
        copy.wait()


def place_rows(block, low, size, out, at):
    width = block.shape[-1]
    for lanes in range(out.shape[1] // width):
        out[pl.ds(at, size), pl.ds(lanes * width, width)] = block[pl.ds(low + lanes * size, size), :]


def pair_matrix_kernel(mine, other, out):
    size = out.shape[0] // 2
    core = core_of()
    place_rows(mine, 0, size, out, pl.multiple_of(core * size, size))
    place_rows(other, 0, size, out, pl.multiple_of((1 - core) * size, size))


def quad_matrix_kernel(mine, other, far, far_other, out):
    size = out.shape[0] // 4
    core, side = core_of(), chip_of() % 2
    start = mine.shape[0] - far.shape[0]
    blocks = [(side, core, mine, start), (side, 1 - core, other, start)]
    blocks += [(1 - side, core, far, 0), (1 - side, 1 - core, far_other, 0)]
    for chip, which, ref, low in blocks:
        place_rows(ref, low, size, out, pl.multiple_of((2 * chip + which) * size, size))


def split_high_kernel(mine, far, levels, top):
    for i, ref in enumerate((mine, far)):
        at = ref.shape[0] - top.shape[1]
        top[i] = ref[pl.ds(at, top.shape[1]), :]
        levels[i] = ref[pl.ds(at - levels.shape[1], levels.shape[1]), :]


def extend_kernel(mine, other, out):
    out[pl.ds(0, mine.shape[0]), :] = mine[...]
    out[pl.ds(mine.shape[0], other.shape[0]), :] = other[...]


def stack_kernel(*refs):
    *ins, out = refs
    at = 0
    for ref in ins:
        if len(ref.shape) == 2:
            out[at] = ref[...]
            at += 1
        else:
            out[pl.ds(at, ref.shape[0])] = ref[...]
            at += ref.shape[0]


def device_blocks(refs, chips):
    inner, core = inner_chips(chips), core_of()
    own = inner.index(chips // 2 - 1)
    order = [inner[own]] + inner[:own] + inner[own + 1 :]
    for source, mine, other in zip(order, refs[::2], refs[1::2]):
        for i, chip in enumerate((source, source ^ 1)):
            for which, ref in ((core, mine), (1 - core, other)):
                yield 2 * mirrored(chip, chips) + which, ref.at[i]


def high_matrix_kernel(*refs, chips, heights):
    refs, outs = refs[: -len(heights)], refs[-len(heights) :]
    rows = sum(heights)
    for device, ref in device_blocks(refs, chips):
        offset = 0
        for out, height in zip(outs, heights):
            width = ref.shape[-1]
            for lanes in range(out.shape[1] // width):
                out[
                    pl.ds(pl.multiple_of(device * height, height), height),
                    pl.ds(lanes * width, width),
                ] = ref[pl.ds(lanes * rows + offset, height), :]
            offset += height


def top_matrix_kernel(*refs, chips):
    refs, top = refs[:-1], refs[-1]
    width = top.shape[1] // (2 * chips)
    for device, ref in device_blocks(refs, chips):
        size = top.shape[0] * width // ref.shape[-1]
        for piece in range(ref.shape[-1] // width):
            top[pl.ds(piece * size, size), pl.ds(pl.multiple_of(device * width, width), width)] = ref[
                :, pl.ds(piece * width, width)
            ]


def pair_up_kernel(mine, other, matrix, paired, coeffs):
    double = paired.shape[1]
    join_lanes(mine[...], other[...], core_of(), paired)
    coeffs[...] = climb(
        paired[...], matrix[:, pl.ds(0, double)], matrix[:, pl.ds(double, double // 2)]
    )


def quad_up_kernel(mine, other, matrix, paired, near, far, work, *, chips):
    double = paired.shape[1]
    join_lanes(mine[...], other[...], chip_of() % 2, paired)
    coeffs = climb(paired[...], matrix[:, pl.ds(0, double)], matrix[:, pl.ds(double, double // 2)])
    split_rows(coeffs, jnp.where(in_lower(chips), 0, 1), near, far, work)


def high_up_kernel(*refs, chips, levels):
    quads = chips // 2
    parts, matrices = refs[:quads], refs[quads : quads + levels]
    kept, coeffs = refs[quads + levels : quads + 2 * levels], refs[-1]
    rank = coeffs.shape[1]
    double = 2 * rank
    for i, part in enumerate(parts):
        at = jnp.where(in_lower(chips), i, quads - 1 - i)
        lanes = pl.ds(pl.multiple_of((at % 2) * rank, rank), rank)
        kept[0][at // 2, :, lanes] = part[...]
    for tier in range(levels):
        nodes = quads >> tier + 1
        for e in range(nodes):
            rows = pl.ds(e * double, double)
            matrix = matrices[tier]
            value = climb(
                kept[tier][e], matrix[rows, pl.ds(0, double)], matrix[rows, pl.ds(double, rank)]
            )
            if tier + 1 < levels:
                kept[tier + 1][e // 2, :, pl.ds((e % 2) * rank, rank)] = value
            else:
                coeffs[...] = value


def high_down_kernel(*refs, chips, levels, roots):
    quads = chips // 2
    own, top, refs = refs[:roots], refs[roots], refs[roots + 1 :]
    matrices, kept, outs = refs[:levels], refs[levels : 2 * levels], refs[2 * levels : -2]
    stacked, below = refs[-2:]
    rank = outs[0].shape[1]
    double = 2 * rank
    me = lax.axis_index("root")
    for mask in range(roots):
        at = pl.multiple_of((me ^ mask) * rank, rank)
        stacked[:, pl.ds(at, rank)] = own[mask][...]
    level = [dot_right_t(stacked[...], top[...]).astype(BF16)]
    for tier in range(levels - 1, -1, -1):
        values = []
        for e in range(quads >> tier + 1):
            rows = pl.ds(e * double, double)
            matrix = matrices[tier]
            children = descend(
                level[e],
                kept[tier][e],
                matrix[rows, pl.ds(0, double)],
                matrix[rows, pl.ds(double, rank)],
            )
            values += [children[:, :rank], children[:, rank:]]
        level = values
    for i in range(quads):
        below[i] = level[i]
    for i in range(quads):
        outs[i][...] = below[jnp.where(in_lower(chips), i, quads - 1 - i)]


def quad_down_kernel(*refs, chips):
    parts, (paired, matrix, keep, send, parent, work) = refs[:-6], refs[-6:]
    double = paired.shape[1]
    at = chip_of()
    line = mirrored(at, chips)
    near, far = parts[0][...], parts[-1][...]
    for source, part in zip(inner_chips(chips), parts):
        near = jnp.where(line == source, part[...], near)
        far = jnp.where(line == chips - 1 - source, part[...], far)
    join_rows(near, far, jnp.where(in_lower(chips), 0, 1), parent)
    children = descend(
        parent[...], paired[...], matrix[:, pl.ds(0, double)], matrix[:, pl.ds(double, double // 2)]
    )
    split_lanes(children, at % 2, keep, send, work)


def pair_down_kernel(mine, other, paired, matrix, keep, send, work, *, chips):
    double = paired.shape[1]
    inner = (chip_of() % 2 == 1) == in_lower(chips)
    parent = jnp.where(inner, mine[...], other[...])
    children = descend(
        parent, paired[...], matrix[:, pl.ds(0, double)], matrix[:, pl.ds(double, double // 2)]
    )
    split_lanes(children, core_of(), keep, send, work)


def body(
    right_side,
    leaf_inverse,
    leaf_basis,
    local_merge,
    local_transfer,
    upper_merge,
    upper_transfer,
    top_inverse,
):
    leaf = leaf_inverse.shape[2]
    rank = leaf_basis.shape[2]
    columns = right_side.shape[2]
    double = 2 * rank
    wide = double + rank
    leaf_count = right_side.shape[1] // leaf
    sub_count = lax.axis_size("sub")
    sub_depth = sub_count.bit_length() - 1
    root_count = lax.axis_size("root")
    chips = sub_count // 2
    middle = chips // 2 - 1
    half, quarter = columns // 2, columns // 4
    heights = [double >> tier for tier in range(3, sub_depth + 1)]
    levels = len(heights)
    quads = chips // 2

    local = [right_side[0], leaf_inverse[0], leaf_basis[0]]
    tree = [local_merge[0], local_transfer[0]]
    head = min(leaf_count // 2, 2) * leaf
    first_shapes = [(head, a.shape[1]) for a in local]
    blocks = wide // rank
    top_rows, top_width = top_inverse.shape
    quad_rows = blocks * (double // 4)
    top_block = top_rows * top_width // rank
    high_rows = blocks * sum(heights) + top_block
    any_spec, vmem_spec = pl.BlockSpec(memory_space=pl.ANY), pl.BlockSpec(memory_space=pltpu.VMEM)
    pair_rows = blocks * (double // 2)
    shapes = [(rows, rank) for rows in (pair_rows + quad_rows, quad_rows, high_rows)]
    shapes += first_shapes
    args = [upper_merge[0], upper_transfer[0], top_inverse] + local
    low, quad, high, *first = pl.pallas_call(
        pack_kernel,
        out_shape=[pltpu.VMEM(shape, BF16) for shape in shapes],
        in_specs=[any_spec] * len(args),
        out_specs=[vmem_spec] * len(shapes),
        scratch_shapes=[pltpu.SemaphoreType.DMA((3 * blocks + rank // top_width + 3,))],
        compiler_params=pltpu.CompilerParams(vmem_limit_bytes=2 * MIB),
        cost_estimate=cost(1.5),
    )(*[pltpu.with_memory_space_constraint(a, pltpu.HBM) for a in args])
    far_high = flip(high, "sub", 2)
    far = flip(quad, "sub", 2)
    low_other = flip(low, "sub", 1)

    shapes = [
        (half, rank),
        (half, rank),
        (leaf_count // 2, columns, double),
        (leaf_count // 4, columns, double),
    ]
    shapes += [(a.shape[0] - head, a.shape[1]) for a in local] + [a.shape for a in tree]
    args = [pltpu.with_memory_space_constraint(a, pltpu.HBM) for a in local + tree]
    args += [pltpu.with_memory_space_constraint(a, pltpu.VMEM) for a in first]
    keep, send, low_paired, high_paired, *local = pl.pallas_call(
        climb_local_kernel,
        out_shape=[pltpu.VMEM(shape, BF16) for shape in shapes],
        in_specs=[any_spec] * 5 + [vmem_spec] * 3,
        out_specs=[vmem_spec] * len(shapes),
        scratch_shapes=[
            pltpu.VMEM((columns, rank), BF16),
            pltpu.SemaphoreType.DMA((5 * leaf_count - 5,)),
        ],
        compiler_params=pltpu.CompilerParams(vmem_limit_bytes=16 * MIB),
        cost_estimate=cost(0.01),
    )(*args)

    recv = flip(send, "sub", 1)
    low_other, far_high, token = lax.optimization_barrier((low_other, far_high, mark(send)))
    (pair_matrix,) = vmem_call(pair_matrix_kernel, [(double, wide)], [low, low_other])
    block_shapes = [(2, high_rows - top_block, rank), (2, top_block, rank)]
    rows_mine, top_mine = vmem_call(split_high_kernel, block_shapes, [high, far_high])
    inner = inner_chips(chips)
    others = [s for s in inner if s != middle]
    rows_rest = [swapped(rows_mine, s, middle, chips) for s in others]
    pair_paired, coeffs = vmem_call(
        pair_up_kernel,
        [(half, double), (half, rank)],
        [keep, recv, pair_matrix],
        micros=0.05,
        after=[token],
    )

    recv = flip(coeffs, "sub", 2)
    recv = passed(recv)
    far, token = lax.optimization_barrier((far, mark(coeffs)))
    far_other = flip(far, "sub", 1)
    (quad_matrix,) = vmem_call(
        quad_matrix_kernel, [(double, wide)], [low, low_other, far, far_other], after=[recv] + rows_rest
    )
    quad_paired, near, send = vmem_call(
        functools.partial(quad_up_kernel, chips=chips),
        [(half, double), (quarter, rank), (quarter, rank)],
        [coeffs, recv, quad_matrix],
        [pltpu.VMEM((half, rank), BF16)],
        micros=0.05,
        after=[token],
    )

    own = inner.index(middle)
    parts = [
        passed(swapped(near if s < middle else send, s, middle, chips)) for s in others
    ]
    top_mine, rows_rest, near = lax.optimization_barrier((top_mine, rows_rest, near))
    top_rest = [swapped(top_mine, s, middle, chips) for s in others]
    stacks = [rows_mine, flip(rows_mine, "sub", 1)]
    for item in rows_rest:
        stacks += [item, flip(item, "sub", 1)]
    *high_matrices, = vmem_call(
        functools.partial(high_matrix_kernel, chips=chips, heights=heights),
        [(sub_count * height, wide) for height in heights],
        stacks,
        limit=8 * MIB,
        micros=0.2,
        after=parts,
    )
    *high_paired_up, coeffs = vmem_call(
        functools.partial(high_up_kernel, chips=chips, levels=levels),
        [(quads >> t + 1, quarter, double) for t in range(levels)] + [(quarter, rank)],
        parts[:own] + [near] + parts[own:] + high_matrices,
        limit=8 * MIB,
        micros=0.4,
    )

    roots = [flip(coeffs, "root", mask) for mask in range(root_count - 1, 0, -1)]
    top_rest, coeffs = lax.optimization_barrier((top_rest, coeffs))
    roots.append(coeffs)
    roots.reverse()
    stacks = [top_mine, flip(top_mine, "sub", 1)]
    for item in top_rest:
        stacks += [item, flip(item, "sub", 1)]
    (top_matrix,) = vmem_call(
        functools.partial(top_matrix_kernel, chips=chips),
        [(top_rows, sub_count * top_width)],
        stacks,
        limit=8 * MIB,
    )
    values = vmem_call(
        functools.partial(high_down_kernel, chips=chips, levels=levels, roots=root_count),
        [(quarter, rank)] * quads,
        roots + [top_matrix] + high_matrices + high_paired_up,
        [
            pltpu.VMEM((quarter, root_count * rank), BF16),
            pltpu.VMEM((quads, quarter, rank), BF16),
        ],
        limit=8 * MIB,
        micros=0.7,
    )

    parts = [
        value if s == middle else swapped(value, s, middle, chips)
        for s, value in zip(inner, values)
    ]
    keep, send = vmem_call(
        functools.partial(quad_down_kernel, chips=chips),
        [(half, rank), (half, rank)],
        parts + [quad_paired, quad_matrix],
        [pltpu.VMEM((half, rank), BF16), pltpu.VMEM((half, double), BF16)],
        micros=0.4,
    )
    recv = flip(send, "sub", 2)
    keep, send = vmem_call(
        functools.partial(pair_down_kernel, chips=chips),
        [(half, rank), (half, rank)],
        [keep, recv, pair_paired, pair_matrix],
        [pltpu.VMEM((half, double), BF16)],
        micros=0.4,
    )
    recv = flip(send, "sub", 1)

    args = [keep, recv, low_paired, high_paired] + first + local
    out = pl.pallas_call(
        descend_local_kernel,
        out_shape=jax.ShapeDtypeStruct((leaf_count * leaf, columns), F32),
        in_specs=[vmem_spec] * len(args),
        out_specs=any_spec,
        scratch_shapes=[
            pltpu.VMEM((columns, rank), BF16),
            pltpu.VMEM((leaf_count, leaf, columns), F32),
            pltpu.SemaphoreType.DMA((leaf_count,)),
        ],
        compiler_params=pltpu.CompilerParams(vmem_limit_bytes=16 * MIB),
        cost_estimate=cost(3),
    )(*[pltpu.with_memory_space_constraint(a, pltpu.VMEM) for a in args])
    return out[None]


def solution(mesh):
    return jax.shard_map(
        body,
        mesh=mesh,
        in_specs=(
            P("root", "sub", None),
            P("root", "sub", None),
            P("root", "sub", None),
            P("root", "sub", None),
            P("root", "sub", None),
            P("root", "sub", None),
            P("root", "sub", None),
            P("root", "sub"),
        ),
        out_specs=P("root", "sub", None),
        check_vma=False,
    )
```

```python
import functools

import jax
import jax.numpy as jnp
from jax import lax
from jax.experimental import pallas as pl
from jax.experimental.pallas import tpu as pltpu
from jax.sharding import PartitionSpec as P

BF16 = jnp.bfloat16
F32 = jnp.float32
MIB = 1 << 20


def dot(left, right):
    return lax.dot_general(left, right, (((1,), (0,)), ((), ())), preferred_element_type=F32)


def dot_left_t(left, right):
    return lax.dot_general(left, right, (((0,), (0,)), ((), ())), preferred_element_type=F32)


def dot_right_t(left, right):
    return lax.dot_general(left, right, (((1,), (1,)), ((), ())), preferred_element_type=F32)


def cost(micros):
    return pl.CostEstimate(flops=int(micros * 1e9), bytes_accessed=1, transcendentals=0)


def vmem_call(kernel, outs, args, scratch=(), limit=4 * MIB, micros=0.1, after=()):
    count = len(args)
    args = list(args) + list(after)
    return pl.pallas_call(
        lambda *refs: kernel(*refs[:count], *refs[len(args) :]),
        out_shape=[pltpu.VMEM(shape, BF16) for shape in outs],
        in_specs=[pl.BlockSpec(memory_space=pltpu.VMEM)] * len(args),
        out_specs=[pl.BlockSpec(memory_space=pltpu.VMEM)] * len(outs),
        scratch_shapes=list(scratch),
        compiler_params=pltpu.CompilerParams(vmem_limit_bytes=limit),
        cost_estimate=cost(micros),
    )(*[pltpu.with_memory_space_constraint(a, pltpu.VMEM) for a in args])


def copy_kernel(value, out):
    out[...] = value[...]


def passed(value, micros):
    return vmem_call(copy_kernel, [value.shape], [value], micros=micros)[0]


def mark_kernel(value, out):
    out[...] = value[pl.ds(0, out.shape[0]), pl.ds(0, out.shape[1])]


def mark(value):
    return vmem_call(mark_kernel, [(16, 128)], [value], micros=0.02)[0]


def flip(block, axis, mask):
    count = lax.axis_size(axis)
    return lax.ppermute(block, axis, [(i, i ^ mask) for i in range(count)])


def swap_with(source, target, chips):
    partner = [device ^ 1 for device in range(2 * chips)]
    for low, high in ((source, target), (chips - 1 - source, chips - 1 - target)):
        for core in range(2):
            partner[2 * low + core], partner[2 * high + core] = 2 * high + core, 2 * low + core
    return list(enumerate(partner))


def inner_chips(chips):
    return [chip for chip in range(chips) if (chip % 2 == 1) == (chip < chips // 2)]


def swapped(block, source, target, chips):
    return lax.ppermute(block, "sub", swap_with(source, target, chips))


def core_of():
    return lax.axis_index("sub") % 2


def chip_of():
    return lax.axis_index("sub") // 2


def in_lower(chips):
    return chip_of() < chips // 2


def mirrored(chip, chips):
    return jnp.where(in_lower(chips), chip, chips - 1 - chip)


def split_rows(value, first, keep, send, work):
    half = value.shape[0] // 2
    work[...] = value
    keep[...] = work[pl.ds(pl.multiple_of(first * half, half), half), :]
    send[...] = work[pl.ds(pl.multiple_of((1 - first) * half, half), half), :]


def split_lanes(value, first, keep, send, work):
    half = value.shape[1] // 2
    work[...] = value
    keep[...] = work[:, pl.ds(pl.multiple_of(first * half, half), half)]
    send[...] = work[:, pl.ds(pl.multiple_of((1 - first) * half, half), half)]


def join_rows(mine, other, first, work):
    half = mine.shape[0]
    work[pl.ds(pl.multiple_of(first * half, half), half), :] = mine
    work[pl.ds(pl.multiple_of((1 - first) * half, half), half), :] = other


def join_lanes(mine, other, first, work):
    half = mine.shape[1]
    work[:, pl.ds(pl.multiple_of(first * half, half), half)] = mine
    work[:, pl.ds(pl.multiple_of((1 - first) * half, half), half)] = other


def climb(paired, merge_mat, transfer):
    inner = dot_right_t(paired, merge_mat).astype(BF16)
    return dot(inner, transfer).astype(BF16)


def descend(parent, paired, merge_mat, transfer):
    rest = (paired.astype(F32) - dot_right_t(parent, transfer)).astype(BF16)
    return dot_right_t(rest, merge_mat).astype(BF16)


def pack_kernel(merge, transfer, top, sides_in, inverse_in, basis_in, *refs):
    low, quad, high, sides, inverse, basis, sems = refs
    rows, double = merge.shape
    rank = transfer.shape[1]
    steps = []

    def fetch(source, target):
        steps.append(pltpu.make_async_copy(source, target, sems.at[len(steps)]))

    def level_rows(low, size, target, at):
        for lanes in range(double // rank):
            fetch(
                merge.at[pl.ds(low, size), pl.ds(lanes * rank, rank)], target.at[pl.ds(at, size), :]
            )
            at += size
        fetch(transfer.at[pl.ds(low, size), :], target.at[pl.ds(at, size), :])
        return at + size

    quad_low, high_low = double // 2, double // 2 + double // 4
    at = level_rows(high_low, rows - high_low, high, 0)
    width = top.shape[1]
    size = top.shape[0] * width // rank
    for piece in range(rank // width):
        fetch(
            top.at[pl.ds(piece * size, size), :],
            high.at[pl.ds(at, size), pl.ds(piece * width, width)],
        )
    level_rows(quad_low, high_low - quad_low, quad, 0)
    pair_rows = level_rows(0, quad_low, low, 0)
    for source, target in ((inverse_in, inverse), (sides_in, sides), (basis_in, basis)):
        fetch(source.at[pl.ds(0, target.shape[0]), :], target)
    for step in steps:
        step.start()
    for step in steps:
        step.wait()
    low[pl.ds(pair_rows, quad.shape[0]), :] = quad[...]


def climb_local_kernel(
    sides_in, inverse_in, basis_in, merge_in, transfer_in, sides_0, inverse_0, basis_0, keep, send,
    low_paired, high_paired, sides, inverse, basis, merge, transfer, work, sems
):
    leaf = inverse.shape[1]
    rank = basis.shape[1]
    double = 2 * rank
    kept = {1: low_paired, 2: high_paired}
    leaf_count = sides_in.shape[0] // leaf
    depth = leaf_count.bit_length() - 1
    nodes = leaf_count - 1
    copies = []

    def fetch(source, target, low, at, size):
        copies.append(
            pltpu.make_async_copy(
                source.at[pl.ds(low, size), :], target.at[pl.ds(at, size), :], sems.at[len(copies)]
            )
        )

    head = sides_0.shape[0] // leaf
    for i in range(head, leaf_count):
        fetch(inverse_in, inverse, i * leaf, (i - head) * leaf, leaf)
        fetch(sides_in, sides, i * leaf, (i - head) * leaf, leaf)
        fetch(basis_in, basis, i * leaf, (i - head) * leaf, leaf)
    first = len(copies)
    for e in range(nodes):
        fetch(merge_in, merge, e * double, e * double, double)
        fetch(transfer_in, transfer, e * double, e * double, double)
    for copy in copies:
        copy.start()
    for i in range(leaf_count):
        rows = pl.ds((i if i < head else i - head) * leaf, leaf)
        if i >= head:
            for copy in copies[3 * (i - head) : 3 * (i - head) + 3]:
                copy.wait()
        arrays = (inverse, sides, basis) if i >= head else (inverse_0, sides_0, basis_0)
        solved = dot(arrays[0][rows, :], arrays[1][rows, :]).astype(BF16)
        coeffs = dot_left_t(solved, arrays[2][rows, :]).astype(BF16)
        kept[1][i // 2, :, pl.ds((i % 2) * rank, rank)] = coeffs
    for tier in range(1, depth + 1):
        count = leaf_count >> tier
        start = leaf_count - 2 * count
        for e in range(count):
            rows = pl.ds((start + e) * double, double)
            for copy in copies[first + 2 * (start + e) : first + 2 * (start + e) + 2]:
                copy.wait()
            coeffs = climb(kept[tier][e], merge[rows, :], transfer[rows, :])
            if tier < depth:
                kept[tier + 1][e // 2, :, pl.ds((e % 2) * rank, rank)] = coeffs
            else:
                split_rows(coeffs, core_of(), keep, send, work)


def descend_local_kernel(
    mine, other, low_paired, high_paired, sides_0, inverse_0, basis_0, sides, inverse, basis, merge,
    transfer, out, parent, result, sems
):
    leaf = inverse.shape[1]
    rank = basis.shape[1]
    double = 2 * rank
    kept = {1: low_paired, 2: high_paired}
    leaf_count = out.shape[0] // leaf
    depth = leaf_count.bit_length() - 1
    join_rows(mine[...], other[...], core_of(), parent)
    level = [parent[...]]
    for tier in range(depth, 0, -1):
        nodes = leaf_count >> tier
        start = leaf_count - 2 * nodes
        below = []
        for e in range(nodes):
            rows = pl.ds((start + e) * double, double)
            children = descend(level[e], kept[tier][e], merge[rows, :], transfer[rows, :])
            below += [children[:, :rank], children[:, rank:]]
        level = below
    copies = []
    for i in range(leaf_count):
        head = sides_0.shape[0] // leaf
        rows = pl.ds((i if i < head else i - head) * leaf, leaf)
        arrays = (inverse, sides, basis) if i >= head else (inverse_0, sides_0, basis_0)
        spread = dot_right_t(arrays[2][rows, :], level[i])
        rest = (arrays[1][rows, :].astype(F32) - spread).astype(BF16)
        result[i] = dot(arrays[0][rows, :], rest)
        copies.append(
            pltpu.make_async_copy(result.at[i], out.at[pl.ds(i * leaf, leaf), :], sems.at[i])
        )
        copies[-1].start()
    for copy in copies:
        copy.wait()


def place_rows(block, low, size, out, at):
    width = block.shape[-1]
    for lanes in range(out.shape[1] // width):
        out[pl.ds(at, size), pl.ds(lanes * width, width)] = block[pl.ds(low + lanes * size, size), :]


def pair_matrix_kernel(mine, other, out):
    size = out.shape[0] // 2
    core = core_of()
    place_rows(mine, 0, size, out, pl.multiple_of(core * size, size))
    place_rows(other, 0, size, out, pl.multiple_of((1 - core) * size, size))


def quad_matrix_kernel(mine, other, far, far_other, out):
    size = out.shape[0] // 4
    core, side = core_of(), chip_of() % 2
    start = mine.shape[0] - far.shape[0]
    blocks = [(side, core, mine, start), (side, 1 - core, other, start)]
    blocks += [(1 - side, core, far, 0), (1 - side, 1 - core, far_other, 0)]
    for chip, which, ref, low in blocks:
        place_rows(ref, low, size, out, pl.multiple_of((2 * chip + which) * size, size))


def split_high_kernel(mine, far, levels, top):
    for i, ref in enumerate((mine, far)):
        at = ref.shape[0] - top.shape[1]
        top[i] = ref[pl.ds(at, top.shape[1]), :]
        levels[i] = ref[pl.ds(at - levels.shape[1], levels.shape[1]), :]


def extend_kernel(mine, other, out):
    out[pl.ds(0, mine.shape[0]), :] = mine[...]
    out[pl.ds(mine.shape[0], other.shape[0]), :] = other[...]


def stack_kernel(*refs):
    *ins, out = refs
    at = 0
    for ref in ins:
        if len(ref.shape) == 2:
            out[at] = ref[...]
            at += 1
        else:
            out[pl.ds(at, ref.shape[0])] = ref[...]
            at += ref.shape[0]


def device_blocks(refs, chips):
    inner, core = inner_chips(chips), core_of()
    own = inner.index(chips // 2 - 1)
    order = [inner[own]] + inner[:own] + inner[own + 1 :]
    for source, mine, other in zip(order, refs[::2], refs[1::2]):
        for i, chip in enumerate((source, source ^ 1)):
            for which, ref in ((core, mine), (1 - core, other)):
                yield 2 * mirrored(chip, chips) + which, ref.at[i]


def high_matrix_kernel(*refs, chips, heights):
    refs, outs = refs[: -len(heights)], refs[-len(heights) :]
    rows = sum(heights)
    for device, ref in device_blocks(refs, chips):
        offset = 0
        for out, height in zip(outs, heights):
            width = ref.shape[-1]
            for lanes in range(out.shape[1] // width):
                out[
                    pl.ds(pl.multiple_of(device * height, height), height),
                    pl.ds(lanes * width, width),
                ] = ref[pl.ds(lanes * rows + offset, height), :]
            offset += height


def top_matrix_kernel(*refs, chips):
    refs, top = refs[:-1], refs[-1]
    width = top.shape[1] // (2 * chips)
    for device, ref in device_blocks(refs, chips):
        size = top.shape[0] * width // ref.shape[-1]
        for piece in range(ref.shape[-1] // width):
            top[pl.ds(piece * size, size), pl.ds(pl.multiple_of(device * width, width), width)] = ref[
                :, pl.ds(piece * width, width)
            ]


def pair_up_kernel(mine, other, matrix, paired, coeffs):
    double = paired.shape[1]
    join_lanes(mine[...], other[...], core_of(), paired)
    coeffs[...] = climb(
        paired[...], matrix[:, pl.ds(0, double)], matrix[:, pl.ds(double, double // 2)]
    )


def quad_up_kernel(mine, other, matrix, paired, near, far, work, *, chips):
    double = paired.shape[1]
    join_lanes(mine[...], other[...], chip_of() % 2, paired)
    coeffs = climb(paired[...], matrix[:, pl.ds(0, double)], matrix[:, pl.ds(double, double // 2)])
    split_rows(coeffs, jnp.where(in_lower(chips), 0, 1), near, far, work)


def high_up_kernel(*refs, chips, levels):
    quads = chips // 2
    parts, matrices = refs[:quads], refs[quads : quads + levels]
    kept, coeffs = refs[quads + levels : quads + 2 * levels], refs[-1]
    rank = coeffs.shape[1]
    double = 2 * rank
    for i, part in enumerate(parts):
        at = jnp.where(in_lower(chips), i, quads - 1 - i)
        lanes = pl.ds(pl.multiple_of((at % 2) * rank, rank), rank)
        kept[0][at // 2, :, lanes] = part[...]
    for tier in range(levels):
        nodes = quads >> tier + 1
        for e in range(nodes):
            rows = pl.ds(e * double, double)
            matrix = matrices[tier]
            value = climb(
                kept[tier][e], matrix[rows, pl.ds(0, double)], matrix[rows, pl.ds(double, rank)]
            )
            if tier + 1 < levels:
                kept[tier + 1][e // 2, :, pl.ds((e % 2) * rank, rank)] = value
            else:
                coeffs[...] = value


def high_down_kernel(*refs, chips, levels, roots):
    quads = chips // 2
    own, top, refs = refs[:roots], refs[roots], refs[roots + 1 :]
    matrices, kept, outs = refs[:levels], refs[levels : 2 * levels], refs[2 * levels : -2]
    stacked, below = refs[-2:]
    rank = outs[0].shape[1]
    double = 2 * rank
    me = lax.axis_index("root")
    for mask in range(roots):
        at = pl.multiple_of((me ^ mask) * rank, rank)
        stacked[:, pl.ds(at, rank)] = own[mask][...]
    level = [dot_right_t(stacked[...], top[...]).astype(BF16)]
    for tier in range(levels - 1, -1, -1):
        values = []
        for e in range(quads >> tier + 1):
            rows = pl.ds(e * double, double)
            matrix = matrices[tier]
            children = descend(
                level[e],
                kept[tier][e],
                matrix[rows, pl.ds(0, double)],
                matrix[rows, pl.ds(double, rank)],
            )
            values += [children[:, :rank], children[:, rank:]]
        level = values
    for i in range(quads):
        below[i] = level[i]
    for i in range(quads):
        outs[i][...] = below[jnp.where(in_lower(chips), i, quads - 1 - i)]


def quad_down_kernel(*refs, chips):
    parts, (paired, matrix, keep, send, parent, work) = refs[:-6], refs[-6:]
    double = paired.shape[1]
    at = chip_of()
    line = mirrored(at, chips)
    near, far = parts[0][...], parts[-1][...]
    for source, part in zip(inner_chips(chips), parts):
        near = jnp.where(line == source, part[...], near)
        far = jnp.where(line == chips - 1 - source, part[...], far)
    join_rows(near, far, jnp.where(in_lower(chips), 0, 1), parent)
    children = descend(
        parent[...], paired[...], matrix[:, pl.ds(0, double)], matrix[:, pl.ds(double, double // 2)]
    )
    split_lanes(children, at % 2, keep, send, work)


def pair_down_kernel(mine, other, paired, matrix, keep, send, work, *, chips):
    double = paired.shape[1]
    inner = (chip_of() % 2 == 1) == in_lower(chips)
    parent = jnp.where(inner, mine[...], other[...])
    children = descend(
        parent, paired[...], matrix[:, pl.ds(0, double)], matrix[:, pl.ds(double, double // 2)]
    )
    split_lanes(children, core_of(), keep, send, work)


def body(
    right_side,
    leaf_inverse,
    leaf_basis,
    local_merge,
    local_transfer,
    upper_merge,
    upper_transfer,
    top_inverse,
):
    leaf = leaf_inverse.shape[2]
    rank = leaf_basis.shape[2]
    columns = right_side.shape[2]
    double = 2 * rank
    wide = double + rank
    leaf_count = right_side.shape[1] // leaf
    sub_count = lax.axis_size("sub")
    sub_depth = sub_count.bit_length() - 1
    root_count = lax.axis_size("root")
    chips = sub_count // 2
    middle = chips // 2 - 1
    half, quarter = columns // 2, columns // 4
    heights = [double >> tier for tier in range(3, sub_depth + 1)]
    levels = len(heights)
    quads = chips // 2

    local = [right_side[0], leaf_inverse[0], leaf_basis[0]]
    tree = [local_merge[0], local_transfer[0]]
    head = min(leaf_count - 1, 3) * leaf
    first_shapes = [(head, a.shape[1]) for a in local]
    blocks = wide // rank
    top_rows, top_width = top_inverse.shape
    quad_rows = blocks * (double // 4)
    top_block = top_rows * top_width // rank
    high_rows = blocks * sum(heights) + top_block
    any_spec, vmem_spec = pl.BlockSpec(memory_space=pl.ANY), pl.BlockSpec(memory_space=pltpu.VMEM)
    pair_rows = blocks * (double // 2)
    shapes = [(rows, rank) for rows in (pair_rows + quad_rows, quad_rows, high_rows)]
    shapes += first_shapes
    args = [upper_merge[0], upper_transfer[0], top_inverse] + local
    low, quad, high, *first = pl.pallas_call(
        pack_kernel,
        out_shape=[pltpu.VMEM(shape, BF16) for shape in shapes],
        in_specs=[any_spec] * len(args),
        out_specs=[vmem_spec] * len(shapes),
        scratch_shapes=[pltpu.SemaphoreType.DMA((3 * blocks + rank // top_width + 3,))],
        compiler_params=pltpu.CompilerParams(vmem_limit_bytes=2 * MIB),
        cost_estimate=cost(1.5),
    )(*[pltpu.with_memory_space_constraint(a, pltpu.HBM) for a in args])
    far_high = flip(high, "sub", 2)
    far = flip(quad, "sub", 2)
    low_other = flip(low, "sub", 1)

    shapes = [
        (half, rank),
        (half, rank),
        (leaf_count // 2, columns, double),
        (leaf_count // 4, columns, double),
    ]
    shapes += [(a.shape[0] - head, a.shape[1]) for a in local] + [a.shape for a in tree]
    args = [pltpu.with_memory_space_constraint(a, pltpu.HBM) for a in local + tree]
    args += [pltpu.with_memory_space_constraint(a, pltpu.VMEM) for a in first]
    keep, send, low_paired, high_paired, *local = pl.pallas_call(
        climb_local_kernel,
        out_shape=[pltpu.VMEM(shape, BF16) for shape in shapes],
        in_specs=[any_spec] * 5 + [vmem_spec] * 3,
        out_specs=[vmem_spec] * len(shapes),
        scratch_shapes=[
            pltpu.VMEM((columns, rank), BF16),
            pltpu.SemaphoreType.DMA((5 * leaf_count - 5,)),
        ],
        compiler_params=pltpu.CompilerParams(vmem_limit_bytes=16 * MIB),
        cost_estimate=cost(0.01),
    )(*args)

    recv = flip(send, "sub", 1)
    recv = passed(recv, 0.4)
    low_other, far_high, token = lax.optimization_barrier((low_other, far_high, mark(send)))
    (pair_matrix,) = vmem_call(pair_matrix_kernel, [(double, wide)], [low, low_other])
    block_shapes = [(2, high_rows - top_block, rank), (2, top_block, rank)]
    rows_mine, top_mine = vmem_call(split_high_kernel, block_shapes, [high, far_high])
    inner = inner_chips(chips)
    others = [s for s in inner if s != middle]
    rows_rest = [swapped(rows_mine, s, middle, chips) for s in others]
    pair_paired, coeffs = vmem_call(
        pair_up_kernel,
        [(half, double), (half, rank)],
        [keep, recv, pair_matrix],
        micros=0.05,
        after=[token],
    )

    recv = flip(coeffs, "sub", 2)
    recv, rows_rest = lax.optimization_barrier((recv, rows_rest))
    recv = passed(recv, 10)
    far, top_mine, token = lax.optimization_barrier((far, top_mine, mark(coeffs)))
    top_rest = [swapped(top_mine, s, middle, chips) for s in others]
    far_other = flip(far, "sub", 1)
    (quad_matrix,) = vmem_call(
        quad_matrix_kernel, [(double, wide)], [low, low_other, far, far_other], after=[recv]
    )
    quad_paired, near, send = vmem_call(
        functools.partial(quad_up_kernel, chips=chips),
        [(half, double), (quarter, rank), (quarter, rank)],
        [coeffs, recv, quad_matrix],
        [pltpu.VMEM((half, rank), BF16)],
        micros=0.05,
        after=[token],
    )

    own = inner.index(middle)
    parts = [swapped(near if s < middle else send, s, middle, chips) for s in others]
    parts, top_rest = lax.optimization_barrier((parts, top_rest))
    parts = [passed(part, 10) for part in parts]
    rows_rest, near = lax.optimization_barrier((rows_rest, near))
    stacks = [rows_mine, flip(rows_mine, "sub", 1)]
    for item in rows_rest:
        stacks += [item, flip(item, "sub", 1)]
    *high_matrices, = vmem_call(
        functools.partial(high_matrix_kernel, chips=chips, heights=heights),
        [(sub_count * height, wide) for height in heights],
        stacks,
        limit=8 * MIB,
        micros=0.2,
        after=parts,
    )
    *high_paired_up, coeffs = vmem_call(
        functools.partial(high_up_kernel, chips=chips, levels=levels),
        [(quads >> t + 1, quarter, double) for t in range(levels)] + [(quarter, rank)],
        parts[:own] + [near] + parts[own:] + high_matrices,
        limit=8 * MIB,
        micros=0.4,
    )

    roots = [flip(coeffs, "root", mask) for mask in range(root_count - 1, 0, -1)]
    roots.append(coeffs)
    roots.reverse()
    stacks = [top_mine, flip(top_mine, "sub", 1)]
    for item in top_rest:
        stacks += [item, flip(item, "sub", 1)]
    (top_matrix,) = vmem_call(
        functools.partial(top_matrix_kernel, chips=chips),
        [(top_rows, sub_count * top_width)],
        stacks,
        limit=8 * MIB,
    )
    values = vmem_call(
        functools.partial(high_down_kernel, chips=chips, levels=levels, roots=root_count),
        [(quarter, rank)] * quads,
        roots + [top_matrix] + high_matrices + high_paired_up,
        [
            pltpu.VMEM((quarter, root_count * rank), BF16),
            pltpu.VMEM((quads, quarter, rank), BF16),
        ],
        limit=8 * MIB,
        micros=0.7,
    )

    parts = [
        value if s == middle else swapped(value, s, middle, chips)
        for s, value in zip(inner, values)
    ]
    keep, send = vmem_call(
        functools.partial(quad_down_kernel, chips=chips),
        [(half, rank), (half, rank)],
        parts + [quad_paired, quad_matrix],
        [pltpu.VMEM((half, rank), BF16), pltpu.VMEM((half, double), BF16)],
        micros=0.4,
    )
    recv = flip(send, "sub", 2)
    keep, send = vmem_call(
        functools.partial(pair_down_kernel, chips=chips),
        [(half, rank), (half, rank)],
        [keep, recv, pair_paired, pair_matrix],
        [pltpu.VMEM((half, double), BF16)],
        micros=0.4,
    )
    recv = flip(send, "sub", 1)

    args = [keep, recv, low_paired, high_paired] + first + local
    out = pl.pallas_call(
        descend_local_kernel,
        out_shape=jax.ShapeDtypeStruct((leaf_count * leaf, columns), F32),
        in_specs=[vmem_spec] * len(args),
        out_specs=any_spec,
        scratch_shapes=[
            pltpu.VMEM((columns, rank), BF16),
            pltpu.VMEM((leaf_count, leaf, columns), F32),
            pltpu.SemaphoreType.DMA((leaf_count,)),
        ],
        compiler_params=pltpu.CompilerParams(vmem_limit_bytes=16 * MIB),
        cost_estimate=cost(3),
    )(*[pltpu.with_memory_space_constraint(a, pltpu.VMEM) for a in args])
    return out[None]


def solution(mesh):
    return jax.shard_map(
        body,
        mesh=mesh,
        in_specs=(
            P("root", "sub", None),
            P("root", "sub", None),
            P("root", "sub", None),
            P("root", "sub", None),
            P("root", "sub", None),
            P("root", "sub", None),
            P("root", "sub", None),
            P("root", "sub"),
        ),
        out_specs=P("root", "sub", None),
        check_vma=False,
    )
```

```python
import functools

import jax
import jax.numpy as jnp
from jax import lax
from jax.experimental import pallas as pl
from jax.experimental.pallas import tpu as pltpu
from jax.sharding import PartitionSpec as P

BF16 = jnp.bfloat16
F32 = jnp.float32
MIB = 1 << 20


def dot(left, right):
    return lax.dot_general(left, right, (((1,), (0,)), ((), ())), preferred_element_type=F32)


def dot_left_t(left, right):
    return lax.dot_general(left, right, (((0,), (0,)), ((), ())), preferred_element_type=F32)


def dot_right_t(left, right):
    return lax.dot_general(left, right, (((1,), (1,)), ((), ())), preferred_element_type=F32)


def cost(micros):
    return pl.CostEstimate(flops=int(micros * 1e9), bytes_accessed=1, transcendentals=0)


def vmem_call(kernel, outs, args, scratch=(), limit=4 * MIB, micros=0.1, after=()):
    count = len(args)
    args = list(args) + list(after)
    return pl.pallas_call(
        lambda *refs: kernel(*refs[:count], *refs[len(args) :]),
        out_shape=[pltpu.VMEM(shape, BF16) for shape in outs],
        in_specs=[pl.BlockSpec(memory_space=pltpu.VMEM)] * len(args),
        out_specs=[pl.BlockSpec(memory_space=pltpu.VMEM)] * len(outs),
        scratch_shapes=list(scratch),
        compiler_params=pltpu.CompilerParams(vmem_limit_bytes=limit),
        cost_estimate=cost(micros),
    )(*[pltpu.with_memory_space_constraint(a, pltpu.VMEM) for a in args])


def copy_kernel(value, out):
    out[...] = value[...]


def passed(value, micros):
    return vmem_call(copy_kernel, [value.shape], [value], micros=micros)[0]


def mark_kernel(value, out):
    out[...] = value[pl.ds(0, out.shape[0]), pl.ds(0, out.shape[1])]


def mark(value):
    return vmem_call(mark_kernel, [(16, 128)], [value], micros=0.02)[0]


def flip(block, axis, mask):
    count = lax.axis_size(axis)
    return lax.ppermute(block, axis, [(i, i ^ mask) for i in range(count)])


def swap_with(source, target, chips):
    partner = [device ^ 1 for device in range(2 * chips)]
    for low, high in ((source, target), (chips - 1 - source, chips - 1 - target)):
        for core in range(2):
            partner[2 * low + core], partner[2 * high + core] = 2 * high + core, 2 * low + core
    return list(enumerate(partner))


def inner_chips(chips):
    return [chip for chip in range(chips) if (chip % 2 == 1) == (chip < chips // 2)]


def swapped(block, source, target, chips):
    return lax.ppermute(block, "sub", swap_with(source, target, chips))


def core_of():
    return lax.axis_index("sub") % 2


def chip_of():
    return lax.axis_index("sub") // 2


def in_lower(chips):
    return chip_of() < chips // 2


def mirrored(chip, chips):
    return jnp.where(in_lower(chips), chip, chips - 1 - chip)


def split_rows(value, first, keep, send, work):
    half = value.shape[0] // 2
    work[...] = value
    keep[...] = work[pl.ds(pl.multiple_of(first * half, half), half), :]
    send[...] = work[pl.ds(pl.multiple_of((1 - first) * half, half), half), :]


def split_lanes(value, first, keep, send, work):
    half = value.shape[1] // 2
    work[...] = value
    keep[...] = work[:, pl.ds(pl.multiple_of(first * half, half), half)]
    send[...] = work[:, pl.ds(pl.multiple_of((1 - first) * half, half), half)]


def join_rows(mine, other, first, work):
    half = mine.shape[0]
    work[pl.ds(pl.multiple_of(first * half, half), half), :] = mine
    work[pl.ds(pl.multiple_of((1 - first) * half, half), half), :] = other


def join_lanes(mine, other, first, work):
    half = mine.shape[1]
    work[:, pl.ds(pl.multiple_of(first * half, half), half)] = mine
    work[:, pl.ds(pl.multiple_of((1 - first) * half, half), half)] = other


def climb(paired, merge_mat, transfer):
    inner = dot_right_t(paired, merge_mat).astype(BF16)
    return dot(inner, transfer).astype(BF16)


def descend(parent, paired, merge_mat, transfer):
    rest = (paired.astype(F32) - dot_right_t(parent, transfer)).astype(BF16)
    return dot_right_t(rest, merge_mat).astype(BF16)


def pack_kernel(merge, transfer, top, sides_in, inverse_in, basis_in, *refs):
    low, quad_top, high, sides, inverse, basis, sems = refs
    rows, double = merge.shape
    rank = transfer.shape[1]
    steps = []

    def fetch(source, target):
        steps.append(pltpu.make_async_copy(source, target, sems.at[len(steps)]))

    def level_rows(low, size, target, at):
        for lanes in range(double // rank):
            fetch(
                merge.at[pl.ds(low, size), pl.ds(lanes * rank, rank)], target.at[pl.ds(at, size), :]
            )
            at += size
        fetch(transfer.at[pl.ds(low, size), :], target.at[pl.ds(at, size), :])
        return at + size

    quad_low, high_low = double // 2, double // 2 + double // 4
    level_rows(high_low, rows - high_low, high, 0)
    quad_rows = level_rows(quad_low, high_low - quad_low, quad_top, 0)
    width = top.shape[1]
    size = top.shape[0] * width // rank
    for piece in range(rank // width):
        fetch(
            top.at[pl.ds(piece * size, size), :],
            quad_top.at[pl.ds(quad_rows, size), pl.ds(piece * width, width)],
        )
    pair_rows = level_rows(0, quad_low, low, 0)
    for source, target in ((inverse_in, inverse), (sides_in, sides), (basis_in, basis)):
        fetch(source.at[pl.ds(0, target.shape[0]), :], target)
    for step in steps:
        step.start()
    for step in steps:
        step.wait()
    low[pl.ds(pair_rows, quad_rows), :] = quad_top[pl.ds(0, quad_rows), :]


def climb_local_kernel(
    sides_in, inverse_in, basis_in, merge_in, transfer_in, sides_0, inverse_0, basis_0, keep, send,
    low_paired, high_paired, sides, inverse, basis, merge, transfer, work, sems
):
    leaf = inverse.shape[1]
    rank = basis.shape[1]
    double = 2 * rank
    kept = {1: low_paired, 2: high_paired}
    leaf_count = sides_in.shape[0] // leaf
    depth = leaf_count.bit_length() - 1
    nodes = leaf_count - 1
    copies = []

    def fetch(source, target, low, at, size):
        copies.append(
            pltpu.make_async_copy(
                source.at[pl.ds(low, size), :], target.at[pl.ds(at, size), :], sems.at[len(copies)]
            )
        )

    head = sides_0.shape[0] // leaf
    for i in range(head, leaf_count):
        fetch(inverse_in, inverse, i * leaf, (i - head) * leaf, leaf)
        fetch(sides_in, sides, i * leaf, (i - head) * leaf, leaf)
        fetch(basis_in, basis, i * leaf, (i - head) * leaf, leaf)
    first = len(copies)
    for e in range(nodes):
        fetch(merge_in, merge, e * double, e * double, double)
        fetch(transfer_in, transfer, e * double, e * double, double)
    for copy in copies:
        copy.start()
    for i in range(leaf_count):
        rows = pl.ds((i if i < head else i - head) * leaf, leaf)
        if i >= head:
            for copy in copies[3 * (i - head) : 3 * (i - head) + 3]:
                copy.wait()
        arrays = (inverse, sides, basis) if i >= head else (inverse_0, sides_0, basis_0)
        solved = dot(arrays[0][rows, :], arrays[1][rows, :]).astype(BF16)
        coeffs = dot_left_t(solved, arrays[2][rows, :]).astype(BF16)
        kept[1][i // 2, :, pl.ds((i % 2) * rank, rank)] = coeffs
    for tier in range(1, depth + 1):
        count = leaf_count >> tier
        start = leaf_count - 2 * count
        for e in range(count):
            rows = pl.ds((start + e) * double, double)
            for copy in copies[first + 2 * (start + e) : first + 2 * (start + e) + 2]:
                copy.wait()
            coeffs = climb(kept[tier][e], merge[rows, :], transfer[rows, :])
            if tier < depth:
                kept[tier + 1][e // 2, :, pl.ds((e % 2) * rank, rank)] = coeffs
            else:
                split_rows(coeffs, core_of(), keep, send, work)


def descend_local_kernel(
    mine, other, low_paired, high_paired, sides_0, inverse_0, basis_0, sides, inverse, basis, merge,
    transfer, out, parent, result, sems
):
    leaf = inverse.shape[1]
    rank = basis.shape[1]
    double = 2 * rank
    kept = {1: low_paired, 2: high_paired}
    leaf_count = out.shape[0] // leaf
    depth = leaf_count.bit_length() - 1
    join_rows(mine[...], other[...], core_of(), parent)
    level = [parent[...]]
    for tier in range(depth, 0, -1):
        nodes = leaf_count >> tier
        start = leaf_count - 2 * nodes
        below = []
        for e in range(nodes):
            rows = pl.ds((start + e) * double, double)
            children = descend(level[e], kept[tier][e], merge[rows, :], transfer[rows, :])
            below += [children[:, :rank], children[:, rank:]]
        level = below
    copies = []
    for i in range(leaf_count):
        head = sides_0.shape[0] // leaf
        rows = pl.ds((i if i < head else i - head) * leaf, leaf)
        arrays = (inverse, sides, basis) if i >= head else (inverse_0, sides_0, basis_0)
        spread = dot_right_t(arrays[2][rows, :], level[i])
        rest = (arrays[1][rows, :].astype(F32) - spread).astype(BF16)
        result[i] = dot(arrays[0][rows, :], rest)
        copies.append(
            pltpu.make_async_copy(result.at[i], out.at[pl.ds(i * leaf, leaf), :], sems.at[i])
        )
        copies[-1].start()
    for copy in copies:
        copy.wait()


def place_rows(block, low, size, out, at):
    width = block.shape[-1]
    for lanes in range(out.shape[1] // width):
        out[pl.ds(at, size), pl.ds(lanes * width, width)] = block[pl.ds(low + lanes * size, size), :]


def pair_matrix_kernel(mine, other, out):
    size = out.shape[0] // 2
    core = core_of()
    place_rows(mine, 0, size, out, pl.multiple_of(core * size, size))
    place_rows(other, 0, size, out, pl.multiple_of((1 - core) * size, size))


def quad_matrix_kernel(mine, other, far, far_other, out):
    size = out.shape[0] // 4
    core, side = core_of(), chip_of() % 2
    start = mine.shape[0] - out.shape[1] // mine.shape[1] * size
    blocks = [(side, core, mine, start), (side, 1 - core, other, start)]
    blocks += [(1 - side, core, far, 0), (1 - side, 1 - core, far_other, 0)]
    for chip, which, ref, low in blocks:
        place_rows(ref, low, size, out, pl.multiple_of((2 * chip + which) * size, size))


def tails_kernel(mine, far, out):
    for i, ref in enumerate((mine, far)):
        out[i] = ref[pl.ds(ref.shape[0] - out.shape[1], out.shape[1]), :]


def extend_kernel(mine, other, out):
    out[pl.ds(0, mine.shape[0]), :] = mine[...]
    out[pl.ds(mine.shape[0], other.shape[0]), :] = other[...]


def stack_kernel(*refs):
    *ins, out = refs
    at = 0
    for ref in ins:
        if len(ref.shape) == 2:
            out[at] = ref[...]
            at += 1
        else:
            out[pl.ds(at, ref.shape[0])] = ref[...]
            at += ref.shape[0]


def device_blocks(refs, chips):
    inner, core = inner_chips(chips), core_of()
    own = inner.index(chips // 2 - 1)
    order = [inner[own]] + inner[:own] + inner[own + 1 :]
    for source, mine, other in zip(order, refs[::2], refs[1::2]):
        for i, chip in enumerate((source, source ^ 1)):
            for which, ref in ((core, mine), (1 - core, other)):
                yield 2 * mirrored(chip, chips) + which, ref.at[i]


def high_matrix_kernel(*refs, chips, heights):
    refs, outs = refs[: -len(heights)], refs[-len(heights) :]
    rows = sum(heights)
    for device, ref in device_blocks(refs, chips):
        offset = 0
        for out, height in zip(outs, heights):
            width = ref.shape[-1]
            for lanes in range(out.shape[1] // width):
                out[
                    pl.ds(pl.multiple_of(device * height, height), height),
                    pl.ds(lanes * width, width),
                ] = ref[pl.ds(lanes * rows + offset, height), :]
            offset += height


def top_matrix_kernel(*refs, chips):
    refs, top = refs[:-1], refs[-1]
    width = top.shape[1] // (2 * chips)
    for device, ref in device_blocks(refs, chips):
        size = top.shape[0] * width // ref.shape[-1]
        for piece in range(ref.shape[-1] // width):
            top[pl.ds(piece * size, size), pl.ds(pl.multiple_of(device * width, width), width)] = ref[
                :, pl.ds(piece * width, width)
            ]


def pair_up_kernel(mine, other, matrix, paired, coeffs):
    double = paired.shape[1]
    join_lanes(mine[...], other[...], core_of(), paired)
    coeffs[...] = climb(
        paired[...], matrix[:, pl.ds(0, double)], matrix[:, pl.ds(double, double // 2)]
    )


def quad_up_kernel(mine, other, matrix, paired, near, far, work, *, chips):
    double = paired.shape[1]
    join_lanes(mine[...], other[...], chip_of() % 2, paired)
    coeffs = climb(paired[...], matrix[:, pl.ds(0, double)], matrix[:, pl.ds(double, double // 2)])
    split_rows(coeffs, jnp.where(in_lower(chips), 0, 1), near, far, work)


def high_up_kernel(*refs, chips, levels):
    quads = chips // 2
    parts, matrices = refs[:quads], refs[quads : quads + levels]
    kept, coeffs = refs[quads + levels : quads + 2 * levels], refs[-1]
    rank = coeffs.shape[1]
    double = 2 * rank
    for i, part in enumerate(parts):
        at = jnp.where(in_lower(chips), i, quads - 1 - i)
        lanes = pl.ds(pl.multiple_of((at % 2) * rank, rank), rank)
        kept[0][at // 2, :, lanes] = part[...]
    for tier in range(levels):
        nodes = quads >> tier + 1
        for e in range(nodes):
            rows = pl.ds(e * double, double)
            matrix = matrices[tier]
            value = climb(
                kept[tier][e], matrix[rows, pl.ds(0, double)], matrix[rows, pl.ds(double, rank)]
            )
            if tier + 1 < levels:
                kept[tier + 1][e // 2, :, pl.ds((e % 2) * rank, rank)] = value
            else:
                coeffs[...] = value


def high_down_kernel(*refs, chips, levels, roots):
    quads = chips // 2
    own, top, refs = refs[:roots], refs[roots], refs[roots + 1 :]
    matrices, kept, outs = refs[:levels], refs[levels : 2 * levels], refs[2 * levels : -2]
    stacked, below = refs[-2:]
    rank = outs[0].shape[1]
    double = 2 * rank
    me = lax.axis_index("root")
    for mask in range(roots):
        at = pl.multiple_of((me ^ mask) * rank, rank)
        stacked[:, pl.ds(at, rank)] = own[mask][...]
    level = [dot_right_t(stacked[...], top[...]).astype(BF16)]
    for tier in range(levels - 1, -1, -1):
        values = []
        for e in range(quads >> tier + 1):
            rows = pl.ds(e * double, double)
            matrix = matrices[tier]
            children = descend(
                level[e],
                kept[tier][e],
                matrix[rows, pl.ds(0, double)],
                matrix[rows, pl.ds(double, rank)],
            )
            values += [children[:, :rank], children[:, rank:]]
        level = values
    for i in range(quads):
        below[i] = level[i]
    for i in range(quads):
        outs[i][...] = below[jnp.where(in_lower(chips), i, quads - 1 - i)]


def quad_down_kernel(*refs, chips):
    parts, (paired, matrix, keep, send, parent, work) = refs[:-6], refs[-6:]
    double = paired.shape[1]
    at = chip_of()
    line = mirrored(at, chips)
    near, far = parts[0][...], parts[-1][...]
    for source, part in zip(inner_chips(chips), parts):
        near = jnp.where(line == source, part[...], near)
        far = jnp.where(line == chips - 1 - source, part[...], far)
    join_rows(near, far, jnp.where(in_lower(chips), 0, 1), parent)
    children = descend(
        parent[...], paired[...], matrix[:, pl.ds(0, double)], matrix[:, pl.ds(double, double // 2)]
    )
    split_lanes(children, at % 2, keep, send, work)


def pair_down_kernel(mine, other, paired, matrix, keep, send, work, *, chips):
    double = paired.shape[1]
    inner = (chip_of() % 2 == 1) == in_lower(chips)
    parent = jnp.where(inner, mine[...], other[...])
    children = descend(
        parent, paired[...], matrix[:, pl.ds(0, double)], matrix[:, pl.ds(double, double // 2)]
    )
    split_lanes(children, core_of(), keep, send, work)


def body(
    right_side,
    leaf_inverse,
    leaf_basis,
    local_merge,
    local_transfer,
    upper_merge,
    upper_transfer,
    top_inverse,
):
    leaf = leaf_inverse.shape[2]
    rank = leaf_basis.shape[2]
    columns = right_side.shape[2]
    double = 2 * rank
    wide = double + rank
    leaf_count = right_side.shape[1] // leaf
    sub_count = lax.axis_size("sub")
    sub_depth = sub_count.bit_length() - 1
    root_count = lax.axis_size("root")
    chips = sub_count // 2
    middle = chips // 2 - 1
    half, quarter = columns // 2, columns // 4
    heights = [double >> tier for tier in range(3, sub_depth + 1)]
    levels = len(heights)
    quads = chips // 2

    local = [right_side[0], leaf_inverse[0], leaf_basis[0]]
    tree = [local_merge[0], local_transfer[0]]
    head = min(leaf_count - 1, 2) * leaf
    first_shapes = [(head, a.shape[1]) for a in local]
    blocks = wide // rank
    top_rows, top_width = top_inverse.shape
    quad_rows = blocks * (double // 4)
    top_block = top_rows * top_width // rank
    high_rows = blocks * sum(heights)
    any_spec, vmem_spec = pl.BlockSpec(memory_space=pl.ANY), pl.BlockSpec(memory_space=pltpu.VMEM)
    pair_rows = blocks * (double // 2)
    shapes = [(rows, rank) for rows in (pair_rows + quad_rows, quad_rows + top_block, high_rows)]
    shapes += first_shapes
    args = [upper_merge[0], upper_transfer[0], top_inverse] + local
    low, quad_top, high, *first = pl.pallas_call(
        pack_kernel,
        out_shape=[pltpu.VMEM(shape, BF16) for shape in shapes],
        in_specs=[any_spec] * len(args),
        out_specs=[vmem_spec] * len(shapes),
        scratch_shapes=[pltpu.SemaphoreType.DMA((3 * blocks + rank // top_width + 3,))],
        compiler_params=pltpu.CompilerParams(vmem_limit_bytes=2 * MIB),
        cost_estimate=cost(1.5),
    )(*[pltpu.with_memory_space_constraint(a, pltpu.HBM) for a in args])
    far_high = flip(high, "sub", 2)
    far = flip(quad_top, "sub", 2)
    low_other = flip(low, "sub", 1)

    shapes = [
        (half, rank),
        (half, rank),
        (leaf_count // 2, columns, double),
        (leaf_count // 4, columns, double),
    ]
    shapes += [(a.shape[0] - head, a.shape[1]) for a in local] + [a.shape for a in tree]
    args = [pltpu.with_memory_space_constraint(a, pltpu.HBM) for a in local + tree]
    args += [pltpu.with_memory_space_constraint(a, pltpu.VMEM) for a in first]
    keep, send, low_paired, high_paired, *local = pl.pallas_call(
        climb_local_kernel,
        out_shape=[pltpu.VMEM(shape, BF16) for shape in shapes],
        in_specs=[any_spec] * 5 + [vmem_spec] * 3,
        out_specs=[vmem_spec] * len(shapes),
        scratch_shapes=[
            pltpu.VMEM((columns, rank), BF16),
            pltpu.SemaphoreType.DMA((5 * leaf_count - 5,)),
        ],
        compiler_params=pltpu.CompilerParams(vmem_limit_bytes=16 * MIB),
        cost_estimate=cost(0.01),
    )(*args)

    recv = flip(send, "sub", 1)
    recv = passed(recv, 0.8)
    low_other, far_high, token = lax.optimization_barrier((low_other, far_high, mark(send)))
    (pair_matrix,) = vmem_call(pair_matrix_kernel, [(double, wide)], [low, low_other])
    (rows_mine,) = vmem_call(tails_kernel, [(2, high_rows, rank)], [high, far_high])
    inner = inner_chips(chips)
    others = [s for s in inner if s != middle]
    rows_rest = [swapped(rows_mine, s, middle, chips) for s in others]
    pair_paired, coeffs = vmem_call(
        pair_up_kernel,
        [(half, double), (half, rank)],
        [keep, recv, pair_matrix],
        micros=0.05,
        after=[token],
    )

    recv = flip(coeffs, "sub", 2)
    recv, rows_rest = lax.optimization_barrier((recv, rows_rest))
    recv = passed(recv, 10)
    far, token = lax.optimization_barrier((far, mark(coeffs)))
    (top_mine,) = vmem_call(tails_kernel, [(2, top_block, rank)], [quad_top, far])
    top_rest = [swapped(top_mine, s, middle, chips) for s in others]
    far_other = flip(far, "sub", 1)
    (quad_matrix,) = vmem_call(
        quad_matrix_kernel, [(double, wide)], [low, low_other, far, far_other], after=[recv]
    )
    quad_paired, near, send = vmem_call(
        functools.partial(quad_up_kernel, chips=chips),
        [(half, double), (quarter, rank), (quarter, rank)],
        [coeffs, recv, quad_matrix],
        [pltpu.VMEM((half, rank), BF16)],
        micros=0.05,
        after=[token],
    )

    own = inner.index(middle)
    parts = [swapped(near if s < middle else send, s, middle, chips) for s in others]
    parts, top_rest = lax.optimization_barrier((parts, top_rest))
    parts = [passed(part, 10) for part in parts]
    rows_rest, near = lax.optimization_barrier((rows_rest, near))
    stacks = [rows_mine, flip(rows_mine, "sub", 1)]
    for item in rows_rest:
        stacks += [item, flip(item, "sub", 1)]
    *high_matrices, = vmem_call(
        functools.partial(high_matrix_kernel, chips=chips, heights=heights),
        [(sub_count * height, wide) for height in heights],
        stacks,
        limit=8 * MIB,
        micros=0.2,
        after=parts,
    )
    *high_paired_up, coeffs = vmem_call(
        functools.partial(high_up_kernel, chips=chips, levels=levels),
        [(quads >> t + 1, quarter, double) for t in range(levels)] + [(quarter, rank)],
        parts[:own] + [near] + parts[own:] + high_matrices,
        limit=8 * MIB,
        micros=0.4,
    )

    roots = [flip(coeffs, "root", mask) for mask in range(root_count - 1, 0, -1)]
    roots[0] = passed(roots[0], 0.01)
    roots.append(coeffs)
    roots.reverse()
    stacks = [top_mine, flip(top_mine, "sub", 1)]
    for item in top_rest:
        stacks += [item, flip(item, "sub", 1)]
    (top_matrix,) = vmem_call(
        functools.partial(top_matrix_kernel, chips=chips),
        [(top_rows, sub_count * top_width)],
        stacks,
        limit=8 * MIB,
    )
    values = vmem_call(
        functools.partial(high_down_kernel, chips=chips, levels=levels, roots=root_count),
        [(quarter, rank)] * quads,
        roots + [top_matrix] + high_matrices + high_paired_up,
        [
            pltpu.VMEM((quarter, root_count * rank), BF16),
            pltpu.VMEM((quads, quarter, rank), BF16),
        ],
        limit=8 * MIB,
        micros=0.7,
    )

    parts = [
        value if s == middle else swapped(value, s, middle, chips)
        for s, value in zip(inner, values)
    ]
    keep, send = vmem_call(
        functools.partial(quad_down_kernel, chips=chips),
        [(half, rank), (half, rank)],
        parts + [quad_paired, quad_matrix],
        [pltpu.VMEM((half, rank), BF16), pltpu.VMEM((half, double), BF16)],
        micros=0.4,
    )
    recv = flip(send, "sub", 2)
    keep, send = vmem_call(
        functools.partial(pair_down_kernel, chips=chips),
        [(half, rank), (half, rank)],
        [keep, recv, pair_paired, pair_matrix],
        [pltpu.VMEM((half, double), BF16)],
        micros=0.4,
    )
    recv = flip(send, "sub", 1)

    args = [keep, recv, low_paired, high_paired] + first + local
    out = pl.pallas_call(
        descend_local_kernel,
        out_shape=jax.ShapeDtypeStruct((leaf_count * leaf, columns), F32),
        in_specs=[vmem_spec] * len(args),
        out_specs=any_spec,
        scratch_shapes=[
            pltpu.VMEM((columns, rank), BF16),
            pltpu.VMEM((leaf_count, leaf, columns), F32),
            pltpu.SemaphoreType.DMA((leaf_count,)),
        ],
        compiler_params=pltpu.CompilerParams(vmem_limit_bytes=16 * MIB),
        cost_estimate=cost(3),
    )(*[pltpu.with_memory_space_constraint(a, pltpu.VMEM) for a in args])
    return out[None]


def solution(mesh):
    return jax.shard_map(
        body,
        mesh=mesh,
        in_specs=(
            P("root", "sub", None),
            P("root", "sub", None),
            P("root", "sub", None),
            P("root", "sub", None),
            P("root", "sub", None),
            P("root", "sub", None),
            P("root", "sub", None),
            P("root", "sub"),
        ),
        out_specs=P("root", "sub", None),
        check_vma=False,
    )
```

```python
import functools

import jax
import jax.numpy as jnp
from jax import lax
from jax.experimental import pallas as pl
from jax.experimental.pallas import tpu as pltpu
from jax.sharding import PartitionSpec as P

BF16 = jnp.bfloat16
F32 = jnp.float32
MIB = 1 << 20


def dot(left, right):
    return lax.dot_general(left, right, (((1,), (0,)), ((), ())), preferred_element_type=F32)


def dot_right_t(left, right):
    return lax.dot_general(left, right, (((1,), (1,)), ((), ())), preferred_element_type=F32)


def cost(micros):
    return pl.CostEstimate(flops=int(micros * 1e9), bytes_accessed=1, transcendentals=0)


def vmem_call(kernel, outs, args, scratch=(), limit=4 * MIB, micros=0.1, after=()):
    count = len(args)
    args = list(args) + list(after)
    return pl.pallas_call(
        lambda *refs: kernel(*refs[:count], *refs[len(args) :]),
        out_shape=[pltpu.VMEM(shape, BF16) for shape in outs],
        in_specs=[pl.BlockSpec(memory_space=pltpu.VMEM)] * len(args),
        out_specs=[pl.BlockSpec(memory_space=pltpu.VMEM)] * len(outs),
        scratch_shapes=list(scratch),
        compiler_params=pltpu.CompilerParams(vmem_limit_bytes=limit),
        cost_estimate=cost(micros),
    )(*[pltpu.with_memory_space_constraint(a, pltpu.VMEM) for a in args])


def copy_kernel(value, out):
    out[...] = value[...]


def passed(value, micros):
    return vmem_call(copy_kernel, [value.shape], [value], micros=micros)[0]


def mark_kernel(value, out):
    out[...] = value[pl.ds(0, out.shape[0]), pl.ds(0, out.shape[1])]


def mark(value):
    return vmem_call(mark_kernel, [(16, 128)], [value], micros=0.02)[0]


def flip(block, axis, mask):
    count = lax.axis_size(axis)
    return lax.ppermute(block, axis, [(i, i ^ mask) for i in range(count)])


def swap_with(source, target, chips):
    partner = [device ^ 1 for device in range(2 * chips)]
    for low, high in ((source, target), (chips - 1 - source, chips - 1 - target)):
        for core in range(2):
            partner[2 * low + core], partner[2 * high + core] = 2 * high + core, 2 * low + core
    return list(enumerate(partner))


def inner_chips(chips):
    return [chip for chip in range(chips) if (chip % 2 == 1) == (chip < chips // 2)]


def swapped(block, source, target, chips):
    return lax.ppermute(block, "sub", swap_with(source, target, chips))


def core_of():
    return lax.axis_index("sub") % 2


def chip_of():
    return lax.axis_index("sub") // 2


def in_lower(chips):
    return chip_of() < chips // 2


def mirrored(chip, chips):
    return jnp.where(in_lower(chips), chip, chips - 1 - chip)


def split_rows(value, first, keep, send, work):
    half = value.shape[0] // 2
    work[...] = value
    keep[...] = work[pl.ds(pl.multiple_of(first * half, half), half), :]
    send[...] = work[pl.ds(pl.multiple_of((1 - first) * half, half), half), :]


def split_lanes(value, first, keep, send, work):
    half = value.shape[1] // 2
    work[...] = value
    keep[...] = work[:, pl.ds(pl.multiple_of(first * half, half), half)]
    send[...] = work[:, pl.ds(pl.multiple_of((1 - first) * half, half), half)]


def join_rows(mine, other, first, work):
    half = mine.shape[0]
    work[pl.ds(pl.multiple_of(first * half, half), half), :] = mine
    work[pl.ds(pl.multiple_of((1 - first) * half, half), half), :] = other


def join_lanes(mine, other, first, work):
    half = mine.shape[1]
    work[:, pl.ds(pl.multiple_of(first * half, half), half)] = mine
    work[:, pl.ds(pl.multiple_of((1 - first) * half, half), half)] = other


def climb(paired, merge_mat, transfer):
    inner = dot_right_t(paired, merge_mat).astype(BF16)
    return dot(inner, transfer).astype(BF16)


def descend(parent, paired, merge_mat, transfer):
    rest = (paired.astype(F32) - dot_right_t(parent, transfer)).astype(BF16)
    return dot_right_t(rest, merge_mat).astype(BF16)


def pack_kernel(merge, transfer, top, sides_in, inverse_in, basis_in, *refs):
    low, quad_top, high, sides, inverse, basis, sems = refs
    rows, double = merge.shape
    rank = transfer.shape[1]
    steps = []

    def fetch(source, target):
        steps.append(pltpu.make_async_copy(source, target, sems.at[len(steps)]))

    def level_rows(low, size, target, at):
        for lanes in range(double // rank):
            fetch(
                merge.at[pl.ds(low, size), pl.ds(lanes * rank, rank)], target.at[pl.ds(at, size), :]
            )
            at += size
        fetch(transfer.at[pl.ds(low, size), :], target.at[pl.ds(at, size), :])
        return at + size

    quad_low, high_low = double // 2, double // 2 + double // 4
    level_rows(high_low, rows - high_low, high, 0)
    quad_rows = level_rows(quad_low, high_low - quad_low, quad_top, 0)
    width = top.shape[1]
    size = top.shape[0] * width // rank
    for piece in range(rank // width):
        fetch(
            top.at[pl.ds(piece * size, size), :],
            quad_top.at[pl.ds(quad_rows, size), pl.ds(piece * width, width)],
        )
    pair_rows = level_rows(0, quad_low, low, 0)
    for source, target in ((inverse_in, inverse), (sides_in, sides), (basis_in, basis)):
        fetch(source.at[pl.ds(0, target.shape[0]), :], target)
    for step in steps:
        step.start()
    for step in steps:
        step.wait()
    low[pl.ds(pair_rows, quad_rows), :] = quad_top[pl.ds(0, quad_rows), :]


def climb_local_kernel(
    sides_in, inverse_in, basis_in, merge_in, transfer_in, sides_0, inverse_0, basis_0, keep, send,
    low_paired, high_paired, sides, inverse, basis, merge, transfer, work, sems
):
    leaf = inverse.shape[1]
    rank = basis.shape[1]
    double = 2 * rank
    kept = {1: low_paired, 2: high_paired}
    leaf_count = sides_in.shape[0] // leaf
    depth = leaf_count.bit_length() - 1
    nodes = leaf_count - 1
    copies = []

    def fetch(source, target, low, at, size):
        copies.append(
            pltpu.make_async_copy(
                source.at[pl.ds(low, size), :], target.at[pl.ds(at, size), :], sems.at[len(copies)]
            )
        )

    head = sides_0.shape[0] // leaf
    for i in range(head, leaf_count):
        fetch(inverse_in, inverse, i * leaf, (i - head) * leaf, leaf)
        fetch(sides_in, sides, i * leaf, (i - head) * leaf, leaf)
        fetch(basis_in, basis, i * leaf, (i - head) * leaf, leaf)
    first = len(copies)
    for e in range(nodes):
        fetch(merge_in, merge, e * double, e * double, double)
        fetch(transfer_in, transfer, e * double, e * double, double)
    for copy in copies:
        copy.start()
    for i in range(leaf_count):
        rows = pl.ds((i if i < head else i - head) * leaf, leaf)
        if i >= head:
            for copy in copies[3 * (i - head) : 3 * (i - head) + 3]:
                copy.wait()
        arrays = (inverse, sides, basis) if i >= head else (inverse_0, sides_0, basis_0)
        columns = jnp.transpose(arrays[1][rows, :])
        solved = dot_right_t(columns, arrays[0][rows, :]).astype(BF16)
        coeffs = dot(solved, arrays[2][rows, :]).astype(BF16)
        kept[1][i // 2, :, pl.ds((i % 2) * rank, rank)] = coeffs
    for tier in range(1, depth + 1):
        count = leaf_count >> tier
        start = leaf_count - 2 * count
        for e in range(count):
            rows = pl.ds((start + e) * double, double)
            for copy in copies[first + 2 * (start + e) : first + 2 * (start + e) + 2]:
                copy.wait()
            coeffs = climb(kept[tier][e], merge[rows, :], transfer[rows, :])
            if tier < depth:
                kept[tier + 1][e // 2, :, pl.ds((e % 2) * rank, rank)] = coeffs
            else:
                split_rows(coeffs, core_of(), keep, send, work)


def descend_local_kernel(
    mine, other, low_paired, high_paired, sides_0, inverse_0, basis_0, sides, inverse, basis, merge,
    transfer, out, parent, result, sems
):
    leaf = inverse.shape[1]
    rank = basis.shape[1]
    double = 2 * rank
    kept = {1: low_paired, 2: high_paired}
    leaf_count = out.shape[0] // leaf
    depth = leaf_count.bit_length() - 1
    join_rows(mine[...], other[...], core_of(), parent)
    level = [parent[...]]
    for tier in range(depth, 0, -1):
        nodes = leaf_count >> tier
        start = leaf_count - 2 * nodes
        below = []
        for e in range(nodes):
            rows = pl.ds((start + e) * double, double)
            children = descend(level[e], kept[tier][e], merge[rows, :], transfer[rows, :])
            below += [children[:, :rank], children[:, rank:]]
        level = below
    copies = []
    for i in range(leaf_count):
        head = sides_0.shape[0] // leaf
        rows = pl.ds((i if i < head else i - head) * leaf, leaf)
        arrays = (inverse, sides, basis) if i >= head else (inverse_0, sides_0, basis_0)
        spread = dot_right_t(arrays[2][rows, :], level[i])
        rest = (arrays[1][rows, :].astype(F32) - spread).astype(BF16)
        result[i] = dot(arrays[0][rows, :], rest)
        copies.append(
            pltpu.make_async_copy(result.at[i], out.at[pl.ds(i * leaf, leaf), :], sems.at[i])
        )
        copies[-1].start()
    for copy in copies:
        copy.wait()


def place_rows(block, low, size, out, at):
    width = block.shape[-1]
    for lanes in range(out.shape[1] // width):
        out[pl.ds(at, size), pl.ds(lanes * width, width)] = block[pl.ds(low + lanes * size, size), :]


def pair_matrix_kernel(mine, other, out):
    size = out.shape[0] // 2
    core = core_of()
    place_rows(mine, 0, size, out, pl.multiple_of(core * size, size))
    place_rows(other, 0, size, out, pl.multiple_of((1 - core) * size, size))


def quad_matrix_kernel(mine, other, far, far_other, out):
    size = out.shape[0] // 4
    core, side = core_of(), chip_of() % 2
    start = mine.shape[0] - out.shape[1] // mine.shape[1] * size
    blocks = [(side, core, mine, start), (side, 1 - core, other, start)]
    blocks += [(1 - side, core, far, 0), (1 - side, 1 - core, far_other, 0)]
    for chip, which, ref, low in blocks:
        place_rows(ref, low, size, out, pl.multiple_of((2 * chip + which) * size, size))


def tails_kernel(mine, far, out):
    for i, ref in enumerate((mine, far)):
        out[i] = ref[pl.ds(ref.shape[0] - out.shape[1], out.shape[1]), :]


def extend_kernel(mine, other, out):
    out[pl.ds(0, mine.shape[0]), :] = mine[...]
    out[pl.ds(mine.shape[0], other.shape[0]), :] = other[...]


def stack_kernel(*refs):
    *ins, out = refs
    at = 0
    for ref in ins:
        if len(ref.shape) == 2:
            out[at] = ref[...]
            at += 1
        else:
            out[pl.ds(at, ref.shape[0])] = ref[...]
            at += ref.shape[0]


def device_blocks(refs, chips):
    inner, core = inner_chips(chips), core_of()
    own = inner.index(chips // 2 - 1)
    order = [inner[own]] + inner[:own] + inner[own + 1 :]
    for source, mine, other in zip(order, refs[::2], refs[1::2]):
        for i, chip in enumerate((source, source ^ 1)):
            for which, ref in ((core, mine), (1 - core, other)):
                yield 2 * mirrored(chip, chips) + which, ref.at[i]


def high_matrix_kernel(*refs, chips, heights):
    refs, outs = refs[: -len(heights)], refs[-len(heights) :]
    rows = sum(heights)
    for device, ref in device_blocks(refs, chips):
        offset = 0
        for out, height in zip(outs, heights):
            width = ref.shape[-1]
            for lanes in range(out.shape[1] // width):
                out[
                    pl.ds(pl.multiple_of(device * height, height), height),
                    pl.ds(lanes * width, width),
                ] = ref[pl.ds(lanes * rows + offset, height), :]
            offset += height


def top_matrix_kernel(*refs, chips):
    refs, top = refs[:-1], refs[-1]
    width = top.shape[1] // (2 * chips)
    for device, ref in device_blocks(refs, chips):
        size = top.shape[0] * width // ref.shape[-1]
        for piece in range(ref.shape[-1] // width):
            top[pl.ds(piece * size, size), pl.ds(pl.multiple_of(device * width, width), width)] = ref[
                :, pl.ds(piece * width, width)
            ]


def pair_up_kernel(mine, other, matrix, paired, coeffs):
    double = paired.shape[1]
    join_lanes(mine[...], other[...], core_of(), paired)
    coeffs[...] = climb(
        paired[...], matrix[:, pl.ds(0, double)], matrix[:, pl.ds(double, double // 2)]
    )


def quad_up_kernel(mine, other, matrix, paired, near, far, work, *, chips):
    double = paired.shape[1]
    join_lanes(mine[...], other[...], chip_of() % 2, paired)
    coeffs = climb(paired[...], matrix[:, pl.ds(0, double)], matrix[:, pl.ds(double, double // 2)])
    split_rows(coeffs, jnp.where(in_lower(chips), 0, 1), near, far, work)


def high_up_kernel(*refs, chips, levels):
    quads = chips // 2
    parts, matrices = refs[:quads], refs[quads : quads + levels]
    kept, coeffs = refs[quads + levels : quads + 2 * levels], refs[-1]
    rank = coeffs.shape[1]
    double = 2 * rank
    for i, part in enumerate(parts):
        at = jnp.where(in_lower(chips), i, quads - 1 - i)
        lanes = pl.ds(pl.multiple_of((at % 2) * rank, rank), rank)
        kept[0][at // 2, :, lanes] = part[...]
    for tier in range(levels):
        nodes = quads >> tier + 1
        for e in range(nodes):
            rows = pl.ds(e * double, double)
            matrix = matrices[tier]
            value = climb(
                kept[tier][e], matrix[rows, pl.ds(0, double)], matrix[rows, pl.ds(double, rank)]
            )
            if tier + 1 < levels:
                kept[tier + 1][e // 2, :, pl.ds((e % 2) * rank, rank)] = value
            else:
                coeffs[...] = value


def high_down_kernel(*refs, chips, levels, roots):
    quads = chips // 2
    own, top, refs = refs[:roots], refs[roots], refs[roots + 1 :]
    matrices, kept, outs = refs[:levels], refs[levels : 2 * levels], refs[2 * levels : -2]
    stacked, below = refs[-2:]
    rank = outs[0].shape[1]
    double = 2 * rank
    me = lax.axis_index("root")
    for mask in range(roots):
        at = pl.multiple_of((me ^ mask) * rank, rank)
        stacked[:, pl.ds(at, rank)] = own[mask][...]
    level = [dot_right_t(stacked[...], top[...]).astype(BF16)]
    for tier in range(levels - 1, -1, -1):
        values = []
        for e in range(quads >> tier + 1):
            rows = pl.ds(e * double, double)
            matrix = matrices[tier]
            children = descend(
                level[e],
                kept[tier][e],
                matrix[rows, pl.ds(0, double)],
                matrix[rows, pl.ds(double, rank)],
            )
            values += [children[:, :rank], children[:, rank:]]
        level = values
    for i in range(quads):
        below[i] = level[i]
    for i in range(quads):
        outs[i][...] = below[jnp.where(in_lower(chips), i, quads - 1 - i)]


def quad_down_kernel(*refs, chips, far):
    parts, (paired, matrix, keep, send, rows, work) = refs[:-6], refs[-6:]
    double = paired.shape[1]
    at = chip_of()
    line = mirrored(at, chips)
    parent = parts[0][...]
    for source, part in zip(inner_chips(chips), parts):
        parent = jnp.where(line == (chips - 1 - source if far else source), part[...], parent)
    half = paired.shape[0] // 2
    first = jnp.where(in_lower(chips), 0, 1)
    first = 1 - first if far else first
    rows[...] = paired[pl.ds(pl.multiple_of(first * half, half), half), :]
    children = descend(
        parent, rows[...], matrix[:, pl.ds(0, double)], matrix[:, pl.ds(double, double // 2)]
    )
    split_lanes(children, at % 2, keep, send, work)


def pair_down_kernel(
    near, near_came, far, far_came, paired, matrix, keep, send, parent, work, *, chips
):
    double = paired.shape[1]
    inner = (chip_of() % 2 == 1) == in_lower(chips)
    near = jnp.where(inner, near[...], near_came[...])
    far = jnp.where(inner, far[...], far_came[...])
    join_rows(near, far, jnp.where(in_lower(chips), 0, 1), parent)
    children = descend(
        parent[...], paired[...], matrix[:, pl.ds(0, double)], matrix[:, pl.ds(double, double // 2)]
    )
    split_lanes(children, core_of(), keep, send, work)


def body(
    right_side,
    leaf_inverse,
    leaf_basis,
    local_merge,
    local_transfer,
    upper_merge,
    upper_transfer,
    top_inverse,
):
    leaf = leaf_inverse.shape[2]
    rank = leaf_basis.shape[2]
    columns = right_side.shape[2]
    double = 2 * rank
    wide = double + rank
    leaf_count = right_side.shape[1] // leaf
    sub_count = lax.axis_size("sub")
    sub_depth = sub_count.bit_length() - 1
    root_count = lax.axis_size("root")
    chips = sub_count // 2
    middle = chips // 2 - 1
    half, quarter = columns // 2, columns // 4
    heights = [double >> tier for tier in range(3, sub_depth + 1)]
    levels = len(heights)
    quads = chips // 2

    local = [right_side[0], leaf_inverse[0], leaf_basis[0]]
    tree = [local_merge[0], local_transfer[0]]
    head = min(leaf_count - 1, 2) * leaf
    first_shapes = [(head, a.shape[1]) for a in local]
    blocks = wide // rank
    top_rows, top_width = top_inverse.shape
    quad_rows = blocks * (double // 4)
    top_block = top_rows * top_width // rank
    high_rows = blocks * sum(heights)
    any_spec, vmem_spec = pl.BlockSpec(memory_space=pl.ANY), pl.BlockSpec(memory_space=pltpu.VMEM)
    pair_rows = blocks * (double // 2)
    shapes = [(rows, rank) for rows in (pair_rows + quad_rows, quad_rows + top_block, high_rows)]
    shapes += first_shapes
    args = [upper_merge[0], upper_transfer[0], top_inverse] + local
    low, quad_top, high, *first = pl.pallas_call(
        pack_kernel,
        out_shape=[pltpu.VMEM(shape, BF16) for shape in shapes],
        in_specs=[any_spec] * len(args),
        out_specs=[vmem_spec] * len(shapes),
        scratch_shapes=[pltpu.SemaphoreType.DMA((3 * blocks + rank // top_width + 3,))],
        compiler_params=pltpu.CompilerParams(vmem_limit_bytes=2 * MIB),
        cost_estimate=cost(1.5),
    )(*[pltpu.with_memory_space_constraint(a, pltpu.HBM) for a in args])
    far_high = flip(high, "sub", 2)
    far = flip(quad_top, "sub", 2)
    low_other = flip(low, "sub", 1)

    shapes = [
        (half, rank),
        (half, rank),
        (leaf_count // 2, columns, double),
        (leaf_count // 4, columns, double),
    ]
    shapes += [(a.shape[0] - head, a.shape[1]) for a in local] + [a.shape for a in tree]
    args = [pltpu.with_memory_space_constraint(a, pltpu.HBM) for a in local + tree]
    args += [pltpu.with_memory_space_constraint(a, pltpu.VMEM) for a in first]
    keep, send, low_paired, high_paired, *local = pl.pallas_call(
        climb_local_kernel,
        out_shape=[pltpu.VMEM(shape, BF16) for shape in shapes],
        in_specs=[any_spec] * 5 + [vmem_spec] * 3,
        out_specs=[vmem_spec] * len(shapes),
        scratch_shapes=[
            pltpu.VMEM((columns, rank), BF16),
            pltpu.SemaphoreType.DMA((5 * leaf_count - 5,)),
        ],
        compiler_params=pltpu.CompilerParams(vmem_limit_bytes=16 * MIB),
        cost_estimate=cost(0.01),
    )(*args)

    recv = flip(send, "sub", 1)
    recv = passed(recv, 0.8)
    low_other, far_high, token = lax.optimization_barrier((low_other, far_high, mark(send)))
    (pair_matrix,) = vmem_call(pair_matrix_kernel, [(double, wide)], [low, low_other])
    (rows_mine,) = vmem_call(tails_kernel, [(2, high_rows, rank)], [high, far_high])
    inner = inner_chips(chips)
    others = [s for s in inner if s != middle]
    rows_rest = [swapped(rows_mine, s, middle, chips) for s in others]
    pair_paired, coeffs = vmem_call(
        pair_up_kernel,
        [(half, double), (half, rank)],
        [keep, recv, pair_matrix],
        micros=0.05,
        after=[token],
    )

    recv = flip(coeffs, "sub", 2)
    recv, rows_rest = lax.optimization_barrier((recv, rows_rest))
    recv = passed(recv, 10)
    far, token = lax.optimization_barrier((far, mark(coeffs)))
    (top_mine,) = vmem_call(tails_kernel, [(2, top_block, rank)], [quad_top, far])
    top_rest = [swapped(top_mine, s, middle, chips) for s in others]
    far_other = flip(far, "sub", 1)
    (quad_matrix,) = vmem_call(
        quad_matrix_kernel, [(double, wide)], [low, low_other, far, far_other], after=[recv]
    )
    quad_paired, near, send = vmem_call(
        functools.partial(quad_up_kernel, chips=chips),
        [(half, double), (quarter, rank), (quarter, rank)],
        [coeffs, recv, quad_matrix],
        [pltpu.VMEM((half, rank), BF16)],
        micros=0.05,
        after=[token],
    )

    own = inner.index(middle)
    parts = [swapped(near if s < middle else send, s, middle, chips) for s in others]
    parts, top_rest = lax.optimization_barrier((parts, top_rest))
    parts = [passed(part, 10) for part in parts]
    rows_rest, near = lax.optimization_barrier((rows_rest, near))
    stacks = [rows_mine, flip(rows_mine, "sub", 1)]
    for item in rows_rest:
        stacks += [item, flip(item, "sub", 1)]
    *high_matrices, = vmem_call(
        functools.partial(high_matrix_kernel, chips=chips, heights=heights),
        [(sub_count * height, wide) for height in heights],
        stacks,
        limit=8 * MIB,
        micros=0.2,
        after=parts,
    )
    *high_paired_up, coeffs = vmem_call(
        functools.partial(high_up_kernel, chips=chips, levels=levels),
        [(quads >> t + 1, quarter, double) for t in range(levels)] + [(quarter, rank)],
        parts[:own] + [near] + parts[own:] + high_matrices,
        limit=8 * MIB,
        micros=0.4,
    )

    roots = [flip(coeffs, "root", mask) for mask in range(root_count - 1, 0, -1)]
    roots[0] = passed(roots[0], 0.01)
    roots.append(coeffs)
    roots.reverse()
    stacks = [top_mine, flip(top_mine, "sub", 1)]
    for item in top_rest:
        stacks += [item, flip(item, "sub", 1)]
    (top_matrix,) = vmem_call(
        functools.partial(top_matrix_kernel, chips=chips),
        [(top_rows, sub_count * top_width)],
        stacks,
        limit=8 * MIB,
    )
    values = vmem_call(
        functools.partial(high_down_kernel, chips=chips, levels=levels, roots=root_count),
        [(quarter, rank)] * quads,
        roots + [top_matrix] + high_matrices + high_paired_up,
        [
            pltpu.VMEM((quarter, root_count * rank), BF16),
            pltpu.VMEM((quads, quarter, rank), BF16),
        ],
        limit=8 * MIB,
        micros=0.7,
    )

    def quad_down(parts, far):
        return vmem_call(
            functools.partial(quad_down_kernel, chips=chips, far=far),
            [(quarter, rank), (quarter, rank)],
            parts + [quad_paired, quad_matrix],
            [pltpu.VMEM((quarter, double), BF16)] * 2,
            micros=0.4,
        )

    def across(value, source):
        return passed(swapped(value, source, middle, chips), 0.01)

    parts = {s: value if s == middle else across(value, s) for s, value in zip(inner, values)}
    lower, upper = inner[: quads // 2], inner[quads // 2 :]
    near, send = quad_down([parts[s] for s in lower] + [values[own]] * len(upper), False)
    near_came = flip(send, "sub", 2)
    far, send = quad_down([values[own]] * len(lower) + [parts[s] for s in upper], True)
    far_came = flip(send, "sub", 2)
    keep, send = vmem_call(
        functools.partial(pair_down_kernel, chips=chips),
        [(half, rank), (half, rank)],
        [near, near_came, far, far_came, pair_paired, pair_matrix],
        [pltpu.VMEM((half, rank), BF16), pltpu.VMEM((half, double), BF16)],
        micros=0.4,
    )
    recv = flip(send, "sub", 1)

    args = [keep, recv, low_paired, high_paired] + first + local
    out = pl.pallas_call(
        descend_local_kernel,
        out_shape=jax.ShapeDtypeStruct((leaf_count * leaf, columns), F32),
        in_specs=[vmem_spec] * len(args),
        out_specs=any_spec,
        scratch_shapes=[
            pltpu.VMEM((columns, rank), BF16),
            pltpu.VMEM((leaf_count, leaf, columns), F32),
            pltpu.SemaphoreType.DMA((leaf_count,)),
        ],
        compiler_params=pltpu.CompilerParams(vmem_limit_bytes=16 * MIB),
        cost_estimate=cost(3),
    )(*[pltpu.with_memory_space_constraint(a, pltpu.VMEM) for a in args])
    return out[None]


def solution(mesh):
    return jax.shard_map(
        body,
        mesh=mesh,
        in_specs=(
            P("root", "sub", None),
            P("root", "sub", None),
            P("root", "sub", None),
            P("root", "sub", None),
            P("root", "sub", None),
            P("root", "sub", None),
            P("root", "sub", None),
            P("root", "sub"),
        ),
        out_specs=P("root", "sub", None),
        check_vma=False,
    )
```

```python
import functools

import jax
import jax.numpy as jnp
from jax import lax
from jax.experimental import pallas as pl
from jax.experimental.pallas import tpu as pltpu
from jax.sharding import PartitionSpec as P

BF16 = jnp.bfloat16
F32 = jnp.float32
MIB = 1 << 20


def dot(left, right):
    return lax.dot_general(left, right, (((1,), (0,)), ((), ())), preferred_element_type=F32)


def dot_left_t(left, right):
    return lax.dot_general(left, right, (((0,), (0,)), ((), ())), preferred_element_type=F32)


def dot_right_t(left, right):
    return lax.dot_general(left, right, (((1,), (1,)), ((), ())), preferred_element_type=F32)


def cost(micros):
    return pl.CostEstimate(flops=int(micros * 1e9), bytes_accessed=1, transcendentals=0)


def vmem_call(kernel, outs, args, scratch=(), limit=4 * MIB, micros=0.1, after=()):
    count = len(args)
    args = list(args) + list(after)
    return pl.pallas_call(
        lambda *refs: kernel(*refs[:count], *refs[len(args) :]),
        out_shape=[pltpu.VMEM(shape, BF16) for shape in outs],
        in_specs=[pl.BlockSpec(memory_space=pltpu.VMEM)] * len(args),
        out_specs=[pl.BlockSpec(memory_space=pltpu.VMEM)] * len(outs),
        scratch_shapes=list(scratch),
        compiler_params=pltpu.CompilerParams(vmem_limit_bytes=limit),
        cost_estimate=cost(micros),
    )(*[pltpu.with_memory_space_constraint(a, pltpu.VMEM) for a in args])


def copy_kernel(value, out):
    out[...] = value[...]


def passed(value, micros):
    return vmem_call(copy_kernel, [value.shape], [value], micros=micros)[0]


def mark_kernel(value, out):
    out[...] = value[pl.ds(0, out.shape[0]), pl.ds(0, out.shape[1])]


def mark(value):
    return vmem_call(mark_kernel, [(16, 128)], [value], micros=0.02)[0]


def flip(block, axis, mask):
    count = lax.axis_size(axis)
    return lax.ppermute(block, axis, [(i, i ^ mask) for i in range(count)])


def swap_with(source, target, chips):
    partner = [device ^ 1 for device in range(2 * chips)]
    for low, high in ((source, target), (chips - 1 - source, chips - 1 - target)):
        for core in range(2):
            partner[2 * low + core], partner[2 * high + core] = 2 * high + core, 2 * low + core
    return list(enumerate(partner))


def inner_chips(chips):
    return [chip for chip in range(chips) if (chip % 2 == 1) == (chip < chips // 2)]


def swapped(block, source, target, chips):
    return lax.ppermute(block, "sub", swap_with(source, target, chips))


def core_of():
    return lax.axis_index("sub") % 2


def chip_of():
    return lax.axis_index("sub") // 2


def in_lower(chips):
    return chip_of() < chips // 2


def mirrored(chip, chips):
    return jnp.where(in_lower(chips), chip, chips - 1 - chip)


def split_rows(value, first, keep, send, work):
    half = value.shape[0] // 2
    work[...] = value
    keep[...] = work[pl.ds(pl.multiple_of(first * half, half), half), :]
    send[...] = work[pl.ds(pl.multiple_of((1 - first) * half, half), half), :]


def split_lanes(value, first, keep, send, work):
    half = value.shape[1] // 2
    work[...] = value
    keep[...] = work[:, pl.ds(pl.multiple_of(first * half, half), half)]
    send[...] = work[:, pl.ds(pl.multiple_of((1 - first) * half, half), half)]


def join_rows(mine, other, first, work):
    half = mine.shape[0]
    work[pl.ds(pl.multiple_of(first * half, half), half), :] = mine
    work[pl.ds(pl.multiple_of((1 - first) * half, half), half), :] = other


def join_lanes(mine, other, first, work):
    half = mine.shape[1]
    work[:, pl.ds(pl.multiple_of(first * half, half), half)] = mine
    work[:, pl.ds(pl.multiple_of((1 - first) * half, half), half)] = other


def climb(paired, merge_mat, transfer):
    inner = dot_right_t(paired, merge_mat).astype(BF16)
    return dot(inner, transfer).astype(BF16)


def descend(parent, paired, merge_mat, transfer):
    rest = (paired.astype(F32) - dot_right_t(parent, transfer)).astype(BF16)
    return dot_right_t(rest, merge_mat).astype(BF16)


def pack_kernel(merge, transfer, top, *refs):
    low, quad_top, high, sems = refs
    rows, double = merge.shape
    rank = transfer.shape[1]
    steps = []

    def fetch(source, target):
        steps.append(pltpu.make_async_copy(source, target, sems.at[len(steps)]))

    def level_rows(low, size, target, at):
        for lanes in range(double // rank):
            fetch(
                merge.at[pl.ds(low, size), pl.ds(lanes * rank, rank)], target.at[pl.ds(at, size), :]
            )
            at += size
        fetch(transfer.at[pl.ds(low, size), :], target.at[pl.ds(at, size), :])
        return at + size

    quad_low, high_low = double // 2, double // 2 + double // 4
    level_rows(high_low, rows - high_low, high, 0)
    quad_rows = level_rows(quad_low, high_low - quad_low, quad_top, 0)
    width = top.shape[1]
    size = top.shape[0] * width // rank
    for piece in range(rank // width):
        fetch(
            top.at[pl.ds(piece * size, size), :],
            quad_top.at[pl.ds(quad_rows, size), pl.ds(piece * width, width)],
        )
    pair_rows = level_rows(0, quad_low, low, 0)
    for step in steps:
        step.start()
    for step in steps:
        step.wait()
    low[pl.ds(pair_rows, quad_rows), :] = quad_top[pl.ds(0, quad_rows), :]


def climb_local_kernel(*refs, leaf_count, fetched):
    arrays = list(refs[:5])
    keep, send, low_paired, high_paired = refs[5:9]
    kept = {1: low_paired, 2: high_paired}
    *outs, work, sems = refs[9:]
    leaf = arrays[0].shape[0] // leaf_count
    rank = arrays[2].shape[1]
    double = 2 * rank
    depth = leaf_count.bit_length() - 1
    copies = {}
    for index, out in zip(fetched, outs):
        block = leaf if index < 3 else double
        for i in range(out.shape[0] // block):
            rows = pl.ds(i * block, block)
            copies[index, i] = pltpu.make_async_copy(
                arrays[index].at[rows, :], out.at[rows, :], sems.at[len(copies)]
            )
        arrays[index] = out
    for key in sorted(copies, key=lambda key: (key[0] // 3, key[1])):
        copies[key].start()

    def ready(index, i):
        if (index, i) in copies:
            copies[index, i].wait()

    sides, inverse, basis, merge, transfer = arrays
    products = []
    for i in range(leaf_count):
        rows = pl.ds(i * leaf, leaf)
        for index in range(2):
            ready(index, i)
        products.append(dot(inverse[rows, :], sides[rows, :]).astype(BF16))
    for i in range(leaf_count):
        ready(2, i)
        coeffs = dot_left_t(products[i], basis[pl.ds(i * leaf, leaf), :]).astype(BF16)
        kept[1][i // 2, :, pl.ds((i % 2) * rank, rank)] = coeffs
    for e in range(leaf_count - 1):
        for index in (3, 4):
            ready(index, e)
    for tier in range(1, depth + 1):
        count = leaf_count >> tier
        start = leaf_count - 2 * count
        for e in range(count):
            rows = pl.ds((start + e) * double, double)
            coeffs = climb(kept[tier][e], merge[rows, :], transfer[rows, :])
            if tier < depth:
                kept[tier + 1][e // 2, :, pl.ds((e % 2) * rank, rank)] = coeffs
            else:
                split_rows(coeffs, core_of(), keep, send, work)


def descend_local_kernel(
    mine, other, low_paired, high_paired, sides, inverse, basis, merge, transfer, out, parent, result, sems
):
    leaf = inverse.shape[1]
    rank = basis.shape[1]
    double = 2 * rank
    kept = {1: low_paired, 2: high_paired}
    leaf_count = out.shape[0] // leaf
    depth = leaf_count.bit_length() - 1
    join_rows(mine[...], other[...], core_of(), parent)
    level = [parent[...]]
    for tier in range(depth, 0, -1):
        nodes = leaf_count >> tier
        start = leaf_count - 2 * nodes
        below = []
        for e in range(nodes):
            rows = pl.ds((start + e) * double, double)
            children = descend(level[e], kept[tier][e], merge[rows, :], transfer[rows, :])
            below += [children[:, :rank], children[:, rank:]]
        level = below
    copies = []
    for i in range(leaf_count):
        rows = pl.ds(i * leaf, leaf)
        arrays = (inverse, sides, basis)
        spread = dot_right_t(arrays[2][rows, :], level[i])
        rest = (arrays[1][rows, :].astype(F32) - spread).astype(BF16)
        result[i] = dot(arrays[0][rows, :], rest)
        copies.append(
            pltpu.make_async_copy(result.at[i], out.at[pl.ds(i * leaf, leaf), :], sems.at[i])
        )
        copies[-1].start()
    for copy in copies:
        copy.wait()


def place_rows(block, low, size, out, at):
    width = block.shape[-1]
    for lanes in range(out.shape[1] // width):
        out[pl.ds(at, size), pl.ds(lanes * width, width)] = block[pl.ds(low + lanes * size, size), :]


def pair_matrix_kernel(mine, other, out):
    size = out.shape[0] // 2
    core = core_of()
    place_rows(mine, 0, size, out, pl.multiple_of(core * size, size))
    place_rows(other, 0, size, out, pl.multiple_of((1 - core) * size, size))


def quad_matrix_kernel(mine, other, far, far_other, out):
    size = out.shape[0] // 4
    core, side = core_of(), chip_of() % 2
    start = mine.shape[0] - out.shape[1] // mine.shape[1] * size
    blocks = [(side, core, mine, start), (side, 1 - core, other, start)]
    blocks += [(1 - side, core, far, 0), (1 - side, 1 - core, far_other, 0)]
    for chip, which, ref, low in blocks:
        place_rows(ref, low, size, out, pl.multiple_of((2 * chip + which) * size, size))


def tails_kernel(mine, far, out):
    for i, ref in enumerate((mine, far)):
        out[i] = ref[pl.ds(ref.shape[0] - out.shape[1], out.shape[1]), :]


def extend_kernel(mine, other, out):
    out[pl.ds(0, mine.shape[0]), :] = mine[...]
    out[pl.ds(mine.shape[0], other.shape[0]), :] = other[...]


def stack_kernel(*refs):
    *ins, out = refs
    at = 0
    for ref in ins:
        if len(ref.shape) == 2:
            out[at] = ref[...]
            at += 1
        else:
            out[pl.ds(at, ref.shape[0])] = ref[...]
            at += ref.shape[0]


def device_blocks(refs, chips):
    inner, core = inner_chips(chips), core_of()
    own = inner.index(chips // 2 - 1)
    order = [inner[own]] + inner[:own] + inner[own + 1 :]
    for source, mine, other in zip(order, refs[::2], refs[1::2]):
        for i, chip in enumerate((source, source ^ 1)):
            for which, ref in ((core, mine), (1 - core, other)):
                yield 2 * mirrored(chip, chips) + which, ref.at[i]


def high_matrix_kernel(*refs, chips, heights):
    refs, outs = refs[: -len(heights)], refs[-len(heights) :]
    rows = sum(heights)
    for device, ref in device_blocks(refs, chips):
        offset = 0
        for out, height in zip(outs, heights):
            width = ref.shape[-1]
            for lanes in range(out.shape[1] // width):
                out[
                    pl.ds(pl.multiple_of(device * height, height), height),
                    pl.ds(lanes * width, width),
                ] = ref[pl.ds(lanes * rows + offset, height), :]
            offset += height


def top_matrix_kernel(*refs, chips):
    refs, top = refs[:-1], refs[-1]
    width = top.shape[1] // (2 * chips)
    for device, ref in device_blocks(refs, chips):
        size = top.shape[0] * width // ref.shape[-1]
        for piece in range(ref.shape[-1] // width):
            top[pl.ds(piece * size, size), pl.ds(pl.multiple_of(device * width, width), width)] = ref[
                :, pl.ds(piece * width, width)
            ]


def pair_up_kernel(mine, other, matrix, paired, coeffs):
    double = paired.shape[1]
    join_lanes(mine[...], other[...], core_of(), paired)
    coeffs[...] = climb(
        paired[...], matrix[:, pl.ds(0, double)], matrix[:, pl.ds(double, double // 2)]
    )


def quad_up_kernel(mine, other, matrix, paired, near, far, work, *, chips):
    double = paired.shape[1]
    join_lanes(mine[...], other[...], chip_of() % 2, paired)
    coeffs = climb(paired[...], matrix[:, pl.ds(0, double)], matrix[:, pl.ds(double, double // 2)])
    split_rows(coeffs, jnp.where(in_lower(chips), 0, 1), near, far, work)


def high_up_kernel(*refs, chips, levels):
    quads = chips // 2
    parts, matrices = refs[:quads], refs[quads : quads + levels]
    kept, coeffs = refs[quads + levels : quads + 2 * levels], refs[-1]
    rank = coeffs.shape[1]
    double = 2 * rank
    for i, part in enumerate(parts):
        at = jnp.where(in_lower(chips), i, quads - 1 - i)
        lanes = pl.ds(pl.multiple_of((at % 2) * rank, rank), rank)
        kept[0][at // 2, :, lanes] = part[...]
    for tier in range(levels):
        nodes = quads >> tier + 1
        for e in range(nodes):
            rows = pl.ds(e * double, double)
            matrix = matrices[tier]
            value = climb(
                kept[tier][e], matrix[rows, pl.ds(0, double)], matrix[rows, pl.ds(double, rank)]
            )
            if tier + 1 < levels:
                kept[tier + 1][e // 2, :, pl.ds((e % 2) * rank, rank)] = value
            else:
                coeffs[...] = value


def high_down_kernel(*refs, chips, levels, roots):
    quads = chips // 2
    own, top, refs = refs[:roots], refs[roots], refs[roots + 1 :]
    matrices, kept, outs = refs[:levels], refs[levels : 2 * levels], refs[2 * levels : -2]
    stacked, below = refs[-2:]
    rank = outs[0].shape[1]
    double = 2 * rank
    me = lax.axis_index("root")
    for mask in range(roots):
        at = pl.multiple_of((me ^ mask) * rank, rank)
        stacked[:, pl.ds(at, rank)] = own[mask][...]
    level = [dot_right_t(stacked[...], top[...]).astype(BF16)]
    for tier in range(levels - 1, -1, -1):
        values = []
        for e in range(quads >> tier + 1):
            rows = pl.ds(e * double, double)
            matrix = matrices[tier]
            children = descend(
                level[e],
                kept[tier][e],
                matrix[rows, pl.ds(0, double)],
                matrix[rows, pl.ds(double, rank)],
            )
            values += [children[:, :rank], children[:, rank:]]
        level = values
    for i in range(quads):
        below[i] = level[i]
    for i in range(quads):
        outs[i][...] = below[jnp.where(in_lower(chips), i, quads - 1 - i)]


def quad_down_kernel(*refs, chips, far):
    parts, (paired, matrix, keep, send, rows, work) = refs[:-6], refs[-6:]
    double = paired.shape[1]
    at = chip_of()
    line = mirrored(at, chips)
    parent = parts[0][...]
    for source, part in zip(inner_chips(chips), parts):
        parent = jnp.where(line == (chips - 1 - source if far else source), part[...], parent)
    half = paired.shape[0] // 2
    first = jnp.where(in_lower(chips), 0, 1)
    first = 1 - first if far else first
    rows[...] = paired[pl.ds(pl.multiple_of(first * half, half), half), :]
    children = descend(
        parent, rows[...], matrix[:, pl.ds(0, double)], matrix[:, pl.ds(double, double // 2)]
    )
    split_lanes(children, at % 2, keep, send, work)


def pair_down_kernel(
    near, near_came, far, far_came, paired, matrix, keep, send, parent, work, *, chips
):
    double = paired.shape[1]
    inner = (chip_of() % 2 == 1) == in_lower(chips)
    near = jnp.where(inner, near[...], near_came[...])
    far = jnp.where(inner, far[...], far_came[...])
    join_rows(near, far, jnp.where(in_lower(chips), 0, 1), parent)
    children = descend(
        parent[...], paired[...], matrix[:, pl.ds(0, double)], matrix[:, pl.ds(double, double // 2)]
    )
    split_lanes(children, core_of(), keep, send, work)


def body(
    right_side,
    leaf_inverse,
    leaf_basis,
    local_merge,
    local_transfer,
    upper_merge,
    upper_transfer,
    top_inverse,
):
    leaf = leaf_inverse.shape[2]
    rank = leaf_basis.shape[2]
    columns = right_side.shape[2]
    double = 2 * rank
    wide = double + rank
    leaf_count = right_side.shape[1] // leaf
    sub_count = lax.axis_size("sub")
    sub_depth = sub_count.bit_length() - 1
    root_count = lax.axis_size("root")
    chips = sub_count // 2
    middle = chips // 2 - 1
    half, quarter = columns // 2, columns // 4
    heights = [double >> tier for tier in range(3, sub_depth + 1)]
    levels = len(heights)
    quads = chips // 2

    local = [right_side[0], leaf_inverse[0], leaf_basis[0]]
    tree = [local_merge[0], local_transfer[0]]
    blocks = wide // rank
    top_rows, top_width = top_inverse.shape
    quad_rows = blocks * (double // 4)
    top_block = top_rows * top_width // rank
    high_rows = blocks * sum(heights)
    any_spec, vmem_spec = pl.BlockSpec(memory_space=pl.ANY), pl.BlockSpec(memory_space=pltpu.VMEM)
    pair_rows = blocks * (double // 2)
    shapes = [(rows, rank) for rows in (pair_rows + quad_rows, quad_rows + top_block, high_rows)]
    args = [upper_merge[0], upper_transfer[0], top_inverse]
    low, quad_top, high = pl.pallas_call(
        pack_kernel,
        out_shape=[pltpu.VMEM(shape, BF16) for shape in shapes],
        in_specs=[any_spec] * len(args),
        out_specs=[vmem_spec] * len(shapes),
        scratch_shapes=[pltpu.SemaphoreType.DMA((3 * blocks + rank // top_width,))],
        compiler_params=pltpu.CompilerParams(vmem_limit_bytes=2 * MIB),
        cost_estimate=cost(1.5),
    )(*[pltpu.with_memory_space_constraint(a, pltpu.HBM) for a in args])
    far_high = flip(high, "sub", 2)
    far = flip(quad_top, "sub", 2)
    low_other = flip(low, "sub", 1)

    shapes = [
        (half, rank),
        (half, rank),
        (leaf_count // 2, columns, double),
        (leaf_count // 4, columns, double),
    ]
    given = local + tree
    fetched = [2]
    shapes += [given[i].shape for i in fetched]
    spaces = [pltpu.HBM if i in fetched else pltpu.VMEM for i in range(5)]
    given = [pltpu.with_memory_space_constraint(a, space) for a, space in zip(given, spaces)]
    keep, send, low_paired, high_paired, *moved = pl.pallas_call(
        functools.partial(climb_local_kernel, leaf_count=leaf_count, fetched=fetched),
        out_shape=[pltpu.VMEM(shape, BF16) for shape in shapes],
        in_specs=[any_spec if i in fetched else vmem_spec for i in range(5)],
        out_specs=[vmem_spec] * len(shapes),
        scratch_shapes=[
            pltpu.VMEM((columns, rank), BF16),
            pltpu.SemaphoreType.DMA((5 * leaf_count,)),
        ],
        compiler_params=pltpu.CompilerParams(vmem_limit_bytes=16 * MIB),
        cost_estimate=cost(0.01),
    )(*given)
    for i, array in zip(fetched, moved):
        given[i] = array

    recv = flip(send, "sub", 1)
    recv = passed(recv, 0.8)
    low_other, far_high, token = lax.optimization_barrier((low_other, far_high, mark(send)))
    (pair_matrix,) = vmem_call(pair_matrix_kernel, [(double, wide)], [low, low_other])
    (rows_mine,) = vmem_call(tails_kernel, [(2, high_rows, rank)], [high, far_high])
    inner = inner_chips(chips)
    others = [s for s in inner if s != middle]
    rows_rest = [swapped(rows_mine, s, middle, chips) for s in others]
    pair_paired, coeffs = vmem_call(
        pair_up_kernel,
        [(half, double), (half, rank)],
        [keep, recv, pair_matrix],
        micros=0.05,
        after=[token],
    )

    recv = flip(coeffs, "sub", 2)
    recv, rows_rest = lax.optimization_barrier((recv, rows_rest))
    recv = passed(recv, 10)
    far, token = lax.optimization_barrier((far, mark(coeffs)))
    (top_mine,) = vmem_call(tails_kernel, [(2, top_block, rank)], [quad_top, far])
    top_rest = [swapped(top_mine, s, middle, chips) for s in others]
    far_other = flip(far, "sub", 1)
    (quad_matrix,) = vmem_call(
        quad_matrix_kernel, [(double, wide)], [low, low_other, far, far_other], after=[recv]
    )
    quad_paired, near, send = vmem_call(
        functools.partial(quad_up_kernel, chips=chips),
        [(half, double), (quarter, rank), (quarter, rank)],
        [coeffs, recv, quad_matrix],
        [pltpu.VMEM((half, rank), BF16)],
        micros=0.05,
        after=[token],
    )

    own = inner.index(middle)
    parts = [swapped(near if s < middle else send, s, middle, chips) for s in others]
    parts, top_rest = lax.optimization_barrier((parts, top_rest))
    parts = [passed(part, 10) for part in parts]
    rows_rest, near = lax.optimization_barrier((rows_rest, near))
    stacks = [rows_mine, flip(rows_mine, "sub", 1)]
    for item in rows_rest:
        stacks += [item, flip(item, "sub", 1)]
    *high_matrices, = vmem_call(
        functools.partial(high_matrix_kernel, chips=chips, heights=heights),
        [(sub_count * height, wide) for height in heights],
        stacks,
        limit=8 * MIB,
        micros=0.2,
        after=parts,
    )
    *high_paired_up, coeffs = vmem_call(
        functools.partial(high_up_kernel, chips=chips, levels=levels),
        [(quads >> t + 1, quarter, double) for t in range(levels)] + [(quarter, rank)],
        parts[:own] + [near] + parts[own:] + high_matrices,
        limit=8 * MIB,
        micros=0.4,
    )

    roots = [flip(coeffs, "root", mask) for mask in range(root_count - 1, 0, -1)]
    roots[0] = passed(roots[0], 0.01)
    roots.append(coeffs)
    roots.reverse()
    stacks = [top_mine, flip(top_mine, "sub", 1)]
    for item in top_rest:
        stacks += [item, flip(item, "sub", 1)]
    (top_matrix,) = vmem_call(
        functools.partial(top_matrix_kernel, chips=chips),
        [(top_rows, sub_count * top_width)],
        stacks,
        limit=8 * MIB,
    )
    values = vmem_call(
        functools.partial(high_down_kernel, chips=chips, levels=levels, roots=root_count),
        [(quarter, rank)] * quads,
        roots + [top_matrix] + high_matrices + high_paired_up,
        [
            pltpu.VMEM((quarter, root_count * rank), BF16),
            pltpu.VMEM((quads, quarter, rank), BF16),
        ],
        limit=8 * MIB,
        micros=0.7,
    )

    def quad_down(parts, far):
        return vmem_call(
            functools.partial(quad_down_kernel, chips=chips, far=far),
            [(quarter, rank), (quarter, rank)],
            parts + [quad_paired, quad_matrix],
            [pltpu.VMEM((quarter, double), BF16)] * 2,
            micros=0.4,
        )

    def across(value, source):
        return passed(swapped(value, source, middle, chips), 0.01)

    parts = {s: value if s == middle else across(value, s) for s, value in zip(inner, values)}
    lower, upper = inner[: quads // 2], inner[quads // 2 :]
    near, send = quad_down([parts[s] for s in lower] + [values[own]] * len(upper), False)
    near_came = flip(send, "sub", 2)
    far, send = quad_down([values[own]] * len(lower) + [parts[s] for s in upper], True)
    far_came = flip(send, "sub", 2)
    keep, send = vmem_call(
        functools.partial(pair_down_kernel, chips=chips),
        [(half, rank), (half, rank)],
        [near, near_came, far, far_came, pair_paired, pair_matrix],
        [pltpu.VMEM((half, rank), BF16), pltpu.VMEM((half, double), BF16)],
        micros=0.4,
    )
    recv = flip(send, "sub", 1)

    args = [keep, recv, low_paired, high_paired] + given
    out = pl.pallas_call(
        descend_local_kernel,
        out_shape=jax.ShapeDtypeStruct((leaf_count * leaf, columns), F32),
        in_specs=[vmem_spec] * len(args),
        out_specs=any_spec,
        scratch_shapes=[
            pltpu.VMEM((columns, rank), BF16),
            pltpu.VMEM((leaf_count, leaf, columns), F32),
            pltpu.SemaphoreType.DMA((leaf_count,)),
        ],
        compiler_params=pltpu.CompilerParams(vmem_limit_bytes=16 * MIB),
        cost_estimate=cost(3),
    )(*[pltpu.with_memory_space_constraint(a, pltpu.VMEM) for a in args])
    return out[None]


def solution(mesh):
    return jax.shard_map(
        body,
        mesh=mesh,
        in_specs=(
            P("root", "sub", None),
            P("root", "sub", None),
            P("root", "sub", None),
            P("root", "sub", None),
            P("root", "sub", None),
            P("root", "sub", None),
            P("root", "sub", None),
            P("root", "sub"),
        ),
        out_specs=P("root", "sub", None),
        check_vma=False,
    )
```

```python
import functools

import jax
import jax.numpy as jnp
from jax import lax
from jax.experimental import pallas as pl
from jax.experimental.pallas import tpu as pltpu
from jax.sharding import PartitionSpec as P

BF16 = jnp.bfloat16
F32 = jnp.float32
MIB = 1 << 20


def dot(left, right):
    return lax.dot_general(left, right, (((1,), (0,)), ((), ())), preferred_element_type=F32)


def dot_left_t(left, right):
    return lax.dot_general(left, right, (((0,), (0,)), ((), ())), preferred_element_type=F32)


def dot_right_t(left, right):
    return lax.dot_general(left, right, (((1,), (1,)), ((), ())), preferred_element_type=F32)


def cost(micros):
    return pl.CostEstimate(flops=int(micros * 1e9), bytes_accessed=1, transcendentals=0)


def vmem_call(kernel, outs, args, scratch=(), limit=4 * MIB, micros=0.1, after=()):
    count = len(args)
    args = list(args) + list(after)
    return pl.pallas_call(
        lambda *refs: kernel(*refs[:count], *refs[len(args) :]),
        out_shape=[pltpu.VMEM(shape, BF16) for shape in outs],
        in_specs=[pl.BlockSpec(memory_space=pltpu.VMEM)] * len(args),
        out_specs=[pl.BlockSpec(memory_space=pltpu.VMEM)] * len(outs),
        scratch_shapes=list(scratch),
        compiler_params=pltpu.CompilerParams(vmem_limit_bytes=limit),
        cost_estimate=cost(micros),
    )(*[pltpu.with_memory_space_constraint(a, pltpu.VMEM) for a in args])


def copy_kernel(value, out):
    out[...] = value[...]


def passed(value, micros):
    return vmem_call(copy_kernel, [value.shape], [value], micros=micros)[0]


def mark_kernel(value, out):
    out[...] = value[pl.ds(0, out.shape[0]), pl.ds(0, out.shape[1])]


def mark(value):
    return vmem_call(mark_kernel, [(16, 128)], [value], micros=0.02)[0]


def flip(block, axis, mask):
    count = lax.axis_size(axis)
    return lax.ppermute(block, axis, [(i, i ^ mask) for i in range(count)])


def swap_with(source, target, chips):
    partner = [device ^ 1 for device in range(2 * chips)]
    for low, high in ((source, target), (chips - 1 - source, chips - 1 - target)):
        for core in range(2):
            partner[2 * low + core], partner[2 * high + core] = 2 * high + core, 2 * low + core
    return list(enumerate(partner))


def inner_chips(chips):
    return [chip for chip in range(chips) if (chip % 2 == 1) == (chip < chips // 2)]


def swapped(block, source, target, chips):
    return lax.ppermute(block, "sub", swap_with(source, target, chips))


def core_of():
    return lax.axis_index("sub") % 2


def chip_of():
    return lax.axis_index("sub") // 2


def in_lower(chips):
    return chip_of() < chips // 2


def mirrored(chip, chips):
    return jnp.where(in_lower(chips), chip, chips - 1 - chip)


def split_rows(value, first, keep, send, work):
    half = value.shape[0] // 2
    work[...] = value
    keep[...] = work[pl.ds(pl.multiple_of(first * half, half), half), :]
    send[...] = work[pl.ds(pl.multiple_of((1 - first) * half, half), half), :]


def split_lanes(value, first, keep, send, work):
    half = value.shape[1] // 2
    work[...] = value
    keep[...] = work[:, pl.ds(pl.multiple_of(first * half, half), half)]
    send[...] = work[:, pl.ds(pl.multiple_of((1 - first) * half, half), half)]


def join_rows(mine, other, first, work):
    half = mine.shape[0]
    work[pl.ds(pl.multiple_of(first * half, half), half), :] = mine
    work[pl.ds(pl.multiple_of((1 - first) * half, half), half), :] = other


def join_lanes(mine, other, first, work):
    half = mine.shape[1]
    work[:, pl.ds(pl.multiple_of(first * half, half), half)] = mine
    work[:, pl.ds(pl.multiple_of((1 - first) * half, half), half)] = other


def climb(paired, merge_mat, transfer):
    inner = dot_right_t(paired, merge_mat).astype(BF16)
    return dot(inner, transfer).astype(BF16)


def descend(parent, paired, merge_mat, transfer):
    rest = (paired.astype(F32) - dot_right_t(parent, transfer)).astype(BF16)
    return dot_right_t(rest, merge_mat).astype(BF16)


def pack_kernel(merge, transfer, top, *refs):
    low, quad_top, high, sems = refs
    rows, double = merge.shape
    rank = transfer.shape[1]
    steps = []

    def fetch(source, target):
        steps.append(pltpu.make_async_copy(source, target, sems.at[len(steps)]))

    def level_rows(low, size, target, at):
        for lanes in range(double // rank):
            fetch(
                merge.at[pl.ds(low, size), pl.ds(lanes * rank, rank)], target.at[pl.ds(at, size), :]
            )
            at += size
        fetch(transfer.at[pl.ds(low, size), :], target.at[pl.ds(at, size), :])
        return at + size

    quad_low, high_low = double // 2, double // 2 + double // 4
    level_rows(high_low, rows - high_low, high, 0)
    quad_rows = level_rows(quad_low, high_low - quad_low, quad_top, 0)
    width = top.shape[1]
    size = top.shape[0] * width // rank
    for piece in range(rank // width):
        fetch(
            top.at[pl.ds(piece * size, size), :],
            quad_top.at[pl.ds(quad_rows, size), pl.ds(piece * width, width)],
        )
    pair_rows = level_rows(0, quad_low, low, 0)
    for step in steps:
        step.start()
    for step in steps:
        step.wait()
    low[pl.ds(pair_rows, quad_rows), :] = quad_top[pl.ds(0, quad_rows), :]


def climb_local_kernel(*refs, leaf_count, fetched):
    arrays = list(refs[:5])
    keep, send, low_paired, high_paired = refs[5:9]
    kept = {1: low_paired, 2: high_paired}
    *outs, work, sems = refs[9:]
    leaf = arrays[0].shape[0] // leaf_count
    rank = arrays[2].shape[1]
    double = 2 * rank
    depth = leaf_count.bit_length() - 1
    copies = {}
    for index, out in zip(fetched, outs):
        block = leaf if index < 3 else double
        for i in range(out.shape[0] // block):
            rows = pl.ds(i * block, block)
            copies[index, i] = pltpu.make_async_copy(
                arrays[index].at[rows, :], out.at[rows, :], sems.at[len(copies)]
            )
        arrays[index] = out
    for key in sorted(copies, key=lambda key: (key[0] // 3, key[1])):
        copies[key].start()

    def ready(index, i):
        if (index, i) in copies:
            copies[index, i].wait()

    sides, inverse, basis, merge, transfer = arrays
    products = []
    for i in range(leaf_count):
        rows = pl.ds(i * leaf, leaf)
        for index in range(2):
            ready(index, i)
        products.append(dot(inverse[rows, :], sides[rows, :]).astype(BF16))
    for i in range(leaf_count):
        ready(2, i)
        coeffs = dot_left_t(products[i], basis[pl.ds(i * leaf, leaf), :]).astype(BF16)
        kept[1][i // 2, :, pl.ds((i % 2) * rank, rank)] = coeffs
    for e in range(leaf_count - 1):
        for index in (3, 4):
            ready(index, e)
    for tier in range(1, depth + 1):
        count = leaf_count >> tier
        start = leaf_count - 2 * count
        for e in range(count):
            rows = pl.ds((start + e) * double, double)
            coeffs = climb(kept[tier][e], merge[rows, :], transfer[rows, :])
            if tier < depth:
                kept[tier + 1][e // 2, :, pl.ds((e % 2) * rank, rank)] = coeffs
            else:
                split_rows(coeffs, core_of(), keep, send, work)


def descend_local_kernel(
    mine, other, low_paired, high_paired, sides, inverse, basis, merge, transfer, out, parent, result, sems
):
    leaf = inverse.shape[1]
    rank = basis.shape[1]
    double = 2 * rank
    kept = {1: low_paired, 2: high_paired}
    leaf_count = out.shape[0] // leaf
    depth = leaf_count.bit_length() - 1
    join_rows(mine[...], other[...], core_of(), parent)
    level = [parent[...]]
    for tier in range(depth, 0, -1):
        nodes = leaf_count >> tier
        start = leaf_count - 2 * nodes
        below = []
        for e in range(nodes):
            rows = pl.ds((start + e) * double, double)
            children = descend(level[e], kept[tier][e], merge[rows, :], transfer[rows, :])
            below += [children[:, :rank], children[:, rank:]]
        level = below
    copies = []
    for i in range(leaf_count):
        rows = pl.ds(i * leaf, leaf)
        arrays = (inverse, sides, basis)
        spread = dot_right_t(arrays[2][rows, :], level[i])
        rest = (arrays[1][rows, :].astype(F32) - spread).astype(BF16)
        result[i] = dot(arrays[0][rows, :], rest)
        copies.append(
            pltpu.make_async_copy(result.at[i], out.at[pl.ds(i * leaf, leaf), :], sems.at[i])
        )
        copies[-1].start()
    for copy in copies:
        copy.wait()


def place_rows(block, low, size, out, at):
    width = block.shape[-1]
    for lanes in range(out.shape[1] // width):
        out[pl.ds(at, size), pl.ds(lanes * width, width)] = block[pl.ds(low + lanes * size, size), :]


def pair_matrix_kernel(mine, other, out):
    size = out.shape[0] // 2
    core = core_of()
    place_rows(mine, 0, size, out, pl.multiple_of(core * size, size))
    place_rows(other, 0, size, out, pl.multiple_of((1 - core) * size, size))


def quad_matrix_kernel(mine, other, far, far_other, out):
    size = out.shape[0] // 4
    core, side = core_of(), chip_of() % 2
    start = mine.shape[0] - out.shape[1] // mine.shape[1] * size
    blocks = [(side, core, mine, start), (side, 1 - core, other, start)]
    blocks += [(1 - side, core, far, 0), (1 - side, 1 - core, far_other, 0)]
    for chip, which, ref, low in blocks:
        place_rows(ref, low, size, out, pl.multiple_of((2 * chip + which) * size, size))


def tails_kernel(mine, far, out):
    for i, ref in enumerate((mine, far)):
        out[i] = ref[pl.ds(ref.shape[0] - out.shape[1], out.shape[1]), :]


def extend_kernel(mine, other, out):
    out[pl.ds(0, mine.shape[0]), :] = mine[...]
    out[pl.ds(mine.shape[0], other.shape[0]), :] = other[...]


def stack_kernel(*refs):
    *ins, out = refs
    at = 0
    for ref in ins:
        if len(ref.shape) == 2:
            out[at] = ref[...]
            at += 1
        else:
            out[pl.ds(at, ref.shape[0])] = ref[...]
            at += ref.shape[0]


def device_blocks(refs, chips):
    inner, core = inner_chips(chips), core_of()
    own = inner.index(chips // 2 - 1)
    order = [inner[own]] + inner[:own] + inner[own + 1 :]
    for source, mine, other in zip(order, refs[::2], refs[1::2]):
        for i, chip in enumerate((source, source ^ 1)):
            for which, ref in ((core, mine), (1 - core, other)):
                yield 2 * mirrored(chip, chips) + which, ref.at[i]


def high_matrix_kernel(*refs, chips, heights):
    refs, outs = refs[: -len(heights)], refs[-len(heights) :]
    rows = sum(heights)
    for device, ref in device_blocks(refs, chips):
        offset = 0
        for out, height in zip(outs, heights):
            width = ref.shape[-1]
            for lanes in range(out.shape[1] // width):
                out[
                    pl.ds(pl.multiple_of(device * height, height), height),
                    pl.ds(lanes * width, width),
                ] = ref[pl.ds(lanes * rows + offset, height), :]
            offset += height


def top_matrix_kernel(*refs, chips):
    refs, top = refs[:-1], refs[-1]
    width = top.shape[1] // (2 * chips)
    for device, ref in device_blocks(refs, chips):
        size = top.shape[0] * width // ref.shape[-1]
        for piece in range(ref.shape[-1] // width):
            top[pl.ds(piece * size, size), pl.ds(pl.multiple_of(device * width, width), width)] = ref[
                :, pl.ds(piece * width, width)
            ]


def pair_up_kernel(mine, other, matrix, paired, coeffs):
    double = paired.shape[1]
    join_lanes(mine[...], other[...], core_of(), paired)
    coeffs[...] = climb(
        paired[...], matrix[:, pl.ds(0, double)], matrix[:, pl.ds(double, double // 2)]
    )


def quad_up_kernel(mine, other, matrix, paired, coeffs):
    double = paired.shape[1]
    join_lanes(mine[...], other[...], chip_of() % 2, paired)
    coeffs[...] = climb(
        paired[...], matrix[:, pl.ds(0, double)], matrix[:, pl.ds(double, double // 2)]
    )


def high_up_kernel(*refs, chips, levels):
    quads = chips // 2
    parts, matrices = refs[:quads], refs[quads : quads + levels]
    kept, coeffs = refs[quads + levels : quads + 2 * levels], refs[-1]
    rank = coeffs.shape[1]
    double = 2 * rank
    for i, part in enumerate(parts):
        at = jnp.where(in_lower(chips), i, quads - 1 - i)
        lanes = pl.ds(pl.multiple_of((at % 2) * rank, rank), rank)
        kept[0][at // 2, :, lanes] = part[...]
    for tier in range(levels):
        nodes = quads >> tier + 1
        for e in range(nodes):
            rows = pl.ds(e * double, double)
            matrix = matrices[tier]
            value = climb(
                kept[tier][e], matrix[rows, pl.ds(0, double)], matrix[rows, pl.ds(double, rank)]
            )
            if tier + 1 < levels:
                kept[tier + 1][e // 2, :, pl.ds((e % 2) * rank, rank)] = value
            else:
                coeffs[...] = value


def high_down_kernel(*refs, chips, levels, roots):
    quads = chips // 2
    own, top, refs = refs[:roots], refs[roots], refs[roots + 1 :]
    matrices, kept, outs = refs[:levels], refs[levels : 2 * levels], refs[2 * levels : -2]
    stacked, below = refs[-2:]
    rank = outs[0].shape[1]
    double = 2 * rank
    me = lax.axis_index("root")
    for mask in range(roots):
        at = pl.multiple_of((me ^ mask) * rank, rank)
        stacked[:, pl.ds(at, rank)] = own[mask][...]
    below[0] = dot_right_t(stacked[...], top[...]).astype(BF16)
    for tier in range(levels - 1, 0, -1):
        values = []
        for e in range(quads >> tier + 1):
            rows = pl.ds(e * double, double)
            matrix = matrices[tier]
            children = descend(
                below[e], kept[tier][e], matrix[rows, pl.ds(0, double)], matrix[rows, pl.ds(double, rank)]
            )
            values += [children[:, :rank], children[:, rank:]]
        for e, value in enumerate(values):
            below[e] = value
    for i, out in enumerate(outs):
        at = jnp.where(in_lower(chips), i, quads - 1 - i)
        node = at // 2 if quads > 2 else 0
        start = node * double
        if quads > 2:
            start = pl.multiple_of(start, double)
        lifted = dot_right_t(below[node], matrices[0][pl.ds(start, double), pl.ds(double, rank)])
        rest = (kept[0][node].astype(F32) - lifted).astype(BF16)
        child = pl.multiple_of(start + at % 2 * rank, rank)
        out[...] = dot_right_t(rest, matrices[0][pl.ds(child, rank), pl.ds(0, double)]).astype(BF16)


def quad_down_kernel(*refs, chips):
    parts, (paired, matrix, keep, send, work) = refs[:-5], refs[-5:]
    double = paired.shape[1]
    at = chip_of()
    parent = parts[0][...]
    for source, part in zip(inner_chips(chips), parts):
        parent = jnp.where(mirrored(at, chips) == source, part[...], parent)
    children = descend(
        parent, paired[...], matrix[:, pl.ds(0, double)], matrix[:, pl.ds(double, double // 2)]
    )
    split_lanes(children, at % 2, keep, send, work)


def pair_down_kernel(mine, other, paired, matrix, keep, send, work, *, chips):
    double = paired.shape[1]
    inner = (chip_of() % 2 == 1) == in_lower(chips)
    parent = jnp.where(inner, mine[...], other[...])
    children = descend(
        parent, paired[...], matrix[:, pl.ds(0, double)], matrix[:, pl.ds(double, double // 2)]
    )
    split_lanes(children, core_of(), keep, send, work)


def body(
    right_side,
    leaf_inverse,
    leaf_basis,
    local_merge,
    local_transfer,
    upper_merge,
    upper_transfer,
    top_inverse,
):
    leaf = leaf_inverse.shape[2]
    rank = leaf_basis.shape[2]
    columns = right_side.shape[2]
    double = 2 * rank
    wide = double + rank
    leaf_count = right_side.shape[1] // leaf
    sub_count = lax.axis_size("sub")
    sub_depth = sub_count.bit_length() - 1
    root_count = lax.axis_size("root")
    chips = sub_count // 2
    middle = chips // 2 - 1
    half = columns // 2
    heights = [double >> tier for tier in range(3, sub_depth + 1)]
    levels = len(heights)
    quads = chips // 2

    local = [right_side[0], leaf_inverse[0], leaf_basis[0]]
    tree = [local_merge[0], local_transfer[0]]
    blocks = wide // rank
    top_rows, top_width = top_inverse.shape
    quad_rows = blocks * (double // 4)
    top_block = top_rows * top_width // rank
    high_rows = blocks * sum(heights)
    any_spec, vmem_spec = pl.BlockSpec(memory_space=pl.ANY), pl.BlockSpec(memory_space=pltpu.VMEM)
    pair_rows = blocks * (double // 2)
    shapes = [(rows, rank) for rows in (pair_rows + quad_rows, quad_rows + top_block, high_rows)]
    args = [upper_merge[0], upper_transfer[0], top_inverse]
    low, quad_top, high = pl.pallas_call(
        pack_kernel,
        out_shape=[pltpu.VMEM(shape, BF16) for shape in shapes],
        in_specs=[any_spec] * len(args),
        out_specs=[vmem_spec] * len(shapes),
        scratch_shapes=[pltpu.SemaphoreType.DMA((3 * blocks + rank // top_width,))],
        compiler_params=pltpu.CompilerParams(vmem_limit_bytes=2 * MIB),
        cost_estimate=cost(1.5),
    )(*[pltpu.with_memory_space_constraint(a, pltpu.HBM) for a in args])
    far_high = flip(high, "sub", 2)
    far = flip(quad_top, "sub", 2)
    low_other = flip(low, "sub", 1)

    shapes = [
        (half, rank),
        (half, rank),
        (leaf_count // 2, columns, double),
        (leaf_count // 4, columns, double),
    ]
    given = local + tree
    fetched = [2]
    shapes += [given[i].shape for i in fetched]
    spaces = [pltpu.HBM if i in fetched else pltpu.VMEM for i in range(5)]
    given = [pltpu.with_memory_space_constraint(a, space) for a, space in zip(given, spaces)]
    keep, send, low_paired, high_paired, *moved = pl.pallas_call(
        functools.partial(climb_local_kernel, leaf_count=leaf_count, fetched=fetched),
        out_shape=[pltpu.VMEM(shape, BF16) for shape in shapes],
        in_specs=[any_spec if i in fetched else vmem_spec for i in range(5)],
        out_specs=[vmem_spec] * len(shapes),
        scratch_shapes=[
            pltpu.VMEM((columns, rank), BF16),
            pltpu.SemaphoreType.DMA((5 * leaf_count,)),
        ],
        compiler_params=pltpu.CompilerParams(vmem_limit_bytes=16 * MIB),
        cost_estimate=cost(0.01),
    )(*given)
    for i, array in zip(fetched, moved):
        given[i] = array

    recv = flip(send, "sub", 1)
    recv = passed(recv, 0.8)
    low_other, far_high, token = lax.optimization_barrier((low_other, far_high, mark(send)))
    (pair_matrix,) = vmem_call(pair_matrix_kernel, [(double, wide)], [low, low_other])
    (rows_mine,) = vmem_call(tails_kernel, [(2, high_rows, rank)], [high, far_high])
    inner = inner_chips(chips)
    others = [s for s in inner if s != middle]
    rows_rest = [swapped(rows_mine, s, middle, chips) for s in others]
    pair_paired, coeffs = vmem_call(
        pair_up_kernel,
        [(half, double), (half, rank)],
        [keep, recv, pair_matrix],
        micros=0.05,
        after=[token],
    )

    recv = flip(coeffs, "sub", 2)
    recv, rows_rest = lax.optimization_barrier((recv, rows_rest))
    recv = passed(recv, 10)
    far, token = lax.optimization_barrier((far, mark(coeffs)))
    (top_mine,) = vmem_call(tails_kernel, [(2, top_block, rank)], [quad_top, far])
    top_rest = [swapped(top_mine, s, middle, chips) for s in others]
    far_other = flip(far, "sub", 1)
    (quad_matrix,) = vmem_call(
        quad_matrix_kernel, [(double, wide)], [low, low_other, far, far_other], after=[recv]
    )
    quad_paired, coeffs = vmem_call(
        quad_up_kernel,
        [(half, double), (half, rank)],
        [coeffs, recv, quad_matrix],
        micros=0.05,
        after=[token],
    )

    own = inner.index(middle)
    parts = [swapped(coeffs, s, middle, chips) for s in others]
    parts, top_rest = lax.optimization_barrier((parts, top_rest))
    parts = [passed(part, 10) for part in parts]
    rows_rest, coeffs = lax.optimization_barrier((rows_rest, coeffs))
    stacks = [rows_mine, flip(rows_mine, "sub", 1)]
    for item in rows_rest:
        stacks += [item, flip(item, "sub", 1)]
    *high_matrices, = vmem_call(
        functools.partial(high_matrix_kernel, chips=chips, heights=heights),
        [(sub_count * height, wide) for height in heights],
        stacks,
        limit=8 * MIB,
        micros=0.2,
        after=parts,
    )
    *high_paired_up, coeffs = vmem_call(
        functools.partial(high_up_kernel, chips=chips, levels=levels),
        [(quads >> t + 1, half, double) for t in range(levels)] + [(half, rank)],
        parts[:own] + [coeffs] + parts[own:] + high_matrices,
        limit=8 * MIB,
        micros=0.4,
    )

    roots = [flip(coeffs, "root", mask) for mask in range(root_count - 1, 0, -1)]
    roots[0] = passed(roots[0], 0.01)
    roots.append(coeffs)
    roots.reverse()
    stacks = [top_mine, flip(top_mine, "sub", 1)]
    for item in top_rest:
        stacks += [item, flip(item, "sub", 1)]
    (top_matrix,) = vmem_call(
        functools.partial(top_matrix_kernel, chips=chips),
        [(top_rows, sub_count * top_width)],
        stacks,
        limit=8 * MIB,
    )
    values = vmem_call(
        functools.partial(high_down_kernel, chips=chips, levels=levels, roots=root_count),
        [(half, rank)] * (quads // 2),
        roots + [top_matrix] + high_matrices + high_paired_up,
        [
            pltpu.VMEM((half, root_count * rank), BF16),
            pltpu.VMEM((max(quads // 2, 1), half, rank), BF16),
        ],
        limit=8 * MIB,
        micros=0.7,
    )

    parts = [
        value if s == middle else swapped(value, s, middle, chips)
        for s, value in zip(inner, values)
    ]
    keep, send = vmem_call(
        functools.partial(quad_down_kernel, chips=chips),
        [(half, rank), (half, rank)],
        parts + [quad_paired, quad_matrix],
        [pltpu.VMEM((half, double), BF16)],
        micros=0.4,
    )
    recv = flip(send, "sub", 2)
    keep, send = vmem_call(
        functools.partial(pair_down_kernel, chips=chips),
        [(half, rank), (half, rank)],
        [keep, recv, pair_paired, pair_matrix],
        [pltpu.VMEM((half, double), BF16)],
        micros=0.4,
    )
    recv = flip(send, "sub", 1)

    args = [keep, recv, low_paired, high_paired] + given
    out = pl.pallas_call(
        descend_local_kernel,
        out_shape=jax.ShapeDtypeStruct((leaf_count * leaf, columns), F32),
        in_specs=[vmem_spec] * len(args),
        out_specs=any_spec,
        scratch_shapes=[
            pltpu.VMEM((columns, rank), BF16),
            pltpu.VMEM((leaf_count, leaf, columns), F32),
            pltpu.SemaphoreType.DMA((leaf_count,)),
        ],
        compiler_params=pltpu.CompilerParams(vmem_limit_bytes=16 * MIB),
        cost_estimate=cost(3),
    )(*[pltpu.with_memory_space_constraint(a, pltpu.VMEM) for a in args])
    return out[None]


def solution(mesh):
    return jax.shard_map(
        body,
        mesh=mesh,
        in_specs=(
            P("root", "sub", None),
            P("root", "sub", None),
            P("root", "sub", None),
            P("root", "sub", None),
            P("root", "sub", None),
            P("root", "sub", None),
            P("root", "sub", None),
            P("root", "sub"),
        ),
        out_specs=P("root", "sub", None),
        check_vma=False,
    )
```

```python
import functools

import jax
import jax.numpy as jnp
from jax import lax
from jax.experimental import pallas as pl
from jax.experimental.pallas import tpu as pltpu
from jax.sharding import PartitionSpec as P

BF16 = jnp.bfloat16
F32 = jnp.float32
MIB = 1 << 20


def dot(left, right):
    return lax.dot_general(left, right, (((1,), (0,)), ((), ())), preferred_element_type=F32)


def dot_left_t(left, right):
    return lax.dot_general(left, right, (((0,), (0,)), ((), ())), preferred_element_type=F32)


def dot_right_t(left, right):
    return lax.dot_general(left, right, (((1,), (1,)), ((), ())), preferred_element_type=F32)


def cost(micros):
    return pl.CostEstimate(flops=int(micros * 1e9), bytes_accessed=1, transcendentals=0)


def vmem_call(kernel, outs, args, scratch=(), limit=4 * MIB, micros=0.1, after=()):
    count = len(args)
    args = list(args) + list(after)
    return pl.pallas_call(
        lambda *refs: kernel(*refs[:count], *refs[len(args) :]),
        out_shape=[pltpu.VMEM(shape, BF16) for shape in outs],
        in_specs=[pl.BlockSpec(memory_space=pltpu.VMEM)] * len(args),
        out_specs=[pl.BlockSpec(memory_space=pltpu.VMEM)] * len(outs),
        scratch_shapes=list(scratch),
        compiler_params=pltpu.CompilerParams(vmem_limit_bytes=limit),
        cost_estimate=cost(micros),
    )(*[pltpu.with_memory_space_constraint(a, pltpu.VMEM) for a in args])


def copy_kernel(value, out):
    out[...] = value[...]


def passed(value, micros):
    return vmem_call(copy_kernel, [value.shape], [value], micros=micros)[0]


def mark_kernel(value, out):
    out[...] = value[pl.ds(0, out.shape[0]), pl.ds(0, out.shape[1])]


def mark(value):
    return vmem_call(mark_kernel, [(16, 128)], [value], micros=0.02)[0]


def flip(block, axis, mask):
    count = lax.axis_size(axis)
    return lax.ppermute(block, axis, [(i, i ^ mask) for i in range(count)])


def side_of(tier):
    return (lax.axis_index("sub") >> (tier - 1)) % 2


def split_rows(value, first, keep, send, work):
    half = value.shape[0] // 2
    work[...] = value
    keep[...] = work[pl.ds(pl.multiple_of(first * half, half), half), :]
    send[...] = work[pl.ds(pl.multiple_of((1 - first) * half, half), half), :]


def join_rows(mine, other, first, work):
    half = mine.shape[0]
    work[pl.ds(pl.multiple_of(first * half, half), half), :] = mine
    work[pl.ds(pl.multiple_of((1 - first) * half, half), half), :] = other


def join_lanes(mine, other, first, work):
    half = mine.shape[1]
    work[:, pl.ds(pl.multiple_of(first * half, half), half)] = mine
    work[:, pl.ds(pl.multiple_of((1 - first) * half, half), half)] = other


def climb(paired, merge_mat, transfer):
    inner = dot_right_t(paired, merge_mat).astype(BF16)
    return dot(inner, transfer).astype(BF16)


def descend(parent, paired, merge_mat, transfer):
    rest = (paired.astype(F32) - dot_right_t(parent, transfer)).astype(BF16)
    return dot_right_t(rest, merge_mat).astype(BF16)


def pack_kernel(merge, transfer, top, *refs):
    low, quad_top, high, sems = refs
    rows, double = merge.shape
    rank = transfer.shape[1]
    steps = []

    def fetch(source, target):
        steps.append(pltpu.make_async_copy(source, target, sems.at[len(steps)]))

    def level_rows(low, size, target, at):
        for lanes in range(double // rank):
            fetch(
                merge.at[pl.ds(low, size), pl.ds(lanes * rank, rank)], target.at[pl.ds(at, size), :]
            )
            at += size
        fetch(transfer.at[pl.ds(low, size), :], target.at[pl.ds(at, size), :])
        return at + size

    quad_low, high_low = double // 2, double // 2 + double // 4
    level_rows(high_low, rows - high_low, high, 0)
    quad_rows = level_rows(quad_low, high_low - quad_low, quad_top, 0)
    width = top.shape[1]
    size = top.shape[0] * width // rank
    for piece in range(rank // width):
        fetch(
            top.at[pl.ds(piece * size, size), :],
            quad_top.at[pl.ds(quad_rows, size), pl.ds(piece * width, width)],
        )
    pair_rows = level_rows(0, quad_low, low, 0)
    for step in steps:
        step.start()
    for step in steps:
        step.wait()
    low[pl.ds(pair_rows, quad_rows), :] = quad_top[pl.ds(0, quad_rows), :]


def climb_local_kernel(*refs, leaf_count, fetched):
    arrays = list(refs[:5])
    keep, send, low_paired, high_paired = refs[5:9]
    kept = {1: low_paired, 2: high_paired}
    *outs, work, sems = refs[9:]
    leaf = arrays[0].shape[0] // leaf_count
    rank = arrays[2].shape[1]
    double = 2 * rank
    depth = leaf_count.bit_length() - 1
    copies = {}
    for index, out in zip(fetched, outs):
        block = leaf if index < 3 else double
        for i in range(out.shape[0] // block):
            rows = pl.ds(i * block, block)
            copies[index, i] = pltpu.make_async_copy(
                arrays[index].at[rows, :], out.at[rows, :], sems.at[len(copies)]
            )
        arrays[index] = out
    for key in sorted(copies, key=lambda key: (key[0] // 3, key[1])):
        copies[key].start()

    def ready(index, i):
        if (index, i) in copies:
            copies[index, i].wait()

    sides, inverse, basis, merge, transfer = arrays
    products = []
    for i in range(leaf_count):
        rows = pl.ds(i * leaf, leaf)
        for index in range(2):
            ready(index, i)
        products.append(dot(inverse[rows, :], sides[rows, :]).astype(BF16))
    for i in range(leaf_count):
        ready(2, i)
        coeffs = dot_left_t(products[i], basis[pl.ds(i * leaf, leaf), :]).astype(BF16)
        kept[1][i // 2, :, pl.ds((i % 2) * rank, rank)] = coeffs
    for e in range(leaf_count - 1):
        for index in (3, 4):
            ready(index, e)
    for tier in range(1, depth + 1):
        count = leaf_count >> tier
        start = leaf_count - 2 * count
        for e in range(count):
            rows = pl.ds((start + e) * double, double)
            coeffs = climb(kept[tier][e], merge[rows, :], transfer[rows, :])
            if tier < depth:
                kept[tier + 1][e // 2, :, pl.ds((e % 2) * rank, rank)] = coeffs
            else:
                split_rows(coeffs, side_of(1), keep, send, work)


def descend_local_kernel(
    mine, other, low_paired, high_paired, sides, inverse, basis, merge, transfer, out, parent, result, sems
):
    leaf = inverse.shape[1]
    rank = basis.shape[1]
    double = 2 * rank
    kept = {1: low_paired, 2: high_paired}
    leaf_count = out.shape[0] // leaf
    depth = leaf_count.bit_length() - 1
    join_rows(mine[...], other[...], side_of(1), parent)
    level = [parent[...]]
    for tier in range(depth, 0, -1):
        nodes = leaf_count >> tier
        start = leaf_count - 2 * nodes
        below = []
        for e in range(nodes):
            rows = pl.ds((start + e) * double, double)
            children = descend(level[e], kept[tier][e], merge[rows, :], transfer[rows, :])
            below += [children[:, :rank], children[:, rank:]]
        level = below
    copies = []
    for i in range(leaf_count):
        rows = pl.ds(i * leaf, leaf)
        arrays = (inverse, sides, basis)
        spread = dot_right_t(arrays[2][rows, :], level[i])
        rest = (arrays[1][rows, :].astype(F32) - spread).astype(BF16)
        result[i] = dot(arrays[0][rows, :], rest)
        copies.append(
            pltpu.make_async_copy(result.at[i], out.at[pl.ds(i * leaf, leaf), :], sems.at[i])
        )
        copies[-1].start()
    for copy in copies:
        copy.wait()


def place_rows(block, low, size, out, at):
    width = block.shape[-1]
    for lanes in range(out.shape[1] // width):
        out[pl.ds(at, size), pl.ds(lanes * width, width)] = block[pl.ds(low + lanes * size, size), :]


def pair_matrix_kernel(mine, other, out):
    size = out.shape[0] // 2
    core = side_of(1)
    place_rows(mine, 0, size, out, pl.multiple_of(core * size, size))
    place_rows(other, 0, size, out, pl.multiple_of((1 - core) * size, size))


def quad_matrix_kernel(mine, other, far, far_other, out):
    size = out.shape[0] // 4
    core, side = side_of(1), side_of(2)
    start = mine.shape[0] - out.shape[1] // mine.shape[1] * size
    blocks = [(side, core, mine, start), (side, 1 - core, other, start)]
    blocks += [(1 - side, core, far, 0), (1 - side, 1 - core, far_other, 0)]
    for chip, which, ref, low in blocks:
        place_rows(ref, low, size, out, pl.multiple_of((2 * chip + which) * size, size))


def tails_kernel(mine, far, out):
    for i, ref in enumerate((mine, far)):
        out[i] = ref[pl.ds(ref.shape[0] - out.shape[1], out.shape[1]), :]


def extend_kernel(mine, other, out):
    out[pl.ds(0, mine.shape[0]), :] = mine[...]
    out[pl.ds(mine.shape[0], other.shape[0]), :] = other[...]


def stack_kernel(*refs):
    *ins, out = refs
    at = 0
    for ref in ins:
        if len(ref.shape) == 2:
            out[at] = ref[...]
            at += 1
        else:
            out[pl.ds(at, ref.shape[0])] = ref[...]
            at += ref.shape[0]


def device_blocks(refs):
    core, chip = side_of(1), lax.axis_index("sub") // 2
    mask = 0
    for mine, other in zip(refs[::2], refs[1::2]):
        for i in range(mine.shape[0]):
            for which, ref in ((core, mine), (1 - core, other)):
                yield 2 * (chip ^ mask) + which, mask, ref.at[i]
            mask += 1


def high_matrix_kernel(*refs, heights):
    refs, outs = refs[: -len(heights)], refs[-len(heights) :]
    rows = sum(heights)
    for device, mask, ref in device_blocks(refs):
        offset = 0
        for out, height in zip(outs, heights):
            count = out.shape[0] // height
            if 2 * mask < count:
                at = pl.multiple_of(device % count * height, height)
                width = ref.shape[-1]
                for lanes in range(out.shape[1] // width):
                    out[pl.ds(at, height), pl.ds(lanes * width, width)] = ref[
                        pl.ds(lanes * rows + offset, height), :
                    ]
            offset += height


def top_matrix_kernel(*refs, devices):
    refs, top = refs[:-1], refs[-1]
    width = top.shape[1] // devices
    for device, _, ref in device_blocks(refs):
        size = top.shape[0] * width // ref.shape[-1]
        for piece in range(ref.shape[-1] // width):
            top[pl.ds(piece * size, size), pl.ds(pl.multiple_of(device * width, width), width)] = ref[
                :, pl.ds(piece * width, width)
            ]


def level_up_kernel(mine, other, matrix, paired, coeffs, *, tier):
    double = paired.shape[1]
    join_lanes(mine[...], other[...], side_of(tier), paired)
    coeffs[...] = climb(
        paired[...], matrix[:, pl.ds(0, double)], matrix[:, pl.ds(double, double // 2)]
    )


def path_down_kernel(*refs, roots):
    own, top, (keep, send, stacked) = refs[:roots], refs[roots], refs[-3:]
    refs = refs[roots + 1 : -3]
    rank = keep.shape[1]
    double = 2 * rank
    me = lax.axis_index("root")
    for mask in range(roots):
        at = pl.multiple_of((me ^ mask) * rank, rank)
        stacked[:, pl.ds(at, rank)] = own[mask][...]
    parent = dot_right_t(stacked[...], top[...]).astype(BF16)
    depth = len(refs) // 2
    for tier in range(depth, 0, -1):
        matrix, paired = refs[2 * tier - 2], refs[2 * tier - 1]
        lifted = dot_right_t(parent, matrix[:, pl.ds(double, rank)])
        rest = (paired[...].astype(F32) - lifted).astype(BF16)

        def child(side):
            rows = pl.ds(pl.multiple_of(side * rank, rank), rank)
            return dot_right_t(rest, matrix[rows, pl.ds(0, double)]).astype(BF16)

        parent = child(side_of(tier))
        if tier == 1:
            keep[...] = parent
            send[...] = child(1 - side_of(tier))


def body(
    right_side,
    leaf_inverse,
    leaf_basis,
    local_merge,
    local_transfer,
    upper_merge,
    upper_transfer,
    top_inverse,
):
    leaf = leaf_inverse.shape[2]
    rank = leaf_basis.shape[2]
    columns = right_side.shape[2]
    double = 2 * rank
    wide = double + rank
    leaf_count = right_side.shape[1] // leaf
    sub_count = lax.axis_size("sub")
    sub_depth = sub_count.bit_length() - 1
    root_count = lax.axis_size("root")
    half = columns // 2
    heights = [double >> tier for tier in range(3, sub_depth + 1)]

    local = [right_side[0], leaf_inverse[0], leaf_basis[0]]
    tree = [local_merge[0], local_transfer[0]]
    blocks = wide // rank
    top_rows, top_width = top_inverse.shape
    quad_rows = blocks * (double // 4)
    top_block = top_rows * top_width // rank
    high_rows = blocks * sum(heights)
    any_spec, vmem_spec = pl.BlockSpec(memory_space=pl.ANY), pl.BlockSpec(memory_space=pltpu.VMEM)
    pair_rows = blocks * (double // 2)
    shapes = [(rows, rank) for rows in (pair_rows + quad_rows, quad_rows + top_block, high_rows)]
    args = [upper_merge[0], upper_transfer[0], top_inverse]
    low, quad_top, high = pl.pallas_call(
        pack_kernel,
        out_shape=[pltpu.VMEM(shape, BF16) for shape in shapes],
        in_specs=[any_spec] * len(args),
        out_specs=[vmem_spec] * len(shapes),
        scratch_shapes=[pltpu.SemaphoreType.DMA((3 * blocks + rank // top_width,))],
        compiler_params=pltpu.CompilerParams(vmem_limit_bytes=2 * MIB),
        cost_estimate=cost(1.5),
    )(*[pltpu.with_memory_space_constraint(a, pltpu.HBM) for a in args])
    far_high = flip(high, "sub", 2)
    far = flip(quad_top, "sub", 2)
    low_other = flip(low, "sub", 1)

    shapes = [
        (half, rank),
        (half, rank),
        (leaf_count // 2, columns, double),
        (leaf_count // 4, columns, double),
    ]
    given = local + tree
    fetched = [2]
    shapes += [given[i].shape for i in fetched]
    spaces = [pltpu.HBM if i in fetched else pltpu.VMEM for i in range(5)]
    given = [pltpu.with_memory_space_constraint(a, space) for a, space in zip(given, spaces)]
    keep, send, low_paired, high_paired, *moved = pl.pallas_call(
        functools.partial(climb_local_kernel, leaf_count=leaf_count, fetched=fetched),
        out_shape=[pltpu.VMEM(shape, BF16) for shape in shapes],
        in_specs=[any_spec if i in fetched else vmem_spec for i in range(5)],
        out_specs=[vmem_spec] * len(shapes),
        scratch_shapes=[
            pltpu.VMEM((columns, rank), BF16),
            pltpu.SemaphoreType.DMA((5 * leaf_count,)),
        ],
        compiler_params=pltpu.CompilerParams(vmem_limit_bytes=16 * MIB),
        cost_estimate=cost(0.01),
    )(*given)
    for i, array in zip(fetched, moved):
        given[i] = array

    recv = flip(send, "sub", 1)
    recv = passed(recv, 0.8)
    low_other, far_high, token = lax.optimization_barrier((low_other, far_high, mark(send)))
    (pair_matrix,) = vmem_call(pair_matrix_kernel, [(double, wide)], [low, low_other])
    (rows_mine,) = vmem_call(tails_kernel, [(2, high_rows, rank)], [high, far_high])
    rows_rest = [flip(rows_mine, "sub", 4)]
    pair_paired, coeffs = vmem_call(
        functools.partial(level_up_kernel, tier=1),
        [(half, double), (half, rank)],
        [keep, recv, pair_matrix],
        micros=0.05,
        after=[token],
    )

    recv = flip(coeffs, "sub", 2)
    recv, rows_rest = lax.optimization_barrier((recv, rows_rest))
    recv = passed(recv, 10)
    far, token = lax.optimization_barrier((far, mark(coeffs)))
    (top_mine,) = vmem_call(tails_kernel, [(2, top_block, rank)], [quad_top, far])
    top_rest = [flip(top_mine, "sub", 4)]
    far_other = flip(far, "sub", 1)
    (quad_matrix,) = vmem_call(
        quad_matrix_kernel, [(double, wide)], [low, low_other, far, far_other], after=[recv]
    )
    quad_paired, coeffs = vmem_call(
        functools.partial(level_up_kernel, tier=2),
        [(half, double), (half, rank)],
        [coeffs, recv, quad_matrix],
        micros=0.05,
        after=[token],
    )

    recv = flip(coeffs, "sub", 4)
    recv, top_rest = lax.optimization_barrier((recv, top_rest))
    recv = passed(recv, 10)
    rows_rest, coeffs = lax.optimization_barrier((rows_rest, coeffs))
    rows_all, top_all = [rows_mine] + list(rows_rest), [top_mine] + list(top_rest)
    for tier in range(4, sub_depth + 1):
        for blocks_all in (rows_all, top_all):
            count = 1 << tier - 2
            shape = (count,) + blocks_all[0].shape[1:]
            (joined,) = vmem_call(stack_kernel, [shape], blocks_all, limit=8 * MIB)
            blocks_all.append(flip(joined, "sub", 1 << tier - 1))

    def with_other(stacks):
        return [block for stack in stacks for block in (stack, flip(stack, "sub", 1))]

    *high_matrices, = vmem_call(
        functools.partial(high_matrix_kernel, heights=heights),
        [(double, wide)] * len(heights),
        with_other(rows_all),
        limit=8 * MIB,
        micros=0.2,
        after=[recv],
    )
    path = [pair_matrix, pair_paired, quad_matrix, quad_paired]
    for tier, matrix in enumerate(high_matrices, 3):
        if tier > 3:
            recv = flip(coeffs, "sub", 1 << tier - 1)
        paired, coeffs = vmem_call(
            functools.partial(level_up_kernel, tier=tier),
            [(half, double), (half, rank)],
            [coeffs, recv, matrix],
            micros=0.4,
        )
        path += [matrix, paired]

    roots = [flip(coeffs, "root", mask) for mask in range(root_count - 1, 0, -1)]
    roots[0] = passed(roots[0], 0.01)
    roots.append(coeffs)
    roots.reverse()
    (top_matrix,) = vmem_call(
        functools.partial(top_matrix_kernel, devices=sub_count),
        [(top_rows, sub_count * top_width)],
        with_other(top_all),
        limit=8 * MIB,
    )

    keep, send = vmem_call(
        functools.partial(path_down_kernel, roots=root_count),
        [(half, rank)] * 2,
        roots + [top_matrix] + path,
        [pltpu.VMEM((half, root_count * rank), BF16)],
        limit=8 * MIB,
        micros=0.7,
    )
    recv = flip(send, "sub", 1)

    args = [keep, recv, low_paired, high_paired] + given
    out = pl.pallas_call(
        descend_local_kernel,
        out_shape=jax.ShapeDtypeStruct((leaf_count * leaf, columns), F32),
        in_specs=[vmem_spec] * len(args),
        out_specs=any_spec,
        scratch_shapes=[
            pltpu.VMEM((columns, rank), BF16),
            pltpu.VMEM((leaf_count, leaf, columns), F32),
            pltpu.SemaphoreType.DMA((leaf_count,)),
        ],
        compiler_params=pltpu.CompilerParams(vmem_limit_bytes=16 * MIB),
        cost_estimate=cost(3),
    )(*[pltpu.with_memory_space_constraint(a, pltpu.VMEM) for a in args])
    return out[None]


def solution(mesh):
    return jax.shard_map(
        body,
        mesh=mesh,
        in_specs=(
            P("root", "sub", None),
            P("root", "sub", None),
            P("root", "sub", None),
            P("root", "sub", None),
            P("root", "sub", None),
            P("root", "sub", None),
            P("root", "sub", None),
            P("root", "sub"),
        ),
        out_specs=P("root", "sub", None),
        check_vma=False,
    )
```

```python
import functools

import jax
import jax.numpy as jnp
from jax import lax
from jax.experimental import pallas as pl
from jax.experimental.pallas import tpu as pltpu
from jax.sharding import PartitionSpec as P

BF16 = jnp.bfloat16
F32 = jnp.float32
MIB = 1 << 20


def dot(left, right):
    return lax.dot_general(left, right, (((1,), (0,)), ((), ())), preferred_element_type=F32)


def dot_left_t(left, right):
    return lax.dot_general(left, right, (((0,), (0,)), ((), ())), preferred_element_type=F32)


def dot_right_t(left, right):
    return lax.dot_general(left, right, (((1,), (1,)), ((), ())), preferred_element_type=F32)


def cost(micros):
    return pl.CostEstimate(flops=int(micros * 1e9), bytes_accessed=1, transcendentals=0)


def vmem_call(kernel, outs, args, scratch=(), limit=4 * MIB, micros=0.1, after=()):
    count = len(args)
    args = list(args) + list(after)
    return pl.pallas_call(
        lambda *refs: kernel(*refs[:count], *refs[len(args) :]),
        out_shape=[pltpu.VMEM(shape, BF16) for shape in outs],
        in_specs=[pl.BlockSpec(memory_space=pltpu.VMEM)] * len(args),
        out_specs=[pl.BlockSpec(memory_space=pltpu.VMEM)] * len(outs),
        scratch_shapes=list(scratch),
        compiler_params=pltpu.CompilerParams(vmem_limit_bytes=limit),
        cost_estimate=cost(micros),
    )(*[pltpu.with_memory_space_constraint(a, pltpu.VMEM) for a in args])


def copy_kernel(value, out):
    out[...] = value[...]


def passed(value, micros):
    return vmem_call(copy_kernel, [value.shape], [value], micros=micros)[0]


def mark_kernel(value, out):
    out[...] = value[pl.ds(0, out.shape[0]), pl.ds(0, out.shape[1])]


def mark(value):
    return vmem_call(mark_kernel, [(16, 128)], [value], micros=0.02)[0]


def flip(block, axis, mask):
    count = lax.axis_size(axis)
    return lax.ppermute(block, axis, [(i, i ^ mask) for i in range(count)])


def swap_with(source, target, chips):
    partner = [device ^ 1 for device in range(2 * chips)]
    for low, high in ((source, target), (chips - 1 - source, chips - 1 - target)):
        for core in range(2):
            partner[2 * low + core], partner[2 * high + core] = 2 * high + core, 2 * low + core
    return list(enumerate(partner))


def inner_chips(chips):
    return [chip for chip in range(chips) if (chip % 2 == 1) == (chip < chips // 2)]


def swapped(block, source, target, chips):
    return lax.ppermute(block, "sub", swap_with(source, target, chips))


def core_of():
    return lax.axis_index("sub") % 2


def chip_of():
    return lax.axis_index("sub") // 2


def in_lower(chips):
    return chip_of() < chips // 2


def mirrored(chip, chips):
    return jnp.where(in_lower(chips), chip, chips - 1 - chip)


def split_rows(value, first, keep, send, work):
    half = value.shape[0] // 2
    work[...] = value
    keep[...] = work[pl.ds(pl.multiple_of(first * half, half), half), :]
    send[...] = work[pl.ds(pl.multiple_of((1 - first) * half, half), half), :]


def join_rows(mine, other, first, work):
    half = mine.shape[0]
    work[pl.ds(pl.multiple_of(first * half, half), half), :] = mine
    work[pl.ds(pl.multiple_of((1 - first) * half, half), half), :] = other


def join_lanes(mine, other, first, work):
    half = mine.shape[1]
    work[:, pl.ds(pl.multiple_of(first * half, half), half)] = mine
    work[:, pl.ds(pl.multiple_of((1 - first) * half, half), half)] = other


def climb(paired, merge_mat, transfer):
    inner = dot_right_t(paired, merge_mat).astype(BF16)
    return dot(inner, transfer).astype(BF16)


def descend(parent, paired, merge_mat, transfer):
    rest = (paired.astype(F32) - dot_right_t(parent, transfer)).astype(BF16)
    return dot_right_t(rest, merge_mat).astype(BF16)


def pack_kernel(merge, transfer, top, *refs):
    low, quad_top, high, sems = refs
    rows, double = merge.shape
    rank = transfer.shape[1]
    steps = []

    def fetch(source, target):
        steps.append(pltpu.make_async_copy(source, target, sems.at[len(steps)]))

    def level_rows(low, size, target, at):
        for lanes in range(double // rank):
            fetch(
                merge.at[pl.ds(low, size), pl.ds(lanes * rank, rank)], target.at[pl.ds(at, size), :]
            )
            at += size
        fetch(transfer.at[pl.ds(low, size), :], target.at[pl.ds(at, size), :])
        return at + size

    quad_low, high_low = double // 2, double // 2 + double // 4
    level_rows(high_low, rows - high_low, high, 0)
    quad_rows = level_rows(quad_low, high_low - quad_low, quad_top, 0)
    width = top.shape[1]
    size = top.shape[0] * width // rank
    for piece in range(rank // width):
        fetch(
            top.at[pl.ds(piece * size, size), :],
            quad_top.at[pl.ds(quad_rows, size), pl.ds(piece * width, width)],
        )
    pair_rows = level_rows(0, quad_low, low, 0)
    for step in steps:
        step.start()
    for step in steps:
        step.wait()
    low[pl.ds(pair_rows, quad_rows), :] = quad_top[pl.ds(0, quad_rows), :]


def climb_local_kernel(*refs, leaf_count, fetched):
    arrays = list(refs[:5])
    keep, send, low_paired, high_paired = refs[5:9]
    kept = {1: low_paired, 2: high_paired}
    *outs, work, sems = refs[9:]
    leaf = arrays[0].shape[0] // leaf_count
    rank = arrays[2].shape[1]
    double = 2 * rank
    depth = leaf_count.bit_length() - 1
    copies = {}
    for index, out in zip(fetched, outs):
        block = leaf if index < 3 else double
        for i in range(out.shape[0] // block):
            rows = pl.ds(i * block, block)
            copies[index, i] = pltpu.make_async_copy(
                arrays[index].at[rows, :], out.at[rows, :], sems.at[len(copies)]
            )
        arrays[index] = out
    for key in sorted(copies, key=lambda key: (key[0] // 3, key[1])):
        copies[key].start()

    def ready(index, i):
        if (index, i) in copies:
            copies[index, i].wait()

    sides, inverse, basis, merge, transfer = arrays
    products = []
    for i in range(leaf_count):
        rows = pl.ds(i * leaf, leaf)
        for index in range(2):
            ready(index, i)
        products.append(dot(inverse[rows, :], sides[rows, :]).astype(BF16))
    for i in range(leaf_count):
        ready(2, i)
        coeffs = dot_left_t(products[i], basis[pl.ds(i * leaf, leaf), :]).astype(BF16)
        kept[1][i // 2, :, pl.ds((i % 2) * rank, rank)] = coeffs
    for e in range(leaf_count - 1):
        for index in (3, 4):
            ready(index, e)
    for tier in range(1, depth + 1):
        count = leaf_count >> tier
        start = leaf_count - 2 * count
        for e in range(count):
            rows = pl.ds((start + e) * double, double)
            coeffs = climb(kept[tier][e], merge[rows, :], transfer[rows, :])
            if tier < depth:
                kept[tier + 1][e // 2, :, pl.ds((e % 2) * rank, rank)] = coeffs
            else:
                split_rows(coeffs, core_of(), keep, send, work)


def descend_local_kernel(
    mine, other, low_paired, high_paired, sides, inverse, basis, merge, transfer, out, parent, result, sems
):
    leaf = inverse.shape[1]
    rank = basis.shape[1]
    double = 2 * rank
    kept = {1: low_paired, 2: high_paired}
    leaf_count = out.shape[0] // leaf
    depth = leaf_count.bit_length() - 1
    join_rows(mine[...], other[...], core_of(), parent)
    level = [parent[...]]
    for tier in range(depth, 0, -1):
        nodes = leaf_count >> tier
        start = leaf_count - 2 * nodes
        below = []
        for e in range(nodes):
            rows = pl.ds((start + e) * double, double)
            children = descend(level[e], kept[tier][e], merge[rows, :], transfer[rows, :])
            below += [children[:, :rank], children[:, rank:]]
        level = below
    copies = []
    for i in range(leaf_count):
        rows = pl.ds(i * leaf, leaf)
        arrays = (inverse, sides, basis)
        spread = dot_right_t(arrays[2][rows, :], level[i])
        rest = (arrays[1][rows, :].astype(F32) - spread).astype(BF16)
        result[i] = dot(arrays[0][rows, :], rest)
        copies.append(
            pltpu.make_async_copy(result.at[i], out.at[pl.ds(i * leaf, leaf), :], sems.at[i])
        )
        copies[-1].start()
    for copy in copies:
        copy.wait()


def place_rows(block, low, size, out, at):
    width = block.shape[-1]
    for lanes in range(out.shape[1] // width):
        out[pl.ds(at, size), pl.ds(lanes * width, width)] = block[pl.ds(low + lanes * size, size), :]


def pair_matrix_kernel(mine, other, out):
    size = out.shape[0] // 2
    core = core_of()
    place_rows(mine, 0, size, out, pl.multiple_of(core * size, size))
    place_rows(other, 0, size, out, pl.multiple_of((1 - core) * size, size))


def quad_matrix_kernel(mine, other, far, far_other, out):
    size = out.shape[0] // 4
    core, side = core_of(), chip_of() % 2
    start = mine.shape[0] - out.shape[1] // mine.shape[1] * size
    blocks = [(side, core, mine, start), (side, 1 - core, other, start)]
    blocks += [(1 - side, core, far, 0), (1 - side, 1 - core, far_other, 0)]
    for chip, which, ref, low in blocks:
        place_rows(ref, low, size, out, pl.multiple_of((2 * chip + which) * size, size))


def tails_kernel(mine, far, out):
    for i, ref in enumerate((mine, far)):
        out[i] = ref[pl.ds(ref.shape[0] - out.shape[1], out.shape[1]), :]


def extend_kernel(mine, other, out):
    out[pl.ds(0, mine.shape[0]), :] = mine[...]
    out[pl.ds(mine.shape[0], other.shape[0]), :] = other[...]


def stack_kernel(*refs):
    *ins, out = refs
    at = 0
    for ref in ins:
        if len(ref.shape) == 2:
            out[at] = ref[...]
            at += 1
        else:
            out[pl.ds(at, ref.shape[0])] = ref[...]
            at += ref.shape[0]


def device_blocks(refs, chips):
    inner, core = inner_chips(chips), core_of()
    own = inner.index(chips // 2 - 1)
    order = [inner[own]] + inner[:own] + inner[own + 1 :]
    for source, mine, other in zip(order, refs[::2], refs[1::2]):
        for i, chip in enumerate((source, source ^ 1)):
            for which, ref in ((core, mine), (1 - core, other)):
                yield 2 * mirrored(chip, chips) + which, ref.at[i]


def high_matrix_kernel(*refs, chips, heights):
    refs, outs = refs[: -len(heights)], refs[-len(heights) :]
    rows = sum(heights)
    for device, ref in device_blocks(refs, chips):
        offset = 0
        for out, height in zip(outs, heights):
            width = ref.shape[-1]
            for lanes in range(out.shape[1] // width):
                out[
                    pl.ds(pl.multiple_of(device * height, height), height),
                    pl.ds(lanes * width, width),
                ] = ref[pl.ds(lanes * rows + offset, height), :]
            offset += height


def top_matrix_kernel(*refs, chips):
    refs, top = refs[:-1], refs[-1]
    width = top.shape[1] // (2 * chips)
    for device, ref in device_blocks(refs, chips):
        size = top.shape[0] * width // ref.shape[-1]
        for piece in range(ref.shape[-1] // width):
            top[pl.ds(piece * size, size), pl.ds(pl.multiple_of(device * width, width), width)] = ref[
                :, pl.ds(piece * width, width)
            ]


def pair_up_kernel(mine, other, matrix, paired, coeffs):
    double = paired.shape[1]
    join_lanes(mine[...], other[...], core_of(), paired)
    coeffs[...] = climb(
        paired[...], matrix[:, pl.ds(0, double)], matrix[:, pl.ds(double, double // 2)]
    )


def quad_up_kernel(mine, other, matrix, paired, coeffs):
    double = paired.shape[1]
    join_lanes(mine[...], other[...], chip_of() % 2, paired)
    coeffs[...] = climb(
        paired[...], matrix[:, pl.ds(0, double)], matrix[:, pl.ds(double, double // 2)]
    )


def high_up_kernel(*refs, chips, levels):
    quads = chips // 2
    parts, matrices = refs[:quads], refs[quads : quads + levels]
    kept, coeffs = refs[quads + levels : quads + 2 * levels], refs[-1]
    rank = coeffs.shape[1]
    double = 2 * rank
    for i, part in enumerate(parts):
        at = jnp.where(in_lower(chips), i, quads - 1 - i)
        lanes = pl.ds(pl.multiple_of((at % 2) * rank, rank), rank)
        kept[0][at // 2, :, lanes] = part[...]
    for tier in range(levels):
        nodes = quads >> tier + 1
        for e in range(nodes):
            rows = pl.ds(e * double, double)
            matrix = matrices[tier]
            value = climb(
                kept[tier][e], matrix[rows, pl.ds(0, double)], matrix[rows, pl.ds(double, rank)]
            )
            if tier + 1 < levels:
                kept[tier + 1][e // 2, :, pl.ds((e % 2) * rank, rank)] = value
            else:
                coeffs[...] = value


def high_down_kernel(*refs, chips, levels, roots):
    quads = chips // 2
    own, top, refs = refs[:roots], refs[roots], refs[roots + 1 :]
    matrices, kept, outs = refs[:levels], refs[levels : 2 * levels], refs[2 * levels : -2]
    stacked, below = refs[-2:]
    rank = outs[0].shape[1]
    double = 2 * rank
    me = lax.axis_index("root")
    for mask in range(roots):
        at = pl.multiple_of((me ^ mask) * rank, rank)
        stacked[:, pl.ds(at, rank)] = own[mask][...]
    below[0] = dot_right_t(stacked[...], top[...]).astype(BF16)
    for tier in range(levels - 1, 0, -1):
        values = []
        for e in range(quads >> tier + 1):
            rows = pl.ds(e * double, double)
            matrix = matrices[tier]
            children = descend(
                below[e], kept[tier][e], matrix[rows, pl.ds(0, double)], matrix[rows, pl.ds(double, rank)]
            )
            values += [children[:, :rank], children[:, rank:]]
        for e, value in enumerate(values):
            below[e] = value
    for i, out in enumerate(outs):
        at = jnp.where(in_lower(chips), i, quads - 1 - i)
        node = at // 2 if quads > 2 else 0
        start = node * double
        if quads > 2:
            start = pl.multiple_of(start, double)
        lifted = dot_right_t(below[node], matrices[0][pl.ds(start, double), pl.ds(double, rank)])
        rest = (kept[0][node].astype(F32) - lifted).astype(BF16)
        child = pl.multiple_of(start + at % 2 * rank, rank)
        out[...] = dot_right_t(rest, matrices[0][pl.ds(child, rank), pl.ds(0, double)]).astype(BF16)


def choose_kernel(*refs, chips):
    *parts, out = refs
    value = parts[0][...]
    for source, part in zip(inner_chips(chips), parts):
        value = jnp.where(mirrored(chip_of(), chips) == source, part[...], value)
    out[...] = value


def path_down_kernel(
    mine, other, quad_paired, quad_matrix, pair_paired, pair_matrix, keep, send, *, chips
):
    rank = keep.shape[1]
    double = 2 * rank
    inner = (chip_of() % 2 == 1) == in_lower(chips)
    parent = jnp.where(inner, mine[...], other[...])

    def children(paired, matrix, sides):
        lifted = dot_right_t(parent, matrix[:, pl.ds(double, rank)])
        rest = (paired[...].astype(F32) - lifted).astype(BF16)
        for side in sides:
            rows = pl.ds(pl.multiple_of(side * rank, rank), rank)
            yield dot_right_t(rest, matrix[rows, pl.ds(0, double)]).astype(BF16)

    (parent,) = children(quad_paired, quad_matrix, [chip_of() % 2])
    keep[...], send[...] = children(pair_paired, pair_matrix, [core_of(), 1 - core_of()])


def body(
    right_side,
    leaf_inverse,
    leaf_basis,
    local_merge,
    local_transfer,
    upper_merge,
    upper_transfer,
    top_inverse,
):
    leaf = leaf_inverse.shape[2]
    rank = leaf_basis.shape[2]
    columns = right_side.shape[2]
    double = 2 * rank
    wide = double + rank
    leaf_count = right_side.shape[1] // leaf
    sub_count = lax.axis_size("sub")
    sub_depth = sub_count.bit_length() - 1
    root_count = lax.axis_size("root")
    chips = sub_count // 2
    middle = chips // 2 - 1
    half = columns // 2
    heights = [double >> tier for tier in range(3, sub_depth + 1)]
    levels = len(heights)
    quads = chips // 2

    local = [right_side[0], leaf_inverse[0], leaf_basis[0]]
    tree = [local_merge[0], local_transfer[0]]
    blocks = wide // rank
    top_rows, top_width = top_inverse.shape
    quad_rows = blocks * (double // 4)
    top_block = top_rows * top_width // rank
    high_rows = blocks * sum(heights)
    any_spec, vmem_spec = pl.BlockSpec(memory_space=pl.ANY), pl.BlockSpec(memory_space=pltpu.VMEM)
    pair_rows = blocks * (double // 2)
    shapes = [(rows, rank) for rows in (pair_rows + quad_rows, quad_rows + top_block, high_rows)]
    args = [upper_merge[0], upper_transfer[0], top_inverse]
    low, quad_top, high = pl.pallas_call(
        pack_kernel,
        out_shape=[pltpu.VMEM(shape, BF16) for shape in shapes],
        in_specs=[any_spec] * len(args),
        out_specs=[vmem_spec] * len(shapes),
        scratch_shapes=[pltpu.SemaphoreType.DMA((3 * blocks + rank // top_width,))],
        compiler_params=pltpu.CompilerParams(vmem_limit_bytes=2 * MIB),
        cost_estimate=cost(1.5),
    )(*[pltpu.with_memory_space_constraint(a, pltpu.HBM) for a in args])
    far_high = flip(high, "sub", 2)
    far = flip(quad_top, "sub", 2)
    low_other = flip(low, "sub", 1)

    shapes = [
        (half, rank),
        (half, rank),
        (leaf_count // 2, columns, double),
        (leaf_count // 4, columns, double),
    ]
    given = local + tree
    fetched = [2]
    shapes += [given[i].shape for i in fetched]
    spaces = [pltpu.HBM if i in fetched else pltpu.VMEM for i in range(5)]
    given = [pltpu.with_memory_space_constraint(a, space) for a, space in zip(given, spaces)]
    keep, send, low_paired, high_paired, *moved = pl.pallas_call(
        functools.partial(climb_local_kernel, leaf_count=leaf_count, fetched=fetched),
        out_shape=[pltpu.VMEM(shape, BF16) for shape in shapes],
        in_specs=[any_spec if i in fetched else vmem_spec for i in range(5)],
        out_specs=[vmem_spec] * len(shapes),
        scratch_shapes=[
            pltpu.VMEM((columns, rank), BF16),
            pltpu.SemaphoreType.DMA((5 * leaf_count,)),
        ],
        compiler_params=pltpu.CompilerParams(vmem_limit_bytes=16 * MIB),
        cost_estimate=cost(0.01),
    )(*given)
    for i, array in zip(fetched, moved):
        given[i] = array

    recv = flip(send, "sub", 1)
    recv = passed(recv, 0.8)
    low_other, far_high, token = lax.optimization_barrier((low_other, far_high, mark(send)))
    (pair_matrix,) = vmem_call(pair_matrix_kernel, [(double, wide)], [low, low_other])
    (rows_mine,) = vmem_call(tails_kernel, [(2, high_rows, rank)], [high, far_high])
    inner = inner_chips(chips)
    others = [s for s in inner if s != middle]
    rows_rest = [swapped(rows_mine, s, middle, chips) for s in others]
    pair_paired, coeffs = vmem_call(
        pair_up_kernel,
        [(half, double), (half, rank)],
        [keep, recv, pair_matrix],
        micros=0.05,
        after=[token],
    )

    recv = flip(coeffs, "sub", 2)
    recv, rows_rest = lax.optimization_barrier((recv, rows_rest))
    recv = passed(recv, 10)
    far, token = lax.optimization_barrier((far, mark(coeffs)))
    (top_mine,) = vmem_call(tails_kernel, [(2, top_block, rank)], [quad_top, far])
    top_rest = [swapped(top_mine, s, middle, chips) for s in others]
    far_other = flip(far, "sub", 1)
    (quad_matrix,) = vmem_call(
        quad_matrix_kernel, [(double, wide)], [low, low_other, far, far_other], after=[recv]
    )
    quad_paired, coeffs = vmem_call(
        quad_up_kernel,
        [(half, double), (half, rank)],
        [coeffs, recv, quad_matrix],
        micros=0.05,
        after=[token],
    )

    own = inner.index(middle)
    parts = [swapped(coeffs, s, middle, chips) for s in others]
    parts, top_rest = lax.optimization_barrier((parts, top_rest))
    parts = [passed(part, 10) for part in parts]
    rows_rest, coeffs = lax.optimization_barrier((rows_rest, coeffs))
    stacks = [rows_mine, flip(rows_mine, "sub", 1)]
    for item in rows_rest:
        stacks += [item, flip(item, "sub", 1)]
    *high_matrices, = vmem_call(
        functools.partial(high_matrix_kernel, chips=chips, heights=heights),
        [(sub_count * height, wide) for height in heights],
        stacks,
        limit=8 * MIB,
        micros=0.2,
        after=parts,
    )
    *high_paired_up, coeffs = vmem_call(
        functools.partial(high_up_kernel, chips=chips, levels=levels),
        [(quads >> t + 1, half, double) for t in range(levels)] + [(half, rank)],
        parts[:own] + [coeffs] + parts[own:] + high_matrices,
        limit=8 * MIB,
        micros=0.4,
    )

    roots = [flip(coeffs, "root", mask) for mask in range(root_count - 1, 0, -1)]
    roots[0] = passed(roots[0], 0.01)
    roots.append(coeffs)
    roots.reverse()
    stacks = [top_mine, flip(top_mine, "sub", 1)]
    for item in top_rest:
        stacks += [item, flip(item, "sub", 1)]
    (top_matrix,) = vmem_call(
        functools.partial(top_matrix_kernel, chips=chips),
        [(top_rows, sub_count * top_width)],
        stacks,
        limit=8 * MIB,
    )
    values = vmem_call(
        functools.partial(high_down_kernel, chips=chips, levels=levels, roots=root_count),
        [(half, rank)] * (quads // 2),
        roots + [top_matrix] + high_matrices + high_paired_up,
        [
            pltpu.VMEM((half, root_count * rank), BF16),
            pltpu.VMEM((max(quads // 2, 1), half, rank), BF16),
        ],
        limit=8 * MIB,
        micros=0.7,
    )

    value = values[0]
    if len(values) > 1:
        parts = [
            part if s == middle else swapped(part, s, middle, chips)
            for s, part in zip(inner, values)
        ]
        (value,) = vmem_call(
            functools.partial(choose_kernel, chips=chips), [(half, rank)], parts
        )
    recv = flip(value, "sub", 2)
    keep, send = vmem_call(
        functools.partial(path_down_kernel, chips=chips),
        [(half, rank), (half, rank)],
        [value, recv, quad_paired, quad_matrix, pair_paired, pair_matrix],
        micros=0.4,
    )
    recv = flip(send, "sub", 1)

    args = [keep, recv, low_paired, high_paired] + given
    out = pl.pallas_call(
        descend_local_kernel,
        out_shape=jax.ShapeDtypeStruct((leaf_count * leaf, columns), F32),
        in_specs=[vmem_spec] * len(args),
        out_specs=any_spec,
        scratch_shapes=[
            pltpu.VMEM((columns, rank), BF16),
            pltpu.VMEM((leaf_count, leaf, columns), F32),
            pltpu.SemaphoreType.DMA((leaf_count,)),
        ],
        compiler_params=pltpu.CompilerParams(vmem_limit_bytes=16 * MIB),
        cost_estimate=cost(3),
    )(*[pltpu.with_memory_space_constraint(a, pltpu.VMEM) for a in args])
    return out[None]


def solution(mesh):
    return jax.shard_map(
        body,
        mesh=mesh,
        in_specs=(
            P("root", "sub", None),
            P("root", "sub", None),
            P("root", "sub", None),
            P("root", "sub", None),
            P("root", "sub", None),
            P("root", "sub", None),
            P("root", "sub", None),
            P("root", "sub"),
        ),
        out_specs=P("root", "sub", None),
        check_vma=False,
    )
```

```python
import functools

import jax
import jax.numpy as jnp
from jax import lax
from jax.experimental import pallas as pl
from jax.experimental.pallas import tpu as pltpu
from jax.sharding import PartitionSpec as P

BF16 = jnp.bfloat16
F32 = jnp.float32
MIB = 1 << 20


def dot(left, right):
    return lax.dot_general(left, right, (((1,), (0,)), ((), ())), preferred_element_type=F32)


def dot_left_t(left, right):
    return lax.dot_general(left, right, (((0,), (0,)), ((), ())), preferred_element_type=F32)


def dot_right_t(left, right):
    return lax.dot_general(left, right, (((1,), (1,)), ((), ())), preferred_element_type=F32)


def cost(micros):
    return pl.CostEstimate(flops=int(micros * 1e9), bytes_accessed=1, transcendentals=0)


def vmem_call(kernel, outs, args, scratch=(), limit=4 * MIB, micros=0.1, after=(), kind=BF16):
    count = len(args)
    args = list(args) + list(after)
    return pl.pallas_call(
        lambda *refs: kernel(*refs[:count], *refs[len(args) :]),
        out_shape=[pltpu.VMEM(shape, kind) for shape in outs],
        in_specs=[pl.BlockSpec(memory_space=pltpu.VMEM)] * len(args),
        out_specs=[pl.BlockSpec(memory_space=pltpu.VMEM)] * len(outs),
        scratch_shapes=list(scratch),
        compiler_params=pltpu.CompilerParams(vmem_limit_bytes=limit),
        cost_estimate=cost(micros),
    )(*[pltpu.with_memory_space_constraint(a, pltpu.VMEM) for a in args])


def copy_kernel(value, out):
    out[...] = value[...]


def passed(value, micros):
    return vmem_call(copy_kernel, [value.shape], [value], micros=micros)[0]


def mark_kernel(value, out):
    out[...] = value[pl.ds(0, out.shape[0]), pl.ds(0, out.shape[1])]


def mark(value):
    return vmem_call(mark_kernel, [(16, 128)], [value], micros=0.02)[0]


def flip(block, axis, mask):
    count = lax.axis_size(axis)
    return lax.ppermute(block, axis, [(i, i ^ mask) for i in range(count)])


def swap_with(source, target, chips):
    partner = [device ^ 1 for device in range(2 * chips)]
    for low, high in ((source, target), (chips - 1 - source, chips - 1 - target)):
        for core in range(2):
            partner[2 * low + core], partner[2 * high + core] = 2 * high + core, 2 * low + core
    return list(enumerate(partner))


def inner_chips(chips):
    return [chip for chip in range(chips) if (chip % 2 == 1) == (chip < chips // 2)]


def swapped(block, source, target, chips):
    return lax.ppermute(block, "sub", swap_with(source, target, chips))


def core_of():
    return lax.axis_index("sub") % 2


def chip_of():
    return lax.axis_index("sub") // 2


def in_lower(chips):
    return chip_of() < chips // 2


def mirrored(chip, chips):
    return jnp.where(in_lower(chips), chip, chips - 1 - chip)


def split_rows(value, first, keep, send, work):
    half = value.shape[0] // 2
    work[...] = value
    keep[...] = work[pl.ds(pl.multiple_of(first * half, half), half), :]
    send[...] = work[pl.ds(pl.multiple_of((1 - first) * half, half), half), :]


def join_rows(mine, other, first, work):
    half = mine.shape[0]
    work[pl.ds(pl.multiple_of(first * half, half), half), :] = mine
    work[pl.ds(pl.multiple_of((1 - first) * half, half), half), :] = other


def join_lanes(mine, other, first, work):
    half = mine.shape[1]
    work[:, pl.ds(pl.multiple_of(first * half, half), half)] = mine
    work[:, pl.ds(pl.multiple_of((1 - first) * half, half), half)] = other


def climb(paired, merge_mat, transfer):
    inner = dot_right_t(paired, merge_mat).astype(BF16)
    return dot(inner, transfer).astype(BF16)


def descend(parent, paired, merge_mat, transfer):
    rest = (paired.astype(F32) - dot_right_t(parent, transfer)).astype(BF16)
    return dot_right_t(rest, merge_mat).astype(BF16)


def pack_kernel(merge, transfer, top, *refs):
    low, quad_top, high, sems = refs
    rows, double = merge.shape
    rank = transfer.shape[1]
    steps = []

    def fetch(source, target):
        steps.append(pltpu.make_async_copy(source, target, sems.at[len(steps)]))

    def level_rows(low, size, target, at):
        for lanes in range(double // rank):
            fetch(
                merge.at[pl.ds(low, size), pl.ds(lanes * rank, rank)], target.at[pl.ds(at, size), :]
            )
            at += size
        fetch(transfer.at[pl.ds(low, size), :], target.at[pl.ds(at, size), :])
        return at + size

    quad_low, high_low = double // 2, double // 2 + double // 4
    level_rows(high_low, rows - high_low, high, 0)
    quad_rows = level_rows(quad_low, high_low - quad_low, quad_top, 0)
    width = top.shape[1]
    size = top.shape[0] * width // rank
    for piece in range(rank // width):
        fetch(
            top.at[pl.ds(piece * size, size), :],
            quad_top.at[pl.ds(quad_rows, size), pl.ds(piece * width, width)],
        )
    pair_rows = level_rows(0, quad_low, low, 0)
    for step in steps:
        step.start()
    for step in steps:
        step.wait()
    low[pl.ds(pair_rows, quad_rows), :] = quad_top[pl.ds(0, quad_rows), :]


def climb_local_kernel(*refs, leaf_count, fetched):
    arrays = list(refs[:5])
    keep, send, low_paired, high_paired = refs[5:9]
    kept = {1: low_paired, 2: high_paired}
    *outs, work, sems = refs[9:]
    leaf = arrays[0].shape[0] // leaf_count
    rank = arrays[2].shape[1]
    double = 2 * rank
    depth = leaf_count.bit_length() - 1
    copies = {}
    for index, out in zip(fetched, outs):
        block = leaf if index < 3 else double
        for i in range(out.shape[0] // block):
            rows = pl.ds(i * block, block)
            copies[index, i] = pltpu.make_async_copy(
                arrays[index].at[rows, :], out.at[rows, :], sems.at[len(copies)]
            )
        arrays[index] = out
    for key in sorted(copies, key=lambda key: (key[0] // 3, key[1])):
        copies[key].start()

    def ready(index, i):
        if (index, i) in copies:
            copies[index, i].wait()

    sides, inverse, basis, merge, transfer = arrays
    products = []
    for i in range(leaf_count):
        rows = pl.ds(i * leaf, leaf)
        for index in range(2):
            ready(index, i)
        products.append(dot(inverse[rows, :], sides[rows, :]).astype(BF16))
    for i in range(leaf_count):
        ready(2, i)
        coeffs = dot_left_t(products[i], basis[pl.ds(i * leaf, leaf), :]).astype(BF16)
        kept[1][i // 2, :, pl.ds((i % 2) * rank, rank)] = coeffs
    for e in range(leaf_count - 1):
        for index in (3, 4):
            ready(index, e)
    for tier in range(1, depth + 1):
        count = leaf_count >> tier
        start = leaf_count - 2 * count
        for e in range(count):
            rows = pl.ds((start + e) * double, double)
            coeffs = climb(kept[tier][e], merge[rows, :], transfer[rows, :])
            if tier < depth:
                kept[tier + 1][e // 2, :, pl.ds((e % 2) * rank, rank)] = coeffs
            else:
                split_rows(coeffs, core_of(), keep, send, work)


def descend_local_kernel(
    mine, other, low_paired, high_paired, sides, inverse, basis, merge, transfer, out, parent, result, sems
):
    leaf = inverse.shape[1]
    rank = basis.shape[1]
    double = 2 * rank
    kept = {1: low_paired, 2: high_paired}
    leaf_count = out.shape[0] // leaf
    depth = leaf_count.bit_length() - 1
    join_rows(mine[...], other[...], core_of(), parent)
    level = [parent[...]]
    for tier in range(depth, 0, -1):
        nodes = leaf_count >> tier
        start = leaf_count - 2 * nodes
        below = []
        for e in range(nodes):
            rows = pl.ds((start + e) * double, double)
            children = descend(level[e], kept[tier][e], merge[rows, :], transfer[rows, :])
            below += [children[:, :rank], children[:, rank:]]
        level = below
    copies = []
    for i in range(leaf_count):
        rows = pl.ds(i * leaf, leaf)
        arrays = (inverse, sides, basis)
        spread = dot_right_t(arrays[2][rows, :], level[i])
        rest = (arrays[1][rows, :].astype(F32) - spread).astype(BF16)
        result[i] = dot(arrays[0][rows, :], rest)
        copies.append(
            pltpu.make_async_copy(result.at[i], out.at[pl.ds(i * leaf, leaf), :], sems.at[i])
        )
        copies[-1].start()
    for copy in copies:
        copy.wait()


def place_rows(block, low, size, out, at):
    width = block.shape[-1]
    for lanes in range(out.shape[1] // width):
        out[pl.ds(at, size), pl.ds(lanes * width, width)] = block[pl.ds(low + lanes * size, size), :]


def pair_matrix_kernel(mine, other, out):
    size = out.shape[0] // 2
    core = core_of()
    place_rows(mine, 0, size, out, pl.multiple_of(core * size, size))
    place_rows(other, 0, size, out, pl.multiple_of((1 - core) * size, size))


def quad_matrix_kernel(mine, other, far, far_other, out):
    size = out.shape[0] // 4
    core, side = core_of(), chip_of() % 2
    start = mine.shape[0] - out.shape[1] // mine.shape[1] * size
    blocks = [(side, core, mine, start), (side, 1 - core, other, start)]
    blocks += [(1 - side, core, far, 0), (1 - side, 1 - core, far_other, 0)]
    for chip, which, ref, low in blocks:
        place_rows(ref, low, size, out, pl.multiple_of((2 * chip + which) * size, size))


def tails_kernel(mine, far, out):
    for i, ref in enumerate((mine, far)):
        out[i] = ref[pl.ds(ref.shape[0] - out.shape[1], out.shape[1]), :]


def extend_kernel(mine, other, out):
    out[pl.ds(0, mine.shape[0]), :] = mine[...]
    out[pl.ds(mine.shape[0], other.shape[0]), :] = other[...]


def stack_kernel(*refs):
    *ins, out = refs
    at = 0
    for ref in ins:
        if len(ref.shape) == 2:
            out[at] = ref[...]
            at += 1
        else:
            out[pl.ds(at, ref.shape[0])] = ref[...]
            at += ref.shape[0]


def device_blocks(refs, chips):
    inner, core = inner_chips(chips), core_of()
    own = inner.index(chips // 2 - 1)
    order = [inner[own]] + inner[:own] + inner[own + 1 :]
    for source, mine, other in zip(order, refs[::2], refs[1::2]):
        for i, chip in enumerate((source, source ^ 1)):
            for which, ref in ((core, mine), (1 - core, other)):
                yield 2 * mirrored(chip, chips) + which, ref.at[i]


def high_matrix_kernel(*refs, chips, heights):
    refs, outs = refs[: -len(heights)], refs[-len(heights) :]
    rows = sum(heights)
    for device, ref in device_blocks(refs, chips):
        offset = 0
        for out, height in zip(outs, heights):
            width = ref.shape[-1]
            for lanes in range(out.shape[1] // width):
                out[
                    pl.ds(pl.multiple_of(device * height, height), height),
                    pl.ds(lanes * width, width),
                ] = ref[pl.ds(lanes * rows + offset, height), :]
            offset += height


def top_matrix_kernel(*refs, chips):
    refs, top = refs[:-1], refs[-1]
    width = top.shape[1] // (2 * chips)
    for device, ref in device_blocks(refs, chips):
        size = top.shape[0] * width // ref.shape[-1]
        for piece in range(ref.shape[-1] // width):
            top[pl.ds(piece * size, size), pl.ds(pl.multiple_of(device * width, width), width)] = ref[
                :, pl.ds(piece * width, width)
            ]


def pair_up_kernel(mine, other, matrix, paired, coeffs):
    double = paired.shape[1]
    join_lanes(mine[...], other[...], core_of(), paired)
    coeffs[...] = climb(
        paired[...], matrix[:, pl.ds(0, double)], matrix[:, pl.ds(double, double // 2)]
    )


def quad_up_kernel(mine, other, matrix, paired, coeffs):
    double = paired.shape[1]
    join_lanes(mine[...], other[...], chip_of() % 2, paired)
    coeffs[...] = climb(
        paired[...], matrix[:, pl.ds(0, double)], matrix[:, pl.ds(double, double // 2)]
    )


def high_up_kernel(*refs, chips, levels):
    quads = chips // 2
    parts, matrices = refs[:quads], refs[quads : quads + levels]
    kept, coeffs = refs[quads + levels : quads + 2 * levels], refs[-1]
    rank = coeffs.shape[1]
    double = 2 * rank
    for i, part in enumerate(parts):
        at = jnp.where(in_lower(chips), i, quads - 1 - i)
        lanes = pl.ds(pl.multiple_of((at % 2) * rank, rank), rank)
        kept[0][at // 2, :, lanes] = part[...]
    for tier in range(levels):
        nodes = quads >> tier + 1
        for e in range(nodes):
            rows = pl.ds(e * double, double)
            matrix = matrices[tier]
            value = climb(
                kept[tier][e], matrix[rows, pl.ds(0, double)], matrix[rows, pl.ds(double, rank)]
            )
            if tier + 1 < levels:
                kept[tier + 1][e // 2, :, pl.ds((e % 2) * rank, rank)] = value
            else:
                coeffs[...] = value


def top_term(block, top, mask):
    rank = block.shape[1]
    at = pl.multiple_of((lax.axis_index("root") ^ mask) * rank, rank)
    return dot_right_t(block[...], top[:, pl.ds(at, rank)])


def first_terms_kernel(own, block, top, sums, *, mask):
    sums[...] = top_term(own, top, 0) + top_term(block, top, mask)


def add_term_kernel(before, block, top, sums, *, mask):
    sums[...] = before[...] + top_term(block, top, mask)


def high_down_kernel(*refs, chips, levels):
    quads = chips // 2
    sums, block, top, refs = refs[0], refs[1], refs[2], refs[3:]
    matrices, kept, outs = refs[:levels], refs[levels : 2 * levels], refs[2 * levels : -1]
    below = refs[-1]
    rank = outs[0].shape[1]
    double = 2 * rank
    below[0] = (sums[...] + top_term(block, top, 1)).astype(BF16)
    for tier in range(levels - 1, 0, -1):
        values = []
        for e in range(quads >> tier + 1):
            rows = pl.ds(e * double, double)
            matrix = matrices[tier]
            children = descend(
                below[e], kept[tier][e], matrix[rows, pl.ds(0, double)], matrix[rows, pl.ds(double, rank)]
            )
            values += [children[:, :rank], children[:, rank:]]
        for e, value in enumerate(values):
            below[e] = value
    for i, out in enumerate(outs):
        at = jnp.where(in_lower(chips), i, quads - 1 - i)
        node = at // 2 if quads > 2 else 0
        start = node * double
        if quads > 2:
            start = pl.multiple_of(start, double)
        lifted = dot_right_t(below[node], matrices[0][pl.ds(start, double), pl.ds(double, rank)])
        rest = (kept[0][node].astype(F32) - lifted).astype(BF16)
        child = pl.multiple_of(start + at % 2 * rank, rank)
        out[...] = dot_right_t(rest, matrices[0][pl.ds(child, rank), pl.ds(0, double)]).astype(BF16)


def choose_kernel(*refs, chips):
    *parts, out = refs
    value = parts[0][...]
    for source, part in zip(inner_chips(chips), parts):
        value = jnp.where(mirrored(chip_of(), chips) == source, part[...], value)
    out[...] = value


def path_down_kernel(
    mine, other, quad_paired, quad_matrix, pair_paired, pair_matrix, keep, send, *, chips
):
    rank = keep.shape[1]
    double = 2 * rank
    inner = (chip_of() % 2 == 1) == in_lower(chips)
    parent = jnp.where(inner, mine[...], other[...])

    def children(paired, matrix, sides):
        lifted = dot_right_t(parent, matrix[:, pl.ds(double, rank)])
        rest = (paired[...].astype(F32) - lifted).astype(BF16)
        for side in sides:
            rows = pl.ds(pl.multiple_of(side * rank, rank), rank)
            yield dot_right_t(rest, matrix[rows, pl.ds(0, double)]).astype(BF16)

    (parent,) = children(quad_paired, quad_matrix, [chip_of() % 2])
    keep[...], send[...] = children(pair_paired, pair_matrix, [core_of(), 1 - core_of()])


def body(
    right_side,
    leaf_inverse,
    leaf_basis,
    local_merge,
    local_transfer,
    upper_merge,
    upper_transfer,
    top_inverse,
):
    leaf = leaf_inverse.shape[2]
    rank = leaf_basis.shape[2]
    columns = right_side.shape[2]
    double = 2 * rank
    wide = double + rank
    leaf_count = right_side.shape[1] // leaf
    sub_count = lax.axis_size("sub")
    sub_depth = sub_count.bit_length() - 1
    root_count = lax.axis_size("root")
    chips = sub_count // 2
    middle = chips // 2 - 1
    half = columns // 2
    heights = [double >> tier for tier in range(3, sub_depth + 1)]
    levels = len(heights)
    quads = chips // 2

    local = [right_side[0], leaf_inverse[0], leaf_basis[0]]
    tree = [local_merge[0], local_transfer[0]]
    blocks = wide // rank
    top_rows, top_width = top_inverse.shape
    quad_rows = blocks * (double // 4)
    top_block = top_rows * top_width // rank
    high_rows = blocks * sum(heights)
    any_spec, vmem_spec = pl.BlockSpec(memory_space=pl.ANY), pl.BlockSpec(memory_space=pltpu.VMEM)
    pair_rows = blocks * (double // 2)
    shapes = [(rows, rank) for rows in (pair_rows + quad_rows, quad_rows + top_block, high_rows)]
    args = [upper_merge[0], upper_transfer[0], top_inverse]
    low, quad_top, high = pl.pallas_call(
        pack_kernel,
        out_shape=[pltpu.VMEM(shape, BF16) for shape in shapes],
        in_specs=[any_spec] * len(args),
        out_specs=[vmem_spec] * len(shapes),
        scratch_shapes=[pltpu.SemaphoreType.DMA((3 * blocks + rank // top_width,))],
        compiler_params=pltpu.CompilerParams(vmem_limit_bytes=2 * MIB),
        cost_estimate=cost(1.5),
    )(*[pltpu.with_memory_space_constraint(a, pltpu.HBM) for a in args])
    far_high = flip(high, "sub", 2)
    far = flip(quad_top, "sub", 2)
    low_other = flip(low, "sub", 1)

    shapes = [
        (half, rank),
        (half, rank),
        (leaf_count // 2, columns, double),
        (leaf_count // 4, columns, double),
    ]
    given = local + tree
    fetched = [2]
    shapes += [given[i].shape for i in fetched]
    spaces = [pltpu.HBM if i in fetched else pltpu.VMEM for i in range(5)]
    given = [pltpu.with_memory_space_constraint(a, space) for a, space in zip(given, spaces)]
    keep, send, low_paired, high_paired, *moved = pl.pallas_call(
        functools.partial(climb_local_kernel, leaf_count=leaf_count, fetched=fetched),
        out_shape=[pltpu.VMEM(shape, BF16) for shape in shapes],
        in_specs=[any_spec if i in fetched else vmem_spec for i in range(5)],
        out_specs=[vmem_spec] * len(shapes),
        scratch_shapes=[
            pltpu.VMEM((columns, rank), BF16),
            pltpu.SemaphoreType.DMA((5 * leaf_count,)),
        ],
        compiler_params=pltpu.CompilerParams(vmem_limit_bytes=16 * MIB),
        cost_estimate=cost(0.01),
    )(*given)
    for i, array in zip(fetched, moved):
        given[i] = array

    recv = flip(send, "sub", 1)
    recv = passed(recv, 0.8)
    low_other, far_high, token = lax.optimization_barrier((low_other, far_high, mark(send)))
    (pair_matrix,) = vmem_call(pair_matrix_kernel, [(double, wide)], [low, low_other])
    (rows_mine,) = vmem_call(tails_kernel, [(2, high_rows, rank)], [high, far_high])
    inner = inner_chips(chips)
    others = [s for s in inner if s != middle]
    rows_rest = [swapped(rows_mine, s, middle, chips) for s in others]
    pair_paired, coeffs = vmem_call(
        pair_up_kernel,
        [(half, double), (half, rank)],
        [keep, recv, pair_matrix],
        micros=0.05,
        after=[token],
    )

    recv = flip(coeffs, "sub", 2)
    recv, rows_rest = lax.optimization_barrier((recv, rows_rest))
    recv = passed(recv, 10)
    far, token = lax.optimization_barrier((far, mark(coeffs)))
    (top_mine,) = vmem_call(tails_kernel, [(2, top_block, rank)], [quad_top, far])
    top_rest = [swapped(top_mine, s, middle, chips) for s in others]
    far_other = flip(far, "sub", 1)
    (quad_matrix,) = vmem_call(
        quad_matrix_kernel, [(double, wide)], [low, low_other, far, far_other], after=[recv]
    )
    quad_paired, coeffs = vmem_call(
        quad_up_kernel,
        [(half, double), (half, rank)],
        [coeffs, recv, quad_matrix],
        micros=0.05,
        after=[token],
    )

    own = inner.index(middle)
    parts = [swapped(coeffs, s, middle, chips) for s in others]
    parts, top_rest = lax.optimization_barrier((parts, top_rest))
    parts = [passed(part, 10) for part in parts]
    rows_rest, coeffs = lax.optimization_barrier((rows_rest, coeffs))
    stacks = [rows_mine, flip(rows_mine, "sub", 1)]
    for item in rows_rest:
        stacks += [item, flip(item, "sub", 1)]
    *high_matrices, = vmem_call(
        functools.partial(high_matrix_kernel, chips=chips, heights=heights),
        [(sub_count * height, wide) for height in heights],
        stacks,
        limit=8 * MIB,
        micros=0.2,
        after=parts,
    )
    *high_paired_up, coeffs = vmem_call(
        functools.partial(high_up_kernel, chips=chips, levels=levels),
        [(quads >> t + 1, half, double) for t in range(levels)] + [(half, rank)],
        parts[:own] + [coeffs] + parts[own:] + high_matrices,
        limit=8 * MIB,
        micros=0.4,
    )

    stacks = [top_mine, flip(top_mine, "sub", 1)]
    for item in top_rest:
        stacks += [item, flip(item, "sub", 1)]
    (top_matrix,) = vmem_call(
        functools.partial(top_matrix_kernel, chips=chips),
        [(top_rows, sub_count * top_width)],
        stacks,
        limit=8 * MIB,
    )
    came = [(mask, flip(coeffs, "root", mask)) for mask in range(root_count - 1, 0, -1)]
    kernel, sums = first_terms_kernel, coeffs
    if root_count == 2:
        came.insert(0, (1, jnp.zeros_like(coeffs)))
    for mask, block in came[:-1]:
        (sums,) = vmem_call(
            functools.partial(kernel, mask=mask),
            [(half, rank)],
            [sums, block, top_matrix],
            micros=0.01,
            kind=F32,
        )
        kernel = add_term_kernel
    values = vmem_call(
        functools.partial(high_down_kernel, chips=chips, levels=levels),
        [(half, rank)] * (quads // 2),
        [sums, came[-1][1], top_matrix] + high_matrices + high_paired_up,
        [pltpu.VMEM((max(quads // 2, 1), half, rank), BF16)],
        limit=8 * MIB,
        micros=0.7,
    )

    value = values[0]
    if len(values) > 1:
        parts = [
            part if s == middle else swapped(part, s, middle, chips)
            for s, part in zip(inner, values)
        ]
        (value,) = vmem_call(
            functools.partial(choose_kernel, chips=chips), [(half, rank)], parts
        )
    recv = flip(value, "sub", 2)
    keep, send = vmem_call(
        functools.partial(path_down_kernel, chips=chips),
        [(half, rank), (half, rank)],
        [value, recv, quad_paired, quad_matrix, pair_paired, pair_matrix],
        micros=0.4,
    )
    recv = flip(send, "sub", 1)

    args = [keep, recv, low_paired, high_paired] + given
    out = pl.pallas_call(
        descend_local_kernel,
        out_shape=jax.ShapeDtypeStruct((leaf_count * leaf, columns), F32),
        in_specs=[vmem_spec] * len(args),
        out_specs=any_spec,
        scratch_shapes=[
            pltpu.VMEM((columns, rank), BF16),
            pltpu.VMEM((leaf_count, leaf, columns), F32),
            pltpu.SemaphoreType.DMA((leaf_count,)),
        ],
        compiler_params=pltpu.CompilerParams(vmem_limit_bytes=16 * MIB),
        cost_estimate=cost(3),
    )(*[pltpu.with_memory_space_constraint(a, pltpu.VMEM) for a in args])
    return out[None]


def solution(mesh):
    return jax.shard_map(
        body,
        mesh=mesh,
        in_specs=(
            P("root", "sub", None),
            P("root", "sub", None),
            P("root", "sub", None),
            P("root", "sub", None),
            P("root", "sub", None),
            P("root", "sub", None),
            P("root", "sub", None),
            P("root", "sub"),
        ),
        out_specs=P("root", "sub", None),
        check_vma=False,
    )
```

```python
import functools

import jax
import jax.numpy as jnp
from jax import lax
from jax.experimental import pallas as pl
from jax.experimental.pallas import tpu as pltpu
from jax.sharding import PartitionSpec as P

BF16 = jnp.bfloat16
F32 = jnp.float32
MIB = 1 << 20


def dot(left, right):
    return lax.dot_general(left, right, (((1,), (0,)), ((), ())), preferred_element_type=F32)


def dot_left_t(left, right):
    return lax.dot_general(left, right, (((0,), (0,)), ((), ())), preferred_element_type=F32)


def dot_right_t(left, right):
    return lax.dot_general(left, right, (((1,), (1,)), ((), ())), preferred_element_type=F32)


def cost(micros):
    return pl.CostEstimate(flops=int(micros * 1e9), bytes_accessed=1, transcendentals=0)


def vmem_call(kernel, outs, args, scratch=(), limit=4 * MIB, micros=0.1, after=(), kind=BF16):
    count = len(args)
    args = list(args) + list(after)
    return pl.pallas_call(
        lambda *refs: kernel(*refs[:count], *refs[len(args) :]),
        out_shape=[pltpu.VMEM(shape, kind) for shape in outs],
        in_specs=[pl.BlockSpec(memory_space=pltpu.VMEM)] * len(args),
        out_specs=[pl.BlockSpec(memory_space=pltpu.VMEM)] * len(outs),
        scratch_shapes=list(scratch),
        compiler_params=pltpu.CompilerParams(vmem_limit_bytes=limit),
        cost_estimate=cost(micros),
    )(*[pltpu.with_memory_space_constraint(a, pltpu.VMEM) for a in args])


def copy_kernel(value, out):
    out[...] = value[...]


def passed(value, micros):
    return vmem_call(copy_kernel, [value.shape], [value], micros=micros)[0]


def mark_kernel(value, out):
    out[...] = value[pl.ds(0, out.shape[0]), pl.ds(0, out.shape[1])]


def mark(value):
    return vmem_call(mark_kernel, [(16, 128)], [value], micros=0.02)[0]


def flip(block, axis, mask):
    count = lax.axis_size(axis)
    return lax.ppermute(block, axis, [(i, i ^ mask) for i in range(count)])


def swap_with(source, target, chips):
    partner = [device ^ 1 for device in range(2 * chips)]
    for low, high in ((source, target), (chips - 1 - source, chips - 1 - target)):
        for core in range(2):
            partner[2 * low + core], partner[2 * high + core] = 2 * high + core, 2 * low + core
    return list(enumerate(partner))


def inner_chips(chips):
    return [chip for chip in range(chips) if (chip % 2 == 1) == (chip < chips // 2)]


def swapped(block, source, target, chips):
    return lax.ppermute(block, "sub", swap_with(source, target, chips))


def core_of():
    return lax.axis_index("sub") % 2


def chip_of():
    return lax.axis_index("sub") // 2


def in_lower(chips):
    return chip_of() < chips // 2


def mirrored(chip, chips):
    return jnp.where(in_lower(chips), chip, chips - 1 - chip)


def split_rows(value, first, keep, send, work):
    half = value.shape[0] // 2
    work[...] = value
    keep[...] = work[pl.ds(pl.multiple_of(first * half, half), half), :]
    send[...] = work[pl.ds(pl.multiple_of((1 - first) * half, half), half), :]


def join_rows(mine, other, first, work):
    half = mine.shape[0]
    work[pl.ds(pl.multiple_of(first * half, half), half), :] = mine
    work[pl.ds(pl.multiple_of((1 - first) * half, half), half), :] = other


def join_lanes(mine, other, first, work):
    half = mine.shape[1]
    work[:, pl.ds(pl.multiple_of(first * half, half), half)] = mine
    work[:, pl.ds(pl.multiple_of((1 - first) * half, half), half)] = other


def climb(paired, merge_mat, transfer):
    inner = dot_right_t(paired, merge_mat).astype(BF16)
    return dot(inner, transfer).astype(BF16)


def descend(parent, paired, merge_mat, transfer):
    rest = (paired.astype(F32) - dot_right_t(parent, transfer)).astype(BF16)
    return dot_right_t(rest, merge_mat).astype(BF16)


def pack_kernel(merge, transfer, top, *refs):
    low, quad_top, high, sems = refs
    rows, double = merge.shape
    rank = transfer.shape[1]
    steps = []

    def fetch(source, target):
        steps.append(pltpu.make_async_copy(source, target, sems.at[len(steps)]))

    def level_rows(low, size, target, at):
        for lanes in range(double // rank):
            fetch(
                merge.at[pl.ds(low, size), pl.ds(lanes * rank, rank)], target.at[pl.ds(at, size), :]
            )
            at += size
        fetch(transfer.at[pl.ds(low, size), :], target.at[pl.ds(at, size), :])
        return at + size

    quad_low, high_low = double // 2, double // 2 + double // 4
    level_rows(high_low, rows - high_low, high, 0)
    quad_rows = level_rows(quad_low, high_low - quad_low, quad_top, 0)
    width = top.shape[1]
    size = top.shape[0] * width // rank
    for piece in range(rank // width):
        fetch(
            top.at[pl.ds(piece * size, size), :],
            quad_top.at[pl.ds(quad_rows, size), pl.ds(piece * width, width)],
        )
    pair_rows = level_rows(0, quad_low, low, 0)
    for step in steps:
        step.start()
    for step in steps:
        step.wait()
    low[pl.ds(pair_rows, quad_rows), :] = quad_top[pl.ds(0, quad_rows), :]


def climb_local_kernel(*refs, leaf_count, fetched):
    arrays = list(refs[:5])
    keep, send, low_paired, high_paired = refs[5:9]
    kept = {1: low_paired, 2: high_paired}
    *outs, work, sems = refs[9:]
    leaf = arrays[0].shape[0] // leaf_count
    rank = arrays[2].shape[1]
    double = 2 * rank
    depth = leaf_count.bit_length() - 1
    copies = {}
    for index, out in zip(fetched, outs):
        block = leaf if index < 3 else double
        for i in range(out.shape[0] // block):
            rows = pl.ds(i * block, block)
            copies[index, i] = pltpu.make_async_copy(
                arrays[index].at[rows, :], out.at[rows, :], sems.at[len(copies)]
            )
        arrays[index] = out
    for key in sorted(copies, key=lambda key: (key[0] // 3, key[1])):
        copies[key].start()

    def ready(index, i):
        if (index, i) in copies:
            copies[index, i].wait()

    sides, inverse, basis, merge, transfer = arrays
    products = []
    for i in range(leaf_count):
        rows = pl.ds(i * leaf, leaf)
        for index in range(2):
            ready(index, i)
        products.append(dot(inverse[rows, :], sides[rows, :]).astype(BF16))
    for i in range(leaf_count):
        ready(2, i)
        coeffs = dot_left_t(products[i], basis[pl.ds(i * leaf, leaf), :]).astype(BF16)
        kept[1][i // 2, :, pl.ds((i % 2) * rank, rank)] = coeffs
    for e in range(leaf_count - 1):
        for index in (3, 4):
            ready(index, e)
    for tier in range(1, depth + 1):
        count = leaf_count >> tier
        start = leaf_count - 2 * count
        for e in range(count):
            rows = pl.ds((start + e) * double, double)
            coeffs = climb(kept[tier][e], merge[rows, :], transfer[rows, :])
            if tier < depth:
                kept[tier + 1][e // 2, :, pl.ds((e % 2) * rank, rank)] = coeffs
            else:
                split_rows(coeffs, core_of(), keep, send, work)


def descend_local_kernel(
    mine, other, low_paired, high_paired, sides, inverse, basis, merge, transfer, out, parent, result, sems
):
    leaf = inverse.shape[1]
    rank = basis.shape[1]
    double = 2 * rank
    kept = {1: low_paired, 2: high_paired}
    leaf_count = out.shape[0] // leaf
    depth = leaf_count.bit_length() - 1
    join_rows(mine[...], other[...], core_of(), parent)
    level = [parent[...]]
    for tier in range(depth, 0, -1):
        nodes = leaf_count >> tier
        start = leaf_count - 2 * nodes
        below = []
        for e in range(nodes):
            rows = pl.ds((start + e) * double, double)
            children = descend(level[e], kept[tier][e], merge[rows, :], transfer[rows, :])
            below += [children[:, :rank], children[:, rank:]]
        level = below
    rests = []
    for i in range(leaf_count):
        rows = pl.ds(i * leaf, leaf)
        spread = dot_right_t(basis[rows, :], level[i])
        rests.append((sides[rows, :].astype(F32) - spread).astype(BF16))
    copies = []
    for i in range(leaf_count):
        rows = pl.ds(i * leaf, leaf)
        result[i] = dot(inverse[rows, :], rests[i])
        copies.append(pltpu.make_async_copy(result.at[i], out.at[rows, :], sems.at[i]))
        copies[-1].start()
    for copy in copies:
        copy.wait()


def place_rows(block, low, size, out, at):
    width = block.shape[-1]
    for lanes in range(out.shape[1] // width):
        out[pl.ds(at, size), pl.ds(lanes * width, width)] = block[pl.ds(low + lanes * size, size), :]


def pair_matrix_kernel(mine, other, out):
    size = out.shape[0] // 2
    core = core_of()
    place_rows(mine, 0, size, out, pl.multiple_of(core * size, size))
    place_rows(other, 0, size, out, pl.multiple_of((1 - core) * size, size))


def quad_matrix_kernel(mine, other, far, far_other, out):
    size = out.shape[0] // 4
    core, side = core_of(), chip_of() % 2
    start = mine.shape[0] - out.shape[1] // mine.shape[1] * size
    blocks = [(side, core, mine, start), (side, 1 - core, other, start)]
    blocks += [(1 - side, core, far, 0), (1 - side, 1 - core, far_other, 0)]
    for chip, which, ref, low in blocks:
        place_rows(ref, low, size, out, pl.multiple_of((2 * chip + which) * size, size))


def tails_kernel(mine, far, out):
    for i, ref in enumerate((mine, far)):
        out[i] = ref[pl.ds(ref.shape[0] - out.shape[1], out.shape[1]), :]


def extend_kernel(mine, other, out):
    out[pl.ds(0, mine.shape[0]), :] = mine[...]
    out[pl.ds(mine.shape[0], other.shape[0]), :] = other[...]


def stack_kernel(*refs):
    *ins, out = refs
    at = 0
    for ref in ins:
        if len(ref.shape) == 2:
            out[at] = ref[...]
            at += 1
        else:
            out[pl.ds(at, ref.shape[0])] = ref[...]
            at += ref.shape[0]


def device_blocks(refs, chips):
    inner, core = inner_chips(chips), core_of()
    own = inner.index(chips // 2 - 1)
    order = [inner[own]] + inner[:own] + inner[own + 1 :]
    for source, mine, other in zip(order, refs[::2], refs[1::2]):
        for i, chip in enumerate((source, source ^ 1)):
            for which, ref in ((core, mine), (1 - core, other)):
                yield 2 * mirrored(chip, chips) + which, ref.at[i]


def high_matrix_kernel(*refs, chips, heights):
    refs, outs = refs[: -len(heights)], refs[-len(heights) :]
    rows = sum(heights)
    for device, ref in device_blocks(refs, chips):
        offset = 0
        for out, height in zip(outs, heights):
            width = ref.shape[-1]
            for lanes in range(out.shape[1] // width):
                out[
                    pl.ds(pl.multiple_of(device * height, height), height),
                    pl.ds(lanes * width, width),
                ] = ref[pl.ds(lanes * rows + offset, height), :]
            offset += height


def top_matrix_kernel(*refs, chips):
    refs, top = refs[:-1], refs[-1]
    width = top.shape[1] // (2 * chips)
    for device, ref in device_blocks(refs, chips):
        size = top.shape[0] * width // ref.shape[-1]
        for piece in range(ref.shape[-1] // width):
            top[pl.ds(piece * size, size), pl.ds(pl.multiple_of(device * width, width), width)] = ref[
                :, pl.ds(piece * width, width)
            ]


def pair_up_kernel(mine, other, matrix, paired, coeffs):
    double = paired.shape[1]
    join_lanes(mine[...], other[...], core_of(), paired)
    coeffs[...] = climb(
        paired[...], matrix[:, pl.ds(0, double)], matrix[:, pl.ds(double, double // 2)]
    )


def quad_up_kernel(mine, other, matrix, paired, coeffs):
    double = paired.shape[1]
    join_lanes(mine[...], other[...], chip_of() % 2, paired)
    coeffs[...] = climb(
        paired[...], matrix[:, pl.ds(0, double)], matrix[:, pl.ds(double, double // 2)]
    )


def high_up_kernel(*refs, chips, levels):
    quads = chips // 2
    parts, matrices = refs[:quads], refs[quads : quads + levels]
    kept, coeffs = refs[quads + levels : quads + 2 * levels], refs[-1]
    rank = coeffs.shape[1]
    double = 2 * rank
    for i, part in enumerate(parts):
        at = jnp.where(in_lower(chips), i, quads - 1 - i)
        lanes = pl.ds(pl.multiple_of((at % 2) * rank, rank), rank)
        kept[0][at // 2, :, lanes] = part[...]
    for tier in range(levels):
        nodes = quads >> tier + 1
        for e in range(nodes):
            rows = pl.ds(e * double, double)
            matrix = matrices[tier]
            value = climb(
                kept[tier][e], matrix[rows, pl.ds(0, double)], matrix[rows, pl.ds(double, rank)]
            )
            if tier + 1 < levels:
                kept[tier + 1][e // 2, :, pl.ds((e % 2) * rank, rank)] = value
            else:
                coeffs[...] = value


def top_term(block, top, mask):
    rank = block.shape[1]
    at = pl.multiple_of((lax.axis_index("root") ^ mask) * rank, rank)
    return dot_right_t(block[...], top[:, pl.ds(at, rank)])


def first_terms_kernel(own, block, top, sums, *, mask):
    sums[...] = top_term(own, top, 0) + top_term(block, top, mask)


def add_term_kernel(before, block, top, sums, *, mask):
    sums[...] = before[...] + top_term(block, top, mask)


def high_down_kernel(*refs, chips, levels):
    quads = chips // 2
    sums, block, top, refs = refs[0], refs[1], refs[2], refs[3:]
    matrices, kept, outs = refs[:levels], refs[levels : 2 * levels], refs[2 * levels : -1]
    below = refs[-1]
    rank = outs[0].shape[1]
    double = 2 * rank
    below[0] = (sums[...] + top_term(block, top, 1)).astype(BF16)
    for tier in range(levels - 1, 0, -1):
        values = []
        for e in range(quads >> tier + 1):
            rows = pl.ds(e * double, double)
            matrix = matrices[tier]
            children = descend(
                below[e], kept[tier][e], matrix[rows, pl.ds(0, double)], matrix[rows, pl.ds(double, rank)]
            )
            values += [children[:, :rank], children[:, rank:]]
        for e, value in enumerate(values):
            below[e] = value
    for i, out in enumerate(outs):
        at = jnp.where(in_lower(chips), i, quads - 1 - i)
        node = at // 2 if quads > 2 else 0
        start = node * double
        if quads > 2:
            start = pl.multiple_of(start, double)
        lifted = dot_right_t(below[node], matrices[0][pl.ds(start, double), pl.ds(double, rank)])
        rest = (kept[0][node].astype(F32) - lifted).astype(BF16)
        child = pl.multiple_of(start + at % 2 * rank, rank)
        out[...] = dot_right_t(rest, matrices[0][pl.ds(child, rank), pl.ds(0, double)]).astype(BF16)


def choose_kernel(*refs, chips):
    *parts, out = refs
    value = parts[0][...]
    for source, part in zip(inner_chips(chips), parts):
        value = jnp.where(mirrored(chip_of(), chips) == source, part[...], value)
    out[...] = value


def path_down_kernel(
    mine, other, quad_paired, quad_matrix, pair_paired, pair_matrix, keep, send, *, chips
):
    rank = keep.shape[1]
    double = 2 * rank
    inner = (chip_of() % 2 == 1) == in_lower(chips)
    parent = jnp.where(inner, mine[...], other[...])

    def children(paired, matrix, sides):
        lifted = dot_right_t(parent, matrix[:, pl.ds(double, rank)])
        rest = (paired[...].astype(F32) - lifted).astype(BF16)
        for side in sides:
            rows = pl.ds(pl.multiple_of(side * rank, rank), rank)
            yield dot_right_t(rest, matrix[rows, pl.ds(0, double)]).astype(BF16)

    (parent,) = children(quad_paired, quad_matrix, [chip_of() % 2])
    keep[...], send[...] = children(pair_paired, pair_matrix, [core_of(), 1 - core_of()])


def body(
    right_side,
    leaf_inverse,
    leaf_basis,
    local_merge,
    local_transfer,
    upper_merge,
    upper_transfer,
    top_inverse,
):
    leaf = leaf_inverse.shape[2]
    rank = leaf_basis.shape[2]
    columns = right_side.shape[2]
    double = 2 * rank
    wide = double + rank
    leaf_count = right_side.shape[1] // leaf
    sub_count = lax.axis_size("sub")
    sub_depth = sub_count.bit_length() - 1
    root_count = lax.axis_size("root")
    chips = sub_count // 2
    middle = chips // 2 - 1
    half = columns // 2
    heights = [double >> tier for tier in range(3, sub_depth + 1)]
    levels = len(heights)
    quads = chips // 2

    local = [right_side[0], leaf_inverse[0], leaf_basis[0]]
    tree = [local_merge[0], local_transfer[0]]
    blocks = wide // rank
    top_rows, top_width = top_inverse.shape
    quad_rows = blocks * (double // 4)
    top_block = top_rows * top_width // rank
    high_rows = blocks * sum(heights)
    any_spec, vmem_spec = pl.BlockSpec(memory_space=pl.ANY), pl.BlockSpec(memory_space=pltpu.VMEM)
    pair_rows = blocks * (double // 2)
    shapes = [(rows, rank) for rows in (pair_rows + quad_rows, quad_rows + top_block, high_rows)]
    args = [upper_merge[0], upper_transfer[0], top_inverse]
    low, quad_top, high = pl.pallas_call(
        pack_kernel,
        out_shape=[pltpu.VMEM(shape, BF16) for shape in shapes],
        in_specs=[any_spec] * len(args),
        out_specs=[vmem_spec] * len(shapes),
        scratch_shapes=[pltpu.SemaphoreType.DMA((3 * blocks + rank // top_width,))],
        compiler_params=pltpu.CompilerParams(vmem_limit_bytes=2 * MIB),
        cost_estimate=cost(1.5),
    )(*[pltpu.with_memory_space_constraint(a, pltpu.HBM) for a in args])
    far_high = flip(high, "sub", 2)
    far = flip(quad_top, "sub", 2)
    low_other = flip(low, "sub", 1)

    shapes = [
        (half, rank),
        (half, rank),
        (leaf_count // 2, columns, double),
        (leaf_count // 4, columns, double),
    ]
    given = local + tree
    fetched = [2]
    shapes += [given[i].shape for i in fetched]
    spaces = [pltpu.HBM if i in fetched else pltpu.VMEM for i in range(5)]
    given = [pltpu.with_memory_space_constraint(a, space) for a, space in zip(given, spaces)]
    keep, send, low_paired, high_paired, *moved = pl.pallas_call(
        functools.partial(climb_local_kernel, leaf_count=leaf_count, fetched=fetched),
        out_shape=[pltpu.VMEM(shape, BF16) for shape in shapes],
        in_specs=[any_spec if i in fetched else vmem_spec for i in range(5)],
        out_specs=[vmem_spec] * len(shapes),
        scratch_shapes=[
            pltpu.VMEM((columns, rank), BF16),
            pltpu.SemaphoreType.DMA((5 * leaf_count,)),
        ],
        compiler_params=pltpu.CompilerParams(vmem_limit_bytes=16 * MIB),
        cost_estimate=cost(0.01),
    )(*given)
    for i, array in zip(fetched, moved):
        given[i] = array

    recv = flip(send, "sub", 1)
    recv = passed(recv, 0.8)
    low_other, far_high, token = lax.optimization_barrier((low_other, far_high, mark(send)))
    (pair_matrix,) = vmem_call(pair_matrix_kernel, [(double, wide)], [low, low_other])
    (rows_mine,) = vmem_call(tails_kernel, [(2, high_rows, rank)], [high, far_high])
    inner = inner_chips(chips)
    others = [s for s in inner if s != middle]
    rows_rest = [swapped(rows_mine, s, middle, chips) for s in others]
    pair_paired, coeffs = vmem_call(
        pair_up_kernel,
        [(half, double), (half, rank)],
        [keep, recv, pair_matrix],
        micros=0.05,
        after=[token],
    )

    recv = flip(coeffs, "sub", 2)
    recv, rows_rest = lax.optimization_barrier((recv, rows_rest))
    recv = passed(recv, 10)
    far, token = lax.optimization_barrier((far, mark(coeffs)))
    (top_mine,) = vmem_call(tails_kernel, [(2, top_block, rank)], [quad_top, far])
    top_rest = [swapped(top_mine, s, middle, chips) for s in others]
    far_other = flip(far, "sub", 1)
    (quad_matrix,) = vmem_call(
        quad_matrix_kernel, [(double, wide)], [low, low_other, far, far_other], after=[recv]
    )
    quad_paired, coeffs = vmem_call(
        quad_up_kernel,
        [(half, double), (half, rank)],
        [coeffs, recv, quad_matrix],
        micros=0.05,
        after=[token],
    )

    own = inner.index(middle)
    parts = [swapped(coeffs, s, middle, chips) for s in others]
    parts, top_rest = lax.optimization_barrier((parts, top_rest))
    parts = [passed(part, 10) for part in parts]
    rows_rest, coeffs = lax.optimization_barrier((rows_rest, coeffs))
    stacks = [rows_mine, flip(rows_mine, "sub", 1)]
    for item in rows_rest:
        stacks += [item, flip(item, "sub", 1)]
    *high_matrices, = vmem_call(
        functools.partial(high_matrix_kernel, chips=chips, heights=heights),
        [(sub_count * height, wide) for height in heights],
        stacks,
        limit=8 * MIB,
        micros=0.2,
        after=parts,
    )
    *high_paired_up, coeffs = vmem_call(
        functools.partial(high_up_kernel, chips=chips, levels=levels),
        [(quads >> t + 1, half, double) for t in range(levels)] + [(half, rank)],
        parts[:own] + [coeffs] + parts[own:] + high_matrices,
        limit=8 * MIB,
        micros=0.4,
    )

    stacks = [top_mine, flip(top_mine, "sub", 1)]
    for item in top_rest:
        stacks += [item, flip(item, "sub", 1)]
    (top_matrix,) = vmem_call(
        functools.partial(top_matrix_kernel, chips=chips),
        [(top_rows, sub_count * top_width)],
        stacks,
        limit=8 * MIB,
    )
    came = [(mask, flip(coeffs, "root", mask)) for mask in range(root_count - 1, 0, -1)]
    kernel, sums = first_terms_kernel, coeffs
    if root_count == 2:
        came.insert(0, (1, jnp.zeros_like(coeffs)))
    for mask, block in came[:-1]:
        (sums,) = vmem_call(
            functools.partial(kernel, mask=mask),
            [(half, rank)],
            [sums, block, top_matrix],
            micros=0.01,
            kind=F32,
        )
        kernel = add_term_kernel
    values = vmem_call(
        functools.partial(high_down_kernel, chips=chips, levels=levels),
        [(half, rank)] * (quads // 2),
        [sums, came[-1][1], top_matrix] + high_matrices + high_paired_up,
        [pltpu.VMEM((max(quads // 2, 1), half, rank), BF16)],
        limit=8 * MIB,
        micros=0.7,
    )

    value = values[0]
    if len(values) > 1:
        parts = [
            part if s == middle else swapped(part, s, middle, chips)
            for s, part in zip(inner, values)
        ]
        (value,) = vmem_call(
            functools.partial(choose_kernel, chips=chips), [(half, rank)], parts
        )
    recv = flip(value, "sub", 2)
    keep, send = vmem_call(
        functools.partial(path_down_kernel, chips=chips),
        [(half, rank), (half, rank)],
        [value, recv, quad_paired, quad_matrix, pair_paired, pair_matrix],
        micros=0.4,
    )
    recv = flip(send, "sub", 1)

    args = [keep, recv, low_paired, high_paired] + given
    out = pl.pallas_call(
        descend_local_kernel,
        out_shape=jax.ShapeDtypeStruct((leaf_count * leaf, columns), F32),
        in_specs=[vmem_spec] * len(args),
        out_specs=any_spec,
        scratch_shapes=[
            pltpu.VMEM((columns, rank), BF16),
            pltpu.VMEM((leaf_count, leaf, columns), F32),
            pltpu.SemaphoreType.DMA((leaf_count,)),
        ],
        compiler_params=pltpu.CompilerParams(vmem_limit_bytes=16 * MIB),
        cost_estimate=cost(3),
    )(*[pltpu.with_memory_space_constraint(a, pltpu.VMEM) for a in args])
    return out[None]


def solution(mesh):
    return jax.shard_map(
        body,
        mesh=mesh,
        in_specs=(
            P("root", "sub", None),
            P("root", "sub", None),
            P("root", "sub", None),
            P("root", "sub", None),
            P("root", "sub", None),
            P("root", "sub", None),
            P("root", "sub", None),
            P("root", "sub"),
        ),
        out_specs=P("root", "sub", None),
        check_vma=False,
    )
```

```python
import functools

import jax
import jax.numpy as jnp
from jax import lax
from jax.experimental import pallas as pl
from jax.experimental.pallas import tpu as pltpu
from jax.sharding import PartitionSpec as P

BF16 = jnp.bfloat16
F32 = jnp.float32
MIB = 1 << 20


def dot(left, right):
    return lax.dot_general(left, right, (((1,), (0,)), ((), ())), preferred_element_type=F32)


def dot_left_t(left, right):
    return lax.dot_general(left, right, (((0,), (0,)), ((), ())), preferred_element_type=F32)


def dot_right_t(left, right):
    return lax.dot_general(left, right, (((1,), (1,)), ((), ())), preferred_element_type=F32)


def cost(micros):
    return pl.CostEstimate(flops=int(micros * 1e9), bytes_accessed=1, transcendentals=0)


def vmem_call(kernel, outs, args, scratch=(), limit=4 * MIB, micros=0.1, after=(), kind=BF16):
    count = len(args)
    args = list(args) + list(after)
    return pl.pallas_call(
        lambda *refs: kernel(*refs[:count], *refs[len(args) :]),
        out_shape=[pltpu.VMEM(shape, kind) for shape in outs],
        in_specs=[pl.BlockSpec(memory_space=pltpu.VMEM)] * len(args),
        out_specs=[pl.BlockSpec(memory_space=pltpu.VMEM)] * len(outs),
        scratch_shapes=list(scratch),
        compiler_params=pltpu.CompilerParams(vmem_limit_bytes=limit),
        cost_estimate=cost(micros),
    )(*[pltpu.with_memory_space_constraint(a, pltpu.VMEM) for a in args])


def copy_kernel(value, out):
    out[...] = value[...]


def passed(value, micros):
    return vmem_call(copy_kernel, [value.shape], [value], micros=micros)[0]


def mark_kernel(value, out):
    out[...] = value[pl.ds(0, out.shape[0]), pl.ds(0, out.shape[1])]


def mark(value):
    return vmem_call(mark_kernel, [(16, 128)], [value], micros=0.02)[0]


def flip(block, axis, mask):
    count = lax.axis_size(axis)
    return lax.ppermute(block, axis, [(i, i ^ mask) for i in range(count)])


def swap_with(source, target, chips):
    partner = [device ^ 1 for device in range(2 * chips)]
    for low, high in ((source, target), (chips - 1 - source, chips - 1 - target)):
        for core in range(2):
            partner[2 * low + core], partner[2 * high + core] = 2 * high + core, 2 * low + core
    return list(enumerate(partner))


def inner_chips(chips):
    return [chip for chip in range(chips) if (chip % 2 == 1) == (chip < chips // 2)]


def swapped(block, source, target, chips):
    return lax.ppermute(block, "sub", swap_with(source, target, chips))


def core_of():
    return lax.axis_index("sub") % 2


def chip_of():
    return lax.axis_index("sub") // 2


def in_lower(chips):
    return chip_of() < chips // 2


def mirrored(chip, chips):
    return jnp.where(in_lower(chips), chip, chips - 1 - chip)


def split_rows(value, first, keep, send, work):
    half = value.shape[0] // 2
    work[...] = value
    keep[...] = work[pl.ds(pl.multiple_of(first * half, half), half), :]
    send[...] = work[pl.ds(pl.multiple_of((1 - first) * half, half), half), :]


def join_rows(mine, other, first, work):
    half = mine.shape[0]
    work[pl.ds(pl.multiple_of(first * half, half), half), :] = mine
    work[pl.ds(pl.multiple_of((1 - first) * half, half), half), :] = other


def join_lanes(mine, other, first, work):
    half = mine.shape[1]
    work[:, pl.ds(pl.multiple_of(first * half, half), half)] = mine
    work[:, pl.ds(pl.multiple_of((1 - first) * half, half), half)] = other


def climb(paired, merge_mat, transfer):
    inner = dot_right_t(paired, merge_mat).astype(BF16)
    return dot(inner, transfer).astype(BF16)


def descend(parent, paired, merge_mat, transfer):
    rest = (paired.astype(F32) - dot_right_t(parent, transfer)).astype(BF16)
    return dot_right_t(rest, merge_mat).astype(BF16)


def pack_kernel(merge, transfer, top, *refs):
    low, quad_top, high, sems = refs
    rows, double = merge.shape
    rank = transfer.shape[1]
    steps = []

    def fetch(source, target):
        steps.append(pltpu.make_async_copy(source, target, sems.at[len(steps)]))

    def level_rows(low, size, target, at):
        for lanes in range(double // rank):
            fetch(
                merge.at[pl.ds(low, size), pl.ds(lanes * rank, rank)], target.at[pl.ds(at, size), :]
            )
            at += size
        fetch(transfer.at[pl.ds(low, size), :], target.at[pl.ds(at, size), :])
        return at + size

    quad_low, high_low = double // 2, double // 2 + double // 4
    level_rows(high_low, rows - high_low, high, 0)
    quad_rows = level_rows(quad_low, high_low - quad_low, quad_top, 0)
    width = top.shape[1]
    size = top.shape[0] * width // rank
    for piece in range(rank // width):
        fetch(
            top.at[pl.ds(piece * size, size), :],
            quad_top.at[pl.ds(quad_rows, size), pl.ds(piece * width, width)],
        )
    pair_rows = level_rows(0, quad_low, low, 0)
    for step in steps:
        step.start()
    for step in steps:
        step.wait()
    low[pl.ds(pair_rows, quad_rows), :] = quad_top[pl.ds(0, quad_rows), :]


def climb_local_kernel(*refs, leaf_count, fetched):
    arrays = list(refs[:5])
    keep, send, low_paired, high_paired = refs[5:9]
    kept = {1: low_paired, 2: high_paired}
    *outs, work, sems = refs[9:]
    leaf = arrays[0].shape[0] // leaf_count
    rank = arrays[2].shape[1]
    double = 2 * rank
    depth = leaf_count.bit_length() - 1
    copies = {}
    for index, out in zip(fetched, outs):
        block = leaf if index < 3 else double
        for i in range(out.shape[0] // block):
            rows = pl.ds(i * block, block)
            copies[index, i] = pltpu.make_async_copy(
                arrays[index].at[rows, :], out.at[rows, :], sems.at[len(copies)]
            )
        arrays[index] = out
    for key in sorted(copies, key=lambda key: (key[0] // 3, key[1])):
        copies[key].start()

    def ready(index, i):
        if (index, i) in copies:
            copies[index, i].wait()

    sides, inverse, basis, merge, transfer = arrays
    products = []
    for i in range(leaf_count):
        rows = pl.ds(i * leaf, leaf)
        for index in range(2):
            ready(index, i)
        products.append(dot(inverse[rows, :], sides[rows, :]).astype(BF16))
    for i in range(leaf_count):
        ready(2, i)
        coeffs = dot_left_t(products[i], basis[pl.ds(i * leaf, leaf), :]).astype(BF16)
        kept[1][i // 2, :, pl.ds((i % 2) * rank, rank)] = coeffs
    for e in range(leaf_count - 1):
        for index in (3, 4):
            ready(index, e)
    for tier in range(1, depth + 1):
        count = leaf_count >> tier
        start = leaf_count - 2 * count
        for e in range(count):
            rows = pl.ds((start + e) * double, double)
            coeffs = climb(kept[tier][e], merge[rows, :], transfer[rows, :])
            if tier < depth:
                kept[tier + 1][e // 2, :, pl.ds((e % 2) * rank, rank)] = coeffs
            else:
                split_rows(coeffs, core_of(), keep, send, work)


def descend_local_kernel(
    mine, other, low_paired, high_paired, sides, inverse, basis, merge, transfer, out, parent, result, sems
):
    leaf = inverse.shape[1]
    rank = basis.shape[1]
    double = 2 * rank
    kept = {1: low_paired, 2: high_paired}
    leaf_count = out.shape[0] // leaf
    depth = leaf_count.bit_length() - 1
    join_rows(mine[...], other[...], core_of(), parent)
    level = [parent[...]]
    for tier in range(depth, 0, -1):
        nodes = leaf_count >> tier
        start = leaf_count - 2 * nodes
        below = []
        for e in range(nodes):
            rows = pl.ds((start + e) * double, double)
            children = descend(level[e], kept[tier][e], merge[rows, :], transfer[rows, :])
            below += [children[:, :rank], children[:, rank:]]
        level = below
    rests = []
    for i in range(leaf_count):
        rows = pl.ds(i * leaf, leaf)
        spread = dot_right_t(basis[rows, :], level[i])
        rests.append((sides[rows, :].astype(F32) - spread).astype(BF16))
    copies = []
    for i in range(leaf_count):
        parts = 2 if i == leaf_count - 1 else 1
        size = leaf // parts
        for part in range(parts):
            rows, place = pl.ds(i * leaf + part * size, size), pl.ds(part * size, size)
            result[i, place, :] = dot(inverse[rows, :], rests[i])
            copies.append(
                pltpu.make_async_copy(
                    result.at[i, place, :], out.at[rows, :], sems.at[len(copies)]
                )
            )
            copies[-1].start()
    for copy in copies:
        copy.wait()


def place_rows(block, low, size, out, at):
    width = block.shape[-1]
    for lanes in range(out.shape[1] // width):
        out[pl.ds(at, size), pl.ds(lanes * width, width)] = block[pl.ds(low + lanes * size, size), :]


def pair_matrix_kernel(mine, other, out):
    size = out.shape[0] // 2
    core = core_of()
    place_rows(mine, 0, size, out, pl.multiple_of(core * size, size))
    place_rows(other, 0, size, out, pl.multiple_of((1 - core) * size, size))


def quad_matrix_kernel(mine, other, far, far_other, out):
    size = out.shape[0] // 4
    core, side = core_of(), chip_of() % 2
    start = mine.shape[0] - out.shape[1] // mine.shape[1] * size
    blocks = [(side, core, mine, start), (side, 1 - core, other, start)]
    blocks += [(1 - side, core, far, 0), (1 - side, 1 - core, far_other, 0)]
    for chip, which, ref, low in blocks:
        place_rows(ref, low, size, out, pl.multiple_of((2 * chip + which) * size, size))


def tails_kernel(mine, far, out):
    for i, ref in enumerate((mine, far)):
        out[i] = ref[pl.ds(ref.shape[0] - out.shape[1], out.shape[1]), :]


def extend_kernel(mine, other, out):
    out[pl.ds(0, mine.shape[0]), :] = mine[...]
    out[pl.ds(mine.shape[0], other.shape[0]), :] = other[...]


def stack_kernel(*refs):
    *ins, out = refs
    at = 0
    for ref in ins:
        if len(ref.shape) == 2:
            out[at] = ref[...]
            at += 1
        else:
            out[pl.ds(at, ref.shape[0])] = ref[...]
            at += ref.shape[0]


def device_blocks(refs, chips):
    inner, core = inner_chips(chips), core_of()
    own = inner.index(chips // 2 - 1)
    order = [inner[own]] + inner[:own] + inner[own + 1 :]
    for source, mine, other in zip(order, refs[::2], refs[1::2]):
        for i, chip in enumerate((source, source ^ 1)):
            for which, ref in ((core, mine), (1 - core, other)):
                yield 2 * mirrored(chip, chips) + which, ref.at[i]


def high_matrix_kernel(*refs, chips, heights):
    refs, outs = refs[: -len(heights)], refs[-len(heights) :]
    rows = sum(heights)
    for device, ref in device_blocks(refs, chips):
        offset = 0
        for out, height in zip(outs, heights):
            width = ref.shape[-1]
            for lanes in range(out.shape[1] // width):
                out[
                    pl.ds(pl.multiple_of(device * height, height), height),
                    pl.ds(lanes * width, width),
                ] = ref[pl.ds(lanes * rows + offset, height), :]
            offset += height


def top_matrix_kernel(*refs, chips):
    refs, top = refs[:-1], refs[-1]
    width = top.shape[1] // (2 * chips)
    for device, ref in device_blocks(refs, chips):
        size = top.shape[0] * width // ref.shape[-1]
        for piece in range(ref.shape[-1] // width):
            top[pl.ds(piece * size, size), pl.ds(pl.multiple_of(device * width, width), width)] = ref[
                :, pl.ds(piece * width, width)
            ]


def pair_up_kernel(mine, other, matrix, paired, coeffs):
    double = paired.shape[1]
    join_lanes(mine[...], other[...], core_of(), paired)
    coeffs[...] = climb(
        paired[...], matrix[:, pl.ds(0, double)], matrix[:, pl.ds(double, double // 2)]
    )


def quad_up_kernel(mine, other, matrix, paired, coeffs):
    double = paired.shape[1]
    join_lanes(mine[...], other[...], chip_of() % 2, paired)
    coeffs[...] = climb(
        paired[...], matrix[:, pl.ds(0, double)], matrix[:, pl.ds(double, double // 2)]
    )


def high_up_kernel(*refs, chips, levels):
    quads = chips // 2
    parts, matrices = refs[:quads], refs[quads : quads + levels]
    kept, coeffs = refs[quads + levels : quads + 2 * levels], refs[-1]
    rank = coeffs.shape[1]
    double = 2 * rank
    for i, part in enumerate(parts):
        at = jnp.where(in_lower(chips), i, quads - 1 - i)
        lanes = pl.ds(pl.multiple_of((at % 2) * rank, rank), rank)
        kept[0][at // 2, :, lanes] = part[...]
    for tier in range(levels):
        nodes = quads >> tier + 1
        for e in range(nodes):
            rows = pl.ds(e * double, double)
            matrix = matrices[tier]
            value = climb(
                kept[tier][e], matrix[rows, pl.ds(0, double)], matrix[rows, pl.ds(double, rank)]
            )
            if tier + 1 < levels:
                kept[tier + 1][e // 2, :, pl.ds((e % 2) * rank, rank)] = value
            else:
                coeffs[...] = value


def top_term(block, top, mask):
    rank = block.shape[1]
    at = pl.multiple_of((lax.axis_index("root") ^ mask) * rank, rank)
    return dot_right_t(block[...], top[:, pl.ds(at, rank)])


def first_terms_kernel(own, block, top, sums, *, mask):
    sums[...] = top_term(own, top, 0) + top_term(block, top, mask)


def add_term_kernel(before, block, top, sums, *, mask):
    sums[...] = before[...] + top_term(block, top, mask)


def high_down_kernel(*refs, chips, levels):
    quads = chips // 2
    sums, block, top, refs = refs[0], refs[1], refs[2], refs[3:]
    matrices, kept, outs = refs[:levels], refs[levels : 2 * levels], refs[2 * levels : -1]
    below = refs[-1]
    rank = outs[0].shape[1]
    double = 2 * rank
    below[0] = (sums[...] + top_term(block, top, 1)).astype(BF16)
    for tier in range(levels - 1, 0, -1):
        values = []
        for e in range(quads >> tier + 1):
            rows = pl.ds(e * double, double)
            matrix = matrices[tier]
            children = descend(
                below[e], kept[tier][e], matrix[rows, pl.ds(0, double)], matrix[rows, pl.ds(double, rank)]
            )
            values += [children[:, :rank], children[:, rank:]]
        for e, value in enumerate(values):
            below[e] = value
    for i, out in enumerate(outs):
        at = jnp.where(in_lower(chips), i, quads - 1 - i)
        node = at // 2 if quads > 2 else 0
        start = node * double
        if quads > 2:
            start = pl.multiple_of(start, double)
        lifted = dot_right_t(below[node], matrices[0][pl.ds(start, double), pl.ds(double, rank)])
        rest = (kept[0][node].astype(F32) - lifted).astype(BF16)
        child = pl.multiple_of(start + at % 2 * rank, rank)
        out[...] = dot_right_t(rest, matrices[0][pl.ds(child, rank), pl.ds(0, double)]).astype(BF16)


def choose_kernel(*refs, chips):
    *parts, out = refs
    value = parts[0][...]
    for source, part in zip(inner_chips(chips), parts):
        value = jnp.where(mirrored(chip_of(), chips) == source, part[...], value)
    out[...] = value


def path_down_kernel(
    mine, other, quad_paired, quad_matrix, pair_paired, pair_matrix, keep, send, *, chips
):
    rank = keep.shape[1]
    double = 2 * rank
    inner = (chip_of() % 2 == 1) == in_lower(chips)
    parent = jnp.where(inner, mine[...], other[...])

    def children(paired, matrix, sides):
        lifted = dot_right_t(parent, matrix[:, pl.ds(double, rank)])
        rest = (paired[...].astype(F32) - lifted).astype(BF16)
        for side in sides:
            rows = pl.ds(pl.multiple_of(side * rank, rank), rank)
            yield dot_right_t(rest, matrix[rows, pl.ds(0, double)]).astype(BF16)

    (parent,) = children(quad_paired, quad_matrix, [chip_of() % 2])
    keep[...], send[...] = children(pair_paired, pair_matrix, [core_of(), 1 - core_of()])


def body(
    right_side,
    leaf_inverse,
    leaf_basis,
    local_merge,
    local_transfer,
    upper_merge,
    upper_transfer,
    top_inverse,
):
    leaf = leaf_inverse.shape[2]
    rank = leaf_basis.shape[2]
    columns = right_side.shape[2]
    double = 2 * rank
    wide = double + rank
    leaf_count = right_side.shape[1] // leaf
    sub_count = lax.axis_size("sub")
    sub_depth = sub_count.bit_length() - 1
    root_count = lax.axis_size("root")
    chips = sub_count // 2
    middle = chips // 2 - 1
    half = columns // 2
    heights = [double >> tier for tier in range(3, sub_depth + 1)]
    levels = len(heights)
    quads = chips // 2

    local = [right_side[0], leaf_inverse[0], leaf_basis[0]]
    tree = [local_merge[0], local_transfer[0]]
    blocks = wide // rank
    top_rows, top_width = top_inverse.shape
    quad_rows = blocks * (double // 4)
    top_block = top_rows * top_width // rank
    high_rows = blocks * sum(heights)
    any_spec, vmem_spec = pl.BlockSpec(memory_space=pl.ANY), pl.BlockSpec(memory_space=pltpu.VMEM)
    pair_rows = blocks * (double // 2)
    shapes = [(rows, rank) for rows in (pair_rows + quad_rows, quad_rows + top_block, high_rows)]
    args = [upper_merge[0], upper_transfer[0], top_inverse]
    low, quad_top, high = pl.pallas_call(
        pack_kernel,
        out_shape=[pltpu.VMEM(shape, BF16) for shape in shapes],
        in_specs=[any_spec] * len(args),
        out_specs=[vmem_spec] * len(shapes),
        scratch_shapes=[pltpu.SemaphoreType.DMA((3 * blocks + rank // top_width,))],
        compiler_params=pltpu.CompilerParams(vmem_limit_bytes=2 * MIB),
        cost_estimate=cost(1.5),
    )(*[pltpu.with_memory_space_constraint(a, pltpu.HBM) for a in args])
    far_high = flip(high, "sub", 2)
    far = flip(quad_top, "sub", 2)
    low_other = flip(low, "sub", 1)

    shapes = [
        (half, rank),
        (half, rank),
        (leaf_count // 2, columns, double),
        (leaf_count // 4, columns, double),
    ]
    given = local + tree
    fetched = [2]
    shapes += [given[i].shape for i in fetched]
    spaces = [pltpu.HBM if i in fetched else pltpu.VMEM for i in range(5)]
    given = [pltpu.with_memory_space_constraint(a, space) for a, space in zip(given, spaces)]
    keep, send, low_paired, high_paired, *moved = pl.pallas_call(
        functools.partial(climb_local_kernel, leaf_count=leaf_count, fetched=fetched),
        out_shape=[pltpu.VMEM(shape, BF16) for shape in shapes],
        in_specs=[any_spec if i in fetched else vmem_spec for i in range(5)],
        out_specs=[vmem_spec] * len(shapes),
        scratch_shapes=[
            pltpu.VMEM((columns, rank), BF16),
            pltpu.SemaphoreType.DMA((5 * leaf_count,)),
        ],
        compiler_params=pltpu.CompilerParams(vmem_limit_bytes=16 * MIB),
        cost_estimate=cost(0.01),
    )(*given)
    for i, array in zip(fetched, moved):
        given[i] = array

    recv = flip(send, "sub", 1)
    recv = passed(recv, 0.8)
    low_other, far_high, token = lax.optimization_barrier((low_other, far_high, mark(send)))
    (pair_matrix,) = vmem_call(pair_matrix_kernel, [(double, wide)], [low, low_other])
    (rows_mine,) = vmem_call(tails_kernel, [(2, high_rows, rank)], [high, far_high])
    inner = inner_chips(chips)
    others = [s for s in inner if s != middle]
    rows_rest = [swapped(rows_mine, s, middle, chips) for s in others]
    pair_paired, coeffs = vmem_call(
        pair_up_kernel,
        [(half, double), (half, rank)],
        [keep, recv, pair_matrix],
        micros=0.05,
        after=[token],
    )

    recv = flip(coeffs, "sub", 2)
    recv, rows_rest = lax.optimization_barrier((recv, rows_rest))
    recv = passed(recv, 10)
    far, token = lax.optimization_barrier((far, mark(coeffs)))
    (top_mine,) = vmem_call(tails_kernel, [(2, top_block, rank)], [quad_top, far])
    top_rest = [swapped(top_mine, s, middle, chips) for s in others]
    far_other = flip(far, "sub", 1)
    (quad_matrix,) = vmem_call(
        quad_matrix_kernel, [(double, wide)], [low, low_other, far, far_other], after=[recv]
    )
    quad_paired, coeffs = vmem_call(
        quad_up_kernel,
        [(half, double), (half, rank)],
        [coeffs, recv, quad_matrix],
        micros=0.05,
        after=[token],
    )

    own = inner.index(middle)
    parts = [swapped(coeffs, s, middle, chips) for s in others]
    parts, top_rest = lax.optimization_barrier((parts, top_rest))
    parts = [passed(part, 10) for part in parts]
    rows_rest, coeffs = lax.optimization_barrier((rows_rest, coeffs))
    stacks = [rows_mine, flip(rows_mine, "sub", 1)]
    for item in rows_rest:
        stacks += [item, flip(item, "sub", 1)]
    *high_matrices, = vmem_call(
        functools.partial(high_matrix_kernel, chips=chips, heights=heights),
        [(sub_count * height, wide) for height in heights],
        stacks,
        limit=8 * MIB,
        micros=0.2,
        after=parts,
    )
    *high_paired_up, coeffs = vmem_call(
        functools.partial(high_up_kernel, chips=chips, levels=levels),
        [(quads >> t + 1, half, double) for t in range(levels)] + [(half, rank)],
        parts[:own] + [coeffs] + parts[own:] + high_matrices,
        limit=8 * MIB,
        micros=0.4,
    )

    stacks = [top_mine, flip(top_mine, "sub", 1)]
    for item in top_rest:
        stacks += [item, flip(item, "sub", 1)]
    (top_matrix,) = vmem_call(
        functools.partial(top_matrix_kernel, chips=chips),
        [(top_rows, sub_count * top_width)],
        stacks,
        limit=8 * MIB,
    )
    came = [(mask, flip(coeffs, "root", mask)) for mask in range(root_count - 1, 0, -1)]
    kernel, sums = first_terms_kernel, coeffs
    if root_count == 2:
        came.insert(0, (1, jnp.zeros_like(coeffs)))
    for mask, block in came[:-1]:
        (sums,) = vmem_call(
            functools.partial(kernel, mask=mask),
            [(half, rank)],
            [sums, block, top_matrix],
            micros=0.01,
            kind=F32,
        )
        kernel = add_term_kernel
    values = vmem_call(
        functools.partial(high_down_kernel, chips=chips, levels=levels),
        [(half, rank)] * (quads // 2),
        [sums, came[-1][1], top_matrix] + high_matrices + high_paired_up,
        [pltpu.VMEM((max(quads // 2, 1), half, rank), BF16)],
        limit=8 * MIB,
        micros=0.7,
    )

    value = values[0]
    if len(values) > 1:
        parts = [
            part if s == middle else swapped(part, s, middle, chips)
            for s, part in zip(inner, values)
        ]
        (value,) = vmem_call(
            functools.partial(choose_kernel, chips=chips), [(half, rank)], parts
        )
    recv = flip(value, "sub", 2)
    keep, send = vmem_call(
        functools.partial(path_down_kernel, chips=chips),
        [(half, rank), (half, rank)],
        [value, recv, quad_paired, quad_matrix, pair_paired, pair_matrix],
        micros=0.4,
    )
    recv = flip(send, "sub", 1)

    args = [keep, recv, low_paired, high_paired] + given
    out = pl.pallas_call(
        descend_local_kernel,
        out_shape=jax.ShapeDtypeStruct((leaf_count * leaf, columns), F32),
        in_specs=[vmem_spec] * len(args),
        out_specs=any_spec,
        scratch_shapes=[
            pltpu.VMEM((columns, rank), BF16),
            pltpu.VMEM((leaf_count, leaf, columns), F32),
            pltpu.SemaphoreType.DMA((leaf_count + 1,)),
        ],
        compiler_params=pltpu.CompilerParams(vmem_limit_bytes=16 * MIB),
        cost_estimate=cost(3),
    )(*[pltpu.with_memory_space_constraint(a, pltpu.VMEM) for a in args])
    return out[None]


def solution(mesh):
    return jax.shard_map(
        body,
        mesh=mesh,
        in_specs=(
            P("root", "sub", None),
            P("root", "sub", None),
            P("root", "sub", None),
            P("root", "sub", None),
            P("root", "sub", None),
            P("root", "sub", None),
            P("root", "sub", None),
            P("root", "sub"),
        ),
        out_specs=P("root", "sub", None),
        check_vma=False,
    )
```

```python
import functools

import jax
import jax.numpy as jnp
from jax import lax
from jax.experimental import pallas as pl
from jax.experimental.pallas import tpu as pltpu
from jax.sharding import PartitionSpec as P

BF16 = jnp.bfloat16
F32 = jnp.float32
MIB = 1 << 20


def dot(left, right):
    return lax.dot_general(left, right, (((1,), (0,)), ((), ())), preferred_element_type=F32)


def dot_left_t(left, right):
    return lax.dot_general(left, right, (((0,), (0,)), ((), ())), preferred_element_type=F32)


def dot_right_t(left, right):
    return lax.dot_general(left, right, (((1,), (1,)), ((), ())), preferred_element_type=F32)


def cost(micros):
    return pl.CostEstimate(flops=int(micros * 1e9), bytes_accessed=1, transcendentals=0)


def vmem_call(kernel, outs, args, scratch=(), limit=4 * MIB, micros=0.1, after=(), kind=BF16):
    count = len(args)
    args = list(args) + list(after)
    return pl.pallas_call(
        lambda *refs: kernel(*refs[:count], *refs[len(args) :]),
        out_shape=[pltpu.VMEM(shape, kind) for shape in outs],
        in_specs=[pl.BlockSpec(memory_space=pltpu.VMEM)] * len(args),
        out_specs=[pl.BlockSpec(memory_space=pltpu.VMEM)] * len(outs),
        scratch_shapes=list(scratch),
        compiler_params=pltpu.CompilerParams(vmem_limit_bytes=limit),
        cost_estimate=cost(micros),
    )(*[pltpu.with_memory_space_constraint(a, pltpu.VMEM) for a in args])


def copy_kernel(value, out):
    out[...] = value[...]


def passed(value, micros):
    return vmem_call(copy_kernel, [value.shape], [value], micros=micros)[0]


def mark_kernel(value, out):
    out[...] = value[pl.ds(0, out.shape[0]), pl.ds(0, out.shape[1])]


def mark(value):
    return vmem_call(mark_kernel, [(16, 128)], [value], micros=0.02)[0]


def flip(block, axis, mask):
    count = lax.axis_size(axis)
    return lax.ppermute(block, axis, [(i, i ^ mask) for i in range(count)])


def swap_with(source, target, chips):
    partner = [device ^ 1 for device in range(2 * chips)]
    for low, high in ((source, target), (chips - 1 - source, chips - 1 - target)):
        for core in range(2):
            partner[2 * low + core], partner[2 * high + core] = 2 * high + core, 2 * low + core
    return list(enumerate(partner))


def inner_chips(chips):
    return [chip for chip in range(chips) if (chip % 2 == 1) == (chip < chips // 2)]


def swapped(block, source, target, chips):
    return lax.ppermute(block, "sub", swap_with(source, target, chips))


def core_of():
    return lax.axis_index("sub") % 2


def chip_of():
    return lax.axis_index("sub") // 2


def in_lower(chips):
    return chip_of() < chips // 2


def mirrored(chip, chips):
    return jnp.where(in_lower(chips), chip, chips - 1 - chip)


def split_rows(value, first, keep, send, work):
    half = value.shape[0] // 2
    work[...] = value
    keep[...] = work[pl.ds(pl.multiple_of(first * half, half), half), :]
    send[...] = work[pl.ds(pl.multiple_of((1 - first) * half, half), half), :]


def join_rows(mine, other, first, work):
    half = mine.shape[0]
    work[pl.ds(pl.multiple_of(first * half, half), half), :] = mine
    work[pl.ds(pl.multiple_of((1 - first) * half, half), half), :] = other


def join_lanes(mine, other, first, work):
    half = mine.shape[1]
    work[:, pl.ds(pl.multiple_of(first * half, half), half)] = mine
    work[:, pl.ds(pl.multiple_of((1 - first) * half, half), half)] = other


def climb(paired, merge_mat, transfer):
    inner = dot_right_t(paired, merge_mat).astype(BF16)
    return dot(inner, transfer).astype(BF16)


def descend(parent, paired, merge_mat, transfer):
    rest = (paired.astype(F32) - dot_right_t(parent, transfer)).astype(BF16)
    return dot_right_t(rest, merge_mat).astype(BF16)


def pack_kernel(merge, transfer, top, *refs):
    low, quad_top, high, sems = refs
    rows, double = merge.shape
    rank = transfer.shape[1]
    steps = []

    def fetch(source, target):
        steps.append(pltpu.make_async_copy(source, target, sems.at[len(steps)]))

    def level_rows(low, size, target, at):
        for lanes in range(double // rank):
            fetch(
                merge.at[pl.ds(low, size), pl.ds(lanes * rank, rank)], target.at[pl.ds(at, size), :]
            )
            at += size
        fetch(transfer.at[pl.ds(low, size), :], target.at[pl.ds(at, size), :])
        return at + size

    quad_low, high_low = double // 2, double // 2 + double // 4
    level_rows(high_low, rows - high_low, high, 0)
    quad_rows = level_rows(quad_low, high_low - quad_low, quad_top, 0)
    width = top.shape[1]
    size = top.shape[0] * width // rank
    for piece in range(rank // width):
        fetch(
            top.at[pl.ds(piece * size, size), :],
            quad_top.at[pl.ds(quad_rows, size), pl.ds(piece * width, width)],
        )
    pair_rows = level_rows(0, quad_low, low, 0)
    for step in steps:
        step.start()
    for step in steps:
        step.wait()
    low[pl.ds(pair_rows, quad_rows), :] = quad_top[pl.ds(0, quad_rows), :]


def climb_local_kernel(*refs, leaf_count, fetched):
    arrays = list(refs[:5])
    keep, send, low_paired, high_paired = refs[5:9]
    kept = {1: low_paired, 2: high_paired}
    *outs, work, sems = refs[9:]
    leaf = arrays[0].shape[0] // leaf_count
    rank = arrays[2].shape[1]
    double = 2 * rank
    depth = leaf_count.bit_length() - 1
    copies = {}
    for index, out in zip(fetched, outs):
        block = leaf if index < 3 else double
        for i in range(out.shape[0] // block):
            rows = pl.ds(i * block, block)
            copies[index, i] = pltpu.make_async_copy(
                arrays[index].at[rows, :], out.at[rows, :], sems.at[len(copies)]
            )
        arrays[index] = out
    for key in sorted(copies, key=lambda key: (key[0] // 3, key[1])):
        copies[key].start()

    def ready(index, i):
        if (index, i) in copies:
            copies[index, i].wait()

    sides, inverse, basis, merge, transfer = arrays
    products = []
    for i in range(leaf_count):
        rows = pl.ds(i * leaf, leaf)
        for index in range(2):
            ready(index, i)
        columns = jnp.transpose(sides[rows, :])
        products.append(dot_right_t(columns, inverse[rows, :]).astype(BF16))
    for i in range(leaf_count):
        ready(2, i)
        coeffs = dot(products[i], basis[pl.ds(i * leaf, leaf), :]).astype(BF16)
        kept[1][i // 2, :, pl.ds((i % 2) * rank, rank)] = coeffs
    for e in range(leaf_count - 1):
        for index in (3, 4):
            ready(index, e)
    for tier in range(1, depth + 1):
        count = leaf_count >> tier
        start = leaf_count - 2 * count
        for e in range(count):
            rows = pl.ds((start + e) * double, double)
            coeffs = climb(kept[tier][e], merge[rows, :], transfer[rows, :])
            if tier < depth:
                kept[tier + 1][e // 2, :, pl.ds((e % 2) * rank, rank)] = coeffs
            else:
                split_rows(coeffs, core_of(), keep, send, work)


def descend_local_kernel(
    mine, other, low_paired, high_paired, sides, inverse, basis, merge, transfer, out, parent, result, sems
):
    leaf = inverse.shape[1]
    rank = basis.shape[1]
    double = 2 * rank
    kept = {1: low_paired, 2: high_paired}
    leaf_count = out.shape[0] // leaf
    depth = leaf_count.bit_length() - 1
    join_rows(mine[...], other[...], core_of(), parent)
    level = [parent[...]]
    for tier in range(depth, 0, -1):
        nodes = leaf_count >> tier
        start = leaf_count - 2 * nodes
        below = []
        for e in range(nodes):
            rows = pl.ds((start + e) * double, double)
            children = descend(level[e], kept[tier][e], merge[rows, :], transfer[rows, :])
            below += [children[:, :rank], children[:, rank:]]
        level = below
    rests = []
    for i in range(leaf_count):
        rows = pl.ds(i * leaf, leaf)
        spread = dot_right_t(basis[rows, :], level[i])
        rests.append((sides[rows, :].astype(F32) - spread).astype(BF16))
    copies = []
    for i in range(leaf_count):
        rows = pl.ds(i * leaf, leaf)
        result[i] = dot(inverse[rows, :], rests[i])
        copies.append(pltpu.make_async_copy(result.at[i], out.at[rows, :], sems.at[i]))
        copies[-1].start()
    for copy in copies:
        copy.wait()


def place_rows(block, low, size, out, at):
    width = block.shape[-1]
    for lanes in range(out.shape[1] // width):
        out[pl.ds(at, size), pl.ds(lanes * width, width)] = block[pl.ds(low + lanes * size, size), :]


def pair_matrix_kernel(mine, other, out):
    size = out.shape[0] // 2
    core = core_of()
    place_rows(mine, 0, size, out, pl.multiple_of(core * size, size))
    place_rows(other, 0, size, out, pl.multiple_of((1 - core) * size, size))


def quad_matrix_kernel(mine, other, far, far_other, out):
    size = out.shape[0] // 4
    core, side = core_of(), chip_of() % 2
    start = mine.shape[0] - out.shape[1] // mine.shape[1] * size
    blocks = [(side, core, mine, start), (side, 1 - core, other, start)]
    blocks += [(1 - side, core, far, 0), (1 - side, 1 - core, far_other, 0)]
    for chip, which, ref, low in blocks:
        place_rows(ref, low, size, out, pl.multiple_of((2 * chip + which) * size, size))


def tails_kernel(mine, far, out):
    for i, ref in enumerate((mine, far)):
        out[i] = ref[pl.ds(ref.shape[0] - out.shape[1], out.shape[1]), :]


def extend_kernel(mine, other, out):
    out[pl.ds(0, mine.shape[0]), :] = mine[...]
    out[pl.ds(mine.shape[0], other.shape[0]), :] = other[...]


def stack_kernel(*refs):
    *ins, out = refs
    at = 0
    for ref in ins:
        if len(ref.shape) == 2:
            out[at] = ref[...]
            at += 1
        else:
            out[pl.ds(at, ref.shape[0])] = ref[...]
            at += ref.shape[0]


def device_blocks(refs, chips):
    inner, core = inner_chips(chips), core_of()
    own = inner.index(chips // 2 - 1)
    order = [inner[own]] + inner[:own] + inner[own + 1 :]
    for source, mine, other in zip(order, refs[::2], refs[1::2]):
        for i, chip in enumerate((source, source ^ 1)):
            for which, ref in ((core, mine), (1 - core, other)):
                yield 2 * mirrored(chip, chips) + which, ref.at[i]


def high_matrix_kernel(*refs, chips, heights):
    refs, outs = refs[: -len(heights)], refs[-len(heights) :]
    rows = sum(heights)
    for device, ref in device_blocks(refs, chips):
        offset = 0
        for out, height in zip(outs, heights):
            width = ref.shape[-1]
            for lanes in range(out.shape[1] // width):
                out[
                    pl.ds(pl.multiple_of(device * height, height), height),
                    pl.ds(lanes * width, width),
                ] = ref[pl.ds(lanes * rows + offset, height), :]
            offset += height


def top_matrix_kernel(*refs, chips):
    refs, top = refs[:-1], refs[-1]
    width = top.shape[1] // (2 * chips)
    for device, ref in device_blocks(refs, chips):
        size = top.shape[0] * width // ref.shape[-1]
        for piece in range(ref.shape[-1] // width):
            top[pl.ds(piece * size, size), pl.ds(pl.multiple_of(device * width, width), width)] = ref[
                :, pl.ds(piece * width, width)
            ]


def pair_up_kernel(mine, other, matrix, paired, coeffs):
    double = paired.shape[1]
    join_lanes(mine[...], other[...], core_of(), paired)
    coeffs[...] = climb(
        paired[...], matrix[:, pl.ds(0, double)], matrix[:, pl.ds(double, double // 2)]
    )


def quad_up_kernel(mine, other, matrix, paired, coeffs):
    double = paired.shape[1]
    join_lanes(mine[...], other[...], chip_of() % 2, paired)
    coeffs[...] = climb(
        paired[...], matrix[:, pl.ds(0, double)], matrix[:, pl.ds(double, double // 2)]
    )


def high_up_kernel(*refs, chips, levels):
    quads = chips // 2
    parts, matrices = refs[:quads], refs[quads : quads + levels]
    kept, coeffs = refs[quads + levels : quads + 2 * levels], refs[-1]
    rank = coeffs.shape[1]
    double = 2 * rank
    for i, part in enumerate(parts):
        at = jnp.where(in_lower(chips), i, quads - 1 - i)
        lanes = pl.ds(pl.multiple_of((at % 2) * rank, rank), rank)
        kept[0][at // 2, :, lanes] = part[...]
    for tier in range(levels):
        nodes = quads >> tier + 1
        for e in range(nodes):
            rows = pl.ds(e * double, double)
            matrix = matrices[tier]
            value = climb(
                kept[tier][e], matrix[rows, pl.ds(0, double)], matrix[rows, pl.ds(double, rank)]
            )
            if tier + 1 < levels:
                kept[tier + 1][e // 2, :, pl.ds((e % 2) * rank, rank)] = value
            else:
                coeffs[...] = value


def top_term(block, top, mask):
    rank = block.shape[1]
    at = pl.multiple_of((lax.axis_index("root") ^ mask) * rank, rank)
    return dot_right_t(block[...], top[:, pl.ds(at, rank)])


def first_terms_kernel(own, block, top, sums, *, mask):
    sums[...] = top_term(own, top, 0) + top_term(block, top, mask)


def add_term_kernel(before, block, top, sums, *, mask):
    sums[...] = before[...] + top_term(block, top, mask)


def high_down_kernel(*refs, chips, levels):
    quads = chips // 2
    sums, block, top, refs = refs[0], refs[1], refs[2], refs[3:]
    matrices, kept, outs = refs[:levels], refs[levels : 2 * levels], refs[2 * levels : -1]
    below = refs[-1]
    rank = outs[0].shape[1]
    double = 2 * rank
    below[0] = (sums[...] + top_term(block, top, 1)).astype(BF16)
    for tier in range(levels - 1, 0, -1):
        values = []
        for e in range(quads >> tier + 1):
            rows = pl.ds(e * double, double)
            matrix = matrices[tier]
            children = descend(
                below[e], kept[tier][e], matrix[rows, pl.ds(0, double)], matrix[rows, pl.ds(double, rank)]
            )
            values += [children[:, :rank], children[:, rank:]]
        for e, value in enumerate(values):
            below[e] = value
    for i, out in enumerate(outs):
        at = jnp.where(in_lower(chips), i, quads - 1 - i)
        node = at // 2 if quads > 2 else 0
        start = node * double
        if quads > 2:
            start = pl.multiple_of(start, double)
        lifted = dot_right_t(below[node], matrices[0][pl.ds(start, double), pl.ds(double, rank)])
        rest = (kept[0][node].astype(F32) - lifted).astype(BF16)
        child = pl.multiple_of(start + at % 2 * rank, rank)
        out[...] = dot_right_t(rest, matrices[0][pl.ds(child, rank), pl.ds(0, double)]).astype(BF16)


def choose_kernel(*refs, chips):
    *parts, out = refs
    value = parts[0][...]
    for source, part in zip(inner_chips(chips), parts):
        value = jnp.where(mirrored(chip_of(), chips) == source, part[...], value)
    out[...] = value


def path_down_kernel(
    mine, other, quad_paired, quad_matrix, pair_paired, pair_matrix, keep, send, *, chips
):
    rank = keep.shape[1]
    double = 2 * rank
    inner = (chip_of() % 2 == 1) == in_lower(chips)
    parent = jnp.where(inner, mine[...], other[...])

    def children(paired, matrix, sides):
        lifted = dot_right_t(parent, matrix[:, pl.ds(double, rank)])
        rest = (paired[...].astype(F32) - lifted).astype(BF16)
        for side in sides:
            rows = pl.ds(pl.multiple_of(side * rank, rank), rank)
            yield dot_right_t(rest, matrix[rows, pl.ds(0, double)]).astype(BF16)

    (parent,) = children(quad_paired, quad_matrix, [chip_of() % 2])
    keep[...], send[...] = children(pair_paired, pair_matrix, [core_of(), 1 - core_of()])


def body(
    right_side,
    leaf_inverse,
    leaf_basis,
    local_merge,
    local_transfer,
    upper_merge,
    upper_transfer,
    top_inverse,
):
    leaf = leaf_inverse.shape[2]
    rank = leaf_basis.shape[2]
    columns = right_side.shape[2]
    double = 2 * rank
    wide = double + rank
    leaf_count = right_side.shape[1] // leaf
    sub_count = lax.axis_size("sub")
    sub_depth = sub_count.bit_length() - 1
    root_count = lax.axis_size("root")
    chips = sub_count // 2
    middle = chips // 2 - 1
    half = columns // 2
    heights = [double >> tier for tier in range(3, sub_depth + 1)]
    levels = len(heights)
    quads = chips // 2

    local = [right_side[0], leaf_inverse[0], leaf_basis[0]]
    tree = [local_merge[0], local_transfer[0]]
    blocks = wide // rank
    top_rows, top_width = top_inverse.shape
    quad_rows = blocks * (double // 4)
    top_block = top_rows * top_width // rank
    high_rows = blocks * sum(heights)
    any_spec, vmem_spec = pl.BlockSpec(memory_space=pl.ANY), pl.BlockSpec(memory_space=pltpu.VMEM)
    pair_rows = blocks * (double // 2)
    shapes = [(rows, rank) for rows in (pair_rows + quad_rows, quad_rows + top_block, high_rows)]
    args = [upper_merge[0], upper_transfer[0], top_inverse]
    low, quad_top, high = pl.pallas_call(
        pack_kernel,
        out_shape=[pltpu.VMEM(shape, BF16) for shape in shapes],
        in_specs=[any_spec] * len(args),
        out_specs=[vmem_spec] * len(shapes),
        scratch_shapes=[pltpu.SemaphoreType.DMA((3 * blocks + rank // top_width,))],
        compiler_params=pltpu.CompilerParams(vmem_limit_bytes=2 * MIB),
        cost_estimate=cost(1.5),
    )(*[pltpu.with_memory_space_constraint(a, pltpu.HBM) for a in args])
    far_high = flip(high, "sub", 2)
    far = flip(quad_top, "sub", 2)
    low_other = flip(low, "sub", 1)

    shapes = [
        (half, rank),
        (half, rank),
        (leaf_count // 2, columns, double),
        (leaf_count // 4, columns, double),
    ]
    given = local + tree
    fetched = [2]
    shapes += [given[i].shape for i in fetched]
    spaces = [pltpu.HBM if i in fetched else pltpu.VMEM for i in range(5)]
    given = [pltpu.with_memory_space_constraint(a, space) for a, space in zip(given, spaces)]
    keep, send, low_paired, high_paired, *moved = pl.pallas_call(
        functools.partial(climb_local_kernel, leaf_count=leaf_count, fetched=fetched),
        out_shape=[pltpu.VMEM(shape, BF16) for shape in shapes],
        in_specs=[any_spec if i in fetched else vmem_spec for i in range(5)],
        out_specs=[vmem_spec] * len(shapes),
        scratch_shapes=[
            pltpu.VMEM((columns, rank), BF16),
            pltpu.SemaphoreType.DMA((5 * leaf_count,)),
        ],
        compiler_params=pltpu.CompilerParams(vmem_limit_bytes=16 * MIB),
        cost_estimate=cost(0.01),
    )(*given)
    for i, array in zip(fetched, moved):
        given[i] = array

    recv = flip(send, "sub", 1)
    recv = passed(recv, 0.8)
    low_other, far_high, token = lax.optimization_barrier((low_other, far_high, mark(send)))
    (pair_matrix,) = vmem_call(pair_matrix_kernel, [(double, wide)], [low, low_other])
    (rows_mine,) = vmem_call(tails_kernel, [(2, high_rows, rank)], [high, far_high])
    inner = inner_chips(chips)
    others = [s for s in inner if s != middle]
    rows_rest = [swapped(rows_mine, s, middle, chips) for s in others]
    pair_paired, coeffs = vmem_call(
        pair_up_kernel,
        [(half, double), (half, rank)],
        [keep, recv, pair_matrix],
        micros=0.05,
        after=[token],
    )

    recv = flip(coeffs, "sub", 2)
    recv, rows_rest = lax.optimization_barrier((recv, rows_rest))
    recv = passed(recv, 10)
    far, token = lax.optimization_barrier((far, mark(coeffs)))
    (top_mine,) = vmem_call(tails_kernel, [(2, top_block, rank)], [quad_top, far])
    top_rest = [swapped(top_mine, s, middle, chips) for s in others]
    far_other = flip(far, "sub", 1)
    (quad_matrix,) = vmem_call(
        quad_matrix_kernel, [(double, wide)], [low, low_other, far, far_other], after=[recv]
    )
    quad_paired, coeffs = vmem_call(
        quad_up_kernel,
        [(half, double), (half, rank)],
        [coeffs, recv, quad_matrix],
        micros=0.05,
        after=[token],
    )

    own = inner.index(middle)
    parts = [swapped(coeffs, s, middle, chips) for s in others]
    parts, top_rest = lax.optimization_barrier((parts, top_rest))
    parts = [passed(part, 10) for part in parts]
    rows_rest, coeffs = lax.optimization_barrier((rows_rest, coeffs))
    stacks = [rows_mine, flip(rows_mine, "sub", 1)]
    for item in rows_rest:
        stacks += [item, flip(item, "sub", 1)]
    *high_matrices, = vmem_call(
        functools.partial(high_matrix_kernel, chips=chips, heights=heights),
        [(sub_count * height, wide) for height in heights],
        stacks,
        limit=8 * MIB,
        micros=0.2,
        after=parts,
    )
    *high_paired_up, coeffs = vmem_call(
        functools.partial(high_up_kernel, chips=chips, levels=levels),
        [(quads >> t + 1, half, double) for t in range(levels)] + [(half, rank)],
        parts[:own] + [coeffs] + parts[own:] + high_matrices,
        limit=8 * MIB,
        micros=0.4,
    )

    stacks = [top_mine, flip(top_mine, "sub", 1)]
    for item in top_rest:
        stacks += [item, flip(item, "sub", 1)]
    (top_matrix,) = vmem_call(
        functools.partial(top_matrix_kernel, chips=chips),
        [(top_rows, sub_count * top_width)],
        stacks,
        limit=8 * MIB,
    )
    came = [(mask, flip(coeffs, "root", mask)) for mask in range(root_count - 1, 0, -1)]
    kernel, sums = first_terms_kernel, coeffs
    if root_count == 2:
        came.insert(0, (1, jnp.zeros_like(coeffs)))
    for mask, block in came[:-1]:
        (sums,) = vmem_call(
            functools.partial(kernel, mask=mask),
            [(half, rank)],
            [sums, block, top_matrix],
            micros=0.01,
            kind=F32,
        )
        kernel = add_term_kernel
    values = vmem_call(
        functools.partial(high_down_kernel, chips=chips, levels=levels),
        [(half, rank)] * (quads // 2),
        [sums, came[-1][1], top_matrix] + high_matrices + high_paired_up,
        [pltpu.VMEM((max(quads // 2, 1), half, rank), BF16)],
        limit=8 * MIB,
        micros=0.7,
    )

    value = values[0]
    if len(values) > 1:
        parts = [
            part if s == middle else swapped(part, s, middle, chips)
            for s, part in zip(inner, values)
        ]
        (value,) = vmem_call(
            functools.partial(choose_kernel, chips=chips), [(half, rank)], parts
        )
    recv = flip(value, "sub", 2)
    keep, send = vmem_call(
        functools.partial(path_down_kernel, chips=chips),
        [(half, rank), (half, rank)],
        [value, recv, quad_paired, quad_matrix, pair_paired, pair_matrix],
        micros=0.4,
    )
    recv = flip(send, "sub", 1)

    args = [keep, recv, low_paired, high_paired] + given
    out = pl.pallas_call(
        descend_local_kernel,
        out_shape=jax.ShapeDtypeStruct((leaf_count * leaf, columns), F32),
        in_specs=[vmem_spec] * len(args),
        out_specs=any_spec,
        scratch_shapes=[
            pltpu.VMEM((columns, rank), BF16),
            pltpu.VMEM((leaf_count, leaf, columns), F32),
            pltpu.SemaphoreType.DMA((leaf_count,)),
        ],
        compiler_params=pltpu.CompilerParams(vmem_limit_bytes=16 * MIB),
        cost_estimate=cost(3),
    )(*[pltpu.with_memory_space_constraint(a, pltpu.VMEM) for a in args])
    return out[None]


def solution(mesh):
    return jax.shard_map(
        body,
        mesh=mesh,
        in_specs=(
            P("root", "sub", None),
            P("root", "sub", None),
            P("root", "sub", None),
            P("root", "sub", None),
            P("root", "sub", None),
            P("root", "sub", None),
            P("root", "sub", None),
            P("root", "sub"),
        ),
        out_specs=P("root", "sub", None),
        check_vma=False,
    )
```
